32 devices in a mesh: dp: 16 (over z, y, core), blk: 2 (over x).
Axes of the slice: x: 2, y: 2, z: 4, core: 2. Of those that a mesh axis runs over, the one named last changes fastest.
Arguments:
- inputs: bfloat16 [16, 1024, 512], P('dp', 'blk'), may hold values from -6 to 6
- memory: bfloat16 [16, 1024, 512], P('dp', 'blk'), may hold values from -6 to 6
- cotangent: bfloat16 [16, 1024, 512], P('dp', 'blk'), may hold values from -6 to 6
- target_segments: int32 [16, 1024], P('dp'), may hold values from 0 to 16, as said below
- memory_segments: int32 [16, 1024], P('dp'), may hold values from 0 to 16, as said below
- self_in_weight: bfloat16 [512, 1536], replicated, may hold values from -0.25 to 0.25
- self_in_bias: float32 [2, 512], replicated, may hold values from -1.75 to 1.75
- self_out_weight: bfloat16 [512, 512], replicated, may hold values from -1 to 1
- self_out_bias: float32 [512], replicated, may hold values from -1.75 to 1.75
- first_gain: float32 [512], replicated, may hold values from 0.5 to 1.5
- first_shift: float32 [512], replicated, may hold values from -1.75 to 1.75
- cross_query_weight: bfloat16 [512, 512], replicated, may hold values from -0.25 to 0.25
- cross_pair_weight: bfloat16 [512, 1024], replicated, may hold values from -0.25 to 0.25
- cross_bias: float32 [2, 512], replicated, may hold values from -1.75 to 1.75
- cross_out_weight: bfloat16 [512, 512], replicated, may hold values from -1 to 1
- cross_out_bias: float32 [512], replicated, may hold values from -1.75 to 1.75
- second_gain: float32 [512], replicated, may hold values from 0.5 to 1.5
- second_shift: float32 [512], replicated, may hold values from -1.75 to 1.75
- feed_in_weight: bfloat16 [512, 2048], replicated, may hold values from -0.25 to 0.25
- feed_in_bias: float32 [2048], replicated, may hold values from -1.75 to 1.75
- feed_out_weight: bfloat16 [2048, 512], replicated, may hold values from -0.125 to 0.125
- feed_out_bias: float32 [512], replicated, may hold values from -1.75 to 1.75
- third_gain: float32 [512], replicated, may hold values from 0.5 to 1.5
- third_shift: float32 [512], replicated, may hold values from -1.75 to 1.75
Outputs:
- layer_output: bfloat16 [16, 1024, 512], P('dp', 'blk')
- input_grad: float32 [16, 1024, 512], P('dp', 'blk')
- memory_grad: float32 [16, 1024, 512], P('dp', 'blk')
- self_in_weight_grad: float32 [512, 1536], P('blk')
- self_in_bias_grad: float32 [2, 512], P(None, 'blk')
- self_out_weight_grad: float32 [512, 512], P('blk')
- self_out_bias_grad: float32 [512], P('blk')
- first_gain_grad: float32 [512], P('blk')
- first_shift_grad: float32 [512], P('blk')
- cross_query_weight_grad: float32 [512, 512], P('blk')
- cross_pair_weight_grad: float32 [512, 1024], P('blk')
- cross_bias_grad: float32 [2, 512], P(None, 'blk')
- cross_out_weight_grad: float32 [512, 512], P('blk')
- cross_out_bias_grad: float32 [512], P('blk')
- second_gain_grad: float32 [512], P('blk')
- second_shift_grad: float32 [512], P('blk')
- feed_in_weight_grad: float32 [512, 2048], P('blk')
- feed_in_bias_grad: float32 [2048], P('blk')
- feed_out_weight_grad: float32 [2048, 512], P('blk')
- feed_out_bias_grad: float32 [512], P('blk')
- third_gain_grad: float32 [512], P('blk')
- third_shift_grad: float32 [512], P('blk')
The draws below stay inside these ranges and needn't reach their ends.
Inputs may be any that keep to these rules, and one draw needn't show every extreme that they name: `target_segments`: numbers never fall along a row, every number occurs in every row, most sentences are short, and one sentence of each row begins among its first 512 positions and ends among its last 512. `memory_segments`: numbers never fall along a row, every number occurs in every row, most sentences are short, and one sentence of each row begins among its first 512 positions and ends among its last 512.
All inputs are finite; a program needn't handle non-finite values.
Results may differ from the reference program's by a relative error of at most 0.03.
Values may be sent and summed in bfloat16 or wider, within the bound.
A program may use at most 192 MiB of HBM per device.

```python
import jax
import jax.numpy as jnp
from jax import lax

D = 512
HEADS = 8
HEAD = 64
FF = 2048
TOK_DEV = 512
ROWS = 16
SEQ = 1024


def segment_numbers(key, row_count, length, device_tokens):
    count = max(1, min(8, device_tokens // 8))
    short_most = max(1, min(250, (device_tokens - 1) // count))
    pieces = jax.random.randint(key, (row_count, 2 * count), 1, short_most + 1, dtype=jnp.int32)
    head_bounds = jnp.cumsum(pieces[:, :count], axis=1).astype(jnp.int32)
    tail_sums = jnp.cumsum(pieces[:, count:], axis=1).astype(jnp.int32)
    tail_start = length - tail_sums[:, -1:]
    tail_bounds = tail_start + jnp.concatenate([jnp.zeros((row_count, 1), jnp.int32), tail_sums[:, :-1]], axis=1)
    bounds = jnp.concatenate([head_bounds, tail_bounds], axis=1)
    positions = jnp.arange(length, dtype=jnp.int32)
    return jnp.sum((positions[None, :, None] >= bounds[:, None, :]).astype(jnp.int32), axis=-1).astype(jnp.int32)


def draw_target_segments(key, part):
    key = jax.random.fold_in(key, 3)
    return segment_numbers(key, ROWS, SEQ, TOK_DEV)


def draw_memory_segments(key, part):
    key = jax.random.fold_in(key, 7)
    return segment_numbers(key, ROWS, SEQ, TOK_DEV)


def steps_of(key, extent, shards, low, high):
    def one(position, shards_of):
        heights = jax.random.uniform(jax.random.fold_in(jax.random.fold_in(key, 6), position), (shards_of,), jnp.float32, low / len(shards), high / len(shards))
        return jnp.repeat(jnp.exp(heights), extent[position] // shards_of).reshape((-1,) + (1,) * (len(extent) - position - 1))

    factor_of = one(*shards[0])
    for cut in shards[1:]:
        factor_of = factor_of * one(*cut)
    return factor_of


def scatter_about(own_key, extent, deviation, most, split=(), held_as=jnp.bfloat16):
    values = jax.random.normal(own_key, extent, jnp.float32) * deviation
    if len(split) > 0:
        values = steps_of(own_key, extent, split, -0.22, 0.18) * values
    return jnp.clip(values, min=-most, max=most).astype(held_as)


def setup_inputs(seed: int = 0) -> dict:
    arg_keys = jax.random.split(jax.random.key(seed), 25)
    inputs = scatter_about(arg_keys[0], (ROWS, SEQ, D), 1.0, 6.0, ((0, 16), (1, 2)))
    memory = scatter_about(arg_keys[1], (ROWS, SEQ, D), 1.0, 6.0, ((0, 16), (1, 2)))
    cotangent = scatter_about(arg_keys[2], (ROWS, SEQ, D), 1.0, 6.0, ((0, 16), (1, 2)))
    target_segments = draw_target_segments(jax.random.fold_in(arg_keys[24], 71), 0)
    memory_segments = draw_memory_segments(jax.random.fold_in(arg_keys[24], 71), 0)
    self_in_weight = scatter_about(arg_keys[5], (D, 3 * D), D ** -0.5, 0.25)
    self_in_bias = scatter_about(arg_keys[6], (2, D), 0.3, 1.75, (), jnp.float32)
    self_out_weight = scatter_about(arg_keys[7], (D, D), (D // 16) ** -0.5, 1.0)
    self_out_bias = scatter_about(arg_keys[8], (D,), 0.3, 1.75, (), jnp.float32)
    first_gain = jnp.clip(1.0 + 0.1 * jax.random.normal(arg_keys[9], (D,), jnp.float32), 0.5, 1.5)
    first_shift = scatter_about(arg_keys[10], (D,), 0.3, 1.75, (), jnp.float32)
    cross_query_weight = scatter_about(arg_keys[11], (D, D), D ** -0.5, 0.25)
    cross_pair_weight = scatter_about(arg_keys[12], (D, 2 * D), D ** -0.5, 0.25)
    cross_bias = scatter_about(arg_keys[13], (2, D), 0.3, 1.75, (), jnp.float32)
    cross_out_weight = scatter_about(arg_keys[14], (D, D), (D // 16) ** -0.5, 1.0)
    cross_out_bias = scatter_about(arg_keys[15], (D,), 0.3, 1.75, (), jnp.float32)
    second_gain = jnp.clip(1.0 + 0.1 * jax.random.normal(arg_keys[16], (D,), jnp.float32), 0.5, 1.5)
    second_shift = scatter_about(arg_keys[17], (D,), 0.3, 1.75, (), jnp.float32)
    feed_in_weight = scatter_about(arg_keys[18], (D, FF), D ** -0.5, 0.25)
    feed_in_bias = scatter_about(arg_keys[19], (FF,), 0.3, 1.75, (), jnp.float32)
    feed_out_weight = scatter_about(arg_keys[20], (FF, D), FF ** -0.5, 0.125)
    feed_out_bias = scatter_about(arg_keys[21], (D,), 0.3, 1.75, (), jnp.float32)
    third_gain = jnp.clip(1.0 + 0.1 * jax.random.normal(arg_keys[22], (D,), jnp.float32), 0.5, 1.5)
    third_shift = scatter_about(arg_keys[23], (D,), 0.3, 1.75, (), jnp.float32)
    return {"inputs": inputs, "memory": memory, "cotangent": cotangent, "target_segments": target_segments, "memory_segments": memory_segments, "self_in_weight": self_in_weight, "self_in_bias": self_in_bias, "self_out_weight": self_out_weight, "self_out_bias": self_out_bias, "first_gain": first_gain, "first_shift": first_shift, "cross_query_weight": cross_query_weight, "cross_pair_weight": cross_pair_weight, "cross_bias": cross_bias, "cross_out_weight": cross_out_weight, "cross_out_bias": cross_out_bias, "second_gain": second_gain, "second_shift": second_shift, "feed_in_weight": feed_in_weight, "feed_in_bias": feed_in_bias, "feed_out_weight": feed_out_weight, "feed_out_bias": feed_out_bias, "third_gain": third_gain, "third_shift": third_shift}


@jax.custom_vjp
def low(v):
    return lax.optimization_barrier(v.astype(jnp.bfloat16)).astype(jnp.float32)

@jax.custom_vjp
def low_back(v):
    return v

def low_keep(v):
    return (low(v), None)

def low_pass(kept, grad):
    return (grad,)

def back_keep(v):
    return (v, None)

def back_low(kept, grad):
    return (low(grad),)
low.defvjp(low_keep, low_pass)
low_back.defvjp(back_keep, back_low)
highest = lax.Precision.HIGHEST

def matmul(left, right):
    return jnp.dot(left, right, precision=highest)

def layer_norm(field, gain, shift):
    centre = field - lax.optimization_barrier(jnp.mean(field, axis=-1, keepdims=True))
    spread = lax.optimization_barrier(jnp.mean(centre * centre, axis=-1, keepdims=True))
    return centre * lax.rsqrt(spread + 1e-05) * gain + shift

def attention(queries, key_rows, value_rows, query_segment, key_segment, causal):
    length = queries.shape[0]
    key_count = key_rows.shape[0]
    block_size = min(length, 512)
    positions = jnp.arange(key_count, dtype=jnp.int32)

    def one_block(block_index):
        begin = (block_index * block_size).astype(jnp.int32)
        query_block = lax.dynamic_slice_in_dim(queries, begin, block_size, 0)
        segment_block = lax.dynamic_slice_in_dim(query_segment, begin, block_size, 0)
        raw_scores = jnp.einsum('qhd,khd->hqk', query_block, key_rows, precision=highest)
        scores = low_back(raw_scores * HEAD ** (-0.5))
        allowed = segment_block[:, None] == key_segment[None, :]
        if causal:
            query_position = begin + jnp.arange(block_size, dtype=jnp.int32)
            allowed = allowed & (positions[None, :] <= query_position[:, None])
        masked = jnp.where(allowed[None], scores, -1e+30)
        row_max = lax.optimization_barrier(jnp.max(masked, axis=-1, keepdims=True))
        log_total = row_max + jnp.log(lax.optimization_barrier(jnp.sum(jnp.exp(masked - row_max), axis=-1, keepdims=True)))
        probs = low(jnp.where(allowed[None], jnp.exp(masked - log_total), 0.0))
        return jnp.einsum('hqk,khd->qhd', probs, value_rows, precision=highest)
    blocks = lax.map(jax.checkpoint(one_block), jnp.arange(length // block_size, dtype=jnp.int32))
    return blocks.reshape(queries.shape)

def layer_row(inputs_row, memory_row, target_row, source_row, weights):
    self_in_weight, self_in_bias, self_out_weight, self_out_bias, first_gain, first_shift, cross_query_weight, cross_pair_weight, cross_bias, cross_out_weight, cross_out_bias, second_gain, second_shift, feed_in_weight, feed_in_bias, feed_out_weight, feed_out_bias, third_gain, third_shift = weights
    length = inputs_row.shape[0]
    blank_row = jnp.zeros_like(self_in_bias[0])
    projected = matmul(inputs_row, self_in_weight) + jnp.concatenate([self_in_bias[0], blank_row, self_in_bias[1]])
    projected = low(projected)
    heads_view = projected.reshape(length, 3, HEADS, HEAD)
    attended = attention(heads_view[:, 0], heads_view[:, 1], heads_view[:, 2], target_row, target_row, True)
    attended = low_back(low(attended.reshape(length, -1)))
    branch = low_back(matmul(attended, self_out_weight) + self_out_bias)
    first = layer_norm(inputs_row + branch, first_gain, first_shift)
    cross_queries = low_back(low(matmul(low(first), cross_query_weight) + cross_bias[0]))
    cross_pairs = low(matmul(memory_row, cross_pair_weight) + jnp.concatenate([blank_row, cross_bias[1]]))
    pair_view = cross_pairs.reshape(memory_row.shape[0], 2, HEADS, HEAD)
    crossed = attention(cross_queries.reshape(length, HEADS, HEAD), pair_view[:, 0], pair_view[:, 1], target_row, source_row, False)
    crossed = low_back(low(crossed.reshape(length, -1)))
    branch = low_back(matmul(crossed, cross_out_weight) + cross_out_bias)
    second = layer_norm(first + branch, second_gain, second_shift)
    hidden = low_back(matmul(low(second), feed_in_weight) + feed_in_bias)
    branch = low_back(matmul(low(jax.nn.gelu(hidden, approximate=False)), feed_out_weight) + feed_out_bias)
    return layer_norm(second + branch, third_gain, third_shift)

def reference(inputs, memory, cotangent, target_segments, memory_segments, self_in_weight, self_in_bias, self_out_weight, self_out_bias, first_gain, first_shift, cross_query_weight, cross_pair_weight, cross_bias, cross_out_weight, cross_out_bias, second_gain, second_shift, feed_in_weight, feed_in_bias, feed_out_weight, feed_out_bias, third_gain, third_shift):
    weights = (self_in_weight.astype(jnp.float32), self_in_bias.astype(jnp.float32), self_out_weight.astype(jnp.float32), self_out_bias.astype(jnp.float32), first_gain.astype(jnp.float32), first_shift.astype(jnp.float32), cross_query_weight.astype(jnp.float32), cross_pair_weight.astype(jnp.float32), cross_bias.astype(jnp.float32), cross_out_weight.astype(jnp.float32), cross_out_bias.astype(jnp.float32), second_gain.astype(jnp.float32), second_shift.astype(jnp.float32), feed_in_weight.astype(jnp.float32), feed_in_bias.astype(jnp.float32), feed_out_weight.astype(jnp.float32), feed_out_bias.astype(jnp.float32), third_gain.astype(jnp.float32), third_shift.astype(jnp.float32))

    def row_step(totals, items):
        inputs_row, memory_row, cotangent_row, target_row, source_row = items

        def forward(inputs_value, memory_value, weight_values):
            return layer_row(inputs_value, memory_value, target_row, source_row, weight_values)
        output, pullback = jax.vjp(forward, inputs_row.astype(jnp.float32), memory_row.astype(jnp.float32), weights)
        input_part, memory_part, weight_grads = pullback(cotangent_row.astype(jnp.float32))
        totals = jax.tree.map(lambda left, right: left + right, totals, weight_grads)
        return (totals, (output.astype(jnp.bfloat16), input_part, memory_part))
    start_totals = jax.tree.map(jnp.zeros_like, weights)
    totals, (layer_output, input_grad, memory_grad) = lax.scan(row_step, start_totals, (inputs, memory, cotangent, target_segments, memory_segments))
    return (layer_output, input_grad, memory_grad, totals[0], totals[1], totals[2], totals[3], totals[4], totals[5], totals[6], totals[7], totals[8], totals[9], totals[10], totals[11], totals[12], totals[13], totals[14], totals[15], totals[16], totals[17], totals[18])
```

```python
import functools

import jax
import jax.numpy as jnp
from jax import lax
from jax.experimental import pallas as pl
from jax.experimental.pallas import tpu as pltpu
from jax.sharding import PartitionSpec as P

HEAD = 64
TILE = 128
PAIR = 2 * HEAD
WIDE = 512
SCALE = HEAD ** (-0.5)
MASKED = -1e30
F32 = jnp.float32
BF16 = jnp.bfloat16
VMEM_LIMIT = 58 << 20


def nn(left, right):
    return lax.dot_general(left, right, (((1,), (0,)), ((), ())), preferred_element_type=F32)


def nt(left, right):
    return lax.dot_general(left, right, (((1,), (1,)), ((), ())), preferred_element_type=F32)


def tn(left, right):
    return lax.dot_general(left, right, (((0,), (0,)), ((), ())), preferred_element_type=F32)


def col_sum(field):
    return jnp.sum(field, axis=0, keepdims=True)


def normalize(field):
    centre = field - jnp.mean(field, axis=-1, keepdims=True)
    spread = jnp.mean(centre * centre, axis=-1, keepdims=True)
    rstd = lax.rsqrt(spread + 1e-05)
    return centre * rstd, rstd


def normalize_back(grad, gain, normal, rstd):
    scaled = grad * gain
    mean = jnp.mean(scaled, axis=-1, keepdims=True)
    along = jnp.mean(scaled * normal, axis=-1, keepdims=True)
    return (scaled - mean - normal * along) * rstd


def gate(hidden):
    size = jnp.abs(hidden)
    bell = jnp.exp(hidden * hidden * -0.5)
    ratio = 1.0 / (1.0 + (0.3275911 * 0.7071067811865476) * size)
    series = 1.061405429 * ratio - 1.453152027
    series = series * ratio + 1.421413741
    series = series * ratio - 0.284496736
    series = series * ratio + 0.254829592
    tail = (0.5 * series) * ratio * bell
    phi = jnp.where(hidden > 0.0, 1.0 - tail, tail)
    return hidden * phi, phi + hidden * (bell * 0.3989422804014327)


def dyn(index, size):
    return pl.ds(pl.multiple_of(index * size, size), size)


def even_lanes(rows, width):
    return (lax.broadcasted_iota(jnp.int32, (rows, width), 1) // HEAD) % 2 == 0


def even_rows(rows, width):
    return (lax.broadcasted_iota(jnp.int32, (rows, width), 0) // HEAD) % 2 == 0


def split_columns(tile_t, out_ref, tile):
    chosen = even_rows(*tile_t.shape)
    blank = jnp.zeros_like(tile_t)
    out_ref[:, pl.ds(pl.multiple_of(tile * 2 * TILE, 2 * TILE), TILE)] = jnp.where(chosen, tile_t, blank)
    out_ref[:, pl.ds(pl.multiple_of(tile * 2 * TILE + TILE, TILE), TILE)] = jnp.where(
        chosen, blank, tile_t
    )


def split_rows(tile_n, out_ref, tile):
    chosen = even_lanes(*tile_n.shape)
    blank = jnp.zeros_like(tile_n)
    out_ref[pl.ds(pl.multiple_of(tile * 2 * TILE, 2 * TILE), TILE), :] = jnp.where(chosen, tile_n, blank)
    out_ref[pl.ds(pl.multiple_of(tile * 2 * TILE + TILE, TILE), TILE), :] = jnp.where(
        chosen, blank, tile_n
    )


def spread_segments(column_ref, wide_ref):
    total = column_ref.shape[0]
    step = min(total, 512)

    @pl.loop(0, total // step)
    def _(block):
        rows = dyn(block, step)
        wide_ref[rows, :] = jnp.broadcast_to(column_ref[rows, :], (step, TILE))


def tile_bias(query_row, key_wide_ref, tile, key_tile, offset, causal):
    allowed = key_wide_ref[dyn(key_tile, TILE), :] == query_row
    if causal:
        key_position = key_tile * TILE + lax.broadcasted_iota(jnp.int32, (TILE, TILE), 0)
        query_position = offset + tile * TILE + lax.broadcasted_iota(jnp.int32, (TILE, TILE), 1)
        allowed = allowed & (key_position <= query_position)
    return jnp.where(allowed, 0.0, MASKED)


def attend(
    tiles, ranges_ref, query_row_ref, key_wide_ref, offset, causal,
    query_cols, keys, values_t, attended_t, lse_ref, peak, total, sums,
):
    pairs = WIDE // PAIR

    @pl.loop(0, tiles)
    def _(tile):
        peak[...] = jnp.full(peak.shape, MASKED, F32)
        total[...] = jnp.zeros(total.shape, F32)
        sums[...] = jnp.zeros(sums.shape, F32)
        query_row = query_row_ref[:, dyn(tile, TILE)]

        @pl.loop(ranges_ref[0, tile], ranges_ref[1, tile])
        def _(key_tile):
            rows = dyn(key_tile, TILE)
            bias = tile_bias(query_row, key_wide_ref, tile, key_tile, offset, causal)
            bias = jnp.concatenate([bias, bias], axis=1)
            for pair in range(pairs):
                lanes = slice(pair * PAIR, (pair + 1) * PAIR)
                scores = nn(keys[rows, lanes], query_cols[lanes, dyn(tile, 2 * TILE)]) + bias
                before = peak[pair : pair + 1, :]
                after = jnp.maximum(before, jnp.max(scores, axis=0, keepdims=True))
                factor = jnp.exp(before - after)
                weights = jnp.exp(scores - after)
                peak[pair : pair + 1, :] = after
                total[pair : pair + 1, :] = total[pair : pair + 1, :] * factor + col_sum(weights)
                mixed = nn(values_t[lanes, rows], weights.astype(BF16))
                first = slice(pair * PAIR, pair * PAIR + HEAD)
                second = slice(pair * PAIR + HEAD, (pair + 1) * PAIR)
                sums[first, :] = sums[first, :] * factor[:, :TILE] + mixed[:HEAD, :TILE]
                sums[second, :] = sums[second, :] * factor[:, TILE:] + mixed[HEAD:, TILE:]

        for pair in range(pairs):
            amount = total[pair : pair + 1, :]
            lse_ref[pair : pair + 1, dyn(tile, 2 * TILE)] = peak[pair : pair + 1, :] + jnp.log(amount)
            share = 1.0 / amount
            first = slice(pair * PAIR, pair * PAIR + HEAD)
            second = slice(pair * PAIR + HEAD, (pair + 1) * PAIR)
            attended_t[first, dyn(tile, TILE)] = (sums[first, :] * share[:, :TILE]).astype(BF16)
            attended_t[second, dyn(tile, TILE)] = (sums[second, :] * share[:, TILE:]).astype(BF16)


def attend_back(
    tiles, ranges_ref, query_row_ref, key_wide_ref, offset, causal,
    query_cols, query_rows, grad_cols, grad_rows, keys, keys_t, values, lse_ref, delta_ref,
    query_grad_t, key_grad, value_grad,
):
    pairs = WIDE // PAIR

    @pl.loop(0, tiles)
    def _(tile):
        query_row = query_row_ref[:, dyn(tile, TILE)]
        both = dyn(tile, 2 * TILE)

        @pl.loop(ranges_ref[0, tile], ranges_ref[1, tile])
        def _(key_tile):
            rows = dyn(key_tile, TILE)
            bias = tile_bias(query_row, key_wide_ref, tile, key_tile, offset, causal)
            bias = jnp.concatenate([bias, bias], axis=1)
            for pair in range(pairs):
                lanes = slice(pair * PAIR, (pair + 1) * PAIR)
                scores = nn(keys[rows, lanes], query_cols[lanes, both]) + bias
                probs = jnp.exp(scores - lse_ref[pair : pair + 1, both])
                prob_grad = nn(values[rows, lanes], grad_cols[lanes, both])
                score_grad = (probs * (prob_grad - delta_ref[pair : pair + 1, both])).astype(BF16)
                value_grad[rows, lanes] += nn(probs.astype(BF16), grad_rows[both, lanes])
                key_grad[rows, lanes] += nn(score_grad, query_rows[both, lanes])
                mixed = nn(keys_t[lanes, rows], score_grad)
                first = slice(pair * PAIR, pair * PAIR + HEAD)
                second = slice(pair * PAIR + HEAD, (pair + 1) * PAIR)
                query_grad_t[first, dyn(tile, TILE)] += mixed[:HEAD, :TILE]
                query_grad_t[second, dyn(tile, TILE)] += mixed[HEAD:, TILE:]


def clear(ref):
    rows = ref.shape[0]
    step = min(rows, 256)

    @pl.loop(0, rows // step)
    def _(block):
        ref[dyn(block, step), :] = jnp.zeros((step, ref.shape[1]), ref.dtype)


def transpose_rows(source, target):
    @pl.loop(0, source.shape[0] // TILE)
    def _(block):
        target[:, dyn(block, TILE)] = source[dyn(block, TILE), :].T


def out_like(shape, dtype):
    return jax.ShapeDtypeStruct(shape, dtype)


def run(body, ins, smem_count, outs, scratch, flops, bytes_accessed):
    vm = pl.BlockSpec(memory_space=pltpu.VMEM)
    sm = pl.BlockSpec(memory_space=pltpu.SMEM)
    return pl.pallas_call(
        body,
        in_specs=[sm] * smem_count + [vm] * (len(ins) - smem_count),
        out_specs=[vm] * len(outs),
        out_shape=outs,
        scratch_shapes=scratch,
        cost_estimate=pl.CostEstimate(
            flops=flops, bytes_accessed=bytes_accessed, transcendentals=0
        ),
        compiler_params=pltpu.CompilerParams(vmem_limit_bytes=VMEM_LIMIT),
    )(*ins)


def self_forward(n, rows_block, place_ref, ranges_ref, *refs):
    pieces, refs = refs[:n], refs[n:]
    (
        query_segment, key_segment, weight, bias, out_weight, out_bias, gain, shift,
        cross_weight, cross_bias,
        query_out, keys, values, attended_t, lse_ref, normal_out, rstd_out, first_low, cross_query,
        wide, values_t, query_cols, peak, total, sums,
    ) = refs
    count = pieces[0].shape[0]
    place = place_ref[0]
    spread_segments(key_segment, wide)

    for step in range(n):
        spot = lax.rem(place + n - step, n)

        @pl.when(spot <= place)
        def _():
            @pl.loop(0, count // rows_block)
            def _(block):
                source = pieces[step][dyn(block, rows_block), :]
                rows = dyn(spot * (count // rows_block) + block, rows_block)
                keys[rows, :] = nn(source, weight[:, WIDE : 2 * WIDE]).astype(BF16)
                values[rows, :] = (nn(source, weight[:, 2 * WIDE :]) + bias[1:2, :]).astype(BF16)
                if step == 0:
                    query = (nn(source, weight[:, :WIDE]) + bias[0:1, :]).astype(BF16)
                    query_out[dyn(block, rows_block), :] = (query.astype(F32) * SCALE).astype(BF16)

        @pl.when(spot > place)
        def _():
            @pl.loop(0, count // rows_block)
            def _(block):
                rows = dyn(spot * (count // rows_block) + block, rows_block)
                keys[rows, :] = jnp.zeros((rows_block, WIDE), BF16)
                values[rows, :] = jnp.zeros((rows_block, WIDE), BF16)

    transpose_rows(values, values_t)
    tiles = count // TILE

    @pl.loop(0, tiles)
    def _(tile):
        split_columns(query_out[dyn(tile, TILE), :].T, query_cols, tile)

    attend(
        tiles, ranges_ref, query_segment, wide, place * count, True,
        query_cols, keys, values_t, attended_t, lse_ref, peak, total, sums,
    )

    @pl.loop(0, count // rows_block)
    def _(block):
        rows = dyn(block, rows_block)
        attended = attended_t[:, rows].T
        field = pieces[0][rows, :].astype(F32) + nn(attended, out_weight[...]) + out_bias[...]
        normal, rstd = normalize(field)
        normal_out[rows, :] = normal
        rstd_out[rows, :] = rstd
        low = (normal * gain[...] + shift[...]).astype(BF16)
        first_low[rows, :] = low
        query = (nn(low, cross_weight[...]) + cross_bias[0:1, :]).astype(BF16)
        cross_query[rows, :] = (query.astype(F32) * SCALE).astype(BF16)


def cross_and_feed(n, rows_block, place_ref, ranges_ref, *refs):
    pieces, refs = refs[:n], refs[n:]
    (
        query_segment, key_segment, cotangent, cross_query, first_normal, first_gain, first_shift,
        pair_weight, cross_bias, out_weight, out_bias, gain, shift,
        in_weight, in_bias, down_weight, down_bias, last_gain, last_shift,
        layer_output, keys, values, lse_ref, delta_ref, out_grad, grad_out, g2_out,
        in_grad, down_grad, cross_out_grad, sums_out, in_bias_grad,
        wide, values_t, query_cols, peak, total, sums, attended_t, second_normal, second_rstd,
        second_low, second_low_t, active, slope, third, branch, branch_t,
    ) = refs
    count = pieces[0].shape[0]
    place = place_ref[0]
    spread_segments(key_segment, wide)
    blocks = count // rows_block

    for step in range(n):
        spot = lax.rem(place + n - step, n)

        @pl.loop(0, blocks)
        def _(block):
            source = pieces[step][dyn(block, rows_block), :]
            rows = dyn(spot * blocks + block, rows_block)
            keys[rows, :] = nn(source, pair_weight[:, :WIDE]).astype(BF16)
            values[rows, :] = (nn(source, pair_weight[:, WIDE:]) + cross_bias[1:2, :]).astype(BF16)

    transpose_rows(values, values_t)
    tiles = count // TILE

    @pl.loop(0, tiles)
    def _(tile):
        split_columns(cross_query[dyn(tile, TILE), :].T, query_cols, tile)

    attend(
        tiles, ranges_ref, query_segment, wide, 0, False,
        query_cols, keys, values_t, attended_t, lse_ref, peak, total, sums,
    )

    @pl.loop(0, blocks)
    def _(block):
        rows = dyn(block, rows_block)
        attended = attended_t[:, rows].T
        first = first_normal[rows, :] * first_gain[...] + first_shift[...]
        field = first + nn(attended, out_weight[...]) + out_bias[...]
        normal, rstd = normalize(field)
        second_normal[rows, :] = normal
        second_rstd[rows, :] = rstd
        second = normal * gain[...] + shift[...]
        third[rows, :] = second + down_bias[...]
        low = second.astype(BF16)
        second_low[rows, :] = low
        second_low_t[:, rows] = low.T

    hidden_size = in_weight.shape[1]
    chunk_size = min(WIDE, hidden_size // n)
    chunks = hidden_size // chunk_size

    @pl.loop(0, chunks)
    def _(chunk):
        lanes = dyn(chunk, chunk_size)

        @pl.loop(0, blocks)
        def _(block):
            rows = dyn(block, rows_block)
            hidden = nn(second_low[rows, :], in_weight[:, lanes]) + in_bias[:, lanes]
            value, derivative = gate(hidden)
            value = value.astype(BF16)
            active[rows, lanes] = value
            slope[rows, lanes] = derivative.astype(slope.dtype)
            third[rows, :] += nn(value, down_weight[dyn(chunk, chunk_size), :])

    sums_out[...] = jnp.zeros(sums_out.shape, F32)
    in_bias_grad[...] = jnp.zeros(in_bias_grad.shape, F32)

    @pl.loop(0, blocks)
    def _(block):
        rows = dyn(block, rows_block)
        normal, rstd = normalize(third[rows, :])
        layer_output[rows, :] = (normal * last_gain[...] + last_shift[...]).astype(BF16)
        outer = cotangent[rows, :].astype(F32)
        grad = normalize_back(outer, last_gain[...], normal, rstd)
        third[rows, :] = grad
        low = grad.astype(BF16)
        branch[rows, :] = low
        sums_out[0:1, :] += col_sum(outer * normal)
        sums_out[1:2, :] += col_sum(outer)
        sums_out[2:3, :] += col_sum(low.astype(F32))

    half = WIDE // n
    down_half = down_weight.shape[0] // n

    @pl.loop(0, chunks)
    def _(chunk):
        lanes = dyn(chunk, chunk_size)
        share = tn(active[:, lanes], branch[...]).astype(BF16)
        per_half = down_half // chunk_size
        down_grad[lax.div(chunk, per_half), dyn(lax.rem(chunk, per_half), chunk_size), :] = share

        @pl.loop(0, blocks)
        def _(block):
            rows = dyn(block, rows_block)
            inner = nt(branch[rows, :], down_weight[dyn(chunk, chunk_size), :])
            hidden_grad = (inner * slope[rows, lanes].astype(F32)).astype(BF16)
            active[rows, lanes] = hidden_grad
            in_bias_grad[:, lanes] += col_sum(hidden_grad.astype(F32))
            third[rows, :] += nt(hidden_grad, in_weight[:, lanes])

        share = nn(second_low_t[...], active[:, lanes]).astype(BF16)
        per_block = WIDE // chunk_size
        block_rows = dyn(lax.div(chunk, per_block), half)
        block_lanes = dyn(lax.rem(chunk, per_block), chunk_size)
        for part in range(n):
            in_grad[part, block_rows, block_lanes] = share[part * half : (part + 1) * half, :]

    @pl.loop(0, blocks)
    def _(block):
        rows = dyn(block, rows_block)
        outer = third[rows, :]
        normal = second_normal[rows, :]
        grad = normalize_back(outer, gain[...], normal, second_rstd[rows, :])
        g2_out[rows, :] = grad
        low = grad.astype(BF16)
        branch[rows, :] = low
        sums_out[3:4, :] += col_sum(outer * normal)
        sums_out[4:5, :] += col_sum(outer)
        sums_out[5:6, :] += col_sum(low.astype(F32))
        grad_out[rows, :] = nt(low, out_weight[...]).astype(BF16)

    share = nn(attended_t[...], branch[...]).astype(BF16)
    for part in range(n):
        cross_out_grad[part] = share[part * half : (part + 1) * half, :]

    write_delta(tiles, grad_out, attended_t, delta_ref)


def write_delta(tiles, grad, attended_t, delta_ref):
    @pl.loop(0, tiles)
    def _(tile):
        product = grad[dyn(tile, TILE), :].astype(F32).T * attended_t[:, dyn(tile, TILE)].astype(F32)
        for pair in range(WIDE // PAIR):
            start = pair * PAIR
            delta_ref[pair : pair + 1, pl.ds(pl.multiple_of(tile * 2 * TILE, 2 * TILE), TILE)] = col_sum(
                product[start : start + HEAD, :]
            )
            delta_ref[
                pair : pair + 1, pl.ds(pl.multiple_of(tile * 2 * TILE + TILE, TILE), TILE)
            ] = col_sum(product[start + HEAD : start + PAIR, :])


def prepare_back(tiles, query, grad, query_cols, query_rows, grad_cols, grad_rows):
    @pl.loop(0, tiles)
    def _(tile):
        here = query[dyn(tile, TILE), :]
        split_columns(here.T, query_cols, tile)
        split_rows(here, query_rows, tile)
        here = grad[dyn(tile, TILE), :]
        split_columns(here.T, grad_cols, tile)
        split_rows(here, grad_rows, tile)


def cross_backward(n, rows_block, place_ref, ranges_ref, *refs):
    pieces, refs = refs[:n], refs[n:]
    (
        query_segment, key_segment, query, grad, keys, values, lse_ref, delta_ref, g2,
        first_normal, first_rstd, first_low, gain, query_weight, pair_weight, self_out_weight,
        self_attended_t,
        own_grad, sent_grad, query_grad_w, pair_grad_w, self_out_grad, self_grad, self_delta, g1_out, sums_out,
        wide, keys_t, query_cols, query_rows, grad_cols, grad_rows, query_grad_t, key_grad, value_grad,
        query_low, branch,
    ) = refs
    count = pieces[0].shape[0]
    place = place_ref[0]
    tiles = count // TILE
    blocks = count // rows_block
    spread_segments(key_segment, wide)
    transpose_rows(keys, keys_t)
    prepare_back(tiles, query, grad, query_cols, query_rows, grad_cols, grad_rows)
    clear(query_grad_t)
    clear(key_grad)
    clear(value_grad)
    attend_back(
        tiles, ranges_ref, query_segment, wide, 0, False,
        query_cols, query_rows, grad_cols, grad_rows, keys, keys_t, values, lse_ref, delta_ref,
        query_grad_t, key_grad, value_grad,
    )
    sums_out[...] = jnp.zeros(sums_out.shape, F32)

    @pl.loop(0, tiles)
    def _(tile):
        rows = dyn(tile, TILE)
        low = (query_grad_t[:, rows].T * SCALE).astype(BF16)
        query_low[rows, :] = low
        sums_out[0:1, :] += col_sum(low.astype(F32))

    half = WIDE // n
    share = tn(first_low[...], query_low[...]).astype(BF16)
    for part in range(n):
        query_grad_w[part] = share[part * half : (part + 1) * half, :]

    for step in range(n):
        spot = lax.rem(place + n - step, n)

        @pl.loop(0, blocks)
        def _(block):
            rows = dyn(spot * blocks + block, rows_block)
            here = dyn(block, rows_block)
            key_low = key_grad[rows, :].astype(BF16)
            value_part = value_grad[rows, :]
            sums_out[1:2, :] += col_sum(value_part)
            value_low = value_part.astype(BF16)
            back = nt(key_low, pair_weight[:, :WIDE]) + nt(value_low, pair_weight[:, WIDE:])
            if step == 0:
                own_grad[here, :] = back
            else:
                sent_grad[step - 1, here, :] = back.astype(BF16)

    half_rows = min(count, 512)
    for side, source in ((0, key_grad), (1, value_grad)):
        share = jnp.zeros((WIDE, WIDE), F32)
        for step in range(n):
            spot = lax.rem(place + n - step, n)
            for block in range(count // half_rows):
                rows = dyn(spot * (count // half_rows) + block, half_rows)
                share += tn(
                    pieces[step][block * half_rows : (block + 1) * half_rows, :],
                    source[rows, :].astype(BF16),
                )
        share = share.astype(BF16)
        for part in range(n):
            pair_grad_w[part, side * half : (side + 1) * half, :] = share[part * half : (part + 1) * half, :]

    @pl.loop(0, blocks)
    def _(block):
        rows = dyn(block, rows_block)
        outer = g2[rows, :] + nt(query_low[rows, :], query_weight[...])
        normal = first_normal[rows, :]
        back = normalize_back(outer, gain[...], normal, first_rstd[rows, :])
        g1_out[rows, :] = back
        low = back.astype(BF16)
        branch[rows, :] = low
        sums_out[2:3, :] += col_sum(outer * normal)
        sums_out[3:4, :] += col_sum(outer)
        sums_out[4:5, :] += col_sum(low.astype(F32))
        self_grad[rows, :] = nt(low, self_out_weight[...]).astype(BF16)

    share = nn(self_attended_t[...], branch[...]).astype(BF16)
    for part in range(n):
        self_out_grad[part] = share[part * half : (part + 1) * half, :]

    write_delta(tiles, self_grad, self_attended_t, self_delta)


def self_backward(n, rows_block, place_ref, ranges_ref, *refs):
    pieces, refs = refs[:n], refs[n:]
    (
        query_segment, key_segment, query, grad, keys, values, lse_ref, delta_ref, g1, weight,
        own_grad, sent_grad, grad_w, sums_out,
        wide, keys_t, query_cols, query_rows, grad_cols, grad_rows, query_grad_t, key_grad, value_grad,
        query_low,
    ) = refs
    count = pieces[0].shape[0]
    place = place_ref[0]
    tiles = count // TILE
    blocks = count // rows_block
    spread_segments(key_segment, wide)
    transpose_rows(keys, keys_t)
    prepare_back(tiles, query, grad, query_cols, query_rows, grad_cols, grad_rows)
    clear(query_grad_t)
    clear(key_grad)
    clear(value_grad)
    attend_back(
        tiles, ranges_ref, query_segment, wide, place * count, True,
        query_cols, query_rows, grad_cols, grad_rows, keys, keys_t, values, lse_ref, delta_ref,
        query_grad_t, key_grad, value_grad,
    )
    sums_out[...] = jnp.zeros(sums_out.shape, F32)

    @pl.loop(0, tiles)
    def _(tile):
        rows = dyn(tile, TILE)
        wide_grad = query_grad_t[:, rows].T * SCALE
        sums_out[0:1, :] += col_sum(wide_grad)
        query_low[rows, :] = wide_grad.astype(BF16)

    for step in range(n):
        spot = lax.rem(place + n - step, n)

        @pl.loop(0, blocks)
        def _(block):
            rows = dyn(spot * blocks + block, rows_block)
            here = dyn(block, rows_block)
            key_low = key_grad[rows, :].astype(BF16)
            value_part = value_grad[rows, :]
            sums_out[1:2, :] += col_sum(value_part)
            value_low = value_part.astype(BF16)
            back = nt(key_low, weight[:, WIDE : 2 * WIDE]) + nt(value_low, weight[:, 2 * WIDE :])
            if step == 0:
                own_grad[here, :] = back + g1[here, :] + nt(query_low[here, :], weight[:, :WIDE])
            else:
                sent_grad[step - 1, here, :] = back.astype(BF16)

    half = WIDE // n
    half_rows = min(count, 512)
    for side, source in ((0, query_low), (1, key_grad), (2, value_grad)):
        share = jnp.zeros((WIDE, WIDE), F32)
        for step in range(1 if side == 0 else n):
            spot = 0 if side == 0 else lax.rem(place + n - step, n)
            for block in range(count // half_rows):
                rows = dyn(spot * (count // half_rows) + block, half_rows)
                share += tn(
                    pieces[step][block * half_rows : (block + 1) * half_rows, :],
                    source[rows, :].astype(BF16),
                )
        share = share.astype(BF16)
        for part in range(n):
            grad_w[part, side * half : (side + 1) * half, :] = share[part * half : (part + 1) * half, :]


def other(value):
    return 1 - value


def reduce_kernel(n, groups, chunk_rows, part_rows, *refs):
    sources, refs = refs[: len(part_rows)], refs[len(part_rows) :]
    (
        small_in, total_out, small_out,
        field, from_core, from_blk, from_y, from_z, total,
        small_held, small_core, small_blk, small_y, small_z,
        load_sem, send, recv, small_send, small_recv, store_sem,
    ) = refs
    depth = groups // 4
    group = lax.axis_index("dp")
    part = lax.axis_index("blk")
    core = lax.rem(group, 2)
    side = lax.rem(lax.div(group, 2), 2)
    level = lax.div(group, 4)
    rows = field.shape[1]
    chunks = rows // chunk_rows
    half = chunk_rows // 2
    quarter = half // 2
    piece = quarter // depth

    loads = []
    start = 0
    for index, source in enumerate(sources):
        loads.append(
            pltpu.make_async_copy(source, field.at[:, pl.ds(start, part_rows[index])], load_sem.at[index])
        )
        loads[-1].start()
        start += part_rows[index]

    core_peer = (group + 1 - 2 * core, part)
    side_peer = (group + 2 - 4 * side, part)
    blk_peers = [(group, lax.rem(part + step, n)) for step in range(1, n)]
    z_peers = [(lax.rem(group + 4 * step, groups), part) for step in range(1, depth)]
    peers = [core_peer, side_peer] + blk_peers + z_peers
    barrier = pltpu.get_barrier_semaphore()
    for peer in peers:
        pl.semaphore_signal(barrier, inc=1, device_id=peer, device_id_type=pl.DeviceIdType.MESH)
    pl.semaphore_wait(barrier, len(peers))

    def remote(source, target, sem, peer, sends=send, receives=recv):
        return pltpu.make_async_remote_copy(
            src_ref=source, dst_ref=target, send_sem=sends.at[sem], recv_sem=receives.at[sem],
            device_id=peer, device_id_type=pl.DeviceIdType.MESH,
        )

    per_chunk = 4 + (n - 1) + 2 * (depth - 1)

    def span(start, size):
        return pl.ds(pl.multiple_of(start, 16), size)

    def core_copy(c):
        theirs = span(c * chunk_rows + other(core) * half, half)
        return remote(
            field.at[:, theirs], from_core.at[:, pl.ds(c * half, half)], c * per_chunk, core_peer
        )

    def blk_copies(c):
        mine = span(c * chunk_rows + core * half, half)
        return [
            remote(
                field.at[lax.rem(part + step, n), mine],
                from_blk.at[step - 1, pl.ds(c * half, half)],
                c * per_chunk + 3 + step,
                blk_peers[step - 1],
            )
            for step in range(1, n)
        ]

    def side_copy(c):
        theirs = span(c * chunk_rows + core * half + other(side) * quarter, quarter)
        return remote(
            field.at[part, theirs], from_y.at[0, pl.ds(c * quarter, quarter)], c * per_chunk + 1, side_peer
        )

    def own_quarter(c):
        return c * chunk_rows + core * half + side * quarter

    def z_copies(c):
        copies = []
        for step in range(1, depth):
            theirs = span(own_quarter(c) + lax.rem(level + step, depth) * piece, piece)
            copies.append(
                remote(
                    field.at[part, theirs], from_z.at[step - 1, pl.ds(c * piece, piece)],
                    c * per_chunk + 3 + n - 1 + step, z_peers[step - 1],
                )
            )
        return copies

    def z_back_copies(c):
        mine = span(own_quarter(c) + level * piece, piece)
        return [
            remote(
                total.at[mine], total.at[mine], c * per_chunk + 3 + n - 1 + depth - 1 + step, z_peers[step - 1]
            )
            for step in range(1, depth)
        ]

    def side_back_copy(c):
        mine = span(own_quarter(c), quarter)
        return remote(total.at[mine], total.at[mine], c * per_chunk + 2, side_peer)

    def core_back_copy(c):
        mine = span(c * chunk_rows + core * half, half)
        return remote(total.at[mine], total.at[mine], c * per_chunk + 3, core_peer)

    def start_all(copies):
        for copy in copies:
            copy.start()

    def wait_all(copies):
        for copy in copies:
            copy.wait()

    def add_rows(target, target_part, start, size, terms, result=None):
        step = min(size, 64)

        @pl.loop(0, size // step)
        def _(block):
            here = span(start + block * step, step)
            value = target[target_part, here, :].astype(F32)
            for ref, index, begin in terms:
                value = value + ref[index, span(begin + block * step, step), :].astype(F32)
            if result is None:
                target[target_part, here, :] = value.astype(BF16)
            else:
                result[here, :] = value.astype(BF16)

    def small_copies(stage):
        if stage == 0:
            return [remote(small_in, small_core, 0, core_peer, small_send, small_recv)]
        if stage == 1:
            return [
                remote(
                    small_held.at[lax.rem(part + step, n)], small_blk.at[step - 1], step,
                    blk_peers[step - 1], small_send, small_recv,
                )
                for step in range(1, n)
            ]
        if stage == 2:
            return [remote(small_held.at[part], small_y, n, side_peer, small_send, small_recv)]
        return [
            remote(small_y, small_z.at[step - 1], n + step, z_peers[step - 1], small_send, small_recv)
            for step in range(1, depth)
        ]

    start_all(small_copies(0))
    waited = 0
    ready = 0
    for c in range(chunks):
        while ready < (c + 1) * chunk_rows:
            loads[waited].wait()
            ready += part_rows[waited]
            waited += 1
        core_copy(c).start()
    for load in loads[waited:]:
        load.wait()
    for c in range(chunks):
        core_copy(c).wait()
        for b in range(n):
            add_rows(field, b, c * chunk_rows + core * half, half, [(from_core, b, c * half)])
        start_all(blk_copies(c))
        if c == 0:
            wait_all(small_copies(0))
            small_held[...] = small_in[...] + small_core[...]
            start_all(small_copies(1))

    for t in range(chunks + 5):
        c = t
        if c < chunks:
            wait_all(blk_copies(c))
            add_rows(
                field, part, c * chunk_rows + core * half, half,
                [(from_blk, step, c * half) for step in range(n - 1)],
            )
            side_copy(c).start()
        c = t - 1
        if 0 <= c < chunks:
            side_copy(c).wait()
            add_rows(field, part, own_quarter(c), quarter, [(from_y, 0, c * quarter)])
            start_all(z_copies(c))
        c = t - 2
        if 0 <= c < chunks:
            wait_all(z_copies(c))
            add_rows(
                field, part, own_quarter(c) + level * piece, piece,
                [(from_z, step, c * piece) for step in range(depth - 1)], total,
            )
            start_all(z_back_copies(c))
        c = t - 3
        if 0 <= c < chunks:
            wait_all(z_back_copies(c))
            side_back_copy(c).start()
        c = t - 4
        if 0 <= c < chunks:
            side_back_copy(c).wait()
            core_back_copy(c).start()
        if t == 0:
            wait_all(small_copies(1))
            held = small_held[part]
            for step in range(n - 1):
                held = held + small_blk[step]
            small_held[part] = held
            start_all(small_copies(2))
        if t == 1:
            wait_all(small_copies(2))
            small_y[...] = small_y[...] + small_held[part]
            start_all(small_copies(3))
        if t == 2:
            wait_all(small_copies(3))
            held = small_y[...]
            for step in range(depth - 1):
                held = held + small_z[step]
            small_out[...] = held
        c = t - 5
        if 0 <= c < chunks:
            core_back_copy(c).wait()
            done = pl.ds(c * chunk_rows, chunk_rows)
            pltpu.make_async_copy(total.at[done], total_out.at[done], store_sem.at[c]).start()
    for c in range(chunks):
        done = pl.ds(c * chunk_rows, chunk_rows)
        pltpu.make_async_copy(total.at[done], total_out.at[done], store_sem.at[c]).wait()


def reduce_all(n, groups, parts, small):
    part_rows = [part.shape[1] for part in parts]
    rows = sum(part_rows)
    depth = groups // 4
    chunk_rows = max(16 * groups, rows // 8)
    chunks = rows // chunk_rows
    small_rows = small.shape[1]
    per_chunk = 4 + (n - 1) + 2 * (depth - 1)
    vm = pl.BlockSpec(memory_space=pltpu.VMEM)
    hbm = pl.BlockSpec(memory_space=pl.ANY)
    small_buffer = pltpu.VMEM((n, small_rows, WIDE), F32)
    return pl.pallas_call(
        functools.partial(reduce_kernel, n, groups, chunk_rows, part_rows),
        in_specs=[hbm] * len(parts) + [vm],
        out_specs=[hbm, vm],
        out_shape=[out_like((rows, WIDE), BF16), out_like((small_rows, WIDE), F32)],
        scratch_shapes=[
            pltpu.VMEM((n, rows, WIDE), BF16),
            pltpu.VMEM((n, rows // 2, WIDE), BF16),
            pltpu.VMEM((n - 1, rows // 2, WIDE), BF16),
            pltpu.VMEM((1, rows // 4, WIDE), BF16),
            pltpu.VMEM((depth - 1, rows // 4 // depth, WIDE), BF16),
            pltpu.VMEM((rows, WIDE), BF16),
            small_buffer, small_buffer, pltpu.VMEM((n - 1, small_rows, WIDE), F32),
            pltpu.VMEM((small_rows, WIDE), F32), pltpu.VMEM((depth - 1, small_rows, WIDE), F32),
            pltpu.SemaphoreType.DMA((len(parts),)),
            pltpu.SemaphoreType.DMA((chunks * per_chunk,)),
            pltpu.SemaphoreType.DMA((chunks * per_chunk,)),
            pltpu.SemaphoreType.DMA((n + depth,)),
            pltpu.SemaphoreType.DMA((n + depth,)),
            pltpu.SemaphoreType.DMA((chunks,)),
        ],
        compiler_params=pltpu.CompilerParams(
            vmem_limit_bytes=VMEM_LIMIT, collective_id=0, has_side_effects=True
        ),
    )(*parts, small)


def widen_kernel(plan, source, *outs):
    for out, (start, columns) in zip(outs, plan):
        height = out.shape[0]
        for column in range(columns):
            out[:, column * WIDE : (column + 1) * WIDE] = source[
                start + column * height : start + (column + 1) * height, :
            ].astype(F32)


def key_ranges(query_segment, key_segment, tiles, limit):
    edges = query_segment.reshape(tiles, TILE)
    low = jnp.sum((key_segment[None, :] < edges[:, :1]).astype(jnp.int32), axis=1)
    high = jnp.sum((key_segment[None, :] <= edges[:, TILE - 1 :]).astype(jnp.int32), axis=1)
    if limit is not None:
        high = jnp.minimum(high, limit)
    return jnp.stack([low // TILE, (high + TILE - 1) // TILE]).astype(jnp.int32)


def on_device(
    n, groups,
    inputs, memory, cotangent, target_segments, memory_segments,
    self_in_weight, self_in_bias, self_out_weight, self_out_bias, first_gain, first_shift,
    cross_query_weight, cross_pair_weight, cross_bias, cross_out_weight, cross_out_bias,
    second_gain, second_shift, feed_in_weight, feed_in_bias, feed_out_weight, feed_out_bias,
    third_gain, third_shift,
):
    input_rows, memory_rows, cotangent_rows = inputs[0], memory[0], cotangent[0]
    count, features = input_rows.shape
    length = n * count
    hidden = feed_in_weight.shape[1]
    rows_block = min(count, 256)
    tiles = count // TILE
    half = features // n
    place = lax.axis_index("blk").astype(jnp.int32)

    def shifted(field, step):
        return lax.ppermute(field, "blk", [(s, (s + step) % n) for s in range(n)])

    def shifted_back(field, step):
        return lax.ppermute(field, "blk", [(s, (s - step) % n) for s in range(n)])

    input_pieces = [input_rows] + [shifted(input_rows, step) for step in range(1, n)]
    memory_pieces = [memory_rows] + [shifted(memory_rows, step) for step in range(1, n)]

    target_row = target_segments[0]
    source_row = memory_segments[0]
    target_here = lax.dynamic_slice_in_dim(target_row, place * count, count, 0)
    self_ranges = key_ranges(
        target_here, target_row, tiles, place * count + TILE * (1 + jnp.arange(tiles, dtype=jnp.int32))
    )
    cross_ranges = key_ranges(target_here, source_row, tiles, None)
    place_one = place[None]
    query_segment = target_here[None, :]
    target_column = target_row[:, None]
    source_column = source_row[:, None]

    def row(vector):
        return vector[None, :]

    stats = out_like((WIDE // PAIR, 2 * count), F32)
    low_rows = out_like((count, features), BF16)
    wide_rows = out_like((count, features), F32)
    low_row_all = out_like((length, features), BF16)
    statistic = out_like((count, 1), F32)
    wide_scratch = pltpu.VMEM((length, TILE), jnp.int32)
    values_t = pltpu.VMEM((features, length), BF16)
    query_cols = pltpu.VMEM((features, 2 * count), BF16)
    query_rows = pltpu.VMEM((2 * count, features), BF16)
    peak = pltpu.VMEM((8, 2 * TILE), F32)
    sums = pltpu.VMEM((features, TILE), F32)
    square = 2 * count * features * features

    (
        query, keys, values, attended_t, lse, normal, rstd, first_low, cross_query
    ) = run(
        functools.partial(self_forward, n, rows_block),
        [place_one, self_ranges, *input_pieces, query_segment, target_column,
         self_in_weight, self_in_bias, self_out_weight, row(self_out_bias), row(first_gain),
         row(first_shift), cross_query_weight, cross_bias],
        2,
        [low_rows, low_row_all, low_row_all, out_like((features, count), BF16), stats, wide_rows,
         statistic, low_rows, low_rows],
        [wide_scratch, values_t, query_cols, peak, peak, sums],
        20 * square, 10 << 20,
    )

    (
        layer_output, cross_keys, cross_values, cross_lse, cross_delta, unused, cross_grad, g2,
        in_grad, down_grad, cross_out_grad, feed_sums, in_bias_grad,
    ) = run(
        functools.partial(cross_and_feed, n, rows_block),
        [place_one, cross_ranges, *memory_pieces, query_segment, source_column, cotangent_rows,
         cross_query, normal, row(first_gain), row(first_shift), cross_pair_weight, cross_bias,
         cross_out_weight, row(cross_out_bias), row(second_gain), row(second_shift),
         feed_in_weight, row(feed_in_bias), feed_out_weight, row(feed_out_bias),
         row(third_gain), row(third_shift)],
        2,
        [low_rows, low_row_all, low_row_all, stats, stats, out_like((8, 128), F32), low_rows, wide_rows,
         out_like((n, hidden // n, features), BF16), out_like((n, hidden // n, features), BF16),
         out_like((n, half, features), BF16), out_like((8, features), F32), out_like((1, hidden), F32)],
        [wide_scratch, values_t, query_cols, peak, peak, sums,
         pltpu.VMEM((features, count), BF16), pltpu.VMEM((count, features), F32),
         pltpu.VMEM((count, 1), F32), pltpu.VMEM((count, features), BF16),
         pltpu.VMEM((features, count), BF16), pltpu.VMEM((count, hidden), BF16),
         pltpu.VMEM((count, hidden), F32), pltpu.VMEM((count, features), F32),
         pltpu.VMEM((count, features), BF16), pltpu.VMEM((features, count), BF16)],
        50 * square, 20 << 20,
    )

    back_scratch = [
        wide_scratch, values_t, query_cols, query_rows, query_cols, query_rows,
        pltpu.VMEM((features, count), F32), pltpu.VMEM((length, features), F32),
        pltpu.VMEM((length, features), F32), pltpu.VMEM((count, features), BF16),
    ]
    sent_like = out_like((max(n - 1, 1), count, features), BF16)
    (
        memory_own, memory_sent, cross_query_grad, cross_pair_grad, self_out_grad, self_grad,
        self_delta, g1, cross_sums,
    ) = run(
        functools.partial(cross_backward, n, rows_block),
        [place_one, cross_ranges, *memory_pieces, query_segment, source_column, cross_query,
         cross_grad, cross_keys, cross_values, cross_lse, cross_delta, g2, normal, rstd, first_low,
         row(first_gain), cross_query_weight, cross_pair_weight, self_out_weight, attended_t],
        2,
        [wide_rows, sent_like, out_like((n, half, features), BF16),
         out_like((n, 2 * half, features), BF16), out_like((n, half, features), BF16), low_rows,
         stats, wide_rows, out_like((8, features), F32)],
        back_scratch + [pltpu.VMEM((count, features), BF16)],
        30 * square, 15 << 20,
    )
    (input_own, input_sent, self_in_grad, self_sums) = run(
        functools.partial(self_backward, n, rows_block),
        [place_one, self_ranges, *input_pieces, query_segment, target_column, query, self_grad,
         keys, values, lse, self_delta, g1, self_in_weight],
        2,
        [wide_rows, sent_like, out_like((n, 3 * half, features), BF16), out_like((8, features), F32)],
        back_scratch,
        30 * square, 15 << 20,
    )

    memory_grad, input_grad = memory_own, input_own
    for step in range(1, n):
        memory_grad = memory_grad + shifted_back(memory_sent[step - 1], step).astype(F32)
        input_grad = input_grad + shifted_back(input_sent[step - 1], step).astype(F32)

    vectors = jnp.concatenate([self_sums[:2], cross_sums[:5], feed_sums[:6]], axis=0)
    count_small = vectors.shape[0]
    small = jnp.concatenate(
        [
            jnp.transpose(vectors.reshape(count_small, n, half), (1, 0, 2)).reshape(n, -1),
            in_bias_grad.reshape(n, -1),
        ],
        axis=1,
    )
    amount = small.shape[1]
    small_rows = -(-amount // (8 * WIDE)) * 8
    small = jnp.pad(small, ((0, 0), (0, small_rows * WIDE - amount))).reshape(n, small_rows, WIDE)
    parts = [in_grad, down_grad, cross_out_grad, cross_query_grad, cross_pair_grad, self_out_grad, self_in_grad]
    packed, small = reduce_all(n, groups, parts, small)
    small = small.reshape(-1)[:amount]
    plan = []
    start = 0
    shapes = []
    for part, columns in zip(parts, (hidden // features, 1, 1, 1, 2, 1, 3)):
        plan.append((start, columns))
        shapes.append(out_like((part.shape[1] // columns, columns * features), F32))
        start += part.shape[1]
    (
        feed_in_grad, feed_out_grad, cross_out_total, cross_query_total, cross_pair_total,
        self_out_total, self_in_total,
    ) = run(functools.partial(widen_kernel, plan), [packed], 0, shapes, [], 0, 12 << 20)
    rows_small = small[: count_small * half].reshape(count_small, half)
    (
        self_query_bias, self_value_bias, cross_query_bias, cross_value_bias, first_gain_grad,
        first_shift_grad, self_out_bias_grad, third_gain_grad, third_shift_grad, feed_out_bias_grad,
        second_gain_grad, second_shift_grad, cross_out_bias_grad,
    ) = [rows_small[index] for index in range(count_small)]
    return (
        layer_output[None],
        input_grad[None],
        memory_grad[None],
        self_in_total,
        jnp.stack([self_query_bias, self_value_bias]),
        self_out_total,
        self_out_bias_grad,
        first_gain_grad,
        first_shift_grad,
        cross_query_total,
        cross_pair_total,
        jnp.stack([cross_query_bias, cross_value_bias]),
        cross_out_total,
        cross_out_bias_grad,
        second_gain_grad,
        second_shift_grad,
        feed_in_grad,
        small[count_small * half :],
        feed_out_grad,
        feed_out_bias_grad,
        third_gain_grad,
        third_shift_grad,
    )


def solution(mesh):
    rows = P("dp", "blk", None)
    everywhere = P()
    split = P("blk", None)
    vector = P("blk")
    pair = P(None, "blk")
    return jax.shard_map(
        functools.partial(on_device, mesh.shape["blk"], mesh.shape["dp"]),
        mesh=mesh,
        in_specs=(rows, rows, rows, P("dp", None), P("dp", None)) + (everywhere,) * 19,
        out_specs=(
            rows, rows, rows, split, pair, split, vector, vector, vector, split, split, pair, split,
            vector, vector, vector, split, vector, split, vector, vector, vector,
        ),
        check_vma=False,
    )
```

```python
import functools

import jax
import jax.numpy as jnp
from jax import lax
from jax.experimental import pallas as pl
from jax.experimental.pallas import tpu as pltpu
from jax.sharding import PartitionSpec as P

HEAD = 64
TILE = 128
KEYS = 256
BACK_KEYS = 256
PAIR = 2 * HEAD
WIDE = 512
SCALE = HEAD ** (-0.5)
MASKED = -1e30
F32 = jnp.float32
BF16 = jnp.bfloat16
VMEM_LIMIT = 58 << 20


def nn(left, right):
    return lax.dot_general(left, right, (((1,), (0,)), ((), ())), preferred_element_type=F32)


def nt(left, right):
    return lax.dot_general(left, right, (((1,), (1,)), ((), ())), preferred_element_type=F32)


def tn(left, right):
    return lax.dot_general(left, right, (((0,), (0,)), ((), ())), preferred_element_type=F32)


def col_sum(field):
    return jnp.sum(field, axis=0, keepdims=True)


def normalize(field):
    centre = field - jnp.mean(field, axis=-1, keepdims=True)
    spread = jnp.mean(centre * centre, axis=-1, keepdims=True)
    rstd = lax.rsqrt(spread + 1e-05)
    return centre * rstd, rstd


def normalize_back(grad, gain, normal, rstd):
    scaled = grad * gain
    mean = jnp.mean(scaled, axis=-1, keepdims=True)
    along = jnp.mean(scaled * normal, axis=-1, keepdims=True)
    return (scaled - mean - normal * along) * rstd


def gate(hidden):
    size = jnp.abs(hidden)
    bell = jnp.exp(hidden * hidden * -0.5)
    ratio = 1.0 / (1.0 + (0.3275911 * 0.7071067811865476) * size)
    series = 1.061405429 * ratio - 1.453152027
    series = series * ratio + 1.421413741
    series = series * ratio - 0.284496736
    series = series * ratio + 0.254829592
    tail = (0.5 * series) * ratio * bell
    phi = jnp.where(hidden > 0.0, 1.0 - tail, tail)
    return hidden * phi, phi + hidden * (bell * 0.3989422804014327)


def dyn(index, size):
    return pl.ds(pl.multiple_of(index * size, size), size)


def even_lanes(rows, width):
    return (lax.broadcasted_iota(jnp.int32, (rows, width), 1) // HEAD) % 2 == 0


def even_rows(rows, width):
    return (lax.broadcasted_iota(jnp.int32, (rows, width), 0) // HEAD) % 2 == 0


def split_columns(tile_t, out_ref, tile):
    chosen = even_rows(*tile_t.shape)
    blank = jnp.zeros_like(tile_t)
    out_ref[:, pl.ds(pl.multiple_of(tile * 2 * TILE, 2 * TILE), TILE)] = jnp.where(chosen, tile_t, blank)
    out_ref[:, pl.ds(pl.multiple_of(tile * 2 * TILE + TILE, TILE), TILE)] = jnp.where(
        chosen, blank, tile_t
    )


def split_rows(tile_n, out_ref, tile):
    chosen = even_lanes(*tile_n.shape)
    blank = jnp.zeros_like(tile_n)
    out_ref[pl.ds(pl.multiple_of(tile * 2 * TILE, 2 * TILE), TILE), :] = jnp.where(chosen, tile_n, blank)
    out_ref[pl.ds(pl.multiple_of(tile * 2 * TILE + TILE, TILE), TILE), :] = jnp.where(
        chosen, blank, tile_n
    )


def spread_segments(column_ref, wide_ref):
    total = column_ref.shape[0]
    step = min(total, 512)

    @pl.loop(0, total // step)
    def _(block):
        rows = dyn(block, step)
        wide_ref[rows, :] = jnp.broadcast_to(column_ref[rows, :], (step, TILE))


def key_rows(low, chunk, length, size):
    wanted = low * TILE + chunk * size
    start = pl.multiple_of(jnp.minimum(wanted, length - size), TILE)
    return pl.ds(start, size), start, wanted


def chunk_bias(query_row, key_wide_ref, tile, rows, start, wanted, offset, causal):
    size = rows.size
    key_position = start + lax.broadcasted_iota(jnp.int32, (size, TILE), 0)
    allowed = (key_wide_ref[rows, :] == query_row) & (key_position >= wanted)
    if causal:
        query_position = offset + tile * TILE + lax.broadcasted_iota(jnp.int32, (size, TILE), 1)
        allowed = allowed & (key_position <= query_position)
    return jnp.where(allowed, 0.0, MASKED)


def attend(
    tiles, ranges_ref, query_row_ref, key_wide_ref, offset, causal,
    query_cols, keys, values_t, attended_t, lse_ref, peak, total, sums, held, held_low,
):
    pairs = WIDE // PAIR

    @pl.loop(0, tiles)
    def _(tile):
        peak[...] = jnp.full(peak.shape, MASKED, F32)
        total[...] = jnp.zeros(total.shape, F32)
        sums[...] = jnp.zeros(sums.shape, F32)
        query_row = query_row_ref[:, dyn(tile, TILE)]

        low, high = ranges_ref[0, tile], ranges_ref[1, tile]

        size = held.shape[1]

        @pl.loop(0, lax.div((high - low) * TILE + size - 1, size))
        def _(chunk):
            rows, start, wanted = key_rows(low, chunk, keys.shape[0], size)
            bias = chunk_bias(query_row, key_wide_ref, tile, rows, start, wanted, offset, causal)
            bias = jnp.concatenate([bias, bias], axis=1)
            factors = []
            for pair in range(pairs):
                lanes = slice(pair * PAIR, (pair + 1) * PAIR)
                scores = nn(keys[rows, lanes], query_cols[lanes, dyn(tile, 2 * TILE)]) + bias
                held[pair] = scores
                before = peak[pair : pair + 1, :]
                after = jnp.maximum(before, jnp.max(scores, axis=0, keepdims=True))
                factors.append(jnp.exp(before - after))
                peak[pair : pair + 1, :] = after
            for pair in range(pairs):
                weights = jnp.exp(held[pair] - peak[pair : pair + 1, :])
                total[pair : pair + 1, :] = total[pair : pair + 1, :] * factors[pair] + col_sum(weights)
                held_low[pair] = weights.astype(BF16)
            for pair in range(pairs):
                factor = factors[pair]
                mixed = nn(values_t[pair * PAIR : (pair + 1) * PAIR, rows], held_low[pair])
                first = slice(pair * PAIR, pair * PAIR + HEAD)
                second = slice(pair * PAIR + HEAD, (pair + 1) * PAIR)
                sums[first, :] = sums[first, :] * factor[:, :TILE] + mixed[:HEAD, :TILE]
                sums[second, :] = sums[second, :] * factor[:, TILE:] + mixed[HEAD:, TILE:]

        for pair in range(pairs):
            amount = total[pair : pair + 1, :]
            lse_ref[pair : pair + 1, dyn(tile, 2 * TILE)] = peak[pair : pair + 1, :] + jnp.log(amount)
            share = 1.0 / amount
            first = slice(pair * PAIR, pair * PAIR + HEAD)
            second = slice(pair * PAIR + HEAD, (pair + 1) * PAIR)
            attended_t[first, dyn(tile, TILE)] = (sums[first, :] * share[:, :TILE]).astype(BF16)
            attended_t[second, dyn(tile, TILE)] = (sums[second, :] * share[:, TILE:]).astype(BF16)


def attend_back(
    tile, low, high, query_row_ref, key_wide_ref, offset, causal,
    query_cols, query_rows, grad_cols, grad_rows, keys, keys_t, values, lse_ref, delta_ref,
    query_grad_t, key_grad, value_grad, held, held_low, held_grad,
):
    pairs = WIDE // PAIR
    query_row = query_row_ref[:, dyn(tile, TILE)]
    both = dyn(tile, 2 * TILE)

    size = held.shape[1]

    @pl.loop(0, lax.div((high - low) * TILE + size - 1, size))
    def _(chunk):
        rows, start, wanted = key_rows(low, chunk, keys.shape[0], size)
        bias = chunk_bias(query_row, key_wide_ref, tile, rows, start, wanted, offset, causal)
        bias = jnp.concatenate([bias, bias], axis=1)
        for pair in range(pairs):
            lanes = slice(pair * PAIR, (pair + 1) * PAIR)
            scores = nn(keys[rows, lanes], query_cols[lanes, both]) + bias
            probs = jnp.exp(scores - lse_ref[pair : pair + 1, both])
            held[pair] = probs
            held_low[pair] = probs.astype(BF16)
        for pair in range(pairs):
            lanes = slice(pair * PAIR, (pair + 1) * PAIR)
            prob_grad = nn(values[rows, lanes], grad_cols[lanes, both])
            held_grad[pair] = (held[pair] * (prob_grad - delta_ref[pair : pair + 1, both])).astype(BF16)
        for pair in range(pairs):
            lanes = slice(pair * PAIR, (pair + 1) * PAIR)
            value_grad[rows, lanes] += nn(held_low[pair], grad_rows[both, lanes])
            key_grad[rows, lanes] += nn(held_grad[pair], query_rows[both, lanes])
            mixed = nn(keys_t[lanes, rows], held_grad[pair])
            first = slice(pair * PAIR, pair * PAIR + HEAD)
            second = slice(pair * PAIR + HEAD, (pair + 1) * PAIR)
            query_grad_t[first, dyn(tile, TILE)] += mixed[:HEAD, :TILE]
            query_grad_t[second, dyn(tile, TILE)] += mixed[HEAD:, TILE:]


def clear(ref):
    rows = ref.shape[0]
    step = min(rows, 256)

    @pl.loop(0, rows // step)
    def _(block):
        ref[dyn(block, step), :] = jnp.zeros((step, ref.shape[1]), ref.dtype)


def transpose_rows(source, target):
    @pl.loop(0, source.shape[0] // TILE)
    def _(block):
        target[:, dyn(block, TILE)] = source[dyn(block, TILE), :].T


def out_like(shape, dtype):
    return jax.ShapeDtypeStruct(shape, dtype)


def run(body, ins, smem_count, outs, scratch, flops, bytes_accessed):
    vm = pl.BlockSpec(memory_space=pltpu.VMEM)
    sm = pl.BlockSpec(memory_space=pltpu.SMEM)
    return pl.pallas_call(
        body,
        in_specs=[sm] * smem_count + [vm] * (len(ins) - smem_count),
        out_specs=[vm] * len(outs),
        out_shape=outs,
        scratch_shapes=scratch,
        cost_estimate=pl.CostEstimate(
            flops=flops, bytes_accessed=bytes_accessed, transcendentals=0
        ),
        compiler_params=pltpu.CompilerParams(vmem_limit_bytes=VMEM_LIMIT),
    )(*ins)


def self_forward(n, rows_block, place_ref, ranges_ref, *refs):
    pieces, refs = refs[:n], refs[n:]
    (
        query_segment, key_segment, weight, bias, out_weight, out_bias, gain, shift,
        cross_weight, cross_bias,
        query_out, keys, values, attended_t, lse_ref, normal_out, rstd_out, first_low, cross_query,
        wide, values_t, query_cols, peak, total, sums, held, held_low,
    ) = refs
    count = pieces[0].shape[0]
    place = place_ref[0]
    spread_segments(key_segment, wide)

    for step in range(n):
        spot = lax.rem(place + n - step, n)

        @pl.when(spot <= place)
        def _():
            @pl.loop(0, count // rows_block)
            def _(block):
                source = pieces[step][dyn(block, rows_block), :]
                rows = dyn(spot * (count // rows_block) + block, rows_block)
                keys[rows, :] = nn(source, weight[:, WIDE : 2 * WIDE]).astype(BF16)
                values[rows, :] = (nn(source, weight[:, 2 * WIDE :]) + bias[1:2, :]).astype(BF16)
                if step == 0:
                    query = (nn(source, weight[:, :WIDE]) + bias[0:1, :]).astype(BF16)
                    query_out[dyn(block, rows_block), :] = (query.astype(F32) * SCALE).astype(BF16)

        @pl.when(spot > place)
        def _():
            @pl.loop(0, count // rows_block)
            def _(block):
                rows = dyn(spot * (count // rows_block) + block, rows_block)
                keys[rows, :] = jnp.zeros((rows_block, WIDE), BF16)
                values[rows, :] = jnp.zeros((rows_block, WIDE), BF16)

    transpose_rows(values, values_t)
    tiles = count // TILE

    @pl.loop(0, tiles)
    def _(tile):
        split_columns(query_out[dyn(tile, TILE), :].T, query_cols, tile)

    attend(
        tiles, ranges_ref, query_segment, wide, place * count, True,
        query_cols, keys, values_t, attended_t, lse_ref, peak, total, sums, held, held_low,
    )

    @pl.loop(0, count // rows_block)
    def _(block):
        rows = dyn(block, rows_block)
        attended = attended_t[:, rows].T
        field = pieces[0][rows, :].astype(F32) + nn(attended, out_weight[...]) + out_bias[...]
        normal, rstd = normalize(field)
        normal_out[rows, :] = normal
        rstd_out[rows, :] = rstd
        low = (normal * gain[...] + shift[...]).astype(BF16)
        first_low[rows, :] = low
        query = (nn(low, cross_weight[...]) + cross_bias[0:1, :]).astype(BF16)
        cross_query[rows, :] = (query.astype(F32) * SCALE).astype(BF16)


def cross_and_feed(n, rows_block, place_ref, ranges_ref, *refs):
    pieces, refs = refs[:n], refs[n:]
    (
        query_segment, key_segment, cotangent, cross_query, first_normal, first_gain, first_shift,
        pair_weight, cross_bias, out_weight, out_bias, gain, shift,
        in_weight, in_bias, down_weight, down_bias, last_gain, last_shift,
        layer_output, keys, values, lse_ref, delta_ref, out_grad, grad_out, g2_out,
        in_grad, down_grad, cross_out_grad, sums_out, in_bias_grad,
        wide, values_t, query_cols, peak, total, sums, held, held_low, attended_t, second_normal, second_rstd,
        second_low, second_low_t, active, slope, third, branch, branch_t,
    ) = refs
    count = pieces[0].shape[0]
    place = place_ref[0]
    spread_segments(key_segment, wide)
    blocks = count // rows_block

    for step in range(n):
        spot = lax.rem(place + n - step, n)

        @pl.loop(0, blocks)
        def _(block):
            source = pieces[step][dyn(block, rows_block), :]
            rows = dyn(spot * blocks + block, rows_block)
            keys[rows, :] = nn(source, pair_weight[:, :WIDE]).astype(BF16)
            values[rows, :] = (nn(source, pair_weight[:, WIDE:]) + cross_bias[1:2, :]).astype(BF16)

    transpose_rows(values, values_t)
    tiles = count // TILE

    @pl.loop(0, tiles)
    def _(tile):
        split_columns(cross_query[dyn(tile, TILE), :].T, query_cols, tile)

    attend(
        tiles, ranges_ref, query_segment, wide, 0, False,
        query_cols, keys, values_t, attended_t, lse_ref, peak, total, sums, held, held_low,
    )

    @pl.loop(0, blocks)
    def _(block):
        rows = dyn(block, rows_block)
        attended = attended_t[:, rows].T
        first = first_normal[rows, :] * first_gain[...] + first_shift[...]
        field = first + nn(attended, out_weight[...]) + out_bias[...]
        normal, rstd = normalize(field)
        second_normal[rows, :] = normal
        second_rstd[rows, :] = rstd
        second = normal * gain[...] + shift[...]
        third[rows, :] = second + down_bias[...]
        low = second.astype(BF16)
        second_low[rows, :] = low
        second_low_t[:, rows] = low.T

    hidden_size = in_weight.shape[1]
    chunk_size = min(WIDE, hidden_size // n)
    chunks = hidden_size // chunk_size

    @pl.loop(0, chunks)
    def _(chunk):
        lanes = dyn(chunk, chunk_size)

        @pl.loop(0, blocks)
        def _(block):
            rows = dyn(block, rows_block)
            hidden = nn(second_low[rows, :], in_weight[:, lanes]) + in_bias[:, lanes]
            value, derivative = gate(hidden)
            value = value.astype(BF16)
            active[rows, lanes] = value
            slope[rows, lanes] = derivative.astype(slope.dtype)
            third[rows, :] += nn(value, down_weight[dyn(chunk, chunk_size), :])

    sums_out[...] = jnp.zeros(sums_out.shape, F32)
    in_bias_grad[...] = jnp.zeros(in_bias_grad.shape, F32)

    @pl.loop(0, blocks)
    def _(block):
        rows = dyn(block, rows_block)
        normal, rstd = normalize(third[rows, :])
        layer_output[rows, :] = (normal * last_gain[...] + last_shift[...]).astype(BF16)
        outer = cotangent[rows, :].astype(F32)
        grad = normalize_back(outer, last_gain[...], normal, rstd)
        third[rows, :] = grad
        low = grad.astype(BF16)
        branch[rows, :] = low
        sums_out[0:1, :] += col_sum(outer * normal)
        sums_out[1:2, :] += col_sum(outer)
        sums_out[2:3, :] += col_sum(low.astype(F32))

    half = WIDE // n
    down_half = down_weight.shape[0] // n

    @pl.loop(0, chunks)
    def _(chunk):
        lanes = dyn(chunk, chunk_size)
        share = tn(active[:, lanes], branch[...]).astype(BF16)
        per_half = down_half // chunk_size
        down_grad[lax.div(chunk, per_half), dyn(lax.rem(chunk, per_half), chunk_size), :] = share

        @pl.loop(0, blocks)
        def _(block):
            rows = dyn(block, rows_block)
            inner = nt(branch[rows, :], down_weight[dyn(chunk, chunk_size), :])
            hidden_grad = (inner * slope[rows, lanes].astype(F32)).astype(BF16)
            active[rows, lanes] = hidden_grad
            in_bias_grad[:, lanes] += col_sum(hidden_grad.astype(F32))
            third[rows, :] += nt(hidden_grad, in_weight[:, lanes])

        share = nn(second_low_t[...], active[:, lanes]).astype(BF16)
        per_block = WIDE // chunk_size
        block_rows = dyn(lax.div(chunk, per_block), half)
        block_lanes = dyn(lax.rem(chunk, per_block), chunk_size)
        for part in range(n):
            in_grad[part, block_rows, block_lanes] = share[part * half : (part + 1) * half, :]

    @pl.loop(0, blocks)
    def _(block):
        rows = dyn(block, rows_block)
        outer = third[rows, :]
        normal = second_normal[rows, :]
        grad = normalize_back(outer, gain[...], normal, second_rstd[rows, :])
        g2_out[rows, :] = grad
        low = grad.astype(BF16)
        branch[rows, :] = low
        sums_out[3:4, :] += col_sum(outer * normal)
        sums_out[4:5, :] += col_sum(outer)
        sums_out[5:6, :] += col_sum(low.astype(F32))
        grad_out[rows, :] = nt(low, out_weight[...]).astype(BF16)

    share = nn(attended_t[...], branch[...]).astype(BF16)
    for part in range(n):
        cross_out_grad[part] = share[part * half : (part + 1) * half, :]

    write_delta(tiles, grad_out, attended_t, delta_ref)


def write_delta(tiles, grad, attended_t, delta_ref):
    @pl.loop(0, tiles)
    def _(tile):
        product = grad[dyn(tile, TILE), :].astype(F32).T * attended_t[:, dyn(tile, TILE)].astype(F32)
        for pair in range(WIDE // PAIR):
            start = pair * PAIR
            delta_ref[pair : pair + 1, pl.ds(pl.multiple_of(tile * 2 * TILE, 2 * TILE), TILE)] = col_sum(
                product[start : start + HEAD, :]
            )
            delta_ref[
                pair : pair + 1, pl.ds(pl.multiple_of(tile * 2 * TILE + TILE, TILE), TILE)
            ] = col_sum(product[start + HEAD : start + PAIR, :])


def prepare_back(tiles, query, grad, query_cols, query_rows, grad_cols, grad_rows):
    @pl.loop(0, tiles)
    def _(tile):
        here = query[dyn(tile, TILE), :]
        split_columns(here.T, query_cols, tile)
        split_rows(here, query_rows, tile)
        here = grad[dyn(tile, TILE), :]
        split_columns(here.T, grad_cols, tile)
        split_rows(here, grad_rows, tile)


def query_finish(tiles, query_grad_t, query_low, sums_out, index, rounded):
    @pl.loop(0, tiles)
    def _(tile):
        rows = dyn(tile, TILE)
        wide_grad = query_grad_t[:, rows].T * SCALE
        low = wide_grad.astype(BF16)
        query_low[rows, :] = low
        sums_out[index : index + 1, :] += col_sum(low.astype(F32) if rounded else wide_grad)


def spread_parts(n, share, target, start):
    half = WIDE // n
    for part in range(n):
        target[part, start : start + half, :] = share[part * half : (part + 1) * half, :].astype(BF16)


def row_product(n, place, pieces, source):
    count = pieces[0].shape[0]
    step_rows = min(count, 512)
    share = jnp.zeros((WIDE, WIDE), F32)
    for step in range(n):
        spot = lax.rem(place + n - step, n)
        for block in range(count // step_rows):
            rows = dyn(spot * (count // step_rows) + block, step_rows)
            share += tn(
                pieces[step][block * step_rows : (block + 1) * step_rows, :], source[rows, :].astype(BF16)
            )
    return share


def pair_back(n, place, rows_block, count, step, key_grad, value_grad, weight, first, sums_out, index, write):
    blocks = count // rows_block
    spot = lax.rem(place + n - step, n)

    @pl.loop(0, blocks)
    def _(block):
        rows = dyn(spot * blocks + block, rows_block)
        key_low = key_grad[rows, :].astype(BF16)
        value_part = value_grad[rows, :]
        sums_out[index : index + 1, :] += col_sum(value_part)
        value_low = value_part.astype(BF16)
        back = nt(key_low, weight[:, first : first + WIDE]) + nt(value_low, weight[:, first + WIDE : first + 2 * WIDE])
        write(dyn(block, rows_block), back)


def first_back(
    blocks, rows_block, g2, query_low, query_weight, first_normal, first_rstd, gain, self_out_weight,
    g1, branch, self_grad, sums_out, index,
):
    @pl.loop(0, blocks)
    def _(block):
        rows = dyn(block, rows_block)
        outer = g2[rows, :] + nt(query_low[rows, :], query_weight[...])
        normal = first_normal[rows, :]
        back = normalize_back(outer, gain[...], normal, first_rstd[rows, :])
        g1[rows, :] = back
        low = back.astype(BF16)
        branch[rows, :] = low
        sums_out[index : index + 1, :] += col_sum(outer * normal)
        sums_out[index + 1 : index + 2, :] += col_sum(outer)
        sums_out[index + 2 : index + 3, :] += col_sum(low.astype(F32))
        self_grad[rows, :] = nt(low, self_out_weight[...]).astype(BF16)


def cross_backward(n, rows_block, place_ref, ranges_ref, *refs):
    pieces, refs = refs[:n], refs[n:]
    (
        query_segment, key_segment, query, grad, keys, values, lse_ref, delta_ref, g2,
        first_normal, first_rstd, first_low, gain, query_weight, pair_weight, self_out_weight,
        self_attended_t,
        own_grad, sent_grad, query_grad_w, pair_grad_w, self_out_grad, self_grad, self_delta, g1_out, sums_out,
        wide, keys_t, query_cols, query_rows, grad_cols, grad_rows, query_grad_t, key_grad, value_grad,
        held, held_low, held_grad, query_low, branch,
    ) = refs
    count = pieces[0].shape[0]
    place = place_ref[0]
    tiles = count // TILE
    blocks = count // rows_block
    half = WIDE // n
    spread_segments(key_segment, wide)
    transpose_rows(keys, keys_t)
    prepare_back(tiles, query, grad, query_cols, query_rows, grad_cols, grad_rows)
    clear(query_grad_t)
    clear(key_grad)
    clear(value_grad)

    @pl.loop(0, tiles)
    def _(tile):
        attend_back(
            tile, ranges_ref[0, tile], ranges_ref[1, tile], query_segment, wide, 0, False,
            query_cols, query_rows, grad_cols, grad_rows, keys, keys_t, values, lse_ref, delta_ref,
            query_grad_t, key_grad, value_grad, held, held_low, held_grad,
        )

    sums_out[...] = jnp.zeros(sums_out.shape, F32)
    query_finish(tiles, query_grad_t, query_low, sums_out, 0, True)
    spread_parts(n, tn(first_low[...], query_low[...]), query_grad_w, 0)
    for step in range(n):

        def write(here, back):
            if step == 0:
                own_grad[here, :] = back
            else:
                sent_grad[step - 1, here, :] = back.astype(BF16)

        pair_back(n, place, rows_block, count, step, key_grad, value_grad, pair_weight, 0, sums_out, 1, write)
    spread_parts(n, row_product(n, place, pieces, key_grad), pair_grad_w, 0)
    spread_parts(n, row_product(n, place, pieces, value_grad), pair_grad_w, half)
    first_back(
        blocks, rows_block, g2, query_low, query_weight, first_normal, first_rstd, gain, self_out_weight,
        g1_out, branch, self_grad, sums_out, 2,
    )
    spread_parts(n, nn(self_attended_t[...], branch[...]), self_out_grad, 0)
    write_delta(tiles, self_grad, self_attended_t, self_delta)


def self_backward(n, rows_block, place_ref, ranges_ref, *refs):
    pieces, refs = refs[:n], refs[n:]
    (
        query_segment, key_segment, query, grad, keys, values, lse_ref, delta_ref, g1, weight,
        own_grad, sent_grad, grad_w, sums_out,
        wide, keys_t, query_cols, query_rows, grad_cols, grad_rows, query_grad_t, key_grad, value_grad,
        held, held_low, held_grad, query_low,
    ) = refs
    count = pieces[0].shape[0]
    place = place_ref[0]
    tiles = count // TILE
    half = WIDE // n
    spread_segments(key_segment, wide)
    transpose_rows(keys, keys_t)
    prepare_back(tiles, query, grad, query_cols, query_rows, grad_cols, grad_rows)
    clear(query_grad_t)
    clear(key_grad)
    clear(value_grad)

    @pl.loop(0, tiles)
    def _(tile):
        attend_back(
            tile, ranges_ref[0, tile], ranges_ref[1, tile], query_segment, wide, place * count, True,
            query_cols, query_rows, grad_cols, grad_rows, keys, keys_t, values, lse_ref, delta_ref,
            query_grad_t, key_grad, value_grad, held, held_low, held_grad,
        )

    sums_out[...] = jnp.zeros(sums_out.shape, F32)
    query_finish(tiles, query_grad_t, query_low, sums_out, 0, False)
    for step in range(n):

        def write(here, back):
            if step == 0:
                own_grad[here, :] = back + g1[here, :] + nt(query_low[here, :], weight[:, :WIDE])
            else:
                sent_grad[step - 1, here, :] = back.astype(BF16)

        pair_back(n, place, rows_block, count, step, key_grad, value_grad, weight, WIDE, sums_out, 1, write)
    spread_parts(n, tn(pieces[0][...], query_low[...]), grad_w, 0)
    spread_parts(n, row_product(n, place, pieces, key_grad), grad_w, half)
    spread_parts(n, row_product(n, place, pieces, value_grad), grad_w, 2 * half)


CORE_RATE = 0.0018
LINK_RATE = 0.0225
LATENCY = {"core": 1.1, "x": 2.4, "y": 2.4, "z": 3.0}
MARGIN = 1.0


def plan_steps(n, chunks, extras, segments):
    free = {"core": 0.0, "x": 0.0, "y": 0.0, "z": 0.0}
    now = 0.0
    pending = []
    plan = []

    def send(link, rows, rate=LINK_RATE):
        free[link] = max(free[link], now) + rows * rate
        return free[link] + LATENCY[link]

    def execute(kind, index, step):
        nonlocal now
        now += 0.15
        if kind == "chunk":
            unused, rows, y_first, unused = chunks[index]
            if step == 0:
                ready = send("core", n * rows // 2, CORE_RATE)
            elif step in (1, 2) and (step == 1) == y_first:
                ready = send("y", (n if y_first else 1) * rows // 4)
            elif step in (1, 2):
                ready = send("x", (n - 1) * rows // (4 if y_first else 2))
            elif step in (3, 4):
                ready = send("z", rows // 4)
            elif step == 5:
                ready = send("y", rows // 4)
            elif step == 6:
                ready = send("core", rows // 2, CORE_RATE)
            else:
                return
        elif kind == "extra":
            if step == 1:
                return
            ready = send("x", extras[index][0])
        else:
            if step == 4:
                return
            ready = now + (1.5, 3.2, 3.2, 4.0)[step]
        pending.append((ready, len(pending), kind, index, step + 1))

    for number in range(len(segments) + 1):
        order = []
        last = number == len(segments)
        if not last:
            now += segments[number]
            released = [("chunk", i) for i, chunk in enumerate(chunks) if chunk[3] == number]
            released += [("extra", i) for i, extra in enumerate(extras) if extra[1] == number]
            if number == len(segments) - 1:
                released.append(("small", 0))
            for kind, index in released:
                execute(kind, index, 0)
                order.append((kind, index, 0))
        while pending:
            pending.sort()
            if not last and pending[0][0] + MARGIN > now:
                break
            ready, unused, kind, index, step = pending.pop(0)
            now = max(now, ready)
            execute(kind, index, step)
            order.append((kind, index, step))
        plan.append(order)
    return plan, now


class Reducer:
    def __init__(self, n, groups, chunks, field, total, total_out, small, small_out, buffers):
        (
            self.from_core, self.from_blk, self.from_y, self.from_z,
            self.small_core, self.small_blk, self.small_y, self.small_z,
            self.sends, self.receives, self.small_sends, self.small_receives, self.stores,
        ) = buffers
        self.n, self.chunks, self.field, self.total, self.total_out = n, chunks, field, total, total_out
        self.small, self.small_out = small, small_out
        self.depth = depth = groups // 4
        self.group = group = lax.axis_index("dp")
        self.part = part = lax.axis_index("blk")
        self.core = lax.rem(group, 2)
        self.side = lax.rem(lax.div(group, 2), 2)
        self.level = lax.div(group, 4)
        self.core_peer = (group + 1 - 2 * self.core, part)
        self.side_peer = (group + 2 - 4 * self.side, part)
        self.blk_peers = [(group, lax.rem(part + step, n)) for step in range(1, n)]
        self.z_peers = [(lax.rem(group + 4 * step, groups), part) for step in range(1, depth)]
        self.per_chunk = 4 + (n - 1) + 2 * (depth - 1)

    def enter(self):
        peers = [self.core_peer, self.side_peer] + self.blk_peers + self.z_peers
        barrier = pltpu.get_barrier_semaphore()
        for peer in peers:
            pl.semaphore_signal(barrier, inc=1, device_id=peer, device_id_type=pl.DeviceIdType.MESH)
        pl.semaphore_wait(barrier, len(peers))

    def copy(self, source, target, sem, peer):
        return pltpu.make_async_remote_copy(
            src_ref=source, dst_ref=target, send_sem=self.sends.at[sem], recv_sem=self.receives.at[sem],
            device_id=peer, device_id_type=pl.DeviceIdType.MESH,
        )

    def small_copy(self, source, target, sem, peer):
        return pltpu.make_async_remote_copy(
            src_ref=source, dst_ref=target, send_sem=self.small_sends.at[sem],
            recv_sem=self.small_receives.at[sem], device_id=peer, device_id_type=pl.DeviceIdType.MESH,
        )

    def span(self, start, size):
        return pl.ds(pl.multiple_of(start, 16), size)

    def copies(self, index, step):
        start, rows, y_first, unused = self.chunks[index]
        n, depth, part = self.n, self.depth, self.part
        half, quarter = rows // 2, rows // 4
        piece = quarter // depth
        own_half = start + self.core * half
        own_quarter = own_half + self.side * quarter
        sem = index * self.per_chunk
        if step == 0:
            theirs = self.span(start + (1 - self.core) * half, half)
            return [
                self.copy(
                    self.field.at[:, theirs], self.from_core.at[:, pl.ds(start // 2, half)], sem, self.core_peer
                )
            ]
        if step in (1, 2) and (step == 1) == y_first:
            theirs = self.span(own_half + (1 - self.side) * quarter, quarter)
            into = pl.ds(start // 4, quarter)
            if y_first:
                return [self.copy(self.field.at[:, theirs], self.from_y.at[:, into], sem + 1, self.side_peer)]
            return [self.copy(self.field.at[part, theirs], self.from_y.at[0, into], sem + 1, self.side_peer)]
        if step in (1, 2):
            if y_first:
                mine, into = self.span(own_quarter, quarter), pl.ds(start // 2, quarter)
            else:
                mine, into = self.span(own_half, half), pl.ds(start // 2, half)
            return [
                self.copy(
                    self.field.at[lax.rem(part + hop, n), mine], self.from_blk.at[hop - 1, into],
                    sem + 3 + hop, self.blk_peers[hop - 1],
                )
                for hop in range(1, n)
            ]
        if step == 3:
            copies = []
            for hop in range(1, depth):
                theirs = self.span(own_quarter + lax.rem(self.level + hop, depth) * piece, piece)
                copies.append(
                    self.copy(
                        self.field.at[part, theirs], self.from_z.at[hop - 1, pl.ds(start // 4 // depth, piece)],
                        sem + 2 + n + hop, self.z_peers[hop - 1],
                    )
                )
            return copies
        if step == 4:
            mine = self.span(own_quarter + self.level * piece, piece)
            return [
                self.copy(
                    self.total.at[mine], self.total.at[mine], sem + 1 + n + depth + hop, self.z_peers[hop - 1]
                )
                for hop in range(1, depth)
            ]
        if step == 5:
            mine = self.span(own_quarter, quarter)
            return [self.copy(self.total.at[mine], self.total.at[mine], sem + 2, self.side_peer)]
        mine = self.span(own_half, half)
        return [self.copy(self.total.at[mine], self.total.at[mine], sem + 3, self.core_peer)]

    def add(self, part, start, size, terms, result=None):
        step = min(size, 64)

        @pl.loop(0, size // step)
        def _(block):
            here = self.span(start + block * step, step)
            value = self.field[part, here, :].astype(F32)
            for ref, index, begin in terms:
                value = value + ref[index, self.span(begin + block * step, step), :].astype(F32)
            if result is None:
                self.field[part, here, :] = value.astype(BF16)
            else:
                result[here, :] = value.astype(BF16)

    def store(self, index):
        rows = pl.ds(self.chunks[index][0], self.chunks[index][1])
        return pltpu.make_async_copy(self.total.at[rows], self.total_out.at[rows], self.stores.at[index])

    def chunk_step(self, index, step):
        start, rows, y_first, unused = self.chunks[index]
        n, depth, part = self.n, self.depth, self.part
        half, quarter = rows // 2, rows // 4
        piece = quarter // depth
        own_half = start + self.core * half
        own_quarter = own_half + self.side * quarter
        if step > 0:
            for copy in self.copies(index, step - 1):
                copy.wait()
        if step == 1:
            for b in range(n):
                self.add(b, own_half, half, [(self.from_core, b, start // 2)])
        elif step in (2, 3) and (step == 2) == y_first:
            for b in range(n) if y_first else [part]:
                self.add(b, own_quarter, quarter, [(self.from_y, b if y_first else 0, start // 4)])
        elif step in (2, 3):
            begin, size = (own_quarter, quarter) if y_first else (own_half, half)
            self.add(part, begin, size, [(self.from_blk, hop, start // 2) for hop in range(n - 1)])
        elif step == 4:
            self.add(
                part, own_quarter + self.level * piece, piece,
                [(self.from_z, hop, start // 4 // depth) for hop in range(depth - 1)], self.total,
            )
        if step < 7:
            for copy in self.copies(index, step):
                copy.start()
        else:
            self.store(index).start()

    def small_copies(self, step):
        part, n = self.part, self.n
        if step == 0:
            return [self.small_copy(self.small.at[0], self.small_core, 0, self.core_peer)]
        if step == 1:
            return [
                self.small_copy(
                    self.small.at[1, lax.rem(part + hop, n)], self.small_blk.at[hop - 1], hop,
                    self.blk_peers[hop - 1],
                )
                for hop in range(1, n)
            ]
        if step == 2:
            return [self.small_copy(self.small.at[1, part], self.small_y, n, self.side_peer)]
        return [
            self.small_copy(self.small_y, self.small_z.at[hop - 1], n + hop, self.z_peers[hop - 1])
            for hop in range(1, self.depth)
        ]

    def small_step(self, step):
        part = self.part
        if step > 0:
            for copy in self.small_copies(step - 1):
                copy.wait()
        if step == 1:
            self.small[1] = self.small[0] + self.small_core[...]
        elif step == 2:
            held = self.small[1, part]
            for hop in range(self.n - 1):
                held = held + self.small_blk[hop]
            self.small[1, part] = held
        elif step == 3:
            self.small_y[...] = self.small_y[...] + self.small[1, part]
        elif step == 4:
            held = self.small_y[...]
            for hop in range(self.depth - 1):
                held = held + self.small_z[hop]
            self.small_out[...] = held
        if step < 4:
            for copy in self.small_copies(step):
                copy.start()

    def finish(self):
        for index in range(len(self.chunks)):
            self.store(index).wait()


def reducer_scratch(n, groups, chunks, rows, small_shape):
    depth = groups // 4
    per_chunk = 4 + (n - 1) + 2 * (depth - 1)
    return [
        pltpu.VMEM((n, rows // 2, WIDE), BF16),
        pltpu.VMEM((n - 1, rows // 2, WIDE), BF16),
        pltpu.VMEM((n, rows // 4, WIDE), BF16),
        pltpu.VMEM((depth - 1, rows // 4 // depth, WIDE), BF16),
        pltpu.VMEM((n, *small_shape), F32),
        pltpu.VMEM((n - 1, *small_shape), F32),
        pltpu.VMEM(small_shape, F32),
        pltpu.VMEM((depth - 1, *small_shape), F32),
        pltpu.SemaphoreType.DMA((len(chunks) * per_chunk,)),
        pltpu.SemaphoreType.DMA((len(chunks) * per_chunk,)),
        pltpu.SemaphoreType.DMA((n + depth,)),
        pltpu.SemaphoreType.DMA((n + depth,)),
        pltpu.SemaphoreType.DMA((len(chunks),)),
    ]


def reduce_kernel(n, groups, chunks, plan, part_rows, *refs):
    sources, refs = refs[: len(part_rows)], refs[len(part_rows) :]
    small_in, total_out, small_out, field, total, small, load_sem = refs[:7]
    loads = []
    start = 0
    for index, source in enumerate(sources):
        loads.append(
            pltpu.make_async_copy(source, field.at[:, pl.ds(start, part_rows[index])], load_sem.at[index])
        )
        loads[-1].start()
        start += part_rows[index]
    reducer = Reducer(n, groups, chunks, field, total, total_out, small, small_out, refs[7:])
    small[0] = small_in[...]
    reducer.enter()
    for load in loads:
        load.wait()
    for order in plan:
        for kind, index, step in order:
            if kind == "chunk":
                reducer.chunk_step(index, step)
            else:
                reducer.small_step(step)
    reducer.finish()


def reduce_all(n, groups, parts, small):
    part_rows = [part.shape[1] for part in parts]
    rows = sum(part_rows)
    chunk_rows = max(16 * groups, rows // 8)
    chunks = [(start, chunk_rows, False, 0) for start in range(0, rows, chunk_rows)]
    plan, unused = plan_steps(n, chunks, [], [0.0])
    small_shape = small.shape[1:]
    vm = pl.BlockSpec(memory_space=pltpu.VMEM)
    hbm = pl.BlockSpec(memory_space=pl.ANY)
    return pl.pallas_call(
        functools.partial(reduce_kernel, n, groups, chunks, plan, part_rows),
        in_specs=[hbm] * len(parts) + [vm],
        out_specs=[hbm, vm],
        out_shape=[out_like((rows, WIDE), BF16), out_like(small_shape, F32)],
        scratch_shapes=[
            pltpu.VMEM((n, rows, WIDE), BF16),
            pltpu.VMEM((rows, WIDE), BF16),
            pltpu.VMEM((2, n, *small_shape), F32),
            pltpu.SemaphoreType.DMA((len(parts),)),
            *reducer_scratch(n, groups, chunks, rows, small_shape),
        ],
        compiler_params=pltpu.CompilerParams(
            vmem_limit_bytes=VMEM_LIMIT, collective_id=0, has_side_effects=True
        ),
    )(*parts, small)


Y_FIRST = [letter == "y" for letter in "yyxyxyxyxxyy"]
BACK_SEGMENTS = [
    3.5, 3.2, 3.2, 3.2, 3.2, 1.5, 3.0, 3.5, 2.2,
    2.5, 2.6, 2.6, 3.2, 3.2, 1.5, 1.2, 1.2, 2.4,
]


def back_chunks(half, hidden_rows):
    released = [(2 * half, 0)] * (hidden_rows // half) + [(half, 0)]
    released += [(half, segment) for segment in (5, 6, 6, 7, 14, 15, 16)]
    chunks = []
    start = 0
    for index, (rows, segment) in enumerate(released):
        chunks.append((start, rows, Y_FIRST[index % len(Y_FIRST)], segment))
        start += rows
    return chunks


def back_kernel(n, groups, rows_block, chunks, plan, load_plan, *refs):
    feed_refs, refs = refs[:3], refs[3:]
    streamed, refs = refs[: len(load_plan)], refs[len(load_plan) :]
    (
        query_segment, memory_segment, target_segment, cross_query, cross_grad, cross_keys, cross_values,
        cross_lse, cross_delta, feed_sums, in_bias_grad, gain, first_rstd, self_lse,
        total_out, small_out, memory_grad, input_grad,
        field, total, small, sums, memory_sent, memory_got, input_sent, input_got,
        wide, keys_t, query_cols, query_rows, grad_cols, grad_rows, query_grad_t, key_grad, value_grad,
        held, held_low, held_grad, query_low, branch, self_grad, self_delta, g1,
        feed_sem, load_sem, extra_send, extra_recv,
    ) = refs[:47]
    refs = refs[47:]
    held_loads, buffers = refs[: len(load_plan)], refs[len(load_plan) :]
    count = cross_query.shape[0]
    length = cross_keys.shape[0]
    tiles = count // TILE
    blocks = count // rows_block
    half = WIDE // n
    place = lax.axis_index("blk")

    feed_loads = []
    start = 0
    for index, source in enumerate(feed_refs):
        rows = source.shape[1]
        feed_loads.append(
            pltpu.make_async_copy(source, field.at[:, pl.ds(start, rows)], feed_sem.at[index])
        )
        feed_loads[-1].start()
        start += rows
    loads = [
        pltpu.make_async_copy(source, target, load_sem.at[index])
        for index, (source, target) in enumerate(zip(streamed, held_loads))
    ]
    for load in loads:
        load.start()
    memory_pieces, held_loads = held_loads[:n], held_loads[n:]
    (
        pair_weight, first_low, query_weight, g2, first_normal, self_out_weight, self_attended_t,
        self_keys, self_values, self_query,
    ) = held_loads[:10]
    input_pieces, (self_in_weight,) = held_loads[10 : 10 + n], held_loads[10 + n :]

    reducer = Reducer(n, groups, chunks, field, total, total_out, small, small_out, buffers)
    reducer.enter()

    def extra_copies(index):
        sent, got = ((memory_sent, memory_got), (input_sent, input_got))[index]
        return [
            pltpu.make_async_remote_copy(
                src_ref=sent.at[step - 1], dst_ref=got.at[step - 1],
                send_sem=extra_send.at[index * (n - 1) + step - 1],
                recv_sem=extra_recv.at[index * (n - 1) + step - 1],
                device_id=(lax.axis_index("dp"), lax.rem(place + n - step, n)),
                device_id_type=pl.DeviceIdType.MESH,
            )
            for step in range(1, n)
        ]

    def run_steps(number):
        for kind, index, step in plan[number]:
            if kind == "chunk":
                reducer.chunk_step(index, step)
            elif kind == "small":
                reducer.small_step(step)
            elif step == 0:
                for copy in extra_copies(index):
                    copy.start()
            else:
                got, result = ((memory_got, memory_grad), (input_got, input_grad))[index]
                for copy in extra_copies(index):
                    copy.wait()

                @pl.loop(0, blocks)
                def _(block):
                    rows = dyn(block, rows_block)
                    value = result[rows, :]
                    for step in range(n - 1):
                        value = value + got[step, rows, :].astype(F32)
                    result[rows, :] = value

    def wait_loads(first, last):
        for load in loads[first:last]:
            load.wait()

    spread_segments(memory_segment, wide)
    transpose_rows(cross_keys, keys_t)
    prepare_back(tiles, cross_query, cross_grad, query_cols, query_rows, grad_cols, grad_rows)
    clear(query_grad_t)
    clear(key_grad)
    clear(value_grad)
    sums[...] = jnp.zeros(sums.shape, F32)
    for load in feed_loads:
        load.wait()
    run_steps(0)
    for tile in range(tiles):
        attend_back(
            tile, 0, length // TILE, query_segment, wide, 0, False,
            query_cols, query_rows, grad_cols, grad_rows, cross_keys, keys_t, cross_values,
            cross_lse, cross_delta, query_grad_t, key_grad, value_grad, held, held_low, held_grad,
        )
        run_steps(1 + tile)
    base = 2 * in_bias_grad.shape[1] // n + half
    wait_loads(0, n + 7)
    query_finish(tiles, query_grad_t, query_low, sums, 2, True)
    spread_parts(n, tn(first_low[...], query_low[...]), field, base)
    run_steps(5)
    spread_parts(n, row_product(n, place, memory_pieces, key_grad), field, base + half)
    spread_parts(n, row_product(n, place, memory_pieces, value_grad), field, base + 2 * half)
    run_steps(6)
    first_back(
        blocks, rows_block, g2, query_low, query_weight, first_normal, first_rstd, gain, self_out_weight,
        g1, branch, self_grad, sums, 4,
    )
    spread_parts(n, nn(self_attended_t[...], branch[...]), field, base + 3 * half)
    write_delta(tiles, self_grad, self_attended_t, self_delta)
    run_steps(7)
    for step in range(n):

        def write(here, back):
            if step == 0:
                memory_grad[here, :] = back
            else:
                memory_sent[step - 1, here, :] = back.astype(BF16)

        pair_back(n, place, rows_block, count, step, key_grad, value_grad, pair_weight, 0, sums, 3, write)
    run_steps(8)

    wait_loads(n + 7, len(loads))
    spread_segments(target_segment, wide)
    transpose_rows(self_keys, keys_t)
    prepare_back(tiles, self_query, self_grad, query_cols, query_rows, grad_cols, grad_rows)
    clear(query_grad_t)
    clear(key_grad)
    clear(value_grad)
    run_steps(9)
    for tile in range(tiles):
        attend_back(
            tile, 0, place * tiles + tile + 1, query_segment, wide, place * count, True,
            query_cols, query_rows, grad_cols, grad_rows, self_keys, keys_t, self_values,
            self_lse, self_delta, query_grad_t, key_grad, value_grad, held, held_low, held_grad,
        )
        run_steps(10 + tile)
    query_finish(tiles, query_grad_t, query_low, sums, 0, False)
    spread_parts(n, tn(input_pieces[0][...], query_low[...]), field, base + 4 * half)
    run_steps(14)
    spread_parts(n, row_product(n, place, input_pieces, key_grad), field, base + 5 * half)
    run_steps(15)
    spread_parts(n, row_product(n, place, input_pieces, value_grad), field, base + 6 * half)
    run_steps(16)
    for step in range(n):

        def write(here, back):
            if step == 0:
                input_grad[here, :] = back + g1[here, :] + nt(query_low[here, :], self_in_weight[:, :WIDE])
            else:
                input_sent[step - 1, here, :] = back.astype(BF16)

        pair_back(n, place, rows_block, count, step, key_grad, value_grad, self_in_weight, WIDE, sums, 1, write)
    small[...] = jnp.zeros(small.shape, F32)
    for part in range(n):
        here = slice(part * half, (part + 1) * half)
        small[0, part, 0:7, :] = sums[0:7, here]
        small[0, part, 7:13, :] = feed_sums[0:6, here]
        wide_half = in_bias_grad.shape[1] // n
        for row in range(wide_half // half):
            begin = part * wide_half + row * half
            small[0, part, 13 + row : 14 + row, :] = in_bias_grad[:, begin : begin + half]
    run_steps(17)
    run_steps(18)
    reducer.finish()


def back_and_reduce(n, groups, rows_block, feed_grads, streamed, resident):
    count, features = resident[3].shape
    length = n * count
    hidden_rows = feed_grads[0].shape[1]
    half = features // n
    rows = sum(part.shape[1] for part in feed_grads) + 7 * half
    chunks = back_chunks(half, hidden_rows)
    extras = [((n - 1) * count, 8), ((n - 1) * count, 17)]
    plan, unused = plan_steps(n, chunks, extras, BACK_SEGMENTS)
    small_shape = (-(-(13 + hidden_rows // half * half * n // features) // 8) * 8 + 8, half)
    vm = pl.BlockSpec(memory_space=pltpu.VMEM)
    hbm = pl.BlockSpec(memory_space=pl.ANY)
    low_rows = pltpu.VMEM((count, features), BF16)
    wide_rows = pltpu.VMEM((count, features), F32)
    columns = pltpu.VMEM((features, 2 * count), BF16)
    doubled = pltpu.VMEM((2 * count, features), BF16)
    all_wide = pltpu.VMEM((length, features), F32)
    sent = pltpu.VMEM((n - 1, count, features), BF16)
    held = (features // PAIR, BACK_KEYS, 2 * TILE)
    return pl.pallas_call(
        functools.partial(back_kernel, n, groups, rows_block, chunks, plan, [part.shape for part in streamed]),
        in_specs=[hbm] * (len(feed_grads) + len(streamed)) + [vm] * len(resident),
        out_specs=[hbm, vm, vm, vm],
        out_shape=[
            out_like((rows, WIDE), BF16), out_like(small_shape, F32),
            out_like((count, features), F32), out_like((count, features), F32),
        ],
        scratch_shapes=[
            pltpu.VMEM((n, rows, WIDE), BF16), pltpu.VMEM((rows, WIDE), BF16),
            pltpu.VMEM((2, n, *small_shape), F32), pltpu.VMEM((8, features), F32),
            sent, sent, sent, sent,
            pltpu.VMEM((length, TILE), jnp.int32), pltpu.VMEM((features, length), BF16),
            columns, doubled, columns, doubled,
            pltpu.VMEM((features, count), F32), all_wide, all_wide,
            pltpu.VMEM(held, F32), pltpu.VMEM(held, BF16), pltpu.VMEM(held, BF16),
            low_rows, low_rows, low_rows, pltpu.VMEM((features // PAIR, 2 * count), F32), wide_rows,
            pltpu.SemaphoreType.DMA((len(feed_grads),)), pltpu.SemaphoreType.DMA((len(streamed),)),
            pltpu.SemaphoreType.DMA((2 * (n - 1),)), pltpu.SemaphoreType.DMA((2 * (n - 1),)),
            *[pltpu.VMEM(part.shape, part.dtype) for part in streamed],
            *reducer_scratch(n, groups, chunks, rows, small_shape),
        ],
        compiler_params=pltpu.CompilerParams(
            vmem_limit_bytes=VMEM_LIMIT, collective_id=0, has_side_effects=True
        ),
    )(*feed_grads, *streamed, *resident)


def widen_kernel(plan, source, *outs):
    for out, (start, columns) in zip(outs, plan):
        height = out.shape[0]
        for column in range(columns):
            out[:, column * WIDE : (column + 1) * WIDE] = source[
                start + column * height : start + (column + 1) * height, :
            ].astype(F32)


def key_ranges(query_segment, key_segment, tiles, limit):
    edges = query_segment.reshape(tiles, TILE)
    low = jnp.sum((key_segment[None, :] < edges[:, :1]).astype(jnp.int32), axis=1)
    high = jnp.sum((key_segment[None, :] <= edges[:, TILE - 1 :]).astype(jnp.int32), axis=1)
    if limit is not None:
        high = jnp.minimum(high, limit)
    return jnp.stack([low // TILE, (high + TILE - 1) // TILE]).astype(jnp.int32)


def on_device(
    n, groups,
    inputs, memory, cotangent, target_segments, memory_segments,
    self_in_weight, self_in_bias, self_out_weight, self_out_bias, first_gain, first_shift,
    cross_query_weight, cross_pair_weight, cross_bias, cross_out_weight, cross_out_bias,
    second_gain, second_shift, feed_in_weight, feed_in_bias, feed_out_weight, feed_out_bias,
    third_gain, third_shift,
):
    input_rows, memory_rows, cotangent_rows = inputs[0], memory[0], cotangent[0]
    count, features = input_rows.shape
    length = n * count
    hidden = feed_in_weight.shape[1]
    rows_block = min(count, 256)
    tiles = count // TILE
    half = features // n
    place = lax.axis_index("blk").astype(jnp.int32)

    def shifted(field, step):
        return lax.ppermute(field, "blk", [(s, (s + step) % n) for s in range(n)])

    def shifted_back(field, step):
        return lax.ppermute(field, "blk", [(s, (s - step) % n) for s in range(n)])

    input_pieces = [input_rows] + [shifted(input_rows, step) for step in range(1, n)]
    memory_pieces = [memory_rows] + [shifted(memory_rows, step) for step in range(1, n)]

    target_row = target_segments[0]
    source_row = memory_segments[0]
    target_here = lax.dynamic_slice_in_dim(target_row, place * count, count, 0)
    self_ranges = key_ranges(
        target_here, target_row, tiles, place * count + TILE * (1 + jnp.arange(tiles, dtype=jnp.int32))
    )
    cross_ranges = key_ranges(target_here, source_row, tiles, None)
    place_one = place[None]
    query_segment = target_here[None, :]
    target_column = target_row[:, None]
    source_column = source_row[:, None]

    def row(vector):
        return vector[None, :]

    stats = out_like((WIDE // PAIR, 2 * count), F32)
    low_rows = out_like((count, features), BF16)
    wide_rows = out_like((count, features), F32)
    low_row_all = out_like((length, features), BF16)
    statistic = out_like((count, 1), F32)
    wide_scratch = pltpu.VMEM((length, TILE), jnp.int32)
    values_t = pltpu.VMEM((features, length), BF16)
    query_cols = pltpu.VMEM((features, 2 * count), BF16)
    query_rows = pltpu.VMEM((2 * count, features), BF16)
    peak = pltpu.VMEM((8, 2 * TILE), F32)
    sums = pltpu.VMEM((features, TILE), F32)
    held = pltpu.VMEM((features // PAIR, KEYS, 2 * TILE), F32)
    held_low = pltpu.VMEM((features // PAIR, KEYS, 2 * TILE), BF16)
    square = 2 * count * features * features

    (
        query, keys, values, attended_t, lse, normal, rstd, first_low, cross_query
    ) = run(
        functools.partial(self_forward, n, rows_block),
        [place_one, self_ranges, *input_pieces, query_segment, target_column,
         self_in_weight, self_in_bias, self_out_weight, row(self_out_bias), row(first_gain),
         row(first_shift), cross_query_weight, cross_bias],
        2,
        [low_rows, low_row_all, low_row_all, out_like((features, count), BF16), stats, wide_rows,
         statistic, low_rows, low_rows],
        [wide_scratch, values_t, query_cols, peak, peak, sums, held, held_low],
        20 * square, 10 << 20,
    )

    (
        layer_output, cross_keys, cross_values, cross_lse, cross_delta, unused, cross_grad, g2,
        in_grad, down_grad, cross_out_grad, feed_sums, in_bias_grad,
    ) = run(
        functools.partial(cross_and_feed, n, rows_block),
        [place_one, cross_ranges, *memory_pieces, query_segment, source_column, cotangent_rows,
         cross_query, normal, row(first_gain), row(first_shift), cross_pair_weight, cross_bias,
         cross_out_weight, row(cross_out_bias), row(second_gain), row(second_shift),
         feed_in_weight, row(feed_in_bias), feed_out_weight, row(feed_out_bias),
         row(third_gain), row(third_shift)],
        2,
        [low_rows, low_row_all, low_row_all, stats, stats, out_like((8, 128), F32), low_rows, wide_rows,
         out_like((n, hidden // n, features), BF16), out_like((n, hidden // n, features), BF16),
         out_like((n, half, features), BF16), out_like((8, features), F32), out_like((1, hidden), F32)],
        [wide_scratch, values_t, query_cols, peak, peak, sums, held, held_low,
         pltpu.VMEM((features, count), BF16), pltpu.VMEM((count, features), F32),
         pltpu.VMEM((count, 1), F32), pltpu.VMEM((count, features), BF16),
         pltpu.VMEM((features, count), BF16), pltpu.VMEM((count, hidden), BF16),
         pltpu.VMEM((count, hidden), F32), pltpu.VMEM((count, features), F32),
         pltpu.VMEM((count, features), BF16), pltpu.VMEM((features, count), BF16)],
        50 * square, 20 << 20,
    )

    if length <= 1024 and half % TILE == 0:
        packed, small, memory_grad, input_grad = back_and_reduce(
            n, groups, rows_block,
            [in_grad, down_grad, cross_out_grad],
            [*memory_pieces, cross_pair_weight, first_low, cross_query_weight, g2, normal, self_out_weight,
             attended_t, keys, values, query, *input_pieces, self_in_weight],
            [query_segment, source_column, target_column, cross_query, cross_grad, cross_keys, cross_values,
             cross_lse, cross_delta, feed_sums, in_bias_grad, row(first_gain), rstd, lse],
        )
        count_small = 13
        small = small.reshape(-1)[: count_small * half + hidden // n]
    else:
        back_scratch = [
            wide_scratch, values_t, query_cols, query_rows, query_cols, query_rows,
            pltpu.VMEM((features, count), F32), pltpu.VMEM((length, features), F32),
            pltpu.VMEM((length, features), F32), held, held_low, held_low, pltpu.VMEM((count, features), BF16),
        ]
        sent_like = out_like((max(n - 1, 1), count, features), BF16)
        (
            memory_own, memory_sent, cross_query_grad, cross_pair_grad, self_out_grad, self_grad,
            self_delta, g1, cross_sums,
        ) = run(
            functools.partial(cross_backward, n, rows_block),
            [place_one, cross_ranges, *memory_pieces, query_segment, source_column, cross_query,
             cross_grad, cross_keys, cross_values, cross_lse, cross_delta, g2, normal, rstd, first_low,
             row(first_gain), cross_query_weight, cross_pair_weight, self_out_weight, attended_t],
            2,
            [wide_rows, sent_like, out_like((n, half, features), BF16),
             out_like((n, 2 * half, features), BF16), out_like((n, half, features), BF16), low_rows,
             stats, wide_rows, out_like((8, features), F32)],
            back_scratch + [pltpu.VMEM((count, features), BF16)],
            30 * square, 15 << 20,
        )
        (input_own, input_sent, self_in_grad, self_sums) = run(
            functools.partial(self_backward, n, rows_block),
            [place_one, self_ranges, *input_pieces, query_segment, target_column, query, self_grad,
             keys, values, lse, self_delta, g1, self_in_weight],
            2,
            [wide_rows, sent_like, out_like((n, 3 * half, features), BF16), out_like((8, features), F32)],
            back_scratch,
            30 * square, 15 << 20,
        )

        memory_grad, input_grad = memory_own, input_own
        for step in range(1, n):
            memory_grad = memory_grad + shifted_back(memory_sent[step - 1], step).astype(F32)
            input_grad = input_grad + shifted_back(input_sent[step - 1], step).astype(F32)

        vectors = jnp.concatenate([self_sums[:2], cross_sums[:5], feed_sums[:6]], axis=0)
        count_small = vectors.shape[0]
        small = jnp.concatenate(
            [
                jnp.transpose(vectors.reshape(count_small, n, half), (1, 0, 2)).reshape(n, -1),
                in_bias_grad.reshape(n, -1),
            ],
            axis=1,
        )
        amount = small.shape[1]
        small_rows = -(-amount // (8 * WIDE)) * 8
        small = jnp.pad(small, ((0, 0), (0, small_rows * WIDE - amount))).reshape(n, small_rows, WIDE)
        packed, small = reduce_all(
            n, groups,
            [in_grad, down_grad, cross_out_grad, cross_query_grad, cross_pair_grad, self_out_grad, self_in_grad],
            small,
        )
        small = small.reshape(-1)[:amount]
    plan = []
    start = 0
    shapes = []
    for height, columns in (
        (half, hidden // features), (hidden // n, 1), (half, 1), (half, 1), (half, 2), (half, 1), (half, 3)
    ):
        plan.append((start, columns))
        shapes.append(out_like((height, columns * features), F32))
        start += height * columns
    (
        feed_in_grad, feed_out_grad, cross_out_total, cross_query_total, cross_pair_total,
        self_out_total, self_in_total,
    ) = run(functools.partial(widen_kernel, plan), [packed], 0, shapes, [], 0, 12 << 20)
    rows_small = small[: count_small * half].reshape(count_small, half)
    (
        self_query_bias, self_value_bias, cross_query_bias, cross_value_bias, first_gain_grad,
        first_shift_grad, self_out_bias_grad, third_gain_grad, third_shift_grad, feed_out_bias_grad,
        second_gain_grad, second_shift_grad, cross_out_bias_grad,
    ) = [rows_small[index] for index in range(count_small)]
    return (
        layer_output[None],
        input_grad[None],
        memory_grad[None],
        self_in_total,
        jnp.stack([self_query_bias, self_value_bias]),
        self_out_total,
        self_out_bias_grad,
        first_gain_grad,
        first_shift_grad,
        cross_query_total,
        cross_pair_total,
        jnp.stack([cross_query_bias, cross_value_bias]),
        cross_out_total,
        cross_out_bias_grad,
        second_gain_grad,
        second_shift_grad,
        feed_in_grad,
        small[count_small * half :],
        feed_out_grad,
        feed_out_bias_grad,
        third_gain_grad,
        third_shift_grad,
    )


def solution(mesh):
    rows = P("dp", "blk", None)
    everywhere = P()
    split = P("blk", None)
    vector = P("blk")
    pair = P(None, "blk")
    return jax.shard_map(
        functools.partial(on_device, mesh.shape["blk"], mesh.shape["dp"]),
        mesh=mesh,
        in_specs=(rows, rows, rows, P("dp", None), P("dp", None)) + (everywhere,) * 19,
        out_specs=(
            rows, rows, rows, split, pair, split, vector, vector, vector, split, split, pair, split,
            vector, vector, vector, split, vector, split, vector, vector, vector,
        ),
        check_vma=False,
    )
```

```python
import functools

import jax
import jax.numpy as jnp
from jax import lax
from jax.experimental import pallas as pl
from jax.experimental.pallas import tpu as pltpu
from jax.sharding import PartitionSpec as P

HEAD = 64
TILE = 128
KEYS = 256
BACK_KEYS = 256
PAIR = 2 * HEAD
WIDE = 512
SCALE = HEAD ** (-0.5)
MASKED = -1e30
F32 = jnp.float32
BF16 = jnp.bfloat16
VMEM_LIMIT = 62 << 20


def nn(left, right):
    return lax.dot_general(left, right, (((1,), (0,)), ((), ())), preferred_element_type=F32)


def nt(left, right):
    return lax.dot_general(left, right, (((1,), (1,)), ((), ())), preferred_element_type=F32)


def tn(left, right):
    return lax.dot_general(left, right, (((0,), (0,)), ((), ())), preferred_element_type=F32)


def col_sum(field):
    return jnp.sum(field, axis=0, keepdims=True)


def normalize(field):
    centre = field - jnp.mean(field, axis=-1, keepdims=True)
    spread = jnp.mean(centre * centre, axis=-1, keepdims=True)
    rstd = lax.rsqrt(spread + 1e-05)
    return centre * rstd, rstd


def normalize_back(grad, gain, normal, rstd):
    scaled = grad * gain
    mean = jnp.mean(scaled, axis=-1, keepdims=True)
    along = jnp.mean(scaled * normal, axis=-1, keepdims=True)
    return (scaled - mean - normal * along) * rstd


def gate(hidden):
    size = jnp.abs(hidden)
    bell = jnp.exp(hidden * hidden * -0.5)
    ratio = 1.0 / (1.0 + (0.3275911 * 0.7071067811865476) * size)
    series = 1.061405429 * ratio - 1.453152027
    series = series * ratio + 1.421413741
    series = series * ratio - 0.284496736
    series = series * ratio + 0.254829592
    tail = (0.5 * series) * ratio * bell
    phi = jnp.where(hidden > 0.0, 1.0 - tail, tail)
    return hidden * phi, phi + hidden * (bell * 0.3989422804014327)


def dyn(index, size):
    return pl.ds(pl.multiple_of(index * size, size), size)


def even_lanes(rows, width):
    return (lax.broadcasted_iota(jnp.int32, (rows, width), 1) // HEAD) % 2 == 0


def even_rows(rows, width):
    return (lax.broadcasted_iota(jnp.int32, (rows, width), 0) // HEAD) % 2 == 0


def split_columns(tile_t, out_ref, tile):
    chosen = even_rows(*tile_t.shape)
    blank = jnp.zeros_like(tile_t)
    out_ref[:, pl.ds(pl.multiple_of(tile * 2 * TILE, 2 * TILE), TILE)] = jnp.where(chosen, tile_t, blank)
    out_ref[:, pl.ds(pl.multiple_of(tile * 2 * TILE + TILE, TILE), TILE)] = jnp.where(
        chosen, blank, tile_t
    )


def split_rows(tile_n, out_ref, tile):
    chosen = even_lanes(*tile_n.shape)
    blank = jnp.zeros_like(tile_n)
    out_ref[pl.ds(pl.multiple_of(tile * 2 * TILE, 2 * TILE), TILE), :] = jnp.where(chosen, tile_n, blank)
    out_ref[pl.ds(pl.multiple_of(tile * 2 * TILE + TILE, TILE), TILE), :] = jnp.where(
        chosen, blank, tile_n
    )


def spread_segments(column_ref, wide_ref):
    total = column_ref.shape[0]
    step = min(total, 512)

    @pl.loop(0, total // step)
    def _(block):
        rows = dyn(block, step)
        wide_ref[rows, :] = jnp.broadcast_to(column_ref[rows, :], (step, TILE))


def key_rows(low, chunk, length, size):
    wanted = low * TILE + chunk * size
    start = pl.multiple_of(jnp.minimum(wanted, length - size), TILE)
    return pl.ds(start, size), start, wanted


def chunk_bias(query_row, key_wide_ref, tile, rows, start, wanted, offset, causal):
    size = rows.size
    key_position = start + lax.broadcasted_iota(jnp.int32, (size, TILE), 0)
    allowed = (key_wide_ref[rows, :] == query_row) & (key_position >= wanted)
    if causal:
        query_position = offset + tile * TILE + lax.broadcasted_iota(jnp.int32, (size, TILE), 1)
        allowed = allowed & (key_position <= query_position)
    return jnp.where(allowed, 0.0, MASKED)


def attend(
    tiles, ranges_ref, query_row_ref, key_wide_ref, offset, causal,
    query_cols, keys, values_t, attended_t, lse_ref, peak, total, sums, held, held_low,
):
    pairs = WIDE // PAIR

    @pl.loop(0, tiles)
    def _(tile):
        peak[...] = jnp.full(peak.shape, MASKED, F32)
        total[...] = jnp.zeros(total.shape, F32)
        sums[...] = jnp.zeros(sums.shape, F32)
        query_row = query_row_ref[:, dyn(tile, TILE)]

        low, high = ranges_ref[0, tile], ranges_ref[1, tile]

        size = held.shape[1]

        @pl.loop(0, lax.div((high - low) * TILE + size - 1, size))
        def _(chunk):
            rows, start, wanted = key_rows(low, chunk, keys.shape[0], size)
            bias = chunk_bias(query_row, key_wide_ref, tile, rows, start, wanted, offset, causal)
            bias = jnp.concatenate([bias, bias], axis=1)
            factors = []
            for pair in range(pairs):
                lanes = slice(pair * PAIR, (pair + 1) * PAIR)
                scores = nn(keys[rows, lanes], query_cols[lanes, dyn(tile, 2 * TILE)]) + bias
                held[pair] = scores
                before = peak[pair : pair + 1, :]
                after = jnp.maximum(before, jnp.max(scores, axis=0, keepdims=True))
                factors.append(jnp.exp(before - after))
                peak[pair : pair + 1, :] = after
            for pair in range(pairs):
                weights = jnp.exp(held[pair] - peak[pair : pair + 1, :])
                total[pair : pair + 1, :] = total[pair : pair + 1, :] * factors[pair] + col_sum(weights)
                held_low[pair] = weights.astype(BF16)
            for pair in range(pairs):
                factor = factors[pair]
                mixed = nn(values_t[pair * PAIR : (pair + 1) * PAIR, rows], held_low[pair])
                first = slice(pair * PAIR, pair * PAIR + HEAD)
                second = slice(pair * PAIR + HEAD, (pair + 1) * PAIR)
                sums[first, :] = sums[first, :] * factor[:, :TILE] + mixed[:HEAD, :TILE]
                sums[second, :] = sums[second, :] * factor[:, TILE:] + mixed[HEAD:, TILE:]

        for pair in range(pairs):
            amount = total[pair : pair + 1, :]
            lse_ref[pair : pair + 1, dyn(tile, 2 * TILE)] = peak[pair : pair + 1, :] + jnp.log(amount)
            share = 1.0 / amount
            first = slice(pair * PAIR, pair * PAIR + HEAD)
            second = slice(pair * PAIR + HEAD, (pair + 1) * PAIR)
            attended_t[first, dyn(tile, TILE)] = (sums[first, :] * share[:, :TILE]).astype(BF16)
            attended_t[second, dyn(tile, TILE)] = (sums[second, :] * share[:, TILE:]).astype(BF16)


def attend_back(
    tile, low, high, query_row_ref, first_query, key_wide_ref, offset, causal,
    query_cols, query_rows, grad_cols, grad_rows, keys, keys_t, values, lse_ref, delta_ref,
    query_grad_t, key_grad, value_grad, held, held_low, held_grad,
):
    pairs = WIDE // PAIR
    query_row = query_row_ref[:, pl.ds(pl.multiple_of(first_query + tile * TILE, TILE), TILE)]
    both = dyn(tile, 2 * TILE)

    size = held.shape[1]

    @pl.loop(0, lax.div((high - low) * TILE + size - 1, size))
    def _(chunk):
        rows, start, wanted = key_rows(low, chunk, keys.shape[0], size)
        bias = chunk_bias(query_row, key_wide_ref, tile, rows, start, wanted, offset, causal)
        bias = jnp.concatenate([bias, bias], axis=1)
        for pair in range(pairs):
            lanes = slice(pair * PAIR, (pair + 1) * PAIR)
            scores = nn(keys[rows, lanes], query_cols[lanes, both]) + bias
            probs = jnp.exp(scores - lse_ref[pair : pair + 1, both])
            held[pair] = probs
            held_low[pair] = probs.astype(BF16)
        for pair in range(pairs):
            lanes = slice(pair * PAIR, (pair + 1) * PAIR)
            prob_grad = nn(values[rows, lanes], grad_cols[lanes, both])
            held_grad[pair] = (held[pair] * (prob_grad - delta_ref[pair : pair + 1, both])).astype(BF16)
        for pair in range(pairs):
            lanes = slice(pair * PAIR, (pair + 1) * PAIR)
            value_grad[rows, lanes] += nn(held_low[pair], grad_rows[both, lanes])
            key_grad[rows, lanes] += nn(held_grad[pair], query_rows[both, lanes])
            mixed = nn(keys_t[lanes, rows], held_grad[pair])
            first = slice(pair * PAIR, pair * PAIR + HEAD)
            second = slice(pair * PAIR + HEAD, (pair + 1) * PAIR)
            query_grad_t[first, dyn(tile, TILE)] += mixed[:HEAD, :TILE]
            query_grad_t[second, dyn(tile, TILE)] += mixed[HEAD:, TILE:]


def clear(ref):
    rows = ref.shape[0]
    step = min(rows, 256)

    @pl.loop(0, rows // step)
    def _(block):
        ref[dyn(block, step), :] = jnp.zeros((step, ref.shape[1]), ref.dtype)


def transpose_rows(source, target):
    @pl.loop(0, source.shape[0] // TILE)
    def _(block):
        target[:, dyn(block, TILE)] = source[dyn(block, TILE), :].T


def out_like(shape, dtype):
    return jax.ShapeDtypeStruct(shape, dtype)


def run(body, ins, smem_count, outs, scratch, flops, bytes_accessed):
    vm = pl.BlockSpec(memory_space=pltpu.VMEM)
    sm = pl.BlockSpec(memory_space=pltpu.SMEM)
    return pl.pallas_call(
        body,
        in_specs=[sm] * smem_count + [vm] * (len(ins) - smem_count),
        out_specs=[vm] * len(outs),
        out_shape=outs,
        scratch_shapes=scratch,
        cost_estimate=pl.CostEstimate(
            flops=flops, bytes_accessed=bytes_accessed, transcendentals=0
        ),
        compiler_params=pltpu.CompilerParams(vmem_limit_bytes=VMEM_LIMIT),
    )(*ins)


def self_forward(n, rows_block, place_ref, ranges_ref, *refs):
    pieces, refs = refs[:n], refs[n:]
    (
        query_segment, key_segment, weight, bias, out_weight, out_bias, gain, shift,
        cross_weight, cross_bias,
        query_out, keys, values, attended_t, lse_ref, normal_out, rstd_out, first_low, cross_query,
        wide, values_t, query_cols, peak, total, sums, held, held_low,
    ) = refs
    count = pieces[0].shape[0]
    place = place_ref[0]
    spread_segments(key_segment, wide)

    for step in range(n):
        spot = lax.rem(place + n - step, n)

        @pl.when(spot <= place)
        def _():
            @pl.loop(0, count // rows_block)
            def _(block):
                source = pieces[step][dyn(block, rows_block), :]
                rows = dyn(spot * (count // rows_block) + block, rows_block)
                keys[rows, :] = nn(source, weight[:, WIDE : 2 * WIDE]).astype(BF16)
                values[rows, :] = (nn(source, weight[:, 2 * WIDE :]) + bias[1:2, :]).astype(BF16)
                if step == 0:
                    query = (nn(source, weight[:, :WIDE]) + bias[0:1, :]).astype(BF16)
                    query_out[dyn(block, rows_block), :] = (query.astype(F32) * SCALE).astype(BF16)

        @pl.when(spot > place)
        def _():
            @pl.loop(0, count // rows_block)
            def _(block):
                rows = dyn(spot * (count // rows_block) + block, rows_block)
                keys[rows, :] = jnp.zeros((rows_block, WIDE), BF16)
                values[rows, :] = jnp.zeros((rows_block, WIDE), BF16)

    transpose_rows(values, values_t)
    tiles = count // TILE

    @pl.loop(0, tiles)
    def _(tile):
        split_columns(query_out[dyn(tile, TILE), :].T, query_cols, tile)

    attend(
        tiles, ranges_ref, query_segment, wide, place * count, True,
        query_cols, keys, values_t, attended_t, lse_ref, peak, total, sums, held, held_low,
    )

    @pl.loop(0, count // rows_block)
    def _(block):
        rows = dyn(block, rows_block)
        attended = attended_t[:, rows].T
        field = pieces[0][rows, :].astype(F32) + nn(attended, out_weight[...]) + out_bias[...]
        normal, rstd = normalize(field)
        normal_out[rows, :] = normal
        rstd_out[rows, :] = rstd
        low = (normal * gain[...] + shift[...]).astype(BF16)
        first_low[rows, :] = low
        query = (nn(low, cross_weight[...]) + cross_bias[0:1, :]).astype(BF16)
        cross_query[rows, :] = (query.astype(F32) * SCALE).astype(BF16)


def cross_and_feed(n, rows_block, place_ref, ranges_ref, *refs):
    pieces, refs = refs[:n], refs[n:]
    (
        query_segment, key_segment, cotangent, cross_query, first_normal, first_gain, first_shift,
        pair_weight, cross_bias, out_weight, out_bias, gain, shift,
        in_weight, in_bias, down_weight, down_bias, last_gain, last_shift,
        layer_output, keys, values, lse_ref, delta_ref, out_grad, grad_out, g2_out,
        in_grad, down_grad, cross_out_grad, sums_out, in_bias_grad,
        wide, values_t, query_cols, peak, total, sums, held, held_low, attended_t, second_normal, second_rstd,
        second_low, second_low_t, active, slope, third, branch, branch_t,
    ) = refs
    count = pieces[0].shape[0]
    place = place_ref[0]
    spread_segments(key_segment, wide)
    blocks = count // rows_block

    for step in range(n):
        spot = lax.rem(place + n - step, n)

        @pl.loop(0, blocks)
        def _(block):
            source = pieces[step][dyn(block, rows_block), :]
            rows = dyn(spot * blocks + block, rows_block)
            keys[rows, :] = nn(source, pair_weight[:, :WIDE]).astype(BF16)
            values[rows, :] = (nn(source, pair_weight[:, WIDE:]) + cross_bias[1:2, :]).astype(BF16)

    transpose_rows(values, values_t)
    tiles = count // TILE

    @pl.loop(0, tiles)
    def _(tile):
        split_columns(cross_query[dyn(tile, TILE), :].T, query_cols, tile)

    attend(
        tiles, ranges_ref, query_segment, wide, 0, False,
        query_cols, keys, values_t, attended_t, lse_ref, peak, total, sums, held, held_low,
    )

    @pl.loop(0, blocks)
    def _(block):
        rows = dyn(block, rows_block)
        attended = attended_t[:, rows].T
        first = first_normal[rows, :] * first_gain[...] + first_shift[...]
        field = first + nn(attended, out_weight[...]) + out_bias[...]
        normal, rstd = normalize(field)
        second_normal[rows, :] = normal
        second_rstd[rows, :] = rstd
        second = normal * gain[...] + shift[...]
        third[rows, :] = second + down_bias[...]
        low = second.astype(BF16)
        second_low[rows, :] = low
        second_low_t[:, rows] = low.T

    hidden_size = in_weight.shape[1]
    chunk_size = min(WIDE, hidden_size // n)
    chunks = hidden_size // chunk_size

    @pl.loop(0, chunks)
    def _(chunk):
        lanes = dyn(chunk, chunk_size)

        @pl.loop(0, blocks)
        def _(block):
            rows = dyn(block, rows_block)
            hidden = nn(second_low[rows, :], in_weight[:, lanes]) + in_bias[:, lanes]
            value, derivative = gate(hidden)
            value = value.astype(BF16)
            active[rows, lanes] = value
            slope[rows, lanes] = derivative.astype(slope.dtype)
            third[rows, :] += nn(value, down_weight[dyn(chunk, chunk_size), :])

    sums_out[...] = jnp.zeros(sums_out.shape, F32)
    in_bias_grad[...] = jnp.zeros(in_bias_grad.shape, F32)

    @pl.loop(0, blocks)
    def _(block):
        rows = dyn(block, rows_block)
        normal, rstd = normalize(third[rows, :])
        layer_output[rows, :] = (normal * last_gain[...] + last_shift[...]).astype(BF16)
        outer = cotangent[rows, :].astype(F32)
        grad = normalize_back(outer, last_gain[...], normal, rstd)
        third[rows, :] = grad
        low = grad.astype(BF16)
        branch[rows, :] = low
        sums_out[0:1, :] += col_sum(outer * normal)
        sums_out[1:2, :] += col_sum(outer)
        sums_out[2:3, :] += col_sum(low.astype(F32))

    half = WIDE // n
    down_half = down_weight.shape[0] // n

    @pl.loop(0, chunks)
    def _(chunk):
        lanes = dyn(chunk, chunk_size)
        share = tn(active[:, lanes], branch[...]).astype(BF16)
        per_half = down_half // chunk_size
        down_grad[lax.div(chunk, per_half), dyn(lax.rem(chunk, per_half), chunk_size), :] = share

        @pl.loop(0, blocks)
        def _(block):
            rows = dyn(block, rows_block)
            inner = nt(branch[rows, :], down_weight[dyn(chunk, chunk_size), :])
            hidden_grad = (inner * slope[rows, lanes].astype(F32)).astype(BF16)
            active[rows, lanes] = hidden_grad
            in_bias_grad[:, lanes] += col_sum(hidden_grad.astype(F32))
            third[rows, :] += nt(hidden_grad, in_weight[:, lanes])

        share = nn(second_low_t[...], active[:, lanes]).astype(BF16)
        per_block = WIDE // chunk_size
        block_rows = dyn(lax.div(chunk, per_block), half)
        block_lanes = dyn(lax.rem(chunk, per_block), chunk_size)
        for part in range(n):
            in_grad[part, block_rows, block_lanes] = share[part * half : (part + 1) * half, :]

    @pl.loop(0, blocks)
    def _(block):
        rows = dyn(block, rows_block)
        outer = third[rows, :]
        normal = second_normal[rows, :]
        grad = normalize_back(outer, gain[...], normal, second_rstd[rows, :])
        g2_out[rows, :] = grad
        low = grad.astype(BF16)
        branch[rows, :] = low
        sums_out[3:4, :] += col_sum(outer * normal)
        sums_out[4:5, :] += col_sum(outer)
        sums_out[5:6, :] += col_sum(low.astype(F32))
        grad_out[rows, :] = nt(low, out_weight[...]).astype(BF16)

    share = nn(attended_t[...], branch[...]).astype(BF16)
    for part in range(n):
        cross_out_grad[part] = share[part * half : (part + 1) * half, :]

    write_delta(tiles, grad_out, attended_t, delta_ref)


def write_delta(tiles, grad, attended_t, delta_ref):
    @pl.loop(0, tiles)
    def _(tile):
        product = grad[dyn(tile, TILE), :].astype(F32).T * attended_t[:, dyn(tile, TILE)].astype(F32)
        for pair in range(WIDE // PAIR):
            start = pair * PAIR
            delta_ref[pair : pair + 1, pl.ds(pl.multiple_of(tile * 2 * TILE, 2 * TILE), TILE)] = col_sum(
                product[start : start + HEAD, :]
            )
            delta_ref[
                pair : pair + 1, pl.ds(pl.multiple_of(tile * 2 * TILE + TILE, TILE), TILE)
            ] = col_sum(product[start + HEAD : start + PAIR, :])


def prepare_back(tiles, query, grad, query_cols, query_rows, grad_cols, grad_rows):
    @pl.loop(0, tiles)
    def _(tile):
        here = query[dyn(tile, TILE), :]
        split_columns(here.T, query_cols, tile)
        split_rows(here, query_rows, tile)
        here = grad[dyn(tile, TILE), :]
        split_columns(here.T, grad_cols, tile)
        split_rows(here, grad_rows, tile)


def query_finish(tiles, query_grad_t, query_low, sums_out, index, rounded):
    @pl.loop(0, tiles)
    def _(tile):
        rows = dyn(tile, TILE)
        wide_grad = query_grad_t[:, rows].T * SCALE
        low = wide_grad.astype(BF16)
        query_low[rows, :] = low
        sums_out[index : index + 1, :] += col_sum(low.astype(F32) if rounded else wide_grad)


def spread_parts(n, share, target, start):
    half = WIDE // n
    for part in range(n):
        target[part, start : start + half, :] = share[part * half : (part + 1) * half, :].astype(BF16)


def row_product(n, place, pieces, source):
    count = pieces[0].shape[0]
    step_rows = min(count, 512)
    share = jnp.zeros((WIDE, WIDE), F32)
    for step in range(n):
        spot = lax.rem(place + n - step, n)
        for block in range(count // step_rows):
            rows = dyn(spot * (count // step_rows) + block, step_rows)
            share += tn(
                pieces[step][block * step_rows : (block + 1) * step_rows, :], source[rows, :].astype(BF16)
            )
    return share


def pair_back(n, place, rows_block, count, step, key_grad, value_grad, weight, first, sums_out, index, write):
    blocks = count // rows_block
    spot = lax.rem(place + n - step, n)

    @pl.loop(0, blocks)
    def _(block):
        rows = dyn(spot * blocks + block, rows_block)
        key_low = key_grad[rows, :].astype(BF16)
        value_part = value_grad[rows, :]
        sums_out[index : index + 1, :] += col_sum(value_part)
        value_low = value_part.astype(BF16)
        back = nt(key_low, weight[:, first : first + WIDE]) + nt(value_low, weight[:, first + WIDE : first + 2 * WIDE])
        write(dyn(block, rows_block), back)


def first_back(
    blocks, rows_block, g2, query_low, query_weight, first_normal, first_rstd, gain, self_out_weight,
    g1, branch, self_grad, sums_out, index,
):
    @pl.loop(0, blocks)
    def _(block):
        rows = dyn(block, rows_block)
        outer = g2[rows, :] + nt(query_low[rows, :], query_weight[...])
        normal = first_normal[rows, :]
        back = normalize_back(outer, gain[...], normal, first_rstd[rows, :])
        g1[rows, :] = back
        low = back.astype(BF16)
        branch[rows, :] = low
        sums_out[index : index + 1, :] += col_sum(outer * normal)
        sums_out[index + 1 : index + 2, :] += col_sum(outer)
        sums_out[index + 2 : index + 3, :] += col_sum(low.astype(F32))
        self_grad[rows, :] = nt(low, self_out_weight[...]).astype(BF16)


def cross_backward(n, rows_block, place_ref, ranges_ref, *refs):
    pieces, refs = refs[:n], refs[n:]
    (
        query_segment, key_segment, query, grad, keys, values, lse_ref, delta_ref, g2,
        first_normal, first_rstd, first_low, gain, query_weight, pair_weight, self_out_weight,
        self_attended_t,
        own_grad, sent_grad, query_grad_w, pair_grad_w, self_out_grad, self_grad, self_delta, g1_out, sums_out,
        wide, keys_t, query_cols, query_rows, grad_cols, grad_rows, query_grad_t, key_grad, value_grad,
        held, held_low, held_grad, query_low, branch,
    ) = refs
    count = pieces[0].shape[0]
    place = place_ref[0]
    tiles = count // TILE
    blocks = count // rows_block
    half = WIDE // n
    spread_segments(key_segment, wide)
    transpose_rows(keys, keys_t)
    prepare_back(tiles, query, grad, query_cols, query_rows, grad_cols, grad_rows)
    clear(query_grad_t)
    clear(key_grad)
    clear(value_grad)

    @pl.loop(0, tiles)
    def _(tile):
        attend_back(
            tile, ranges_ref[0, tile], ranges_ref[1, tile], query_segment, 0, wide, 0, False,
            query_cols, query_rows, grad_cols, grad_rows, keys, keys_t, values, lse_ref, delta_ref,
            query_grad_t, key_grad, value_grad, held, held_low, held_grad,
        )

    sums_out[...] = jnp.zeros(sums_out.shape, F32)
    query_finish(tiles, query_grad_t, query_low, sums_out, 0, True)
    spread_parts(n, tn(first_low[...], query_low[...]), query_grad_w, 0)
    for step in range(n):

        def write(here, back):
            if step == 0:
                own_grad[here, :] = back
            else:
                sent_grad[step - 1, here, :] = back.astype(BF16)

        pair_back(n, place, rows_block, count, step, key_grad, value_grad, pair_weight, 0, sums_out, 1, write)
    spread_parts(n, row_product(n, place, pieces, key_grad), pair_grad_w, 0)
    spread_parts(n, row_product(n, place, pieces, value_grad), pair_grad_w, half)
    first_back(
        blocks, rows_block, g2, query_low, query_weight, first_normal, first_rstd, gain, self_out_weight,
        g1_out, branch, self_grad, sums_out, 2,
    )
    spread_parts(n, nn(self_attended_t[...], branch[...]), self_out_grad, 0)
    write_delta(tiles, self_grad, self_attended_t, self_delta)


def self_backward(n, rows_block, place_ref, ranges_ref, *refs):
    pieces, refs = refs[:n], refs[n:]
    (
        query_segment, key_segment, query, grad, keys, values, lse_ref, delta_ref, g1, weight,
        own_grad, sent_grad, grad_w, sums_out,
        wide, keys_t, query_cols, query_rows, grad_cols, grad_rows, query_grad_t, key_grad, value_grad,
        held, held_low, held_grad, query_low,
    ) = refs
    count = pieces[0].shape[0]
    place = place_ref[0]
    tiles = count // TILE
    half = WIDE // n
    spread_segments(key_segment, wide)
    transpose_rows(keys, keys_t)
    prepare_back(tiles, query, grad, query_cols, query_rows, grad_cols, grad_rows)
    clear(query_grad_t)
    clear(key_grad)
    clear(value_grad)

    @pl.loop(0, tiles)
    def _(tile):
        attend_back(
            tile, ranges_ref[0, tile], ranges_ref[1, tile], query_segment, 0, wide, place * count, True,
            query_cols, query_rows, grad_cols, grad_rows, keys, keys_t, values, lse_ref, delta_ref,
            query_grad_t, key_grad, value_grad, held, held_low, held_grad,
        )

    sums_out[...] = jnp.zeros(sums_out.shape, F32)
    query_finish(tiles, query_grad_t, query_low, sums_out, 0, False)
    for step in range(n):

        def write(here, back):
            if step == 0:
                own_grad[here, :] = back + g1[here, :] + nt(query_low[here, :], weight[:, :WIDE])
            else:
                sent_grad[step - 1, here, :] = back.astype(BF16)

        pair_back(n, place, rows_block, count, step, key_grad, value_grad, weight, WIDE, sums_out, 1, write)
    spread_parts(n, tn(pieces[0][...], query_low[...]), grad_w, 0)
    spread_parts(n, row_product(n, place, pieces, key_grad), grad_w, half)
    spread_parts(n, row_product(n, place, pieces, value_grad), grad_w, 2 * half)


CORE_RATE = 0.0018
LINK_RATE = 0.0225
LATENCY = {"core": 1.1, "x": 2.4, "y": 2.4, "z": 3.0}
MARGIN = 1.0


def plan_steps(n, chunks, extras, segments):
    free = {"core": 0.0, "x": 0.0, "y": 0.0, "z": 0.0}
    now = 0.0
    pending = []
    plan = []
    crossed = set()

    def send(link, rows, rate=LINK_RATE):
        free[link] = max(free[link], now) + rows * rate
        return free[link] + LATENCY[link]

    def execute(kind, index, step):
        nonlocal now
        now += 0.15
        if kind == "chunk":
            unused, rows, y_first, unused = chunks[index]
            if step == 0:
                ready = send("core", n * rows // 2, CORE_RATE)
            elif step in (1, 2) and (step == 1) == y_first:
                ready = send("y", (n if y_first else 1) * rows // 4)
            elif step in (1, 2):
                crossed.add(index)
                ready = send("x", (n - 1) * rows // (4 if y_first else 2))
            elif step in (3, 4):
                ready = send("z", rows // 4)
            elif step == 5:
                ready = send("y", rows // 4)
            elif step == 6:
                ready = send("core", rows // 2, CORE_RATE)
            else:
                return
        elif kind == "extra":
            if step == 2:
                return
            rows = extras[index][0]
            ready = send("core", rows, CORE_RATE) if step == 0 else send("x", rows // 2)
        else:
            if step == 4:
                return
            ready = now + (1.5, 3.2, 3.2, 4.0)[step]
        pending.append((ready, len(pending), kind, index, step + 1))

    for number in range(len(segments) + 1):
        order = []
        last = number == len(segments)
        if not last:
            now += segments[number]
            released = [("chunk", i) for i, chunk in enumerate(chunks) if chunk[3] == number]
            released += [("extra", i) for i, extra in enumerate(extras) if extra[1] == number]
            if number == max(len(segments) - 2, 0):
                released.append(("small", 0))
            for kind, index in released:
                execute(kind, index, 0)
                order.append((kind, index, 0))
        while pending:
            pending.sort()
            first = 0
            if len(crossed) < len(chunks):
                while first < len(pending) and pending[first][2:] == ("extra", pending[first][3], 1):
                    first += 1
            if first == len(pending) or (not last and pending[first][0] + MARGIN > now):
                break
            ready, unused, kind, index, step = pending.pop(first)
            now = max(now, ready)
            execute(kind, index, step)
            order.append((kind, index, step))
        plan.append(order)
    return plan, now


class Reducer:
    def __init__(self, n, groups, chunks, field, total, total_out, small, small_out, buffers):
        (
            self.from_core, self.from_blk, self.from_y, self.from_z,
            self.small_core, self.small_blk, self.small_y, self.small_z,
            self.sends, self.receives, self.small_sends, self.small_receives, self.stores,
        ) = buffers
        self.n, self.chunks, self.field, self.total, self.total_out = n, chunks, field, total, total_out
        self.small, self.small_out = small, small_out
        self.depth = depth = groups // 4
        self.group = group = lax.axis_index("dp")
        self.part = part = lax.axis_index("blk")
        self.core = lax.rem(group, 2)
        self.side = lax.rem(lax.div(group, 2), 2)
        self.level = lax.div(group, 4)
        self.core_peer = (group + 1 - 2 * self.core, part)
        self.side_peer = (group + 2 - 4 * self.side, part)
        self.blk_peers = [(group, lax.rem(part + step, n)) for step in range(1, n)]
        self.z_peers = [(lax.rem(group + 4 * step, groups), part) for step in range(1, depth)]
        self.per_chunk = 4 + (n - 1) + 2 * (depth - 1)

    def enter(self, far_peer=None, has_far=None):
        peers = [self.core_peer, self.side_peer] + self.blk_peers + self.z_peers
        barrier = pltpu.get_barrier_semaphore()
        for peer in peers:
            pl.semaphore_signal(barrier, inc=1, device_id=peer, device_id_type=pl.DeviceIdType.MESH)
        if far_peer is not None:

            @pl.when(has_far)
            def _():
                pl.semaphore_signal(barrier, inc=1, device_id=far_peer, device_id_type=pl.DeviceIdType.MESH)

            pl.semaphore_wait(barrier, jnp.where(has_far, len(peers) + 1, len(peers)))
        else:
            pl.semaphore_wait(barrier, len(peers))

    def copy(self, source, target, sem, peer):
        return pltpu.make_async_remote_copy(
            src_ref=source, dst_ref=target, send_sem=self.sends.at[sem], recv_sem=self.receives.at[sem],
            device_id=peer, device_id_type=pl.DeviceIdType.MESH,
        )

    def small_copy(self, source, target, sem, peer):
        return pltpu.make_async_remote_copy(
            src_ref=source, dst_ref=target, send_sem=self.small_sends.at[sem],
            recv_sem=self.small_receives.at[sem], device_id=peer, device_id_type=pl.DeviceIdType.MESH,
        )

    def span(self, start, size):
        return pl.ds(pl.multiple_of(start, 16), size)

    def copies(self, index, step):
        start, rows, y_first, unused = self.chunks[index]
        n, depth, part = self.n, self.depth, self.part
        half, quarter = rows // 2, rows // 4
        piece = quarter // depth
        own_half = start + self.core * half
        own_quarter = own_half + self.side * quarter
        sem = index * self.per_chunk
        if step == 0:
            theirs = self.span(start + (1 - self.core) * half, half)
            return [
                self.copy(
                    self.field.at[:, theirs], self.from_core.at[:, pl.ds(start // 2, half)], sem, self.core_peer
                )
            ]
        if step in (1, 2) and (step == 1) == y_first:
            theirs = self.span(own_half + (1 - self.side) * quarter, quarter)
            into = pl.ds(start // 4, quarter)
            if y_first:
                return [self.copy(self.field.at[:, theirs], self.from_y.at[:, into], sem + 1, self.side_peer)]
            return [self.copy(self.field.at[part, theirs], self.from_y.at[0, into], sem + 1, self.side_peer)]
        if step in (1, 2):
            if y_first:
                mine, into = self.span(own_quarter, quarter), pl.ds(start // 2, quarter)
            else:
                mine, into = self.span(own_half, half), pl.ds(start // 2, half)
            return [
                self.copy(
                    self.field.at[lax.rem(part + hop, n), mine], self.from_blk.at[hop - 1, into],
                    sem + 3 + hop, self.blk_peers[hop - 1],
                )
                for hop in range(1, n)
            ]
        if step == 3:
            copies = []
            for hop in range(1, depth):
                theirs = self.span(own_quarter + lax.rem(self.level + hop, depth) * piece, piece)
                copies.append(
                    self.copy(
                        self.field.at[part, theirs], self.from_z.at[hop - 1, pl.ds(start // 4 // depth, piece)],
                        sem + 2 + n + hop, self.z_peers[hop - 1],
                    )
                )
            return copies
        if step == 4:
            mine = self.span(own_quarter + self.level * piece, piece)
            return [
                self.copy(
                    self.total.at[mine], self.total.at[mine], sem + 1 + n + depth + hop, self.z_peers[hop - 1]
                )
                for hop in range(1, depth)
            ]
        if step == 5:
            mine = self.span(own_quarter, quarter)
            return [self.copy(self.total.at[mine], self.total.at[mine], sem + 2, self.side_peer)]
        mine = self.span(own_half, half)
        return [self.copy(self.total.at[mine], self.total.at[mine], sem + 3, self.core_peer)]

    def add(self, part, start, size, terms, result=None):
        step = min(size, 64)

        @pl.loop(0, size // step)
        def _(block):
            here = self.span(start + block * step, step)
            value = self.field[part, here, :].astype(F32)
            for ref, index, begin in terms:
                value = value + ref[index, self.span(begin + block * step, step), :].astype(F32)
            if result is None:
                self.field[part, here, :] = value.astype(BF16)
            else:
                result[here, :] = value.astype(BF16)

    def store(self, index):
        rows = pl.ds(self.chunks[index][0], self.chunks[index][1])
        return pltpu.make_async_copy(self.total.at[rows], self.total_out.at[rows], self.stores.at[index])

    def chunk_step(self, index, step):
        start, rows, y_first, unused = self.chunks[index]
        n, depth, part = self.n, self.depth, self.part
        half, quarter = rows // 2, rows // 4
        piece = quarter // depth
        own_half = start + self.core * half
        own_quarter = own_half + self.side * quarter
        if step > 0:
            for copy in self.copies(index, step - 1):
                copy.wait()
        if step == 1:
            for b in range(n):
                self.add(b, own_half, half, [(self.from_core, b, start // 2)])
        elif step in (2, 3) and (step == 2) == y_first:
            for b in range(n) if y_first else [part]:
                self.add(b, own_quarter, quarter, [(self.from_y, b if y_first else 0, start // 4)])
        elif step in (2, 3):
            begin, size = (own_quarter, quarter) if y_first else (own_half, half)
            self.add(part, begin, size, [(self.from_blk, hop, start // 2) for hop in range(n - 1)])
        elif step == 4:
            self.add(
                part, own_quarter + self.level * piece, piece,
                [(self.from_z, hop, start // 4 // depth) for hop in range(depth - 1)], self.total,
            )
        if step < 7:
            for copy in self.copies(index, step):
                copy.start()
        else:
            self.store(index).start()

    def small_copies(self, step):
        part, n = self.part, self.n
        if step == 0:
            return [self.small_copy(self.small.at[0], self.small_core, 0, self.core_peer)]
        if step == 1:
            return [
                self.small_copy(
                    self.small.at[1, lax.rem(part + hop, n)], self.small_blk.at[hop - 1], hop,
                    self.blk_peers[hop - 1],
                )
                for hop in range(1, n)
            ]
        if step == 2:
            return [self.small_copy(self.small.at[1, part], self.small_y, n, self.side_peer)]
        return [
            self.small_copy(self.small_y, self.small_z.at[hop - 1], n + hop, self.z_peers[hop - 1])
            for hop in range(1, self.depth)
        ]

    def small_step(self, step):
        part = self.part
        if step > 0:
            for copy in self.small_copies(step - 1):
                copy.wait()
        if step == 1:
            self.small[1] = self.small[0] + self.small_core[...]
        elif step == 2:
            held = self.small[1, part]
            for hop in range(self.n - 1):
                held = held + self.small_blk[hop]
            self.small[1, part] = held
        elif step == 3:
            self.small_y[...] = self.small_y[...] + self.small[1, part]
        elif step == 4:
            held = self.small_y[...]
            for hop in range(self.depth - 1):
                held = held + self.small_z[hop]
            self.small_out[...] = held
        if step < 4:
            for copy in self.small_copies(step):
                copy.start()

    def finish(self):
        for index in range(len(self.chunks)):
            self.store(index).wait()


def reducer_scratch(n, groups, chunks, rows, small_shape):
    depth = groups // 4
    per_chunk = 4 + (n - 1) + 2 * (depth - 1)
    return [
        pltpu.VMEM((n, rows // 2, WIDE), BF16),
        pltpu.VMEM((n - 1, rows // 2, WIDE), BF16),
        pltpu.VMEM((n, rows // 4, WIDE), BF16),
        pltpu.VMEM((depth - 1, rows // 4 // depth, WIDE), BF16),
        pltpu.VMEM((n, *small_shape), F32),
        pltpu.VMEM((n - 1, *small_shape), F32),
        pltpu.VMEM(small_shape, F32),
        pltpu.VMEM((depth - 1, *small_shape), F32),
        pltpu.SemaphoreType.DMA((len(chunks) * per_chunk,)),
        pltpu.SemaphoreType.DMA((len(chunks) * per_chunk,)),
        pltpu.SemaphoreType.DMA((n + depth,)),
        pltpu.SemaphoreType.DMA((n + depth,)),
        pltpu.SemaphoreType.DMA((len(chunks),)),
    ]


def reduce_kernel(n, groups, chunks, plan, part_rows, *refs):
    sources, refs = refs[: len(part_rows)], refs[len(part_rows) :]
    small_in, total_out, small_out, field, total, small, load_sem = refs[:7]
    loads = []
    start = 0
    for index, source in enumerate(sources):
        loads.append(
            pltpu.make_async_copy(source, field.at[:, pl.ds(start, part_rows[index])], load_sem.at[index])
        )
        loads[-1].start()
        start += part_rows[index]
    reducer = Reducer(n, groups, chunks, field, total, total_out, small, small_out, refs[7:])
    small[0] = small_in[...]
    reducer.enter()
    for load in loads:
        load.wait()
    for order in plan:
        for kind, index, step in order:
            if kind == "chunk":
                reducer.chunk_step(index, step)
            else:
                reducer.small_step(step)
    reducer.finish()


def reduce_all(n, groups, parts, small):
    part_rows = [part.shape[1] for part in parts]
    rows = sum(part_rows)
    chunk_rows = max(16 * groups, rows // 8)
    chunks = [(start, chunk_rows, False, 0) for start in range(0, rows, chunk_rows)]
    plan, unused = plan_steps(n, chunks, [], [0.0])
    small_shape = small.shape[1:]
    vm = pl.BlockSpec(memory_space=pltpu.VMEM)
    hbm = pl.BlockSpec(memory_space=pl.ANY)
    return pl.pallas_call(
        functools.partial(reduce_kernel, n, groups, chunks, plan, part_rows),
        in_specs=[hbm] * len(parts) + [vm],
        out_specs=[hbm, vm],
        out_shape=[out_like((rows, WIDE), BF16), out_like(small_shape, F32)],
        scratch_shapes=[
            pltpu.VMEM((n, rows, WIDE), BF16),
            pltpu.VMEM((rows, WIDE), BF16),
            pltpu.VMEM((2, n, *small_shape), F32),
            pltpu.SemaphoreType.DMA((len(parts),)),
            *reducer_scratch(n, groups, chunks, rows, small_shape),
        ],
        compiler_params=pltpu.CompilerParams(
            vmem_limit_bytes=VMEM_LIMIT, collective_id=0, has_side_effects=True
        ),
    )(*parts, small)


Y_FIRST = [letter == "y" for letter in "yyxyxyxyxxyy"]
BACK_SEGMENTS = [
    3.5, 3.2, 3.2, 3.2, 3.2, 1.5, 3.0, 3.5,
    2.5, 2.6, 2.6, 3.2, 3.2, 1.5, 1.2, 1.2, 2.4, 2.2,
]


def back_chunks(half, hidden_rows):
    released = [(2 * half, 0)] * (hidden_rows // half) + [(half, 0)]
    released += [(half, segment) for segment in (5, 6, 6, 7, 13, 14, 15)]
    chunks = []
    start = 0
    for index, (rows, segment) in enumerate(released):
        chunks.append((start, rows, Y_FIRST[index % len(Y_FIRST)], segment))
        start += rows
    return chunks


def back_kernel(n, groups, rows_block, chunks, plan, load_plan, *refs):
    feed_refs, refs = refs[:3], refs[3:]
    streamed, refs = refs[: len(load_plan)], refs[len(load_plan) :]
    (
        target_row, memory_row, cross_query, cross_grad, cross_keys, cross_values,
        cross_lse, cross_delta, feed_sums, in_bias_grad, gain, first_rstd, self_lse,
        total_out, small_out, memory_grad, input_grad,
        field, total, small, sums, memory_sent, memory_got, input_sent, input_got, pair_low,
        wide, keys_t, query_cols, query_rows, grad_cols, grad_rows, query_grad_t, key_grad, value_grad,
        held, held_low, held_grad, query_low, branch, self_grad, self_delta, g1,
        feed_sem, load_sem, extra_send, extra_recv,
    ) = refs[:47]
    refs = refs[47:]
    held_loads, buffers = refs[: len(load_plan)], refs[len(load_plan) :]
    count = cross_query.shape[0]
    length = cross_keys.shape[0]
    tiles = count // TILE
    blocks = count // rows_block
    half = WIDE // n
    group, part = lax.axis_index("dp"), lax.axis_index("blk")
    place = lax.rem(group, 2)
    away = place != part
    owner = (group - place + part, place)

    feed_loads = []
    start = 0
    for index, source in enumerate(feed_refs):
        rows = source.shape[1]
        feed_loads.append(
            pltpu.make_async_copy(source, field.at[:, pl.ds(start, rows)], feed_sem.at[index])
        )
        feed_loads[-1].start()
        start += rows
    loads = [
        pltpu.make_async_copy(source, target, load_sem.at[index])
        for index, (source, target) in enumerate(zip(streamed, held_loads))
    ]
    for load in loads:
        load.start()
    memory_pieces = [held_loads[0].at[step] for step in range(n)]
    held_loads = held_loads[1:]
    (
        pair_weight, first_low, query_weight, g2, first_normal, self_out_weight, self_attended_t,
        self_keys, self_values, self_query,
    ) = held_loads[:10]
    input_pieces = [held_loads[10].at[step] for step in range(n)]
    self_in_weight = held_loads[11]

    reducer = Reducer(n, groups, chunks, field, total, total_out, small, small_out, buffers)
    reducer.enter(owner, away)

    extras = ((memory_sent, memory_got, memory_grad), (input_sent, input_got, input_grad))

    def extra_copy(index, hop):
        sent, got, unused = extras[index]
        return pltpu.make_async_remote_copy(
            src_ref=sent.at[hop], dst_ref=got.at[hop],
            send_sem=extra_send.at[2 * index + hop], recv_sem=extra_recv.at[2 * index + hop],
            device_id=reducer.core_peer if hop == 0 else owner, device_id_type=pl.DeviceIdType.MESH,
        )

    def extra_step(index, step):
        sent, got, result = extras[index]
        if step == 0:
            extra_copy(index, 0).start()
        elif step == 1:
            extra_copy(index, 0).wait()

            @pl.loop(0, blocks)
            def _(block):
                rows = dyn(block, rows_block)
                value = result[rows, :] + got[0, rows, :].astype(F32)
                result[rows, :] = value
                sent[1, rows, :] = value.astype(BF16)

            @pl.when(away)
            def _():
                extra_copy(index, 1).start()
        else:

            @pl.when(away)
            def _():
                extra_copy(index, 1).wait()

                @pl.loop(0, blocks)
                def _(block):
                    rows = dyn(block, rows_block)
                    result[rows, :] = got[1, rows, :].astype(F32)

    def run_steps(number):
        for kind, index, step in plan[number]:
            if kind == "chunk":
                reducer.chunk_step(index, step)
            elif kind == "small":
                reducer.small_step(step)
            else:
                extra_step(index, step)

    def wait_loads(first, last):
        for load in loads[first:last]:
            load.wait()

    spread_row(memory_row, wide)
    transpose_rows(cross_keys, keys_t)
    prepare_back(tiles, cross_query, cross_grad, query_cols, query_rows, grad_cols, grad_rows)
    clear(query_grad_t)
    clear(key_grad)
    clear(value_grad)
    sums[...] = jnp.zeros(sums.shape, F32)
    for load in feed_loads:
        load.wait()
    run_steps(0)
    for tile in range(tiles):
        attend_back(
            tile, 0, length // TILE, target_row, place * count, wide, place * count, False,
            query_cols, query_rows, grad_cols, grad_rows, cross_keys, keys_t, cross_values,
            cross_lse, cross_delta, query_grad_t, key_grad, value_grad, held, held_low, held_grad,
        )
        run_steps(1 + tile)
    base = 2 * in_bias_grad.shape[1] // n + half
    wait_loads(0, 8)
    query_finish(tiles, query_grad_t, query_low, sums, 2, True)
    spread_parts(n, tn(first_low[...], query_low[...]), field, base)
    run_steps(5)
    for side, source in ((0, key_grad), (1, value_grad)):

        @pl.loop(0, length // rows_block)
        def _(block):
            rows = dyn(block, rows_block)
            value = source[rows, :]
            pair_low[side, rows, :] = value.astype(BF16)
            if side == 1:
                sums[3:4, :] += col_sum(value)

        spread_parts(
            n, row_product(n, place, memory_pieces, pair_low.at[side]), field, base + half + side * half
        )
    run_steps(6)
    first_back(
        blocks, rows_block, g2, query_low, query_weight, first_normal, first_rstd, gain, self_out_weight,
        g1, branch, self_grad, sums, 4,
    )
    spread_parts(n, nn(self_attended_t[...], branch[...]), field, base + 3 * half)
    write_delta(tiles, self_grad, self_attended_t, self_delta)
    run_steps(7)

    wait_loads(8, len(loads))
    spread_row(target_row, wide)
    transpose_rows(self_keys, keys_t)
    prepare_back(tiles, self_query, self_grad, query_cols, query_rows, grad_cols, grad_rows)
    clear(query_grad_t)
    clear(key_grad)
    clear(value_grad)
    run_steps(8)
    for tile in range(tiles):
        attend_back(
            tile, 0, place * tiles + tile + 1, target_row, place * count, wide, place * count, True,
            query_cols, query_rows, grad_cols, grad_rows, self_keys, keys_t, self_values,
            self_lse, self_delta, query_grad_t, key_grad, value_grad, held, held_low, held_grad,
        )
        run_steps(9 + tile)
    query_finish(tiles, query_grad_t, query_low, sums, 0, False)
    spread_parts(n, tn(input_pieces[0][...], query_low[...]), field, base + 4 * half)
    run_steps(13)
    spread_parts(n, row_product(n, place, input_pieces, key_grad), field, base + 5 * half)
    run_steps(14)
    spread_parts(n, row_product(n, place, input_pieces, value_grad), field, base + 6 * half)
    run_steps(15)
    for step in range(n):

        def write(here, back):
            if step == 0:
                input_grad[here, :] = back + g1[here, :] + nt(query_low[here, :], self_in_weight[:, :WIDE])
            else:
                input_sent[0, here, :] = back.astype(BF16)

        pair_back(n, place, rows_block, count, step, key_grad, value_grad, self_in_weight, WIDE, sums, 1, write)
    small[...] = jnp.zeros(small.shape, F32)
    for part in range(n):
        here = slice(part * half, (part + 1) * half)
        small[0, part, 0:7, :] = sums[0:7, here]
        small[0, part, 7:13, :] = feed_sums[0:6, here]
        wide_half = in_bias_grad.shape[1] // n
        for row in range(wide_half // half):
            begin = part * wide_half + row * half
            small[0, part, 13 + row : 14 + row, :] = in_bias_grad[:, begin : begin + half]
    run_steps(16)
    for step in range(n):
        spot = lax.rem(place + n - step, n)

        @pl.loop(0, blocks)
        def _(block):
            rows, here = dyn(spot * blocks + block, rows_block), dyn(block, rows_block)
            back = nt(pair_low[0, rows, :], pair_weight[:, :WIDE]) + nt(pair_low[1, rows, :], pair_weight[:, WIDE:])
            if step == 0:
                memory_grad[here, :] = back
            else:
                memory_sent[0, here, :] = back.astype(BF16)

    run_steps(17)
    run_steps(18)
    reducer.finish()


def back_and_reduce(n, groups, rows_block, feed_grads, streamed, resident):
    count, features = resident[2].shape
    length = n * count
    hidden_rows = feed_grads[0].shape[1]
    half = features // n
    rows = sum(part.shape[1] for part in feed_grads) + 7 * half
    chunks = back_chunks(half, hidden_rows)
    extras = [(count, 17), (count, 16)]
    plan, unused = plan_steps(n, chunks, extras, BACK_SEGMENTS)
    small_shape = (-(-(13 + hidden_rows // half * half * n // features) // 8) * 8 + 8, half)
    vm = pl.BlockSpec(memory_space=pltpu.VMEM)
    hbm = pl.BlockSpec(memory_space=pl.ANY)
    low_rows = pltpu.VMEM((count, features), BF16)
    wide_rows = pltpu.VMEM((count, features), F32)
    columns = pltpu.VMEM((features, 2 * count), BF16)
    doubled = pltpu.VMEM((2 * count, features), BF16)
    all_wide = pltpu.VMEM((length, features), F32)
    sent = pltpu.VMEM((2, count, features), BF16)
    held = (features // PAIR, BACK_KEYS, 2 * TILE)
    return pl.pallas_call(
        functools.partial(back_kernel, n, groups, rows_block, chunks, plan, [part.shape for part in streamed]),
        in_specs=[hbm] * (len(feed_grads) + len(streamed)) + [vm] * len(resident),
        out_specs=[hbm, vm, vm, vm],
        out_shape=[
            out_like((rows, WIDE), BF16), out_like(small_shape, F32),
            out_like((count, features), F32), out_like((count, features), F32),
        ],
        scratch_shapes=[
            pltpu.VMEM((n, rows, WIDE), BF16), pltpu.VMEM((rows, WIDE), BF16),
            pltpu.VMEM((2, n, *small_shape), F32), pltpu.VMEM((8, features), F32),
            sent, sent, sent, sent, pltpu.VMEM((2, length, features), BF16),
            pltpu.VMEM((length, TILE), jnp.int32), pltpu.VMEM((features, length), BF16),
            columns, doubled, columns, doubled,
            pltpu.VMEM((features, count), F32), all_wide, all_wide,
            pltpu.VMEM(held, F32), pltpu.VMEM(held, BF16), pltpu.VMEM(held, BF16),
            low_rows, low_rows, low_rows, pltpu.VMEM((features // PAIR, 2 * count), F32), wide_rows,
            pltpu.SemaphoreType.DMA((len(feed_grads),)), pltpu.SemaphoreType.DMA((len(streamed),)),
            pltpu.SemaphoreType.DMA((4,)), pltpu.SemaphoreType.DMA((4,)),
            *[pltpu.VMEM(part.shape, part.dtype) for part in streamed],
            *reducer_scratch(n, groups, chunks, rows, small_shape),
        ],
        compiler_params=pltpu.CompilerParams(
            vmem_limit_bytes=VMEM_LIMIT, collective_id=0, has_side_effects=True
        ),
    )(*feed_grads, *streamed, *resident)


def spread_row(row_ref, wide_ref):
    @pl.loop(0, row_ref.shape[1] // TILE)
    def _(block):
        wide_ref[dyn(block, TILE), :] = jnp.broadcast_to(row_ref[:, dyn(block, TILE)], (TILE, TILE)).T


def attend_whole(
    tiles, query_row_ref, first_query, key_wide_ref, causal, query_cols, keys, values_t, attended_t, lse_ref,
    held, held_low,
):
    pairs = WIDE // PAIR
    length = keys.shape[0]

    @pl.loop(0, tiles)
    def _(tile):
        begin = pl.multiple_of(first_query + tile * TILE, TILE)
        allowed = key_wide_ref[...] == query_row_ref[:, pl.ds(begin, TILE)]
        if causal:
            key_position = lax.broadcasted_iota(jnp.int32, (length, TILE), 0)
            query_position = begin + lax.broadcasted_iota(jnp.int32, (length, TILE), 1)
            allowed = allowed & (key_position <= query_position)
        bias = jnp.where(allowed, 0.0, MASKED)
        bias = jnp.concatenate([bias, bias], axis=1)
        both = dyn(tile, 2 * TILE)
        peaks, shares = [], []
        for pair in range(pairs):
            lanes = slice(pair * PAIR, (pair + 1) * PAIR)
            scores = nn(keys[:, lanes], query_cols[lanes, both]) + bias
            held[pair] = scores
            peaks.append(jnp.max(scores, axis=0, keepdims=True))
        for pair in range(pairs):
            weights = jnp.exp(held[pair] - peaks[pair])
            total = col_sum(weights)
            held_low[pair] = weights.astype(BF16)
            lse_ref[pair : pair + 1, both] = peaks[pair] + jnp.log(total)
            shares.append(1.0 / total)
        for pair in range(pairs):
            share = shares[pair]
            mixed = nn(values_t[pair * PAIR : (pair + 1) * PAIR, :], held_low[pair])
            first = slice(pair * PAIR, pair * PAIR + HEAD)
            second = slice(pair * PAIR + HEAD, (pair + 1) * PAIR)
            attended_t[first, dyn(tile, TILE)] = (mixed[:HEAD, :TILE] * share[:, :TILE]).astype(BF16)
            attended_t[second, dyn(tile, TILE)] = (mixed[HEAD:, TILE:] * share[:, TILE:]).astype(BF16)


FORWARD_LOADS = 7
FORWARD_STORES = 16


def forward_kernel(n, groups, rows_block, *refs):
    (
        inputs, memory, cotangent, *weights_in
    ) = refs[: 3 + FORWARD_LOADS]
    refs = refs[3 + FORWARD_LOADS :]
    (
        target_here, memory_here, in_bias, self_out_bias, first_gain, first_shift, cross_bias, cross_out_bias,
        second_gain, second_shift, feed_bias, down_bias, last_gain, last_shift,
    ) = refs[:14]
    refs = refs[14:]
    stores_out, refs = refs[:FORWARD_STORES], refs[FORWARD_STORES:]
    (
        layer_output, lse_one, lse_two, delta_ref, first_rstd, sums_out, in_bias_grad, target_row, memory_row,
    ) = refs[:9]
    refs = refs[9:]
    held_weights, refs = refs[:FORWARD_LOADS], refs[FORWARD_LOADS:]
    held_stores, refs = refs[:FORWARD_STORES], refs[FORWARD_STORES:]
    (
        self_in_weight, self_out_weight, cross_weight, pair_weight, cross_out_weight, in_weight, down_weight
    ) = held_weights
    (
        input_pieces, memory_pieces, query_low, keys, values, attended_one, first_normal, first_low, cross_query,
        cross_keys, cross_values, grad_out, g2_out, in_grad, down_grad, cross_out_grad,
    ) = held_stores
    (
        cot, output_low, output_got, target_there, memory_there, wide, values_t, query_cols, held, held_low,
        attended_two, second_normal, second_rstd, second_low, second_low_t, active, slope, third, branch,
        load_sem, store_sem, own_sem, far_send, far_recv, core_send, core_recv,
    ) = refs
    count = inputs.shape[0]
    tiles = count // TILE
    blocks = count // rows_block
    half = WIDE // n
    group, part = lax.axis_index("dp"), lax.axis_index("blk")
    place = lax.rem(group, 2)
    away = place != part
    owner = (group - place + part, place)
    core_peer = (group + 1 - 2 * place, part)
    mesh_type = pl.DeviceIdType.MESH

    loads = [
        pltpu.make_async_copy(source, target, load_sem.at[index])
        for index, (source, target) in enumerate(zip(weights_in, held_weights))
    ]
    for load in loads:
        load.start()
    barrier = pltpu.get_barrier_semaphore()
    pl.semaphore_signal(barrier, inc=1, device_id=core_peer, device_id_type=mesh_type)

    @pl.when(away)
    def _():
        pl.semaphore_signal(barrier, inc=1, device_id=owner, device_id_type=mesh_type)

    pl.semaphore_wait(barrier, jnp.where(away, 2, 1))

    pieces_of = (count // 2, count // 2)
    arrivals = []
    for index, (source, target) in enumerate(((inputs, input_pieces), (memory, memory_pieces))):
        for block in range(2):
            rows = pl.ds(block * (count // 2), count // 2)
            arrivals.append((source.at[rows], target.at[0, rows], 2 * index + block))
    arrivals.append((cotangent, cot, 4))

    def far_copy(entry):
        source, target, sem = entry
        return pltpu.make_async_remote_copy(
            src_ref=source, dst_ref=target, send_sem=far_send.at[sem], recv_sem=far_recv.at[sem],
            device_id=owner, device_id_type=mesh_type,
        )

    def own_copy(entry):
        source, target, sem = entry
        return pltpu.make_async_copy(source, target, own_sem.at[sem])

    def core_copy(source, target, sem):
        return pltpu.make_async_remote_copy(
            src_ref=source, dst_ref=target, send_sem=core_send.at[sem], recv_sem=core_recv.at[sem],
            device_id=core_peer, device_id_type=mesh_type,
        )

    @pl.when(away)
    def _():
        for entry in arrivals:
            far_copy(entry).start()

    @pl.when(jnp.logical_not(away))
    def _():
        for entry in arrivals:
            own_copy(entry).start()

    def arrive(entry):
        @pl.when(away)
        def _():
            far_copy(entry).wait()

        @pl.when(jnp.logical_not(away))
        def _():
            own_copy(entry).wait()

    def forward_copy(index):
        held_piece = (input_pieces, memory_pieces)[index // 2]
        rows = pl.ds((index % 2) * (count // 2), count // 2)
        return core_copy(held_piece.at[0, rows], held_piece.at[1, rows], index)

    segment_copies = [
        core_copy(target_here, target_there, 4), core_copy(memory_here, memory_there, 5)
    ]
    for copy in segment_copies:
        copy.start()

    stores = {}

    def store(index):
        stores[index] = pltpu.make_async_copy(held_stores[index], stores_out[index], store_sem.at[index])
        stores[index].start()

    for copy in segment_copies:
        copy.wait()
    target_row[...] = jnp.where(away, target_there[...], target_here[...])
    memory_row[...] = jnp.where(away, memory_there[...], memory_here[...])
    spread_row(target_row, wide)
    loads[0].wait()

    def project(piece, block, spot):
        rows = slice(block * (count // 2), (block + 1) * (count // 2))
        source = input_pieces[piece, rows, :]
        here = dyn(spot * 2 + block, count // 2)
        keys[here, :] = nn(source, self_in_weight[:, WIDE : 2 * WIDE]).astype(BF16)
        value = (nn(source, self_in_weight[:, 2 * WIDE :]) + in_bias[1:2, :]).astype(BF16)
        values[here, :] = value
        values_t[:, here] = value.T
        if piece == 0:
            query = (nn(source, self_in_weight[:, :WIDE]) + in_bias[0:1, :]).astype(BF16)
            query = (query.astype(F32) * SCALE).astype(BF16)
            query_low[rows, :] = query
            for tile in range(count // 2 // TILE):
                split_columns(
                    query[tile * TILE : (tile + 1) * TILE, :].T, query_cols, block * (count // 2 // TILE) + tile
                )

    for block in range(2):
        arrive(arrivals[block])
        forward_copy(block).start()
        project(0, block, place)
    for block in range(2):
        forward_copy(block).wait()
        project(1, block, 1 - place)
    store(0)
    store(2)
    store(3)
    store(4)
    attend_whole(
        tiles, target_row, place * count, wide, True, query_cols, keys, values_t, attended_one, lse_one,
        held, held_low,
    )
    store(5)
    for load in loads[1:4]:
        load.wait()
    for block in range(2):
        arrive(arrivals[2 + block])
        forward_copy(2 + block).start()

    @pl.loop(0, blocks)
    def _(block):
        rows = dyn(block, rows_block)
        attended = attended_one[:, rows].T
        field = input_pieces[0, rows, :].astype(F32) + nn(attended, self_out_weight[...]) + self_out_bias[...]
        normal, rstd = normalize(field)
        first_normal[rows, :] = normal
        first_rstd[rows, :] = rstd
        low = (normal * first_gain[...] + first_shift[...]).astype(BF16)
        first_low[rows, :] = low
        query = (nn(low, cross_weight[...]) + cross_bias[0:1, :]).astype(BF16)
        query = (query.astype(F32) * SCALE).astype(BF16)
        cross_query[rows, :] = query
        for tile in range(rows_block // TILE):
            split_columns(
                query[tile * TILE : (tile + 1) * TILE, :].T, query_cols, block * (rows_block // TILE) + tile
            )

    store(6)
    store(7)
    store(8)

    def project_memory(piece, block, spot):
        rows = slice(block * (count // 2), (block + 1) * (count // 2))
        source = memory_pieces[piece, rows, :]
        here = dyn(spot * 2 + block, count // 2)
        cross_keys[here, :] = nn(source, pair_weight[:, :WIDE]).astype(BF16)
        value = (nn(source, pair_weight[:, WIDE:]) + cross_bias[1:2, :]).astype(BF16)
        cross_values[here, :] = value
        values_t[:, here] = value.T

    for block in range(2):
        project_memory(0, block, place)
    for block in range(2):
        forward_copy(2 + block).wait()
        project_memory(1, block, 1 - place)
    store(1)
    store(9)
    store(10)
    spread_row(memory_row, wide)
    attend_whole(
        tiles, target_row, place * count, wide, False, query_cols, cross_keys, values_t, attended_two, lse_two,
        held, held_low,
    )
    for load in loads[4:]:
        load.wait()

    @pl.loop(0, blocks)
    def _(block):
        rows = dyn(block, rows_block)
        attended = attended_two[:, rows].T
        first = first_normal[rows, :] * first_gain[...] + first_shift[...]
        field = first + nn(attended, cross_out_weight[...]) + cross_out_bias[...]
        normal, rstd = normalize(field)
        second_normal[rows, :] = normal
        second_rstd[rows, :] = rstd
        second = normal * second_gain[...] + second_shift[...]
        third[rows, :] = second + down_bias[...]
        low = second.astype(BF16)
        second_low[rows, :] = low
        second_low_t[:, rows] = low.T

    chunks, chunk_size = in_weight.shape[1] // WIDE, WIDE
    arrive(arrivals[4])

    @pl.loop(0, chunks)
    def _(chunk):
        lanes = dyn(chunk, chunk_size)
        hidden = nn(second_low[...], in_weight[:, lanes]) + feed_bias[:, lanes]
        value, derivative = gate(hidden)
        value = value.astype(BF16)
        active[:, lanes] = value
        slope[:, lanes] = derivative
        third[...] += nn(value, down_weight[lanes, :])

    sums_out[...] = jnp.zeros(sums_out.shape, F32)

    @pl.loop(0, blocks)
    def _(block):
        rows = dyn(block, rows_block)
        normal, rstd = normalize(third[rows, :])
        output_low[rows, :] = (normal * last_gain[...] + last_shift[...]).astype(BF16)
        outer = cot[rows, :].astype(F32)
        grad = normalize_back(outer, last_gain[...], normal, rstd)
        third[rows, :] = grad
        low = grad.astype(BF16)
        branch[rows, :] = low
        sums_out[0:1, :] += col_sum(outer * normal)
        sums_out[1:2, :] += col_sum(outer)
        sums_out[2:3, :] += col_sum(low.astype(F32))

    output_copy = (output_low, output_got, 5)

    @pl.when(away)
    def _():
        far_copy(output_copy).start()

    per_half = chunks // n

    @pl.loop(0, chunks)
    def _(chunk):
        lanes = dyn(chunk, chunk_size)
        share = tn(active[:, lanes], branch[...]).astype(BF16)
        down_grad[lax.div(chunk, per_half), dyn(lax.rem(chunk, per_half), chunk_size), :] = share
        inner = nt(branch[...], down_weight[lanes, :])
        hidden_grad = (inner * slope[:, lanes]).astype(BF16)
        in_bias_grad[:, lanes] = col_sum(hidden_grad.astype(F32))
        third[...] += nt(hidden_grad, in_weight[:, lanes])
        share = nn(second_low_t[...], hidden_grad).astype(BF16)
        for b in range(n):
            in_grad[b, dyn(chunk, half), :] = share[b * half : (b + 1) * half, :]

    store(13)
    store(14)

    @pl.loop(0, blocks)
    def _(block):
        rows = dyn(block, rows_block)
        outer = third[rows, :]
        normal = second_normal[rows, :]
        grad = normalize_back(outer, second_gain[...], normal, second_rstd[rows, :])
        g2_out[rows, :] = grad
        low = grad.astype(BF16)
        branch[rows, :] = low
        sums_out[3:4, :] += col_sum(outer * normal)
        sums_out[4:5, :] += col_sum(outer)
        sums_out[5:6, :] += col_sum(low.astype(F32))
        grad_out[rows, :] = nt(low, cross_out_weight[...]).astype(BF16)

    store(11)
    store(12)
    spread_parts(n, nn(attended_two[...], branch[...]), cross_out_grad, 0)
    store(15)
    write_delta(tiles, grad_out, attended_two, delta_ref)

    @pl.when(away)
    def _():
        far_copy(output_copy).wait()
        layer_output[...] = output_got[...]

    @pl.when(jnp.logical_not(away))
    def _():
        layer_output[...] = output_low[...]

    for index in range(FORWARD_STORES):
        stores[index].wait()


def forward_all(n, groups, rows_block, activations, weights, resident):
    count, features = activations[0].shape
    length = n * count
    hidden = weights[5].shape[1]
    half = features // n
    vm = pl.BlockSpec(memory_space=pltpu.VMEM)
    hbm = pl.BlockSpec(memory_space=pl.ANY)
    low, wide, every = (count, features), (count, features), (length, features)
    stored = [
        ((2, *low), BF16), ((2, *low), BF16), (low, BF16), (every, BF16), (every, BF16), ((features, count), BF16),
        (wide, F32), (low, BF16), (low, BF16), (every, BF16), (every, BF16), (low, BF16), (wide, F32),
        ((n, hidden // n, features), BF16), ((n, hidden // n, features), BF16), ((n, half, features), BF16),
    ]
    stats = out_like((features // PAIR, 2 * count), F32)
    row_like = out_like((1, length), jnp.int32)
    row_scratch = pltpu.VMEM((1, length), jnp.int32)
    held = (features // PAIR, length, 2 * TILE)
    low_rows, wide_rows = pltpu.VMEM(low, BF16), pltpu.VMEM(wide, F32)
    return pl.pallas_call(
        functools.partial(forward_kernel, n, groups, rows_block),
        in_specs=[hbm] * (len(activations) + len(weights)) + [vm] * len(resident),
        out_specs=[hbm] * len(stored) + [vm] * 9,
        out_shape=[out_like(*entry) for entry in stored] + [
            out_like(low, BF16), stats, stats, stats, out_like((count, 1), F32), out_like((8, features), F32),
            out_like((1, hidden), F32), row_like, row_like,
        ],
        scratch_shapes=[
            *[pltpu.VMEM(weight.shape, weight.dtype) for weight in weights],
            *[pltpu.VMEM(*entry) for entry in stored],
            low_rows, low_rows, low_rows, row_scratch, row_scratch,
            pltpu.VMEM((length, TILE), jnp.int32), pltpu.VMEM((features, length), BF16),
            pltpu.VMEM((features, 2 * count), BF16), pltpu.VMEM(held, F32), pltpu.VMEM(held, BF16),
            pltpu.VMEM((features, count), BF16), wide_rows, pltpu.VMEM((count, 1), F32), low_rows,
            pltpu.VMEM((features, count), BF16), pltpu.VMEM((count, hidden), BF16),
            pltpu.VMEM((count, hidden), F32), wide_rows, low_rows,
            pltpu.SemaphoreType.DMA((len(weights),)), pltpu.SemaphoreType.DMA((len(stored),)),
            pltpu.SemaphoreType.DMA((5,)), pltpu.SemaphoreType.DMA((6,)), pltpu.SemaphoreType.DMA((6,)),
            pltpu.SemaphoreType.DMA((6,)), pltpu.SemaphoreType.DMA((6,)),
        ],
        compiler_params=pltpu.CompilerParams(
            vmem_limit_bytes=VMEM_LIMIT, collective_id=1, has_side_effects=True
        ),
    )(*activations, *weights, *resident)


def widen_kernel(plan, source, *outs):
    for out, (start, columns) in zip(outs, plan):
        height = out.shape[0]
        for column in range(columns):
            out[:, column * WIDE : (column + 1) * WIDE] = source[
                start + column * height : start + (column + 1) * height, :
            ].astype(F32)


def key_ranges(query_segment, key_segment, tiles, limit):
    edges = query_segment.reshape(tiles, TILE)
    low = jnp.sum((key_segment[None, :] < edges[:, :1]).astype(jnp.int32), axis=1)
    high = jnp.sum((key_segment[None, :] <= edges[:, TILE - 1 :]).astype(jnp.int32), axis=1)
    if limit is not None:
        high = jnp.minimum(high, limit)
    return jnp.stack([low // TILE, (high + TILE - 1) // TILE]).astype(jnp.int32)


def apart(
    n, groups, rows_block, input_rows, memory_rows, cotangent_rows, target_segments, memory_segments,
    self_in_weight, self_in_bias, self_out_weight, self_out_bias, first_gain, first_shift,
    cross_query_weight, cross_pair_weight, cross_bias, cross_out_weight, cross_out_bias,
    second_gain, second_shift, feed_in_weight, feed_in_bias, feed_out_weight, feed_out_bias,
    third_gain, third_shift,
):
    count, features = input_rows.shape
    length = n * count
    hidden = feed_in_weight.shape[1]
    tiles = count // TILE
    half = features // n
    place = lax.axis_index("blk").astype(jnp.int32)

    def row(vector):
        return vector[None, :]

    def shifted(field, step):
        return lax.ppermute(field, "blk", [(s, (s + step) % n) for s in range(n)])

    def shifted_back(field, step):
        return lax.ppermute(field, "blk", [(s, (s - step) % n) for s in range(n)])

    input_pieces = [input_rows] + [shifted(input_rows, step) for step in range(1, n)]
    memory_pieces = [memory_rows] + [shifted(memory_rows, step) for step in range(1, n)]
    target_row, source_row = target_segments[0], memory_segments[0]
    target_here = lax.dynamic_slice_in_dim(target_row, place * count, count, 0)
    self_ranges = key_ranges(
        target_here, target_row, tiles, place * count + TILE * (1 + jnp.arange(tiles, dtype=jnp.int32))
    )
    cross_ranges = key_ranges(target_here, source_row, tiles, None)
    place_one = place[None]
    query_segment = target_here[None, :]
    target_column = target_row[:, None]
    source_column = source_row[:, None]

    stats = out_like((WIDE // PAIR, 2 * count), F32)
    low_rows = out_like((count, features), BF16)
    wide_rows = out_like((count, features), F32)
    low_row_all = out_like((length, features), BF16)
    statistic = out_like((count, 1), F32)
    wide_scratch = pltpu.VMEM((length, TILE), jnp.int32)
    values_t = pltpu.VMEM((features, length), BF16)
    query_cols = pltpu.VMEM((features, 2 * count), BF16)
    query_rows = pltpu.VMEM((2 * count, features), BF16)
    peak = pltpu.VMEM((8, 2 * TILE), F32)
    sums = pltpu.VMEM((features, TILE), F32)
    held = pltpu.VMEM((features // PAIR, KEYS, 2 * TILE), F32)
    held_low = pltpu.VMEM((features // PAIR, KEYS, 2 * TILE), BF16)
    square = 2 * count * features * features

    (
        query, keys, values, attended_t, lse, normal, rstd, first_low, cross_query
    ) = run(
        functools.partial(self_forward, n, rows_block),
        [place_one, self_ranges, *input_pieces, query_segment, target_column,
         self_in_weight, self_in_bias, self_out_weight, row(self_out_bias), row(first_gain),
         row(first_shift), cross_query_weight, cross_bias],
        2,
        [low_rows, low_row_all, low_row_all, out_like((features, count), BF16), stats, wide_rows,
         statistic, low_rows, low_rows],
        [wide_scratch, values_t, query_cols, peak, peak, sums, held, held_low],
        20 * square, 10 << 20,
    )

    (
        layer_output, cross_keys, cross_values, cross_lse, cross_delta, unused, cross_grad, g2,
        in_grad, down_grad, cross_out_grad, feed_sums, in_bias_grad,
    ) = run(
        functools.partial(cross_and_feed, n, rows_block),
        [place_one, cross_ranges, *memory_pieces, query_segment, source_column, cotangent_rows,
         cross_query, normal, row(first_gain), row(first_shift), cross_pair_weight, cross_bias,
         cross_out_weight, row(cross_out_bias), row(second_gain), row(second_shift),
         feed_in_weight, row(feed_in_bias), feed_out_weight, row(feed_out_bias),
         row(third_gain), row(third_shift)],
        2,
        [low_rows, low_row_all, low_row_all, stats, stats, out_like((8, 128), F32), low_rows, wide_rows,
         out_like((n, hidden // n, features), BF16), out_like((n, hidden // n, features), BF16),
         out_like((n, half, features), BF16), out_like((8, features), F32), out_like((1, hidden), F32)],
        [wide_scratch, values_t, query_cols, peak, peak, sums, held, held_low,
         pltpu.VMEM((features, count), BF16), pltpu.VMEM((count, features), F32),
         pltpu.VMEM((count, 1), F32), pltpu.VMEM((count, features), BF16),
         pltpu.VMEM((features, count), BF16), pltpu.VMEM((count, hidden), BF16),
         pltpu.VMEM((count, hidden), F32), pltpu.VMEM((count, features), F32),
         pltpu.VMEM((count, features), BF16), pltpu.VMEM((features, count), BF16)],
        50 * square, 20 << 20,
    )

    back_scratch = [
        wide_scratch, values_t, query_cols, query_rows, query_cols, query_rows,
        pltpu.VMEM((features, count), F32), pltpu.VMEM((length, features), F32),
        pltpu.VMEM((length, features), F32), held, held_low, held_low, pltpu.VMEM((count, features), BF16),
    ]
    sent_like = out_like((max(n - 1, 1), count, features), BF16)
    (
        memory_own, memory_sent, cross_query_grad, cross_pair_grad, self_out_grad, self_grad,
        self_delta, g1, cross_sums,
    ) = run(
        functools.partial(cross_backward, n, rows_block),
        [place_one, cross_ranges, *memory_pieces, query_segment, source_column, cross_query,
         cross_grad, cross_keys, cross_values, cross_lse, cross_delta, g2, normal, rstd, first_low,
         row(first_gain), cross_query_weight, cross_pair_weight, self_out_weight, attended_t],
        2,
        [wide_rows, sent_like, out_like((n, half, features), BF16),
         out_like((n, 2 * half, features), BF16), out_like((n, half, features), BF16), low_rows,
         stats, wide_rows, out_like((8, features), F32)],
        back_scratch + [pltpu.VMEM((count, features), BF16)],
        30 * square, 15 << 20,
    )
    (input_own, input_sent, self_in_grad, self_sums) = run(
        functools.partial(self_backward, n, rows_block),
        [place_one, self_ranges, *input_pieces, query_segment, target_column, query, self_grad,
         keys, values, lse, self_delta, g1, self_in_weight],
        2,
        [wide_rows, sent_like, out_like((n, 3 * half, features), BF16), out_like((8, features), F32)],
        back_scratch,
        30 * square, 15 << 20,
    )

    memory_grad, input_grad = memory_own, input_own
    for step in range(1, n):
        memory_grad = memory_grad + shifted_back(memory_sent[step - 1], step).astype(F32)
        input_grad = input_grad + shifted_back(input_sent[step - 1], step).astype(F32)

    vectors = jnp.concatenate([self_sums[:2], cross_sums[:5], feed_sums[:6]], axis=0)
    count_small = vectors.shape[0]
    small = jnp.concatenate(
        [
            jnp.transpose(vectors.reshape(count_small, n, half), (1, 0, 2)).reshape(n, -1),
            in_bias_grad.reshape(n, -1),
        ],
        axis=1,
    )
    amount = small.shape[1]
    small_rows = -(-amount // (8 * WIDE)) * 8
    small = jnp.pad(small, ((0, 0), (0, small_rows * WIDE - amount))).reshape(n, small_rows, WIDE)
    packed, small = reduce_all(
        n, groups,
        [in_grad, down_grad, cross_out_grad, cross_query_grad, cross_pair_grad, self_out_grad, self_in_grad],
        small,
    )
    small = small.reshape(-1)[:amount]
    return packed, small, memory_grad, input_grad, layer_output, count_small


def on_device(
    n, groups,
    inputs, memory, cotangent, target_segments, memory_segments,
    self_in_weight, self_in_bias, self_out_weight, self_out_bias, first_gain, first_shift,
    cross_query_weight, cross_pair_weight, cross_bias, cross_out_weight, cross_out_bias,
    second_gain, second_shift, feed_in_weight, feed_in_bias, feed_out_weight, feed_out_bias,
    third_gain, third_shift,
):
    input_rows, memory_rows, cotangent_rows = inputs[0], memory[0], cotangent[0]
    count, features = input_rows.shape
    length = n * count
    hidden = feed_in_weight.shape[1]
    rows_block = min(count, 256)
    tiles = count // TILE
    half = features // n
    near = n == 2 and groups % 4 == 0 and length <= 1024 and half % TILE == 0

    def row(vector):
        return vector[None, :]

    if near:
        (
            input_pieces, memory_pieces, query, keys, values, attended_t, normal, first_low, cross_query,
            cross_keys, cross_values, cross_grad, g2, in_grad, down_grad, cross_out_grad,
            layer_output, lse, cross_lse, cross_delta, rstd, feed_sums, in_bias_grad, target_row, memory_row,
        ) = forward_all(
            n, groups, rows_block,
            [input_rows, memory_rows, cotangent_rows],
            [self_in_weight, self_out_weight, cross_query_weight, cross_pair_weight, cross_out_weight,
             feed_in_weight, feed_out_weight],
            [target_segments, memory_segments, self_in_bias, row(self_out_bias), row(first_gain),
             row(first_shift), cross_bias, row(cross_out_bias), row(second_gain), row(second_shift),
             row(feed_in_bias), row(feed_out_bias), row(third_gain), row(third_shift)],
        )
        packed, small, memory_grad, input_grad = back_and_reduce(
            n, groups, rows_block,
            [in_grad, down_grad, cross_out_grad],
            [memory_pieces, cross_pair_weight, first_low, cross_query_weight, g2, normal, self_out_weight,
             attended_t, keys, values, query, input_pieces, self_in_weight],
            [target_row, memory_row, cross_query, cross_grad, cross_keys, cross_values,
             cross_lse, cross_delta, feed_sums, in_bias_grad, row(first_gain), rstd, lse],
        )
        count_small = 13
        small = small.reshape(-1)[: count_small * half + hidden // n]
    else:
        packed, small, memory_grad, input_grad, layer_output, count_small = apart(
            n, groups, rows_block, input_rows, memory_rows, cotangent_rows, target_segments, memory_segments,
            self_in_weight, self_in_bias, self_out_weight, self_out_bias, first_gain, first_shift,
            cross_query_weight, cross_pair_weight, cross_bias, cross_out_weight, cross_out_bias,
            second_gain, second_shift, feed_in_weight, feed_in_bias, feed_out_weight, feed_out_bias,
            third_gain, third_shift,
        )
    plan = []
    start = 0
    shapes = []
    for height, columns in (
        (half, hidden // features), (hidden // n, 1), (half, 1), (half, 1), (half, 2), (half, 1), (half, 3)
    ):
        plan.append((start, columns))
        shapes.append(out_like((height, columns * features), F32))
        start += height * columns
    (
        feed_in_grad, feed_out_grad, cross_out_total, cross_query_total, cross_pair_total,
        self_out_total, self_in_total,
    ) = run(functools.partial(widen_kernel, plan), [packed], 0, shapes, [], 0, 12 << 20)
    rows_small = small[: count_small * half].reshape(count_small, half)
    (
        self_query_bias, self_value_bias, cross_query_bias, cross_value_bias, first_gain_grad,
        first_shift_grad, self_out_bias_grad, third_gain_grad, third_shift_grad, feed_out_bias_grad,
        second_gain_grad, second_shift_grad, cross_out_bias_grad,
    ) = [rows_small[index] for index in range(count_small)]
    return (
        layer_output[None],
        input_grad[None],
        memory_grad[None],
        self_in_total,
        jnp.stack([self_query_bias, self_value_bias]),
        self_out_total,
        self_out_bias_grad,
        first_gain_grad,
        first_shift_grad,
        cross_query_total,
        cross_pair_total,
        jnp.stack([cross_query_bias, cross_value_bias]),
        cross_out_total,
        cross_out_bias_grad,
        second_gain_grad,
        second_shift_grad,
        feed_in_grad,
        small[count_small * half :],
        feed_out_grad,
        feed_out_bias_grad,
        third_gain_grad,
        third_shift_grad,
    )


def solution(mesh):
    rows = P("dp", "blk", None)
    everywhere = P()
    split = P("blk", None)
    vector = P("blk")
    pair = P(None, "blk")
    return jax.shard_map(
        functools.partial(on_device, mesh.shape["blk"], mesh.shape["dp"]),
        mesh=mesh,
        in_specs=(rows, rows, rows, P("dp", None), P("dp", None)) + (everywhere,) * 19,
        out_specs=(
            rows, rows, rows, split, pair, split, vector, vector, vector, split, split, pair, split,
            vector, vector, vector, split, vector, split, vector, vector, vector,
        ),
        check_vma=False,
    )
```

```python
import functools

import jax
import jax.numpy as jnp
from jax import lax
from jax.experimental import pallas as pl
from jax.experimental.pallas import tpu as pltpu
from jax.sharding import PartitionSpec as P

HEAD = 64
TILE = 128
KEYS = 256
BACK_KEYS = 256
PAIR = 2 * HEAD
WIDE = 512
SCALE = HEAD ** (-0.5)
MASKED = -1e30
F32 = jnp.float32
BF16 = jnp.bfloat16
VMEM_LIMIT = 62 << 20


def nn(left, right):
    return lax.dot_general(left, right, (((1,), (0,)), ((), ())), preferred_element_type=F32)


def nt(left, right):
    return lax.dot_general(left, right, (((1,), (1,)), ((), ())), preferred_element_type=F32)


def tn(left, right):
    return lax.dot_general(left, right, (((0,), (0,)), ((), ())), preferred_element_type=F32)


def col_sum(field):
    return jnp.sum(field, axis=0, keepdims=True)


def normalize(field):
    centre = field - jnp.mean(field, axis=-1, keepdims=True)
    spread = jnp.mean(centre * centre, axis=-1, keepdims=True)
    rstd = lax.rsqrt(spread + 1e-05)
    return centre * rstd, rstd


def normalize_back(grad, gain, normal, rstd):
    scaled = grad * gain
    mean = jnp.mean(scaled, axis=-1, keepdims=True)
    along = jnp.mean(scaled * normal, axis=-1, keepdims=True)
    return (scaled - mean - normal * along) * rstd


def gate(hidden):
    size = jnp.abs(hidden)
    bell = jnp.exp(hidden * hidden * -0.5)
    ratio = 1.0 / (1.0 + (0.3275911 * 0.7071067811865476) * size)
    series = 1.061405429 * ratio - 1.453152027
    series = series * ratio + 1.421413741
    series = series * ratio - 0.284496736
    series = series * ratio + 0.254829592
    tail = (0.5 * series) * ratio * bell
    phi = jnp.where(hidden > 0.0, 1.0 - tail, tail)
    return hidden * phi, phi + hidden * (bell * 0.3989422804014327)


def dyn(index, size):
    return pl.ds(pl.multiple_of(index * size, size), size)


def even_lanes(rows, width):
    return (lax.broadcasted_iota(jnp.int32, (rows, width), 1) // HEAD) % 2 == 0


def even_rows(rows, width):
    return (lax.broadcasted_iota(jnp.int32, (rows, width), 0) // HEAD) % 2 == 0


def split_columns(tile_t, out_ref, tile):
    chosen = even_rows(*tile_t.shape)
    blank = jnp.zeros_like(tile_t)
    out_ref[:, pl.ds(pl.multiple_of(tile * 2 * TILE, 2 * TILE), TILE)] = jnp.where(chosen, tile_t, blank)
    out_ref[:, pl.ds(pl.multiple_of(tile * 2 * TILE + TILE, TILE), TILE)] = jnp.where(
        chosen, blank, tile_t
    )


def split_rows(tile_n, out_ref, tile):
    chosen = even_lanes(*tile_n.shape)
    blank = jnp.zeros_like(tile_n)
    out_ref[pl.ds(pl.multiple_of(tile * 2 * TILE, 2 * TILE), TILE), :] = jnp.where(chosen, tile_n, blank)
    out_ref[pl.ds(pl.multiple_of(tile * 2 * TILE + TILE, TILE), TILE), :] = jnp.where(
        chosen, blank, tile_n
    )


def spread_segments(column_ref, wide_ref):
    total = column_ref.shape[0]
    step = min(total, 512)

    @pl.loop(0, total // step)
    def _(block):
        rows = dyn(block, step)
        wide_ref[rows, :] = jnp.broadcast_to(column_ref[rows, :], (step, TILE))


def key_rows(low, chunk, length, size):
    wanted = low * TILE + chunk * size
    start = pl.multiple_of(jnp.minimum(wanted, length - size), TILE)
    return pl.ds(start, size), start, wanted


def chunk_bias(query_row, key_wide_ref, tile, rows, start, wanted, offset, causal):
    size = rows.size
    key_position = start + lax.broadcasted_iota(jnp.int32, (size, TILE), 0)
    allowed = (key_wide_ref[rows, :] == query_row) & (key_position >= wanted)
    if causal:
        query_position = offset + tile * TILE + lax.broadcasted_iota(jnp.int32, (size, TILE), 1)
        allowed = allowed & (key_position <= query_position)
    return jnp.where(allowed, 0.0, MASKED)


def attend(
    tiles, ranges_ref, query_row_ref, key_wide_ref, offset, causal,
    query_cols, keys, values_t, attended_t, lse_ref, peak, total, sums, held, held_low,
):
    pairs = WIDE // PAIR

    @pl.loop(0, tiles)
    def _(tile):
        peak[...] = jnp.full(peak.shape, MASKED, F32)
        total[...] = jnp.zeros(total.shape, F32)
        sums[...] = jnp.zeros(sums.shape, F32)
        query_row = query_row_ref[:, dyn(tile, TILE)]

        low, high = ranges_ref[0, tile], ranges_ref[1, tile]

        size = held.shape[1]

        @pl.loop(0, lax.div((high - low) * TILE + size - 1, size))
        def _(chunk):
            rows, start, wanted = key_rows(low, chunk, keys.shape[0], size)
            bias = chunk_bias(query_row, key_wide_ref, tile, rows, start, wanted, offset, causal)
            bias = jnp.concatenate([bias, bias], axis=1)
            factors = []
            for pair in range(pairs):
                lanes = slice(pair * PAIR, (pair + 1) * PAIR)
                scores = nn(keys[rows, lanes], query_cols[lanes, dyn(tile, 2 * TILE)]) + bias
                held[pair] = scores
                before = peak[pair : pair + 1, :]
                after = jnp.maximum(before, jnp.max(scores, axis=0, keepdims=True))
                factors.append(jnp.exp(before - after))
                peak[pair : pair + 1, :] = after
            for pair in range(pairs):
                weights = jnp.exp(held[pair] - peak[pair : pair + 1, :])
                total[pair : pair + 1, :] = total[pair : pair + 1, :] * factors[pair] + col_sum(weights)
                held_low[pair] = weights.astype(BF16)
            for pair in range(pairs):
                factor = factors[pair]
                mixed = nn(values_t[pair * PAIR : (pair + 1) * PAIR, rows], held_low[pair])
                first = slice(pair * PAIR, pair * PAIR + HEAD)
                second = slice(pair * PAIR + HEAD, (pair + 1) * PAIR)
                sums[first, :] = sums[first, :] * factor[:, :TILE] + mixed[:HEAD, :TILE]
                sums[second, :] = sums[second, :] * factor[:, TILE:] + mixed[HEAD:, TILE:]

        for pair in range(pairs):
            amount = total[pair : pair + 1, :]
            lse_ref[pair : pair + 1, dyn(tile, 2 * TILE)] = peak[pair : pair + 1, :] + jnp.log(amount)
            share = 1.0 / amount
            first = slice(pair * PAIR, pair * PAIR + HEAD)
            second = slice(pair * PAIR + HEAD, (pair + 1) * PAIR)
            attended_t[first, dyn(tile, TILE)] = (sums[first, :] * share[:, :TILE]).astype(BF16)
            attended_t[second, dyn(tile, TILE)] = (sums[second, :] * share[:, TILE:]).astype(BF16)


def attend_back(
    tile, low, high, query_row_ref, first_query, key_wide_ref, offset, causal,
    query_cols, query_rows, grad_cols, grad_rows, keys, keys_t, values, lse_ref, delta_ref,
    query_grad_t, key_grad, value_grad, held, held_low, held_grad,
):
    pairs = WIDE // PAIR
    query_row = query_row_ref[:, pl.ds(pl.multiple_of(first_query + tile * TILE, TILE), TILE)]
    both = dyn(tile, 2 * TILE)

    size = held.shape[1]

    @pl.loop(0, lax.div((high - low) * TILE + size - 1, size))
    def _(chunk):
        rows, start, wanted = key_rows(low, chunk, keys.shape[0], size)
        bias = chunk_bias(query_row, key_wide_ref, tile, rows, start, wanted, offset, causal)
        bias = jnp.concatenate([bias, bias], axis=1)
        for pair in range(pairs):
            lanes = slice(pair * PAIR, (pair + 1) * PAIR)
            scores = nn(keys[rows, lanes], query_cols[lanes, both]) + bias
            probs = jnp.exp(scores - lse_ref[pair : pair + 1, both])
            held[pair] = probs
            held_low[pair] = probs.astype(BF16)
        for pair in range(pairs):
            lanes = slice(pair * PAIR, (pair + 1) * PAIR)
            prob_grad = nn(values[rows, lanes], grad_cols[lanes, both])
            held_grad[pair] = (held[pair] * (prob_grad - delta_ref[pair : pair + 1, both])).astype(BF16)
        for pair in range(pairs):
            lanes = slice(pair * PAIR, (pair + 1) * PAIR)
            value_grad[rows, lanes] += nn(held_low[pair], grad_rows[both, lanes])
            key_grad[rows, lanes] += nn(held_grad[pair], query_rows[both, lanes])
            mixed = nn(keys_t[lanes, rows], held_grad[pair])
            first = slice(pair * PAIR, pair * PAIR + HEAD)
            second = slice(pair * PAIR + HEAD, (pair + 1) * PAIR)
            query_grad_t[first, dyn(tile, TILE)] += mixed[:HEAD, :TILE]
            query_grad_t[second, dyn(tile, TILE)] += mixed[HEAD:, TILE:]


def clear(ref):
    rows = ref.shape[0]
    step = min(rows, 256)

    @pl.loop(0, rows // step)
    def _(block):
        ref[dyn(block, step), :] = jnp.zeros((step, ref.shape[1]), ref.dtype)


def transpose_rows(source, target):
    @pl.loop(0, source.shape[0] // TILE)
    def _(block):
        target[:, dyn(block, TILE)] = source[dyn(block, TILE), :].T


def out_like(shape, dtype):
    return jax.ShapeDtypeStruct(shape, dtype)


def run(body, ins, smem_count, outs, scratch, flops, bytes_accessed):
    vm = pl.BlockSpec(memory_space=pltpu.VMEM)
    sm = pl.BlockSpec(memory_space=pltpu.SMEM)
    return pl.pallas_call(
        body,
        in_specs=[sm] * smem_count + [vm] * (len(ins) - smem_count),
        out_specs=[vm] * len(outs),
        out_shape=outs,
        scratch_shapes=scratch,
        cost_estimate=pl.CostEstimate(
            flops=flops, bytes_accessed=bytes_accessed, transcendentals=0
        ),
        compiler_params=pltpu.CompilerParams(vmem_limit_bytes=VMEM_LIMIT),
    )(*ins)


def self_forward(n, rows_block, place_ref, ranges_ref, *refs):
    pieces, refs = refs[:n], refs[n:]
    (
        query_segment, key_segment, weight, bias, out_weight, out_bias, gain, shift,
        cross_weight, cross_bias,
        query_out, keys, values, attended_t, lse_ref, normal_out, rstd_out, first_low, cross_query,
        wide, values_t, query_cols, peak, total, sums, held, held_low,
    ) = refs
    count = pieces[0].shape[0]
    place = place_ref[0]
    spread_segments(key_segment, wide)

    for step in range(n):
        spot = lax.rem(place + n - step, n)

        @pl.when(spot <= place)
        def _():
            @pl.loop(0, count // rows_block)
            def _(block):
                source = pieces[step][dyn(block, rows_block), :]
                rows = dyn(spot * (count // rows_block) + block, rows_block)
                keys[rows, :] = nn(source, weight[:, WIDE : 2 * WIDE]).astype(BF16)
                values[rows, :] = (nn(source, weight[:, 2 * WIDE :]) + bias[1:2, :]).astype(BF16)
                if step == 0:
                    query = (nn(source, weight[:, :WIDE]) + bias[0:1, :]).astype(BF16)
                    query_out[dyn(block, rows_block), :] = (query.astype(F32) * SCALE).astype(BF16)

        @pl.when(spot > place)
        def _():
            @pl.loop(0, count // rows_block)
            def _(block):
                rows = dyn(spot * (count // rows_block) + block, rows_block)
                keys[rows, :] = jnp.zeros((rows_block, WIDE), BF16)
                values[rows, :] = jnp.zeros((rows_block, WIDE), BF16)

    transpose_rows(values, values_t)
    tiles = count // TILE

    @pl.loop(0, tiles)
    def _(tile):
        split_columns(query_out[dyn(tile, TILE), :].T, query_cols, tile)

    attend(
        tiles, ranges_ref, query_segment, wide, place * count, True,
        query_cols, keys, values_t, attended_t, lse_ref, peak, total, sums, held, held_low,
    )

    @pl.loop(0, count // rows_block)
    def _(block):
        rows = dyn(block, rows_block)
        attended = attended_t[:, rows].T
        field = pieces[0][rows, :].astype(F32) + nn(attended, out_weight[...]) + out_bias[...]
        normal, rstd = normalize(field)
        normal_out[rows, :] = normal
        rstd_out[rows, :] = rstd
        low = (normal * gain[...] + shift[...]).astype(BF16)
        first_low[rows, :] = low
        query = (nn(low, cross_weight[...]) + cross_bias[0:1, :]).astype(BF16)
        cross_query[rows, :] = (query.astype(F32) * SCALE).astype(BF16)


def cross_and_feed(n, rows_block, place_ref, ranges_ref, *refs):
    pieces, refs = refs[:n], refs[n:]
    (
        query_segment, key_segment, cotangent, cross_query, first_normal, first_gain, first_shift,
        pair_weight, cross_bias, out_weight, out_bias, gain, shift,
        in_weight, in_bias, down_weight, down_bias, last_gain, last_shift,
        layer_output, keys, values, lse_ref, delta_ref, out_grad, grad_out, g2_out,
        in_grad, down_grad, cross_out_grad, sums_out, in_bias_grad,
        wide, values_t, query_cols, peak, total, sums, held, held_low, attended_t, second_normal, second_rstd,
        second_low, second_low_t, active, slope, third, branch, branch_t,
    ) = refs
    count = pieces[0].shape[0]
    place = place_ref[0]
    spread_segments(key_segment, wide)
    blocks = count // rows_block

    for step in range(n):
        spot = lax.rem(place + n - step, n)

        @pl.loop(0, blocks)
        def _(block):
            source = pieces[step][dyn(block, rows_block), :]
            rows = dyn(spot * blocks + block, rows_block)
            keys[rows, :] = nn(source, pair_weight[:, :WIDE]).astype(BF16)
            values[rows, :] = (nn(source, pair_weight[:, WIDE:]) + cross_bias[1:2, :]).astype(BF16)

    transpose_rows(values, values_t)
    tiles = count // TILE

    @pl.loop(0, tiles)
    def _(tile):
        split_columns(cross_query[dyn(tile, TILE), :].T, query_cols, tile)

    attend(
        tiles, ranges_ref, query_segment, wide, 0, False,
        query_cols, keys, values_t, attended_t, lse_ref, peak, total, sums, held, held_low,
    )

    @pl.loop(0, blocks)
    def _(block):
        rows = dyn(block, rows_block)
        attended = attended_t[:, rows].T
        first = first_normal[rows, :] * first_gain[...] + first_shift[...]
        field = first + nn(attended, out_weight[...]) + out_bias[...]
        normal, rstd = normalize(field)
        second_normal[rows, :] = normal
        second_rstd[rows, :] = rstd
        second = normal * gain[...] + shift[...]
        third[rows, :] = second + down_bias[...]
        low = second.astype(BF16)
        second_low[rows, :] = low
        second_low_t[:, rows] = low.T

    hidden_size = in_weight.shape[1]
    chunk_size = min(WIDE, hidden_size // n)
    chunks = hidden_size // chunk_size

    @pl.loop(0, chunks)
    def _(chunk):
        lanes = dyn(chunk, chunk_size)

        @pl.loop(0, blocks)
        def _(block):
            rows = dyn(block, rows_block)
            hidden = nn(second_low[rows, :], in_weight[:, lanes]) + in_bias[:, lanes]
            value, derivative = gate(hidden)
            value = value.astype(BF16)
            active[rows, lanes] = value
            slope[rows, lanes] = derivative.astype(slope.dtype)
            third[rows, :] += nn(value, down_weight[dyn(chunk, chunk_size), :])

    sums_out[...] = jnp.zeros(sums_out.shape, F32)
    in_bias_grad[...] = jnp.zeros(in_bias_grad.shape, F32)

    @pl.loop(0, blocks)
    def _(block):
        rows = dyn(block, rows_block)
        normal, rstd = normalize(third[rows, :])
        layer_output[rows, :] = (normal * last_gain[...] + last_shift[...]).astype(BF16)
        outer = cotangent[rows, :].astype(F32)
        grad = normalize_back(outer, last_gain[...], normal, rstd)
        third[rows, :] = grad
        low = grad.astype(BF16)
        branch[rows, :] = low
        sums_out[0:1, :] += col_sum(outer * normal)
        sums_out[1:2, :] += col_sum(outer)
        sums_out[2:3, :] += col_sum(low.astype(F32))

    half = WIDE // n
    down_half = down_weight.shape[0] // n

    @pl.loop(0, chunks)
    def _(chunk):
        lanes = dyn(chunk, chunk_size)
        share = tn(active[:, lanes], branch[...]).astype(BF16)
        per_half = down_half // chunk_size
        down_grad[lax.div(chunk, per_half), dyn(lax.rem(chunk, per_half), chunk_size), :] = share

        @pl.loop(0, blocks)
        def _(block):
            rows = dyn(block, rows_block)
            inner = nt(branch[rows, :], down_weight[dyn(chunk, chunk_size), :])
            hidden_grad = (inner * slope[rows, lanes].astype(F32)).astype(BF16)
            active[rows, lanes] = hidden_grad
            in_bias_grad[:, lanes] += col_sum(hidden_grad.astype(F32))
            third[rows, :] += nt(hidden_grad, in_weight[:, lanes])

        share = nn(second_low_t[...], active[:, lanes]).astype(BF16)
        per_block = WIDE // chunk_size
        block_rows = dyn(lax.div(chunk, per_block), half)
        block_lanes = dyn(lax.rem(chunk, per_block), chunk_size)
        for part in range(n):
            in_grad[part, block_rows, block_lanes] = share[part * half : (part + 1) * half, :]

    @pl.loop(0, blocks)
    def _(block):
        rows = dyn(block, rows_block)
        outer = third[rows, :]
        normal = second_normal[rows, :]
        grad = normalize_back(outer, gain[...], normal, second_rstd[rows, :])
        g2_out[rows, :] = grad
        low = grad.astype(BF16)
        branch[rows, :] = low
        sums_out[3:4, :] += col_sum(outer * normal)
        sums_out[4:5, :] += col_sum(outer)
        sums_out[5:6, :] += col_sum(low.astype(F32))
        grad_out[rows, :] = nt(low, out_weight[...]).astype(BF16)

    share = nn(attended_t[...], branch[...]).astype(BF16)
    for part in range(n):
        cross_out_grad[part] = share[part * half : (part + 1) * half, :]

    write_delta(tiles, grad_out, attended_t, delta_ref)


def write_delta(tiles, grad, attended_t, delta_ref):
    @pl.loop(0, tiles)
    def _(tile):
        product = grad[dyn(tile, TILE), :].astype(F32).T * attended_t[:, dyn(tile, TILE)].astype(F32)
        for pair in range(WIDE // PAIR):
            start = pair * PAIR
            delta_ref[pair : pair + 1, pl.ds(pl.multiple_of(tile * 2 * TILE, 2 * TILE), TILE)] = col_sum(
                product[start : start + HEAD, :]
            )
            delta_ref[
                pair : pair + 1, pl.ds(pl.multiple_of(tile * 2 * TILE + TILE, TILE), TILE)
            ] = col_sum(product[start + HEAD : start + PAIR, :])


def prepare_back(tiles, query, grad, query_cols, query_rows, grad_cols, grad_rows):
    @pl.loop(0, tiles)
    def _(tile):
        here = query[dyn(tile, TILE), :]
        split_columns(here.T, query_cols, tile)
        split_rows(here, query_rows, tile)
        here = grad[dyn(tile, TILE), :]
        split_columns(here.T, grad_cols, tile)
        split_rows(here, grad_rows, tile)


def query_finish(tiles, query_grad_t, query_low, sums_out, index, rounded):
    @pl.loop(0, tiles)
    def _(tile):
        rows = dyn(tile, TILE)
        wide_grad = query_grad_t[:, rows].T * SCALE
        low = wide_grad.astype(BF16)
        query_low[rows, :] = low
        sums_out[index : index + 1, :] += col_sum(low.astype(F32) if rounded else wide_grad)


def spread_parts(n, share, target, start):
    half = WIDE // n
    for part in range(n):
        target[part, start : start + half, :] = share[part * half : (part + 1) * half, :].astype(BF16)


def row_product(n, place, pieces, source):
    count = pieces[0].shape[0]
    step_rows = min(count, 512)
    share = jnp.zeros((WIDE, WIDE), F32)
    for step in range(n):
        spot = lax.rem(place + n - step, n)
        for block in range(count // step_rows):
            rows = dyn(spot * (count // step_rows) + block, step_rows)
            share += tn(
                pieces[step][block * step_rows : (block + 1) * step_rows, :], source[rows, :].astype(BF16)
            )
    return share


def pair_back(n, place, rows_block, count, step, key_grad, value_grad, weight, first, sums_out, index, write):
    blocks = count // rows_block
    spot = lax.rem(place + n - step, n)

    @pl.loop(0, blocks)
    def _(block):
        rows = dyn(spot * blocks + block, rows_block)
        key_low = key_grad[rows, :].astype(BF16)
        value_part = value_grad[rows, :]
        sums_out[index : index + 1, :] += col_sum(value_part)
        value_low = value_part.astype(BF16)
        back = nt(key_low, weight[:, first : first + WIDE]) + nt(value_low, weight[:, first + WIDE : first + 2 * WIDE])
        write(dyn(block, rows_block), back)


def first_back(
    blocks, rows_block, g2, query_low, query_weight, first_normal, first_rstd, gain, self_out_weight,
    g1, branch, self_grad, sums_out, index,
):
    @pl.loop(0, blocks)
    def _(block):
        rows = dyn(block, rows_block)
        outer = g2[rows, :] + nt(query_low[rows, :], query_weight[...])
        normal = first_normal[rows, :]
        back = normalize_back(outer, gain[...], normal, first_rstd[rows, :])
        g1[rows, :] = back
        low = back.astype(BF16)
        branch[rows, :] = low
        sums_out[index : index + 1, :] += col_sum(outer * normal)
        sums_out[index + 1 : index + 2, :] += col_sum(outer)
        sums_out[index + 2 : index + 3, :] += col_sum(low.astype(F32))
        self_grad[rows, :] = nt(low, self_out_weight[...]).astype(BF16)


def cross_backward(n, rows_block, place_ref, ranges_ref, *refs):
    pieces, refs = refs[:n], refs[n:]
    (
        query_segment, key_segment, query, grad, keys, values, lse_ref, delta_ref, g2,
        first_normal, first_rstd, first_low, gain, query_weight, pair_weight, self_out_weight,
        self_attended_t,
        own_grad, sent_grad, query_grad_w, pair_grad_w, self_out_grad, self_grad, self_delta, g1_out, sums_out,
        wide, keys_t, query_cols, query_rows, grad_cols, grad_rows, query_grad_t, key_grad, value_grad,
        held, held_low, held_grad, query_low, branch,
    ) = refs
    count = pieces[0].shape[0]
    place = place_ref[0]
    tiles = count // TILE
    blocks = count // rows_block
    half = WIDE // n
    spread_segments(key_segment, wide)
    transpose_rows(keys, keys_t)
    prepare_back(tiles, query, grad, query_cols, query_rows, grad_cols, grad_rows)
    clear(query_grad_t)
    clear(key_grad)
    clear(value_grad)

    @pl.loop(0, tiles)
    def _(tile):
        attend_back(
            tile, ranges_ref[0, tile], ranges_ref[1, tile], query_segment, 0, wide, 0, False,
            query_cols, query_rows, grad_cols, grad_rows, keys, keys_t, values, lse_ref, delta_ref,
            query_grad_t, key_grad, value_grad, held, held_low, held_grad,
        )

    sums_out[...] = jnp.zeros(sums_out.shape, F32)
    query_finish(tiles, query_grad_t, query_low, sums_out, 0, True)
    spread_parts(n, tn(first_low[...], query_low[...]), query_grad_w, 0)
    for step in range(n):

        def write(here, back):
            if step == 0:
                own_grad[here, :] = back
            else:
                sent_grad[step - 1, here, :] = back.astype(BF16)

        pair_back(n, place, rows_block, count, step, key_grad, value_grad, pair_weight, 0, sums_out, 1, write)
    spread_parts(n, row_product(n, place, pieces, key_grad), pair_grad_w, 0)
    spread_parts(n, row_product(n, place, pieces, value_grad), pair_grad_w, half)
    first_back(
        blocks, rows_block, g2, query_low, query_weight, first_normal, first_rstd, gain, self_out_weight,
        g1_out, branch, self_grad, sums_out, 2,
    )
    spread_parts(n, nn(self_attended_t[...], branch[...]), self_out_grad, 0)
    write_delta(tiles, self_grad, self_attended_t, self_delta)


def self_backward(n, rows_block, place_ref, ranges_ref, *refs):
    pieces, refs = refs[:n], refs[n:]
    (
        query_segment, key_segment, query, grad, keys, values, lse_ref, delta_ref, g1, weight,
        own_grad, sent_grad, grad_w, sums_out,
        wide, keys_t, query_cols, query_rows, grad_cols, grad_rows, query_grad_t, key_grad, value_grad,
        held, held_low, held_grad, query_low,
    ) = refs
    count = pieces[0].shape[0]
    place = place_ref[0]
    tiles = count // TILE
    half = WIDE // n
    spread_segments(key_segment, wide)
    transpose_rows(keys, keys_t)
    prepare_back(tiles, query, grad, query_cols, query_rows, grad_cols, grad_rows)
    clear(query_grad_t)
    clear(key_grad)
    clear(value_grad)

    @pl.loop(0, tiles)
    def _(tile):
        attend_back(
            tile, ranges_ref[0, tile], ranges_ref[1, tile], query_segment, 0, wide, place * count, True,
            query_cols, query_rows, grad_cols, grad_rows, keys, keys_t, values, lse_ref, delta_ref,
            query_grad_t, key_grad, value_grad, held, held_low, held_grad,
        )

    sums_out[...] = jnp.zeros(sums_out.shape, F32)
    query_finish(tiles, query_grad_t, query_low, sums_out, 0, False)
    for step in range(n):

        def write(here, back):
            if step == 0:
                own_grad[here, :] = back + g1[here, :] + nt(query_low[here, :], weight[:, :WIDE])
            else:
                sent_grad[step - 1, here, :] = back.astype(BF16)

        pair_back(n, place, rows_block, count, step, key_grad, value_grad, weight, WIDE, sums_out, 1, write)
    spread_parts(n, tn(pieces[0][...], query_low[...]), grad_w, 0)
    spread_parts(n, row_product(n, place, pieces, key_grad), grad_w, half)
    spread_parts(n, row_product(n, place, pieces, value_grad), grad_w, 2 * half)


CORE_RATE = 0.0018
LINK_RATE = 0.0225
LATENCY = {"core": 1.0, "x": 2.2, "y": 2.2, "z": 2.6}
MARGIN = 0.5


def plan_steps(n, chunks, extras, segments):
    free = {"core": 0.0, "x": 0.0, "y": 0.0, "z": 0.0}
    now = 0.0
    pending = []
    plan = []
    crossed = set()

    def send(link, rows, rate=LINK_RATE):
        free[link] = max(free[link], now) + rows * rate
        return free[link] + LATENCY[link]

    def execute(kind, index, step):
        nonlocal now
        now += 0.15
        if kind == "chunk":
            unused, rows, y_first, unused = chunks[index]
            if step == 0:
                ready = send("core", n * rows // 2, CORE_RATE)
            elif step in (1, 2) and (step == 1) == y_first:
                ready = send("y", (n if y_first else 1) * rows // 4)
            elif step in (1, 2):
                crossed.add(index)
                ready = send("x", (n - 1) * rows // (4 if y_first else 2))
            elif step in (3, 4):
                ready = send("z", rows // 4)
            elif step == 5:
                ready = send("y", rows // 4)
            elif step == 6:
                ready = send("core", rows // 2, CORE_RATE)
            else:
                return
        elif kind == "extra":
            if step == 2:
                return
            rows = extras[index][0]
            ready = send("core", rows, CORE_RATE) if step == 0 else send("x", rows // 2)
        else:
            if step == 4:
                return
            link, rows = (("core", 64), ("x", 32), ("y", 32), ("z", 128))[step]
            ready = send(link, rows, CORE_RATE if link == "core" else LINK_RATE)
        pending.append((ready, len(pending), kind, index, step + 1))

    for number in range(len(segments) + 1):
        order = []
        last = number == len(segments)
        if not last:
            now += segments[number]
            released = [("chunk", i) for i, chunk in enumerate(chunks) if chunk[3] == number]
            released += [("extra", i) for i, extra in enumerate(extras) if extra[1] == number]
            if number == max(len(segments) - 2, 0):
                released.append(("small", 0))
            for kind, index in released:
                execute(kind, index, 0)
                order.append((kind, index, 0))
        while pending:
            pending.sort()
            first = 0
            if len(crossed) < len(chunks):
                while first < len(pending) and pending[first][2:] == ("extra", pending[first][3], 1):
                    first += 1
            if first == len(pending) or (not last and pending[first][0] + MARGIN > now):
                break
            ready, unused, kind, index, step = pending.pop(first)
            now = max(now, ready)
            execute(kind, index, step)
            order.append((kind, index, step))
        plan.append(order)
    return plan, now


class Reducer:
    def __init__(self, n, groups, chunks, field, total, total_out, small, small_out, buffers):
        (
            self.from_core, self.from_blk, self.from_y, self.from_z,
            self.small_core, self.small_blk, self.small_y, self.small_z,
            self.sends, self.receives, self.small_sends, self.small_receives, self.stores,
        ) = buffers
        self.n, self.chunks, self.field, self.total, self.total_out = n, chunks, field, total, total_out
        self.small, self.small_out = small, small_out
        self.depth = depth = groups // 4
        self.group = group = lax.axis_index("dp")
        self.part = part = lax.axis_index("blk")
        self.core = lax.rem(group, 2)
        self.side = lax.rem(lax.div(group, 2), 2)
        self.level = lax.div(group, 4)
        self.core_peer = (group + 1 - 2 * self.core, part)
        self.side_peer = (group + 2 - 4 * self.side, part)
        self.blk_peers = [(group, lax.rem(part + step, n)) for step in range(1, n)]
        self.z_peers = [(lax.rem(group + 4 * step, groups), part) for step in range(1, depth)]
        self.per_chunk = 4 + (n - 1) + 2 * (depth - 1)

    def greet(self, far_peer=None, has_far=None):
        peers = [self.core_peer, self.side_peer] + self.blk_peers + self.z_peers
        barrier = pltpu.get_barrier_semaphore()
        for peer in peers:
            pl.semaphore_signal(barrier, inc=1, device_id=peer, device_id_type=pl.DeviceIdType.MESH)
        if far_peer is not None:

            @pl.when(has_far)
            def _():
                pl.semaphore_signal(barrier, inc=1, device_id=far_peer, device_id_type=pl.DeviceIdType.MESH)

            self.greetings = jnp.where(has_far, len(peers) + 1, len(peers))
        else:
            self.greetings = len(peers)

    def enter(self):
        pl.semaphore_wait(pltpu.get_barrier_semaphore(), self.greetings)

    def copy(self, source, target, sem, peer):
        return pltpu.make_async_remote_copy(
            src_ref=source, dst_ref=target, send_sem=self.sends.at[sem], recv_sem=self.receives.at[sem],
            device_id=peer, device_id_type=pl.DeviceIdType.MESH,
        )

    def small_copy(self, source, target, sem, peer):
        return pltpu.make_async_remote_copy(
            src_ref=source, dst_ref=target, send_sem=self.small_sends.at[sem],
            recv_sem=self.small_receives.at[sem], device_id=peer, device_id_type=pl.DeviceIdType.MESH,
        )

    def span(self, start, size):
        return pl.ds(pl.multiple_of(start, 16), size)

    def copies(self, index, step):
        start, rows, y_first, unused = self.chunks[index]
        n, depth, part = self.n, self.depth, self.part
        half, quarter = rows // 2, rows // 4
        piece = quarter // depth
        own_half = start + self.core * half
        own_quarter = own_half + self.side * quarter
        sem = index * self.per_chunk
        if step == 0:
            theirs = self.span(start + (1 - self.core) * half, half)
            return [
                self.copy(
                    self.field.at[:, theirs], self.from_core.at[:, pl.ds(start // 2, half)], sem, self.core_peer
                )
            ]
        if step in (1, 2) and (step == 1) == y_first:
            theirs = self.span(own_half + (1 - self.side) * quarter, quarter)
            into = pl.ds(start // 4, quarter)
            if y_first:
                return [self.copy(self.field.at[:, theirs], self.from_y.at[:, into], sem + 1, self.side_peer)]
            return [self.copy(self.field.at[part, theirs], self.from_y.at[0, into], sem + 1, self.side_peer)]
        if step in (1, 2):
            if y_first:
                mine, into = self.span(own_quarter, quarter), pl.ds(start // 2, quarter)
            else:
                mine, into = self.span(own_half, half), pl.ds(start // 2, half)
            return [
                self.copy(
                    self.field.at[lax.rem(part + hop, n), mine], self.from_blk.at[hop - 1, into],
                    sem + 3 + hop, self.blk_peers[hop - 1],
                )
                for hop in range(1, n)
            ]
        if step == 3:
            copies = []
            for hop in range(1, depth):
                theirs = self.span(own_quarter + lax.rem(self.level + hop, depth) * piece, piece)
                copies.append(
                    self.copy(
                        self.field.at[part, theirs], self.from_z.at[hop - 1, pl.ds(start // 4 // depth, piece)],
                        sem + 2 + n + hop, self.z_peers[hop - 1],
                    )
                )
            return copies
        if step == 4:
            mine = self.span(own_quarter + self.level * piece, piece)
            return [
                self.copy(
                    self.total.at[mine], self.total.at[mine], sem + 1 + n + depth + hop, self.z_peers[hop - 1]
                )
                for hop in range(1, depth)
            ]
        if step == 5:
            mine = self.span(own_quarter, quarter)
            return [self.copy(self.total.at[mine], self.total.at[mine], sem + 2, self.side_peer)]
        mine = self.span(own_half, half)
        return [self.copy(self.total.at[mine], self.total.at[mine], sem + 3, self.core_peer)]

    def add(self, part, start, size, terms, result=None):
        step = min(size, 64)

        @pl.loop(0, size // step)
        def _(block):
            here = self.span(start + block * step, step)
            value = self.field[part, here, :].astype(F32)
            for ref, index, begin in terms:
                value = value + ref[index, self.span(begin + block * step, step), :].astype(F32)
            if result is None:
                self.field[part, here, :] = value.astype(BF16)
            else:
                result[here, :] = value.astype(BF16)

    def store(self, index):
        rows = pl.ds(self.chunks[index][0], self.chunks[index][1])
        return pltpu.make_async_copy(self.total.at[rows], self.total_out.at[rows], self.stores.at[index])

    def chunk_step(self, index, step):
        start, rows, y_first, unused = self.chunks[index]
        n, depth, part = self.n, self.depth, self.part
        half, quarter = rows // 2, rows // 4
        piece = quarter // depth
        own_half = start + self.core * half
        own_quarter = own_half + self.side * quarter
        if step > 0:
            for copy in self.copies(index, step - 1):
                copy.wait()
        if step == 1:
            for b in range(n):
                self.add(b, own_half, half, [(self.from_core, b, start // 2)])
        elif step in (2, 3) and (step == 2) == y_first:
            for b in range(n) if y_first else [part]:
                self.add(b, own_quarter, quarter, [(self.from_y, b if y_first else 0, start // 4)])
        elif step in (2, 3):
            begin, size = (own_quarter, quarter) if y_first else (own_half, half)
            self.add(part, begin, size, [(self.from_blk, hop, start // 2) for hop in range(n - 1)])
        elif step == 4:
            self.add(
                part, own_quarter + self.level * piece, piece,
                [(self.from_z, hop, start // 4 // depth) for hop in range(depth - 1)], self.total,
            )
        if step < 7:
            for copy in self.copies(index, step):
                copy.start()
        else:
            self.store(index).start()

    def small_copies(self, step):
        part, n = self.part, self.n
        if step == 0:
            return [self.small_copy(self.small.at[0], self.small_core, 0, self.core_peer)]
        if step == 1:
            return [
                self.small_copy(
                    self.small.at[1, lax.rem(part + hop, n)], self.small_blk.at[hop - 1], hop,
                    self.blk_peers[hop - 1],
                )
                for hop in range(1, n)
            ]
        if step == 2:
            return [self.small_copy(self.small.at[1, part], self.small_y, n, self.side_peer)]
        return [
            self.small_copy(self.small_y, self.small_z.at[hop - 1], n + hop, self.z_peers[hop - 1])
            for hop in range(1, self.depth)
        ]

    def small_step(self, step):
        part = self.part
        if step > 0:
            for copy in self.small_copies(step - 1):
                copy.wait()
        if step == 1:
            self.small[1] = self.small[0] + self.small_core[...]
        elif step == 2:
            held = self.small[1, part]
            for hop in range(self.n - 1):
                held = held + self.small_blk[hop]
            self.small[1, part] = held
        elif step == 3:
            self.small_y[...] = self.small_y[...] + self.small[1, part]
        elif step == 4:
            held = self.small_y[...]
            for hop in range(self.depth - 1):
                held = held + self.small_z[hop]
            self.small_out[...] = held
        if step < 4:
            for copy in self.small_copies(step):
                copy.start()

    def finish(self):
        for index in range(len(self.chunks)):
            self.store(index).wait()


def reducer_scratch(n, groups, chunks, rows, small_shape):
    depth = groups // 4
    per_chunk = 4 + (n - 1) + 2 * (depth - 1)
    return [
        pltpu.VMEM((n, rows // 2, WIDE), BF16),
        pltpu.VMEM((n - 1, rows // 2, WIDE), BF16),
        pltpu.VMEM((n, rows // 4, WIDE), BF16),
        pltpu.VMEM((depth - 1, rows // 4 // depth, WIDE), BF16),
        pltpu.VMEM((n, *small_shape), F32),
        pltpu.VMEM((n - 1, *small_shape), F32),
        pltpu.VMEM(small_shape, F32),
        pltpu.VMEM((depth - 1, *small_shape), F32),
        pltpu.SemaphoreType.DMA((len(chunks) * per_chunk,)),
        pltpu.SemaphoreType.DMA((len(chunks) * per_chunk,)),
        pltpu.SemaphoreType.DMA((n + depth,)),
        pltpu.SemaphoreType.DMA((n + depth,)),
        pltpu.SemaphoreType.DMA((len(chunks),)),
    ]


def reduce_kernel(n, groups, chunks, plan, part_rows, *refs):
    sources, refs = refs[: len(part_rows)], refs[len(part_rows) :]
    small_in, total_out, small_out, field, total, small, load_sem = refs[:7]
    loads = []
    start = 0
    for index, source in enumerate(sources):
        loads.append(
            pltpu.make_async_copy(source, field.at[:, pl.ds(start, part_rows[index])], load_sem.at[index])
        )
        loads[-1].start()
        start += part_rows[index]
    reducer = Reducer(n, groups, chunks, field, total, total_out, small, small_out, refs[7:])
    small[0] = small_in[...]
    reducer.greet()
    reducer.enter()
    for load in loads:
        load.wait()
    for order in plan:
        for kind, index, step in order:
            if kind == "chunk":
                reducer.chunk_step(index, step)
            else:
                reducer.small_step(step)
    reducer.finish()


def reduce_all(n, groups, parts, small):
    part_rows = [part.shape[1] for part in parts]
    rows = sum(part_rows)
    chunk_rows = max(16 * groups, rows // 8)
    chunks = [(start, chunk_rows, False, 0) for start in range(0, rows, chunk_rows)]
    plan, unused = plan_steps(n, chunks, [], [0.0])
    small_shape = small.shape[1:]
    vm = pl.BlockSpec(memory_space=pltpu.VMEM)
    hbm = pl.BlockSpec(memory_space=pl.ANY)
    return pl.pallas_call(
        functools.partial(reduce_kernel, n, groups, chunks, plan, part_rows),
        in_specs=[hbm] * len(parts) + [vm],
        out_specs=[hbm, vm],
        out_shape=[out_like((rows, WIDE), BF16), out_like(small_shape, F32)],
        scratch_shapes=[
            pltpu.VMEM((n, rows, WIDE), BF16),
            pltpu.VMEM((rows, WIDE), BF16),
            pltpu.VMEM((2, n, *small_shape), F32),
            pltpu.SemaphoreType.DMA((len(parts),)),
            *reducer_scratch(n, groups, chunks, rows, small_shape),
        ],
        compiler_params=pltpu.CompilerParams(
            vmem_limit_bytes=VMEM_LIMIT, collective_id=0, has_side_effects=True
        ),
    )(*parts, small)


Y_FIRST = [letter == "y" for letter in "yxxyyxyyyyyyyxxx"]
BACK_SEGMENTS = [
    3.2, 2.9, 2.9, 2.9, 2.9, 1.4, 2.8, 3.2, 2.3, 2.4, 2.4, 2.9, 2.9, 1.4, 1.1, 1.1, 2.2, 2.0,
]


def back_chunks(half, hidden_rows):
    released = [(half, 0)] * (2 * hidden_rows // half + 1)
    released += [(half, segment) for segment in (5, 6, 6, 7, 13, 14, 15)]
    chunks = []
    start = 0
    for index, (rows, segment) in enumerate(released):
        chunks.append((start, rows, Y_FIRST[index % len(Y_FIRST)], segment))
        start += rows
    return chunks


def back_kernel(n, groups, rows_block, chunks, plan, load_plan, *refs):
    feed_refs, refs = refs[:3], refs[3:]
    streamed, refs = refs[: len(load_plan)], refs[len(load_plan) :]
    (
        target_row, memory_row, cross_query, cross_grad, cross_keys, cross_values,
        cross_lse, cross_delta, feed_sums, in_bias_grad, gain, first_rstd, self_lse,
        total_out, small_out, memory_out, input_out,
        field, total, small, sums, memory_grad, input_grad, memory_sent, memory_got, input_sent, input_got, pair_low,
        wide, keys_t, query_cols, query_rows, grad_cols, grad_rows, query_grad_t, key_grad, value_grad,
        held, held_low, held_grad, query_low, branch, self_grad, self_delta, g1,
        feed_sem, load_sem, extra_send, extra_recv, extra_store,
    ) = refs[:50]
    refs = refs[50:]
    held_loads, buffers = refs[: len(load_plan)], refs[len(load_plan) :]
    count = cross_query.shape[0]
    length = cross_keys.shape[0]
    tiles = count // TILE
    blocks = count // rows_block
    half = WIDE // n
    group, part = lax.axis_index("dp"), lax.axis_index("blk")
    place = lax.rem(group, 2)
    away = place != part
    owner = (group - place + part, place)

    feed_loads = []
    start = 0
    for index, source in enumerate(feed_refs):
        rows = source.shape[1]
        feed_loads.append(
            pltpu.make_async_copy(source, field.at[:, pl.ds(start, rows)], feed_sem.at[index])
        )
        feed_loads[-1].start()
        start += rows
    loads = [
        pltpu.make_async_copy(source, target, load_sem.at[index])
        for index, (source, target) in enumerate(zip(streamed, held_loads))
    ]
    for load in loads:
        load.start()
    memory_pieces = [held_loads[0].at[step] for step in range(n)]
    held_loads = held_loads[1:]
    (
        pair_weight, first_low, query_weight, g2, first_normal, self_out_weight, self_attended_t,
        self_keys, self_values, self_query,
    ) = held_loads[:10]
    input_pieces = [held_loads[10].at[step] for step in range(n)]
    self_in_weight = held_loads[11]

    reducer = Reducer(n, groups, chunks, field, total, total_out, small, small_out, buffers)
    reducer.greet(owner, away)

    extras = (
        (memory_sent, memory_got, memory_grad, memory_out), (input_sent, input_got, input_grad, input_out)
    )

    def extra_copy(index, hop):
        sent, got, *unused = extras[index]
        return pltpu.make_async_remote_copy(
            src_ref=sent.at[hop], dst_ref=got.at[hop],
            send_sem=extra_send.at[2 * index + hop], recv_sem=extra_recv.at[2 * index + hop],
            device_id=reducer.core_peer if hop == 0 else owner, device_id_type=pl.DeviceIdType.MESH,
        )

    def extra_store_copy(index, from_owner):
        sent, got, unused, out = extras[index]
        return pltpu.make_async_copy((got if from_owner else sent).at[1], out, extra_store.at[index])

    def extra_step(index, step):
        sent, got, result, unused = extras[index]
        if step == 0:
            extra_copy(index, 0).start()
        elif step == 1:
            extra_copy(index, 0).wait()

            @pl.loop(0, blocks)
            def _(block):
                rows = dyn(block, rows_block)
                value = result[rows, :] + got[0, rows, :].astype(F32)
                sent[1, rows, :] = value.astype(BF16)

            @pl.when(away)
            def _():
                extra_copy(index, 1).start()

            @pl.when(jnp.logical_not(away))
            def _():
                extra_store_copy(index, False).start()
        else:

            @pl.when(away)
            def _():
                extra_copy(index, 1).wait()
                extra_store_copy(index, True).start()

    def run_steps(number):
        for kind, index, step in plan[number]:
            if kind == "chunk":
                reducer.chunk_step(index, step)
            elif kind == "small":
                reducer.small_step(step)
            else:
                extra_step(index, step)

    def wait_loads(first, last):
        for load in loads[first:last]:
            load.wait()

    spread_row(memory_row, wide)
    transpose_rows(cross_keys, keys_t)
    prepare_back(tiles, cross_query, cross_grad, query_cols, query_rows, grad_cols, grad_rows)
    clear(query_grad_t)
    clear(key_grad)
    clear(value_grad)
    sums[...] = jnp.zeros(sums.shape, F32)
    for load in feed_loads:
        load.wait()
    reducer.enter()
    run_steps(0)
    for tile in range(tiles):
        attend_back(
            tile, 0, length // TILE, target_row, place * count, wide, place * count, False,
            query_cols, query_rows, grad_cols, grad_rows, cross_keys, keys_t, cross_values,
            cross_lse, cross_delta, query_grad_t, key_grad, value_grad, held, held_low, held_grad,
        )
        run_steps(1 + tile)
    base = 2 * in_bias_grad.shape[1] // n + half
    wait_loads(0, 8)
    query_finish(tiles, query_grad_t, query_low, sums, 2, True)
    spread_parts(n, tn(first_low[...], query_low[...]), field, base)
    run_steps(5)
    for side, source in ((0, key_grad), (1, value_grad)):

        @pl.loop(0, length // rows_block)
        def _(block):
            rows = dyn(block, rows_block)
            value = source[rows, :]
            pair_low[side, rows, :] = value.astype(BF16)
            if side == 1:
                sums[3:4, :] += col_sum(value)

        spread_parts(
            n, row_product(n, place, memory_pieces, pair_low.at[side]), field, base + half + side * half
        )
    run_steps(6)
    first_back(
        blocks, rows_block, g2, query_low, query_weight, first_normal, first_rstd, gain, self_out_weight,
        g1, branch, self_grad, sums, 4,
    )
    spread_parts(n, nn(self_attended_t[...], branch[...]), field, base + 3 * half)
    write_delta(tiles, self_grad, self_attended_t, self_delta)
    run_steps(7)

    wait_loads(8, len(loads))
    spread_row(target_row, wide)
    transpose_rows(self_keys, keys_t)
    prepare_back(tiles, self_query, self_grad, query_cols, query_rows, grad_cols, grad_rows)
    clear(query_grad_t)
    clear(key_grad)
    clear(value_grad)
    run_steps(8)
    for tile in range(tiles):
        attend_back(
            tile, 0, place * tiles + tile + 1, target_row, place * count, wide, place * count, True,
            query_cols, query_rows, grad_cols, grad_rows, self_keys, keys_t, self_values,
            self_lse, self_delta, query_grad_t, key_grad, value_grad, held, held_low, held_grad,
        )
        run_steps(9 + tile)
    query_finish(tiles, query_grad_t, query_low, sums, 0, False)
    spread_parts(n, tn(input_pieces[0][...], query_low[...]), field, base + 4 * half)
    run_steps(13)
    spread_parts(n, row_product(n, place, input_pieces, key_grad), field, base + 5 * half)
    run_steps(14)
    spread_parts(n, row_product(n, place, input_pieces, value_grad), field, base + 6 * half)
    run_steps(15)
    for step in range(n):

        def write(here, back):
            if step == 0:
                input_grad[here, :] = back + g1[here, :] + nt(query_low[here, :], self_in_weight[:, :WIDE])
            else:
                input_sent[0, here, :] = back.astype(BF16)

        pair_back(n, place, rows_block, count, step, key_grad, value_grad, self_in_weight, WIDE, sums, 1, write)
    small[...] = jnp.zeros(small.shape, F32)
    for part in range(n):
        here = slice(part * half, (part + 1) * half)
        small[0, part, 0:7, :] = sums[0:7, here]
        small[0, part, 7:13, :] = feed_sums[0:6, here]
        wide_half = in_bias_grad.shape[1] // n
        for row in range(wide_half // half):
            begin = part * wide_half + row * half
            small[0, part, 13 + row : 14 + row, :] = in_bias_grad[:, begin : begin + half]
    run_steps(16)
    for step in range(n):
        spot = lax.rem(place + n - step, n)

        @pl.loop(0, blocks)
        def _(block):
            rows, here = dyn(spot * blocks + block, rows_block), dyn(block, rows_block)
            back = nt(pair_low[0, rows, :], pair_weight[:, :WIDE]) + nt(pair_low[1, rows, :], pair_weight[:, WIDE:])
            if step == 0:
                memory_grad[here, :] = back
            else:
                memory_sent[0, here, :] = back.astype(BF16)

    run_steps(17)
    run_steps(18)
    for index in range(2):

        @pl.when(away)
        def _():
            extra_store_copy(index, True).wait()

        @pl.when(jnp.logical_not(away))
        def _():
            extra_store_copy(index, False).wait()

    reducer.finish()


def back_and_reduce(n, groups, rows_block, feed_grads, streamed, resident):
    count, features = resident[2].shape
    length = n * count
    hidden_rows = feed_grads[0].shape[1]
    half = features // n
    rows = sum(part.shape[1] for part in feed_grads) + 7 * half
    chunks = back_chunks(half, hidden_rows)
    extras = [(count, 17), (count, 16)]
    plan, unused = plan_steps(n, chunks, extras, BACK_SEGMENTS)
    small_shape = (-(-(13 + hidden_rows // half * half * n // features) // 8) * 8 + 8, half)
    vm = pl.BlockSpec(memory_space=pltpu.VMEM)
    hbm = pl.BlockSpec(memory_space=pl.ANY)
    low_rows = pltpu.VMEM((count, features), BF16)
    wide_rows = pltpu.VMEM((count, features), F32)
    columns = pltpu.VMEM((features, 2 * count), BF16)
    doubled = pltpu.VMEM((2 * count, features), BF16)
    all_wide = pltpu.VMEM((length, features), F32)
    sent = pltpu.VMEM((2, count, features), BF16)
    held = (features // PAIR, BACK_KEYS, 2 * TILE)
    return pl.pallas_call(
        functools.partial(back_kernel, n, groups, rows_block, chunks, plan, [part.shape for part in streamed]),
        in_specs=[hbm] * (len(feed_grads) + len(streamed)) + [vm] * len(resident),
        out_specs=[hbm, vm, hbm, hbm],
        out_shape=[
            out_like((rows, WIDE), BF16), out_like(small_shape, F32),
            out_like((count, features), BF16), out_like((count, features), BF16),
        ],
        scratch_shapes=[
            pltpu.VMEM((n, rows, WIDE), BF16), pltpu.VMEM((rows, WIDE), BF16),
            pltpu.VMEM((2, n, *small_shape), F32), pltpu.VMEM((8, features), F32),
            wide_rows, wide_rows, sent, sent, sent, sent, pltpu.VMEM((2, length, features), BF16),
            pltpu.VMEM((length, TILE), jnp.int32), pltpu.VMEM((features, length), BF16),
            columns, doubled, columns, doubled,
            pltpu.VMEM((features, count), F32), all_wide, all_wide,
            pltpu.VMEM(held, F32), pltpu.VMEM(held, BF16), pltpu.VMEM(held, BF16),
            low_rows, low_rows, low_rows, pltpu.VMEM((features // PAIR, 2 * count), F32), wide_rows,
            pltpu.SemaphoreType.DMA((len(feed_grads),)), pltpu.SemaphoreType.DMA((len(streamed),)),
            pltpu.SemaphoreType.DMA((4,)), pltpu.SemaphoreType.DMA((4,)), pltpu.SemaphoreType.DMA((2,)),
            *[pltpu.VMEM(part.shape, part.dtype) for part in streamed],
            *reducer_scratch(n, groups, chunks, rows, small_shape),
        ],
        compiler_params=pltpu.CompilerParams(
            vmem_limit_bytes=VMEM_LIMIT, collective_id=0, has_side_effects=True
        ),
    )(*feed_grads, *streamed, *resident)


def spread_row(row_ref, wide_ref):
    @pl.loop(0, row_ref.shape[1] // TILE)
    def _(block):
        wide_ref[dyn(block, TILE), :] = jnp.broadcast_to(row_ref[:, dyn(block, TILE)], (TILE, TILE)).T


def attend_whole(
    tiles, query_row_ref, first_query, key_wide_ref, causal, query_cols, keys, values_t, attended_t, lse_ref,
    held, held_low,
):
    pairs = WIDE // PAIR
    length = keys.shape[0]

    @pl.loop(0, tiles)
    def _(tile):
        begin = pl.multiple_of(first_query + tile * TILE, TILE)
        allowed = key_wide_ref[...] == query_row_ref[:, pl.ds(begin, TILE)]
        if causal:
            key_position = lax.broadcasted_iota(jnp.int32, (length, TILE), 0)
            query_position = begin + lax.broadcasted_iota(jnp.int32, (length, TILE), 1)
            allowed = allowed & (key_position <= query_position)
        bias = jnp.where(allowed, 0.0, MASKED)
        bias = jnp.concatenate([bias, bias], axis=1)
        both = dyn(tile, 2 * TILE)
        peaks, shares = [], []
        for pair in range(pairs):
            lanes = slice(pair * PAIR, (pair + 1) * PAIR)
            scores = nn(keys[:, lanes], query_cols[lanes, both]) + bias
            held[pair] = scores
            peaks.append(jnp.max(scores, axis=0, keepdims=True))
        for pair in range(pairs):
            weights = jnp.exp(held[pair] - peaks[pair])
            total = col_sum(weights)
            held_low[pair] = weights.astype(BF16)
            lse_ref[pair : pair + 1, both] = peaks[pair] + jnp.log(total)
            shares.append(1.0 / total)
        for pair in range(pairs):
            share = shares[pair]
            mixed = nn(values_t[pair * PAIR : (pair + 1) * PAIR, :], held_low[pair])
            first = slice(pair * PAIR, pair * PAIR + HEAD)
            second = slice(pair * PAIR + HEAD, (pair + 1) * PAIR)
            attended_t[first, dyn(tile, TILE)] = (mixed[:HEAD, :TILE] * share[:, :TILE]).astype(BF16)
            attended_t[second, dyn(tile, TILE)] = (mixed[HEAD:, TILE:] * share[:, TILE:]).astype(BF16)


FORWARD_LOADS = 7
FORWARD_STORES = 16


def forward_kernel(n, groups, rows_block, *refs):
    (
        inputs, memory, cotangent, *weights_in
    ) = refs[: 3 + FORWARD_LOADS]
    refs = refs[3 + FORWARD_LOADS :]
    (
        target_here, memory_here, in_bias, self_out_bias, first_gain, first_shift, cross_bias, cross_out_bias,
        second_gain, second_shift, feed_bias, down_bias, last_gain, last_shift,
    ) = refs[:14]
    refs = refs[14:]
    stores_out, refs = refs[:FORWARD_STORES], refs[FORWARD_STORES:]
    (
        layer_output, lse_one, lse_two, delta_ref, first_rstd, sums_out, in_bias_grad, target_row, memory_row,
    ) = refs[:9]
    refs = refs[9:]
    held_weights, refs = refs[:FORWARD_LOADS], refs[FORWARD_LOADS:]
    held_stores, refs = refs[:FORWARD_STORES], refs[FORWARD_STORES:]
    (
        self_in_weight, self_out_weight, cross_weight, pair_weight, cross_out_weight, in_weight, down_weight
    ) = held_weights
    (
        input_pieces, memory_pieces, query_low, keys, values, attended_one, first_normal, first_low, cross_query,
        cross_keys, cross_values, grad_out, g2_out, in_grad, down_grad, cross_out_grad,
    ) = held_stores
    (
        cot, output_low, output_got, target_there, memory_there, wide, values_t, query_cols, held, held_low,
        attended_two, second_normal, second_rstd, second_low, second_low_t, active, slope, third, branch,
        load_sem, store_sem, own_sem, far_send, far_recv, core_send, core_recv,
    ) = refs
    count = inputs.shape[0]
    tiles = count // TILE
    blocks = count // rows_block
    half = WIDE // n
    group, part = lax.axis_index("dp"), lax.axis_index("blk")
    place = lax.rem(group, 2)
    away = place != part
    owner = (group - place + part, place)
    core_peer = (group + 1 - 2 * place, part)
    mesh_type = pl.DeviceIdType.MESH

    loads = [
        pltpu.make_async_copy(source, target, load_sem.at[index])
        for index, (source, target) in enumerate(zip(weights_in, held_weights))
    ]
    for load in loads:
        load.start()
    barrier = pltpu.get_barrier_semaphore()
    pl.semaphore_signal(barrier, inc=1, device_id=core_peer, device_id_type=mesh_type)

    @pl.when(away)
    def _():
        pl.semaphore_signal(barrier, inc=1, device_id=owner, device_id_type=mesh_type)

    pl.semaphore_wait(barrier, jnp.where(away, 2, 1))

    pieces_of = (count // 2, count // 2)
    arrivals = []
    for index, (source, target) in enumerate(((inputs, input_pieces), (memory, memory_pieces))):
        for block in range(2):
            rows = pl.ds(block * (count // 2), count // 2)
            arrivals.append((source.at[rows], target.at[0, rows], 2 * index + block))
    arrivals.append((cotangent, cot, 4))

    def far_copy(entry):
        source, target, sem = entry
        return pltpu.make_async_remote_copy(
            src_ref=source, dst_ref=target, send_sem=far_send.at[sem], recv_sem=far_recv.at[sem],
            device_id=owner, device_id_type=mesh_type,
        )

    def own_copy(entry):
        source, target, sem = entry
        return pltpu.make_async_copy(source, target, own_sem.at[sem])

    def core_copy(source, target, sem):
        return pltpu.make_async_remote_copy(
            src_ref=source, dst_ref=target, send_sem=core_send.at[sem], recv_sem=core_recv.at[sem],
            device_id=core_peer, device_id_type=mesh_type,
        )

    @pl.when(away)
    def _():
        for entry in arrivals:
            far_copy(entry).start()

    @pl.when(jnp.logical_not(away))
    def _():
        for entry in arrivals:
            own_copy(entry).start()

    def arrive(entry):
        @pl.when(away)
        def _():
            far_copy(entry).wait()

        @pl.when(jnp.logical_not(away))
        def _():
            own_copy(entry).wait()

    def forward_copy(index):
        held_piece = (input_pieces, memory_pieces)[index // 2]
        rows = pl.ds((index % 2) * (count // 2), count // 2)
        return core_copy(held_piece.at[0, rows], held_piece.at[1, rows], index)

    segment_copies = [
        core_copy(target_here, target_there, 4), core_copy(memory_here, memory_there, 5)
    ]
    for copy in segment_copies:
        copy.start()

    stores = {}

    def store(index):
        stores[index] = pltpu.make_async_copy(held_stores[index], stores_out[index], store_sem.at[index])
        stores[index].start()

    for copy in segment_copies:
        copy.wait()
    target_row[...] = jnp.where(away, target_there[...], target_here[...])
    memory_row[...] = jnp.where(away, memory_there[...], memory_here[...])
    spread_row(target_row, wide)
    loads[0].wait()

    def project(piece, block, spot):
        rows = slice(block * (count // 2), (block + 1) * (count // 2))
        source = input_pieces[piece, rows, :]
        here = dyn(spot * 2 + block, count // 2)
        keys[here, :] = nn(source, self_in_weight[:, WIDE : 2 * WIDE]).astype(BF16)
        value = (nn(source, self_in_weight[:, 2 * WIDE :]) + in_bias[1:2, :]).astype(BF16)
        values[here, :] = value
        values_t[:, here] = value.T
        if piece == 0:
            query = (nn(source, self_in_weight[:, :WIDE]) + in_bias[0:1, :]).astype(BF16)
            query = (query.astype(F32) * SCALE).astype(BF16)
            query_low[rows, :] = query
            for tile in range(count // 2 // TILE):
                split_columns(
                    query[tile * TILE : (tile + 1) * TILE, :].T, query_cols, block * (count // 2 // TILE) + tile
                )

    for block in range(2):
        arrive(arrivals[block])
        forward_copy(block).start()
        project(0, block, place)
    for block in range(2):
        forward_copy(block).wait()
        project(1, block, 1 - place)
    store(0)
    store(2)
    store(3)
    store(4)
    attend_whole(
        tiles, target_row, place * count, wide, True, query_cols, keys, values_t, attended_one, lse_one,
        held, held_low,
    )
    store(5)
    for load in loads[1:4]:
        load.wait()
    for block in range(2):
        arrive(arrivals[2 + block])
        forward_copy(2 + block).start()

    @pl.loop(0, blocks)
    def _(block):
        rows = dyn(block, rows_block)
        attended = attended_one[:, rows].T
        field = input_pieces[0, rows, :].astype(F32) + nn(attended, self_out_weight[...]) + self_out_bias[...]
        normal, rstd = normalize(field)
        first_normal[rows, :] = normal
        first_rstd[rows, :] = rstd
        low = (normal * first_gain[...] + first_shift[...]).astype(BF16)
        first_low[rows, :] = low
        query = (nn(low, cross_weight[...]) + cross_bias[0:1, :]).astype(BF16)
        query = (query.astype(F32) * SCALE).astype(BF16)
        cross_query[rows, :] = query
        for tile in range(rows_block // TILE):
            split_columns(
                query[tile * TILE : (tile + 1) * TILE, :].T, query_cols, block * (rows_block // TILE) + tile
            )

    store(6)
    store(7)
    store(8)

    def project_memory(piece, block, spot):
        rows = slice(block * (count // 2), (block + 1) * (count // 2))
        source = memory_pieces[piece, rows, :]
        here = dyn(spot * 2 + block, count // 2)
        cross_keys[here, :] = nn(source, pair_weight[:, :WIDE]).astype(BF16)
        value = (nn(source, pair_weight[:, WIDE:]) + cross_bias[1:2, :]).astype(BF16)
        cross_values[here, :] = value
        values_t[:, here] = value.T

    for block in range(2):
        project_memory(0, block, place)
    for block in range(2):
        forward_copy(2 + block).wait()
        project_memory(1, block, 1 - place)
    store(1)
    store(9)
    store(10)
    spread_row(memory_row, wide)
    attend_whole(
        tiles, target_row, place * count, wide, False, query_cols, cross_keys, values_t, attended_two, lse_two,
        held, held_low,
    )
    for load in loads[4:]:
        load.wait()

    @pl.loop(0, blocks)
    def _(block):
        rows = dyn(block, rows_block)
        attended = attended_two[:, rows].T
        first = first_normal[rows, :] * first_gain[...] + first_shift[...]
        field = first + nn(attended, cross_out_weight[...]) + cross_out_bias[...]
        normal, rstd = normalize(field)
        second_normal[rows, :] = normal
        second_rstd[rows, :] = rstd
        second = normal * second_gain[...] + second_shift[...]
        third[rows, :] = second + down_bias[...]
        low = second.astype(BF16)
        second_low[rows, :] = low
        second_low_t[:, rows] = low.T

    chunks, chunk_size = in_weight.shape[1] // WIDE, WIDE
    arrive(arrivals[4])

    @pl.loop(0, chunks)
    def _(chunk):
        lanes = dyn(chunk, chunk_size)
        hidden = nn(second_low[...], in_weight[:, lanes]) + feed_bias[:, lanes]
        value, derivative = gate(hidden)
        value = value.astype(BF16)
        active[:, lanes] = value
        slope[:, lanes] = derivative
        third[...] += nn(value, down_weight[lanes, :])

    sums_out[...] = jnp.zeros(sums_out.shape, F32)

    @pl.loop(0, blocks)
    def _(block):
        rows = dyn(block, rows_block)
        normal, rstd = normalize(third[rows, :])
        output_low[rows, :] = (normal * last_gain[...] + last_shift[...]).astype(BF16)
        outer = cot[rows, :].astype(F32)
        grad = normalize_back(outer, last_gain[...], normal, rstd)
        third[rows, :] = grad
        low = grad.astype(BF16)
        branch[rows, :] = low
        sums_out[0:1, :] += col_sum(outer * normal)
        sums_out[1:2, :] += col_sum(outer)
        sums_out[2:3, :] += col_sum(low.astype(F32))

    output_copy = (output_low, output_got, 5)

    @pl.when(away)
    def _():
        far_copy(output_copy).start()

    per_half = chunks // n

    @pl.loop(0, chunks)
    def _(chunk):
        lanes = dyn(chunk, chunk_size)
        share = tn(active[:, lanes], branch[...]).astype(BF16)
        down_grad[lax.div(chunk, per_half), dyn(lax.rem(chunk, per_half), chunk_size), :] = share
        inner = nt(branch[...], down_weight[lanes, :])
        hidden_grad = (inner * slope[:, lanes]).astype(BF16)
        in_bias_grad[:, lanes] = col_sum(hidden_grad.astype(F32))
        third[...] += nt(hidden_grad, in_weight[:, lanes])
        share = nn(second_low_t[...], hidden_grad).astype(BF16)
        for b in range(n):
            in_grad[b, dyn(chunk, half), :] = share[b * half : (b + 1) * half, :]

    store(13)
    store(14)

    @pl.loop(0, blocks)
    def _(block):
        rows = dyn(block, rows_block)
        outer = third[rows, :]
        normal = second_normal[rows, :]
        grad = normalize_back(outer, second_gain[...], normal, second_rstd[rows, :])
        g2_out[rows, :] = grad
        low = grad.astype(BF16)
        branch[rows, :] = low
        sums_out[3:4, :] += col_sum(outer * normal)
        sums_out[4:5, :] += col_sum(outer)
        sums_out[5:6, :] += col_sum(low.astype(F32))
        grad_out[rows, :] = nt(low, cross_out_weight[...]).astype(BF16)

    store(11)
    store(12)
    spread_parts(n, nn(attended_two[...], branch[...]), cross_out_grad, 0)
    store(15)
    write_delta(tiles, grad_out, attended_two, delta_ref)

    @pl.when(away)
    def _():
        far_copy(output_copy).wait()
        layer_output[...] = output_got[...]

    @pl.when(jnp.logical_not(away))
    def _():
        layer_output[...] = output_low[...]

    for index in range(FORWARD_STORES):
        stores[index].wait()


def forward_all(n, groups, rows_block, activations, weights, resident):
    count, features = activations[0].shape
    length = n * count
    hidden = weights[5].shape[1]
    half = features // n
    vm = pl.BlockSpec(memory_space=pltpu.VMEM)
    hbm = pl.BlockSpec(memory_space=pl.ANY)
    low, wide, every = (count, features), (count, features), (length, features)
    stored = [
        ((2, *low), BF16), ((2, *low), BF16), (low, BF16), (every, BF16), (every, BF16), ((features, count), BF16),
        (wide, F32), (low, BF16), (low, BF16), (every, BF16), (every, BF16), (low, BF16), (wide, F32),
        ((n, hidden // n, features), BF16), ((n, hidden // n, features), BF16), ((n, half, features), BF16),
    ]
    stats = out_like((features // PAIR, 2 * count), F32)
    row_like = out_like((1, length), jnp.int32)
    row_scratch = pltpu.VMEM((1, length), jnp.int32)
    held = (features // PAIR, length, 2 * TILE)
    low_rows, wide_rows = pltpu.VMEM(low, BF16), pltpu.VMEM(wide, F32)
    return pl.pallas_call(
        functools.partial(forward_kernel, n, groups, rows_block),
        in_specs=[hbm] * (len(activations) + len(weights)) + [vm] * len(resident),
        out_specs=[hbm] * len(stored) + [vm] * 9,
        out_shape=[out_like(*entry) for entry in stored] + [
            out_like(low, BF16), stats, stats, stats, out_like((count, 1), F32), out_like((8, features), F32),
            out_like((1, hidden), F32), row_like, row_like,
        ],
        scratch_shapes=[
            *[pltpu.VMEM(weight.shape, weight.dtype) for weight in weights],
            *[pltpu.VMEM(*entry) for entry in stored],
            low_rows, low_rows, low_rows, row_scratch, row_scratch,
            pltpu.VMEM((length, TILE), jnp.int32), pltpu.VMEM((features, length), BF16),
            pltpu.VMEM((features, 2 * count), BF16), pltpu.VMEM(held, F32), pltpu.VMEM(held, BF16),
            pltpu.VMEM((features, count), BF16), wide_rows, pltpu.VMEM((count, 1), F32), low_rows,
            pltpu.VMEM((features, count), BF16), pltpu.VMEM((count, hidden), BF16),
            pltpu.VMEM((count, hidden), F32), wide_rows, low_rows,
            pltpu.SemaphoreType.DMA((len(weights),)), pltpu.SemaphoreType.DMA((len(stored),)),
            pltpu.SemaphoreType.DMA((5,)), pltpu.SemaphoreType.DMA((6,)), pltpu.SemaphoreType.DMA((6,)),
            pltpu.SemaphoreType.DMA((6,)), pltpu.SemaphoreType.DMA((6,)),
        ],
        compiler_params=pltpu.CompilerParams(
            vmem_limit_bytes=VMEM_LIMIT, collective_id=1, has_side_effects=True
        ),
    )(*activations, *weights, *resident)


def widen_kernel(plan, source, *outs):
    for out, (start, columns) in zip(outs, plan):
        height = out.shape[0]
        for column in range(columns):
            out[:, column * WIDE : (column + 1) * WIDE] = source[
                start + column * height : start + (column + 1) * height, :
            ].astype(F32)


def finish_kernel(plan, packed, *refs):
    count = len(plan)
    input_low, memory_low, output_low, small, *refs = refs
    (
        *weights, input_grad, memory_grad, layer_output, self_bias, cross_bias, feed_bias,
    ) = refs[: count + 6]
    refs = refs[count + 6 :]
    vectors, refs = refs[:9], refs[9:]
    held, refs = refs[:count], refs[count:]
    wide, refs = refs[:count], refs[count:]
    input_held, memory_held, output_held, input_wide, memory_wide, load_sem, store_sem = refs

    def load(index):
        start, columns = plan[index]
        return pltpu.make_async_copy(
            packed.at[pl.ds(start, held[index].shape[0])], held[index], load_sem.at[index]
        )

    extra = [
        pltpu.make_async_copy(input_low, input_held, load_sem.at[count]),
        pltpu.make_async_copy(memory_low, memory_held, load_sem.at[count + 1]),
    ]
    output = pltpu.make_async_copy(output_low, output_held, load_sem.at[count + 2])
    loads = [load(index) for index in range(count)]
    for copy in loads + extra + [output]:
        copy.start()
    stores = [pltpu.make_async_copy(output_held, layer_output, store_sem.at[count + 2])]
    output.wait()
    stores[0].start()
    for index, (start, columns) in enumerate(plan):
        loads[index].wait()
        height = wide[index].shape[0]

        @pl.loop(0, height // 64)
        def _(block):
            for column in range(columns):
                here = pl.ds(pl.multiple_of(column * height + block * 64, 64), 64)
                wide[index][dyn(block, 64), column * WIDE : (column + 1) * WIDE] = held[index][here, :].astype(F32)

        stores.append(pltpu.make_async_copy(wide[index], weights[index], store_sem.at[index]))
        stores[-1].start()
    for index, (source, target, result) in enumerate(
        ((input_held, input_wide, input_grad), (memory_held, memory_wide, memory_grad))
    ):
        extra[index].wait()

        @pl.loop(0, target.shape[0] // 128)
        def _(block):
            target[dyn(block, 128), :] = source[dyn(block, 128), :].astype(F32)

        stores.append(pltpu.make_async_copy(target, result, store_sem.at[count + index]))
        stores[-1].start()
    self_bias[...] = small[0:2, :]
    cross_bias[...] = small[2:4, :]
    for index, vector in enumerate(vectors):
        vector[...] = small[4 + index, :]
    half = small.shape[1]
    for row in range(feed_bias.shape[0] // half):
        feed_bias[row * half : (row + 1) * half] = small[13 + row, :]
    for copy in stores:
        copy.wait()


def finish_all(n, packed, small, input_low, memory_low, layer_output, hidden):
    count, features = input_low.shape
    half = features // n
    plan, shapes, parts = [], [], []
    start = 0
    for height, columns in (
        (half, hidden // features), (hidden // n, 1), (half, 1), (half, 1), (half, 2), (half, 1), (half, 3)
    ):
        plan.append((start, columns))
        parts.append((height * columns, features))
        shapes.append((height, columns * features))
        start += height * columns
    vm = pl.BlockSpec(memory_space=pltpu.VMEM)
    hbm = pl.BlockSpec(memory_space=pl.ANY)
    wide = (count, features)
    return pl.pallas_call(
        functools.partial(finish_kernel, plan),
        in_specs=[hbm] * 4 + [vm],
        out_specs=[hbm] * (len(plan) + 3) + [vm] * 12,
        out_shape=[out_like(shape, F32) for shape in shapes] + [
            out_like(wide, F32), out_like(wide, F32), out_like(wide, BF16),
            out_like((2, half), F32), out_like((2, half), F32), out_like((hidden // n,), F32),
        ] + [out_like((half,), F32)] * 9,
        scratch_shapes=[pltpu.VMEM(shape, BF16) for shape in parts]
        + [pltpu.VMEM(shape, F32) for shape in shapes]
        + [
            pltpu.VMEM(wide, BF16), pltpu.VMEM(wide, BF16), pltpu.VMEM(wide, BF16), pltpu.VMEM(wide, F32),
            pltpu.VMEM(wide, F32),
            pltpu.SemaphoreType.DMA((len(plan) + 3,)), pltpu.SemaphoreType.DMA((len(plan) + 3,)),
        ],
        compiler_params=pltpu.CompilerParams(vmem_limit_bytes=VMEM_LIMIT),
    )(packed, input_low, memory_low, layer_output, small)


def key_ranges(query_segment, key_segment, tiles, limit):
    edges = query_segment.reshape(tiles, TILE)
    low = jnp.sum((key_segment[None, :] < edges[:, :1]).astype(jnp.int32), axis=1)
    high = jnp.sum((key_segment[None, :] <= edges[:, TILE - 1 :]).astype(jnp.int32), axis=1)
    if limit is not None:
        high = jnp.minimum(high, limit)
    return jnp.stack([low // TILE, (high + TILE - 1) // TILE]).astype(jnp.int32)


def apart(
    n, groups, rows_block, input_rows, memory_rows, cotangent_rows, target_segments, memory_segments,
    self_in_weight, self_in_bias, self_out_weight, self_out_bias, first_gain, first_shift,
    cross_query_weight, cross_pair_weight, cross_bias, cross_out_weight, cross_out_bias,
    second_gain, second_shift, feed_in_weight, feed_in_bias, feed_out_weight, feed_out_bias,
    third_gain, third_shift,
):
    count, features = input_rows.shape
    length = n * count
    hidden = feed_in_weight.shape[1]
    tiles = count // TILE
    half = features // n
    place = lax.axis_index("blk").astype(jnp.int32)

    def row(vector):
        return vector[None, :]

    def shifted(field, step):
        return lax.ppermute(field, "blk", [(s, (s + step) % n) for s in range(n)])

    def shifted_back(field, step):
        return lax.ppermute(field, "blk", [(s, (s - step) % n) for s in range(n)])

    input_pieces = [input_rows] + [shifted(input_rows, step) for step in range(1, n)]
    memory_pieces = [memory_rows] + [shifted(memory_rows, step) for step in range(1, n)]
    target_row, source_row = target_segments[0], memory_segments[0]
    target_here = lax.dynamic_slice_in_dim(target_row, place * count, count, 0)
    self_ranges = key_ranges(
        target_here, target_row, tiles, place * count + TILE * (1 + jnp.arange(tiles, dtype=jnp.int32))
    )
    cross_ranges = key_ranges(target_here, source_row, tiles, None)
    place_one = place[None]
    query_segment = target_here[None, :]
    target_column = target_row[:, None]
    source_column = source_row[:, None]

    stats = out_like((WIDE // PAIR, 2 * count), F32)
    low_rows = out_like((count, features), BF16)
    wide_rows = out_like((count, features), F32)
    low_row_all = out_like((length, features), BF16)
    statistic = out_like((count, 1), F32)
    wide_scratch = pltpu.VMEM((length, TILE), jnp.int32)
    values_t = pltpu.VMEM((features, length), BF16)
    query_cols = pltpu.VMEM((features, 2 * count), BF16)
    query_rows = pltpu.VMEM((2 * count, features), BF16)
    peak = pltpu.VMEM((8, 2 * TILE), F32)
    sums = pltpu.VMEM((features, TILE), F32)
    held = pltpu.VMEM((features // PAIR, KEYS, 2 * TILE), F32)
    held_low = pltpu.VMEM((features // PAIR, KEYS, 2 * TILE), BF16)
    square = 2 * count * features * features

    (
        query, keys, values, attended_t, lse, normal, rstd, first_low, cross_query
    ) = run(
        functools.partial(self_forward, n, rows_block),
        [place_one, self_ranges, *input_pieces, query_segment, target_column,
         self_in_weight, self_in_bias, self_out_weight, row(self_out_bias), row(first_gain),
         row(first_shift), cross_query_weight, cross_bias],
        2,
        [low_rows, low_row_all, low_row_all, out_like((features, count), BF16), stats, wide_rows,
         statistic, low_rows, low_rows],
        [wide_scratch, values_t, query_cols, peak, peak, sums, held, held_low],
        20 * square, 10 << 20,
    )

    (
        layer_output, cross_keys, cross_values, cross_lse, cross_delta, unused, cross_grad, g2,
        in_grad, down_grad, cross_out_grad, feed_sums, in_bias_grad,
    ) = run(
        functools.partial(cross_and_feed, n, rows_block),
        [place_one, cross_ranges, *memory_pieces, query_segment, source_column, cotangent_rows,
         cross_query, normal, row(first_gain), row(first_shift), cross_pair_weight, cross_bias,
         cross_out_weight, row(cross_out_bias), row(second_gain), row(second_shift),
         feed_in_weight, row(feed_in_bias), feed_out_weight, row(feed_out_bias),
         row(third_gain), row(third_shift)],
        2,
        [low_rows, low_row_all, low_row_all, stats, stats, out_like((8, 128), F32), low_rows, wide_rows,
         out_like((n, hidden // n, features), BF16), out_like((n, hidden // n, features), BF16),
         out_like((n, half, features), BF16), out_like((8, features), F32), out_like((1, hidden), F32)],
        [wide_scratch, values_t, query_cols, peak, peak, sums, held, held_low,
         pltpu.VMEM((features, count), BF16), pltpu.VMEM((count, features), F32),
         pltpu.VMEM((count, 1), F32), pltpu.VMEM((count, features), BF16),
         pltpu.VMEM((features, count), BF16), pltpu.VMEM((count, hidden), BF16),
         pltpu.VMEM((count, hidden), F32), pltpu.VMEM((count, features), F32),
         pltpu.VMEM((count, features), BF16), pltpu.VMEM((features, count), BF16)],
        50 * square, 20 << 20,
    )

    back_scratch = [
        wide_scratch, values_t, query_cols, query_rows, query_cols, query_rows,
        pltpu.VMEM((features, count), F32), pltpu.VMEM((length, features), F32),
        pltpu.VMEM((length, features), F32), held, held_low, held_low, pltpu.VMEM((count, features), BF16),
    ]
    sent_like = out_like((max(n - 1, 1), count, features), BF16)
    (
        memory_own, memory_sent, cross_query_grad, cross_pair_grad, self_out_grad, self_grad,
        self_delta, g1, cross_sums,
    ) = run(
        functools.partial(cross_backward, n, rows_block),
        [place_one, cross_ranges, *memory_pieces, query_segment, source_column, cross_query,
         cross_grad, cross_keys, cross_values, cross_lse, cross_delta, g2, normal, rstd, first_low,
         row(first_gain), cross_query_weight, cross_pair_weight, self_out_weight, attended_t],
        2,
        [wide_rows, sent_like, out_like((n, half, features), BF16),
         out_like((n, 2 * half, features), BF16), out_like((n, half, features), BF16), low_rows,
         stats, wide_rows, out_like((8, features), F32)],
        back_scratch + [pltpu.VMEM((count, features), BF16)],
        30 * square, 15 << 20,
    )
    (input_own, input_sent, self_in_grad, self_sums) = run(
        functools.partial(self_backward, n, rows_block),
        [place_one, self_ranges, *input_pieces, query_segment, target_column, query, self_grad,
         keys, values, lse, self_delta, g1, self_in_weight],
        2,
        [wide_rows, sent_like, out_like((n, 3 * half, features), BF16), out_like((8, features), F32)],
        back_scratch,
        30 * square, 15 << 20,
    )

    memory_grad, input_grad = memory_own, input_own
    for step in range(1, n):
        memory_grad = memory_grad + shifted_back(memory_sent[step - 1], step).astype(F32)
        input_grad = input_grad + shifted_back(input_sent[step - 1], step).astype(F32)

    vectors = jnp.concatenate([self_sums[:2], cross_sums[:5], feed_sums[:6]], axis=0)
    count_small = vectors.shape[0]
    small = jnp.concatenate(
        [
            jnp.transpose(vectors.reshape(count_small, n, half), (1, 0, 2)).reshape(n, -1),
            in_bias_grad.reshape(n, -1),
        ],
        axis=1,
    )
    amount = small.shape[1]
    small_rows = -(-amount // (8 * WIDE)) * 8
    small = jnp.pad(small, ((0, 0), (0, small_rows * WIDE - amount))).reshape(n, small_rows, WIDE)
    packed, small = reduce_all(
        n, groups,
        [in_grad, down_grad, cross_out_grad, cross_query_grad, cross_pair_grad, self_out_grad, self_in_grad],
        small,
    )
    small = small.reshape(-1)[:amount]
    return packed, small, memory_grad, input_grad, layer_output, count_small


def on_device(
    n, groups,
    inputs, memory, cotangent, target_segments, memory_segments,
    self_in_weight, self_in_bias, self_out_weight, self_out_bias, first_gain, first_shift,
    cross_query_weight, cross_pair_weight, cross_bias, cross_out_weight, cross_out_bias,
    second_gain, second_shift, feed_in_weight, feed_in_bias, feed_out_weight, feed_out_bias,
    third_gain, third_shift,
):
    input_rows, memory_rows, cotangent_rows = inputs[0], memory[0], cotangent[0]
    count, features = input_rows.shape
    length = n * count
    hidden = feed_in_weight.shape[1]
    rows_block = min(count, 256)
    tiles = count // TILE
    half = features // n
    near = n == 2 and groups % 4 == 0 and length <= 1024 and half % TILE == 0

    def row(vector):
        return vector[None, :]

    if near:
        (
            input_pieces, memory_pieces, query, keys, values, attended_t, normal, first_low, cross_query,
            cross_keys, cross_values, cross_grad, g2, in_grad, down_grad, cross_out_grad,
            layer_output, lse, cross_lse, cross_delta, rstd, feed_sums, in_bias_grad, target_row, memory_row,
        ) = forward_all(
            n, groups, rows_block,
            [input_rows, memory_rows, cotangent_rows],
            [self_in_weight, self_out_weight, cross_query_weight, cross_pair_weight, cross_out_weight,
             feed_in_weight, feed_out_weight],
            [target_segments, memory_segments, self_in_bias, row(self_out_bias), row(first_gain),
             row(first_shift), cross_bias, row(cross_out_bias), row(second_gain), row(second_shift),
             row(feed_in_bias), row(feed_out_bias), row(third_gain), row(third_shift)],
        )
        packed, small, memory_grad, input_grad = back_and_reduce(
            n, groups, rows_block,
            [in_grad, down_grad, cross_out_grad],
            [memory_pieces, cross_pair_weight, first_low, cross_query_weight, g2, normal, self_out_weight,
             attended_t, keys, values, query, input_pieces, self_in_weight],
            [target_row, memory_row, cross_query, cross_grad, cross_keys, cross_values,
             cross_lse, cross_delta, feed_sums, in_bias_grad, row(first_gain), rstd, lse],
        )
        (
            feed_in_grad, feed_out_grad, cross_out_total, cross_query_total, cross_pair_total,
            self_out_total, self_in_total, input_grad, memory_grad, layer_output, self_bias_grad,
            cross_bias_grad, in_bias_total, first_gain_grad, first_shift_grad, self_out_bias_grad,
            third_gain_grad, third_shift_grad, feed_out_bias_grad, second_gain_grad, second_shift_grad,
            cross_out_bias_grad,
        ) = finish_all(n, packed, small, input_grad, memory_grad, layer_output, hidden)
    else:
        packed, small, memory_grad, input_grad, layer_output, count_small = apart(
            n, groups, rows_block, input_rows, memory_rows, cotangent_rows, target_segments, memory_segments,
            self_in_weight, self_in_bias, self_out_weight, self_out_bias, first_gain, first_shift,
            cross_query_weight, cross_pair_weight, cross_bias, cross_out_weight, cross_out_bias,
            second_gain, second_shift, feed_in_weight, feed_in_bias, feed_out_weight, feed_out_bias,
            third_gain, third_shift,
        )
        plan = []
        start = 0
        shapes = []
        for height, columns in (
            (half, hidden // features), (hidden // n, 1), (half, 1), (half, 1), (half, 2), (half, 1), (half, 3)
        ):
            plan.append((start, columns))
            shapes.append(out_like((height, columns * features), F32))
            start += height * columns
        (
            feed_in_grad, feed_out_grad, cross_out_total, cross_query_total, cross_pair_total,
            self_out_total, self_in_total,
        ) = run(functools.partial(widen_kernel, plan), [packed], 0, shapes, [], 0, 12 << 20)
        rows_small = small[: count_small * half].reshape(count_small, half)
        (
            self_query_bias, self_value_bias, cross_query_bias, cross_value_bias, first_gain_grad,
            first_shift_grad, self_out_bias_grad, third_gain_grad, third_shift_grad, feed_out_bias_grad,
            second_gain_grad, second_shift_grad, cross_out_bias_grad,
        ) = [rows_small[index] for index in range(count_small)]
        self_bias_grad = jnp.stack([self_query_bias, self_value_bias])
        cross_bias_grad = jnp.stack([cross_query_bias, cross_value_bias])
        in_bias_total = small[count_small * half :]
    return (
        layer_output[None],
        input_grad[None],
        memory_grad[None],
        self_in_total,
        self_bias_grad,
        self_out_total,
        self_out_bias_grad,
        first_gain_grad,
        first_shift_grad,
        cross_query_total,
        cross_pair_total,
        cross_bias_grad,
        cross_out_total,
        cross_out_bias_grad,
        second_gain_grad,
        second_shift_grad,
        feed_in_grad,
        in_bias_total,
        feed_out_grad,
        feed_out_bias_grad,
        third_gain_grad,
        third_shift_grad,
    )


def solution(mesh):
    rows = P("dp", "blk", None)
    everywhere = P()
    split = P("blk", None)
    vector = P("blk")
    pair = P(None, "blk")
    return jax.shard_map(
        functools.partial(on_device, mesh.shape["blk"], mesh.shape["dp"]),
        mesh=mesh,
        in_specs=(rows, rows, rows, P("dp", None), P("dp", None)) + (everywhere,) * 19,
        out_specs=(
            rows, rows, rows, split, pair, split, vector, vector, vector, split, split, pair, split,
            vector, vector, vector, split, vector, split, vector, vector, vector,
        ),
        check_vma=False,
    )
```

```python
import functools

import jax
import jax.numpy as jnp
from jax import lax
from jax.experimental import pallas as pl
from jax.experimental.pallas import tpu as pltpu
from jax.sharding import PartitionSpec as P

HEAD = 64
TILE = 128
KEYS = 256
BACK_KEYS = 256
PAIR = 2 * HEAD
WIDE = 512
SCALE = HEAD ** (-0.5)
MASKED = -1e30
F32 = jnp.float32
BF16 = jnp.bfloat16
VMEM_LIMIT = 62 << 20


def nn(left, right):
    return lax.dot_general(left, right, (((1,), (0,)), ((), ())), preferred_element_type=F32)


def nt(left, right):
    return lax.dot_general(left, right, (((1,), (1,)), ((), ())), preferred_element_type=F32)


def tn(left, right):
    return lax.dot_general(left, right, (((0,), (0,)), ((), ())), preferred_element_type=F32)


def col_sum(field):
    return jnp.sum(field, axis=0, keepdims=True)


def normalize(field):
    centre = field - jnp.mean(field, axis=-1, keepdims=True)
    spread = jnp.mean(centre * centre, axis=-1, keepdims=True)
    rstd = lax.rsqrt(spread + 1e-05)
    return centre * rstd, rstd


def normalize_back(grad, gain, normal, rstd):
    scaled = grad * gain
    mean = jnp.mean(scaled, axis=-1, keepdims=True)
    along = jnp.mean(scaled * normal, axis=-1, keepdims=True)
    return (scaled - mean - normal * along) * rstd


def gate(hidden):
    bell = jnp.exp2(hidden * hidden * (-0.5 * 1.4426950408889634))
    ratio = 1.0 / (1.0 + (0.3275911 * 0.7071067811865476) * jnp.abs(hidden))
    series = (0.5 * 1.061405429) * ratio - 0.5 * 1.453152027
    series = series * ratio + 0.5 * 1.421413741
    series = series * ratio - 0.5 * 0.284496736
    series = series * ratio + 0.5 * 0.254829592
    tail = series * ratio * bell
    phi = jnp.where(hidden > 0.0, 1.0 - tail, tail)
    return hidden * phi, phi + hidden * (bell * 0.3989422804014327)


def dyn(index, size):
    return pl.ds(pl.multiple_of(index * size, size), size)


def even_lanes(rows, width):
    return (lax.broadcasted_iota(jnp.int32, (rows, width), 1) // HEAD) % 2 == 0


def even_rows(rows, width):
    return (lax.broadcasted_iota(jnp.int32, (rows, width), 0) // HEAD) % 2 == 0


def split_columns(tile_t, out_ref, tile):
    chosen = even_rows(*tile_t.shape)
    blank = jnp.zeros_like(tile_t)
    out_ref[:, pl.ds(pl.multiple_of(tile * 2 * TILE, 2 * TILE), TILE)] = jnp.where(chosen, tile_t, blank)
    out_ref[:, pl.ds(pl.multiple_of(tile * 2 * TILE + TILE, TILE), TILE)] = jnp.where(
        chosen, blank, tile_t
    )


def split_rows(tile_n, out_ref, tile):
    chosen = even_lanes(*tile_n.shape)
    blank = jnp.zeros_like(tile_n)
    out_ref[pl.ds(pl.multiple_of(tile * 2 * TILE, 2 * TILE), TILE), :] = jnp.where(chosen, tile_n, blank)
    out_ref[pl.ds(pl.multiple_of(tile * 2 * TILE + TILE, TILE), TILE), :] = jnp.where(
        chosen, blank, tile_n
    )


def spread_segments(column_ref, wide_ref):
    total = column_ref.shape[0]
    step = min(total, 512)

    @pl.loop(0, total // step)
    def _(block):
        rows = dyn(block, step)
        wide_ref[rows, :] = jnp.broadcast_to(column_ref[rows, :], (step, TILE))


def key_rows(low, chunk, length, size):
    wanted = low * TILE + chunk * size
    start = pl.multiple_of(jnp.minimum(wanted, length - size), TILE)
    return pl.ds(start, size), start, wanted


def chunk_bias(query_row, key_wide_ref, tile, rows, start, wanted, offset, causal):
    size = rows.size
    key_position = start + lax.broadcasted_iota(jnp.int32, (size, TILE), 0)
    allowed = (key_wide_ref[rows, :] == query_row) & (key_position >= wanted)
    if causal:
        query_position = offset + tile * TILE + lax.broadcasted_iota(jnp.int32, (size, TILE), 1)
        allowed = allowed & (key_position <= query_position)
    return jnp.where(allowed, 0.0, MASKED)


def attend(
    tiles, ranges_ref, query_row_ref, key_wide_ref, offset, causal,
    query_cols, keys, values_t, attended_t, lse_ref, peak, total, sums, held, held_low,
):
    pairs = WIDE // PAIR

    @pl.loop(0, tiles)
    def _(tile):
        peak[...] = jnp.full(peak.shape, MASKED, F32)
        total[...] = jnp.zeros(total.shape, F32)
        sums[...] = jnp.zeros(sums.shape, F32)
        query_row = query_row_ref[:, dyn(tile, TILE)]

        low, high = ranges_ref[0, tile], ranges_ref[1, tile]

        size = held.shape[1]

        @pl.loop(0, lax.div((high - low) * TILE + size - 1, size))
        def _(chunk):
            rows, start, wanted = key_rows(low, chunk, keys.shape[0], size)
            bias = chunk_bias(query_row, key_wide_ref, tile, rows, start, wanted, offset, causal)
            bias = jnp.concatenate([bias, bias], axis=1)
            factors = []
            for pair in range(pairs):
                lanes = slice(pair * PAIR, (pair + 1) * PAIR)
                scores = nn(keys[rows, lanes], query_cols[lanes, dyn(tile, 2 * TILE)]) + bias
                held[pair] = scores
                before = peak[pair : pair + 1, :]
                after = jnp.maximum(before, jnp.max(scores, axis=0, keepdims=True))
                factors.append(jnp.exp(before - after))
                peak[pair : pair + 1, :] = after
            for pair in range(pairs):
                weights = jnp.exp(held[pair] - peak[pair : pair + 1, :])
                total[pair : pair + 1, :] = total[pair : pair + 1, :] * factors[pair] + col_sum(weights)
                held_low[pair] = weights.astype(BF16)
            for pair in range(pairs):
                factor = factors[pair]
                mixed = nn(values_t[pair * PAIR : (pair + 1) * PAIR, rows], held_low[pair])
                first = slice(pair * PAIR, pair * PAIR + HEAD)
                second = slice(pair * PAIR + HEAD, (pair + 1) * PAIR)
                sums[first, :] = sums[first, :] * factor[:, :TILE] + mixed[:HEAD, :TILE]
                sums[second, :] = sums[second, :] * factor[:, TILE:] + mixed[HEAD:, TILE:]

        for pair in range(pairs):
            amount = total[pair : pair + 1, :]
            lse_ref[pair : pair + 1, dyn(tile, 2 * TILE)] = peak[pair : pair + 1, :] + jnp.log(amount)
            share = 1.0 / amount
            first = slice(pair * PAIR, pair * PAIR + HEAD)
            second = slice(pair * PAIR + HEAD, (pair + 1) * PAIR)
            attended_t[first, dyn(tile, TILE)] = (sums[first, :] * share[:, :TILE]).astype(BF16)
            attended_t[second, dyn(tile, TILE)] = (sums[second, :] * share[:, TILE:]).astype(BF16)


def attend_back(
    tile, low, high, query_row_ref, first_query, key_wide_ref, offset, causal,
    query_cols, query_rows, grad_cols, grad_rows, keys, keys_t, values, lse_ref, delta_ref,
    query_grad_t, key_grad, value_grad, held, held_low, held_grad,
):
    pairs = WIDE // PAIR
    query_row = query_row_ref[:, pl.ds(pl.multiple_of(first_query + tile * TILE, TILE), TILE)]
    both = dyn(tile, 2 * TILE)

    size = held.shape[1]

    @pl.loop(0, lax.div((high - low) * TILE + size - 1, size))
    def _(chunk):
        rows, start, wanted = key_rows(low, chunk, keys.shape[0], size)
        bias = chunk_bias(query_row, key_wide_ref, tile, rows, start, wanted, offset, causal)
        bias = jnp.concatenate([bias, bias], axis=1)
        for pair in range(pairs):
            lanes = slice(pair * PAIR, (pair + 1) * PAIR)
            scores = nn(keys[rows, lanes], query_cols[lanes, both]) + bias
            probs = jnp.exp(scores - lse_ref[pair : pair + 1, both])
            held[pair] = probs
            held_low[pair] = probs.astype(BF16)
        for pair in range(pairs):
            lanes = slice(pair * PAIR, (pair + 1) * PAIR)
            prob_grad = nn(values[rows, lanes], grad_cols[lanes, both])
            held_grad[pair] = (held[pair] * (prob_grad - delta_ref[pair : pair + 1, both])).astype(BF16)
        for pair in range(pairs):
            lanes = slice(pair * PAIR, (pair + 1) * PAIR)
            value_grad[rows, lanes] += nn(held_low[pair], grad_rows[both, lanes])
            key_grad[rows, lanes] += nn(held_grad[pair], query_rows[both, lanes])
            mixed = nn(keys_t[lanes, rows], held_grad[pair])
            first = slice(pair * PAIR, pair * PAIR + HEAD)
            second = slice(pair * PAIR + HEAD, (pair + 1) * PAIR)
            query_grad_t[first, dyn(tile, TILE)] += mixed[:HEAD, :TILE]
            query_grad_t[second, dyn(tile, TILE)] += mixed[HEAD:, TILE:]


def clear(ref):
    rows = ref.shape[0]
    step = min(rows, 256)

    @pl.loop(0, rows // step)
    def _(block):
        ref[dyn(block, step), :] = jnp.zeros((step, ref.shape[1]), ref.dtype)


def transpose_rows(source, target):
    @pl.loop(0, source.shape[0] // TILE)
    def _(block):
        target[:, dyn(block, TILE)] = source[dyn(block, TILE), :].T


def out_like(shape, dtype):
    return jax.ShapeDtypeStruct(shape, dtype)


def run(body, ins, smem_count, outs, scratch, flops, bytes_accessed):
    vm = pl.BlockSpec(memory_space=pltpu.VMEM)
    sm = pl.BlockSpec(memory_space=pltpu.SMEM)
    return pl.pallas_call(
        body,
        in_specs=[sm] * smem_count + [vm] * (len(ins) - smem_count),
        out_specs=[vm] * len(outs),
        out_shape=outs,
        scratch_shapes=scratch,
        cost_estimate=pl.CostEstimate(
            flops=flops, bytes_accessed=bytes_accessed, transcendentals=0
        ),
        compiler_params=pltpu.CompilerParams(vmem_limit_bytes=VMEM_LIMIT),
    )(*ins)


def self_forward(n, rows_block, place_ref, ranges_ref, *refs):
    pieces, refs = refs[:n], refs[n:]
    (
        query_segment, key_segment, weight, bias, out_weight, out_bias, gain, shift,
        cross_weight, cross_bias,
        query_out, keys, values, attended_t, lse_ref, normal_out, rstd_out, first_low, cross_query,
        wide, values_t, query_cols, peak, total, sums, held, held_low,
    ) = refs
    count = pieces[0].shape[0]
    place = place_ref[0]
    spread_segments(key_segment, wide)

    for step in range(n):
        spot = lax.rem(place + n - step, n)

        @pl.when(spot <= place)
        def _():
            @pl.loop(0, count // rows_block)
            def _(block):
                source = pieces[step][dyn(block, rows_block), :]
                rows = dyn(spot * (count // rows_block) + block, rows_block)
                keys[rows, :] = nn(source, weight[:, WIDE : 2 * WIDE]).astype(BF16)
                values[rows, :] = (nn(source, weight[:, 2 * WIDE :]) + bias[1:2, :]).astype(BF16)
                if step == 0:
                    query = (nn(source, weight[:, :WIDE]) + bias[0:1, :]).astype(BF16)
                    query_out[dyn(block, rows_block), :] = (query.astype(F32) * SCALE).astype(BF16)

        @pl.when(spot > place)
        def _():
            @pl.loop(0, count // rows_block)
            def _(block):
                rows = dyn(spot * (count // rows_block) + block, rows_block)
                keys[rows, :] = jnp.zeros((rows_block, WIDE), BF16)
                values[rows, :] = jnp.zeros((rows_block, WIDE), BF16)

    transpose_rows(values, values_t)
    tiles = count // TILE

    @pl.loop(0, tiles)
    def _(tile):
        split_columns(query_out[dyn(tile, TILE), :].T, query_cols, tile)

    attend(
        tiles, ranges_ref, query_segment, wide, place * count, True,
        query_cols, keys, values_t, attended_t, lse_ref, peak, total, sums, held, held_low,
    )

    @pl.loop(0, count // rows_block)
    def _(block):
        rows = dyn(block, rows_block)
        attended = attended_t[:, rows].T
        field = pieces[0][rows, :].astype(F32) + nn(attended, out_weight[...]) + out_bias[...]
        normal, rstd = normalize(field)
        normal_out[rows, :] = normal
        rstd_out[rows, :] = rstd
        low = (normal * gain[...] + shift[...]).astype(BF16)
        first_low[rows, :] = low
        query = (nn(low, cross_weight[...]) + cross_bias[0:1, :]).astype(BF16)
        cross_query[rows, :] = (query.astype(F32) * SCALE).astype(BF16)


def cross_and_feed(n, rows_block, place_ref, ranges_ref, *refs):
    pieces, refs = refs[:n], refs[n:]
    (
        query_segment, key_segment, cotangent, cross_query, first_normal, first_gain, first_shift,
        pair_weight, cross_bias, out_weight, out_bias, gain, shift,
        in_weight, in_bias, down_weight, down_bias, last_gain, last_shift,
        layer_output, keys, values, lse_ref, delta_ref, out_grad, grad_out, g2_out,
        in_grad, down_grad, cross_out_grad, sums_out, in_bias_grad,
        wide, values_t, query_cols, peak, total, sums, held, held_low, attended_t, second_normal, second_rstd,
        second_low, second_low_t, active, slope, third, branch, branch_t,
    ) = refs
    count = pieces[0].shape[0]
    place = place_ref[0]
    spread_segments(key_segment, wide)
    blocks = count // rows_block

    for step in range(n):
        spot = lax.rem(place + n - step, n)

        @pl.loop(0, blocks)
        def _(block):
            source = pieces[step][dyn(block, rows_block), :]
            rows = dyn(spot * blocks + block, rows_block)
            keys[rows, :] = nn(source, pair_weight[:, :WIDE]).astype(BF16)
            values[rows, :] = (nn(source, pair_weight[:, WIDE:]) + cross_bias[1:2, :]).astype(BF16)

    transpose_rows(values, values_t)
    tiles = count // TILE

    @pl.loop(0, tiles)
    def _(tile):
        split_columns(cross_query[dyn(tile, TILE), :].T, query_cols, tile)

    attend(
        tiles, ranges_ref, query_segment, wide, 0, False,
        query_cols, keys, values_t, attended_t, lse_ref, peak, total, sums, held, held_low,
    )

    @pl.loop(0, blocks)
    def _(block):
        rows = dyn(block, rows_block)
        attended = attended_t[:, rows].T
        first = first_normal[rows, :] * first_gain[...] + first_shift[...]
        field = first + nn(attended, out_weight[...]) + out_bias[...]
        normal, rstd = normalize(field)
        second_normal[rows, :] = normal
        second_rstd[rows, :] = rstd
        second = normal * gain[...] + shift[...]
        third[rows, :] = second + down_bias[...]
        low = second.astype(BF16)
        second_low[rows, :] = low
        second_low_t[:, rows] = low.T

    hidden_size = in_weight.shape[1]
    chunk_size = min(WIDE, hidden_size // n)
    chunks = hidden_size // chunk_size

    @pl.loop(0, chunks)
    def _(chunk):
        lanes = dyn(chunk, chunk_size)

        @pl.loop(0, blocks)
        def _(block):
            rows = dyn(block, rows_block)
            hidden = nn(second_low[rows, :], in_weight[:, lanes]) + in_bias[:, lanes]
            value, derivative = gate(hidden)
            value = value.astype(BF16)
            active[rows, lanes] = value
            slope[rows, lanes] = derivative.astype(slope.dtype)
            third[rows, :] += nn(value, down_weight[dyn(chunk, chunk_size), :])

    sums_out[...] = jnp.zeros(sums_out.shape, F32)
    in_bias_grad[...] = jnp.zeros(in_bias_grad.shape, F32)

    @pl.loop(0, blocks)
    def _(block):
        rows = dyn(block, rows_block)
        normal, rstd = normalize(third[rows, :])
        layer_output[rows, :] = (normal * last_gain[...] + last_shift[...]).astype(BF16)
        outer = cotangent[rows, :].astype(F32)
        grad = normalize_back(outer, last_gain[...], normal, rstd)
        third[rows, :] = grad
        low = grad.astype(BF16)
        branch[rows, :] = low
        sums_out[0:1, :] += col_sum(outer * normal)
        sums_out[1:2, :] += col_sum(outer)
        sums_out[2:3, :] += col_sum(low.astype(F32))

    half = WIDE // n
    down_half = down_weight.shape[0] // n

    @pl.loop(0, chunks)
    def _(chunk):
        lanes = dyn(chunk, chunk_size)
        share = tn(active[:, lanes], branch[...]).astype(BF16)
        per_half = down_half // chunk_size
        down_grad[lax.div(chunk, per_half), dyn(lax.rem(chunk, per_half), chunk_size), :] = share

        @pl.loop(0, blocks)
        def _(block):
            rows = dyn(block, rows_block)
            inner = nt(branch[rows, :], down_weight[dyn(chunk, chunk_size), :])
            hidden_grad = (inner * slope[rows, lanes].astype(F32)).astype(BF16)
            active[rows, lanes] = hidden_grad
            in_bias_grad[:, lanes] += col_sum(hidden_grad.astype(F32))
            third[rows, :] += nt(hidden_grad, in_weight[:, lanes])

        share = nn(second_low_t[...], active[:, lanes]).astype(BF16)
        per_block = WIDE // chunk_size
        block_rows = dyn(lax.div(chunk, per_block), half)
        block_lanes = dyn(lax.rem(chunk, per_block), chunk_size)
        for part in range(n):
            in_grad[part, block_rows, block_lanes] = share[part * half : (part + 1) * half, :]

    @pl.loop(0, blocks)
    def _(block):
        rows = dyn(block, rows_block)
        outer = third[rows, :]
        normal = second_normal[rows, :]
        grad = normalize_back(outer, gain[...], normal, second_rstd[rows, :])
        g2_out[rows, :] = grad
        low = grad.astype(BF16)
        branch[rows, :] = low
        sums_out[3:4, :] += col_sum(outer * normal)
        sums_out[4:5, :] += col_sum(outer)
        sums_out[5:6, :] += col_sum(low.astype(F32))
        grad_out[rows, :] = nt(low, out_weight[...]).astype(BF16)

    share = nn(attended_t[...], branch[...]).astype(BF16)
    for part in range(n):
        cross_out_grad[part] = share[part * half : (part + 1) * half, :]

    write_delta(tiles, grad_out, attended_t, delta_ref)


def write_delta(tiles, grad, attended_t, delta_ref):
    @pl.loop(0, tiles)
    def _(tile):
        product = grad[dyn(tile, TILE), :].astype(F32).T * attended_t[:, dyn(tile, TILE)].astype(F32)
        for pair in range(WIDE // PAIR):
            start = pair * PAIR
            delta_ref[pair : pair + 1, pl.ds(pl.multiple_of(tile * 2 * TILE, 2 * TILE), TILE)] = col_sum(
                product[start : start + HEAD, :]
            )
            delta_ref[
                pair : pair + 1, pl.ds(pl.multiple_of(tile * 2 * TILE + TILE, TILE), TILE)
            ] = col_sum(product[start + HEAD : start + PAIR, :])


def prepare_back(tiles, query, grad, query_cols, query_rows, grad_cols, grad_rows):
    @pl.loop(0, tiles)
    def _(tile):
        here = query[dyn(tile, TILE), :]
        split_columns(here.T, query_cols, tile)
        split_rows(here, query_rows, tile)
        here = grad[dyn(tile, TILE), :]
        split_columns(here.T, grad_cols, tile)
        split_rows(here, grad_rows, tile)


def query_finish(tiles, query_grad_t, query_low, sums_out, index, rounded):
    @pl.loop(0, tiles)
    def _(tile):
        rows = dyn(tile, TILE)
        wide_grad = query_grad_t[:, rows].T * SCALE
        low = wide_grad.astype(BF16)
        query_low[rows, :] = low
        sums_out[index : index + 1, :] += col_sum(low.astype(F32) if rounded else wide_grad)


def spread_parts(n, share, target, start):
    half = WIDE // n
    for part in range(n):
        target[part, start : start + half, :] = share[part * half : (part + 1) * half, :].astype(BF16)


def row_product(n, place, pieces, source):
    count = pieces[0].shape[0]
    step_rows = min(count, 512)
    share = jnp.zeros((WIDE, WIDE), F32)
    for step in range(n):
        spot = lax.rem(place + n - step, n)
        for block in range(count // step_rows):
            rows = dyn(spot * (count // step_rows) + block, step_rows)
            share += tn(
                pieces[step][block * step_rows : (block + 1) * step_rows, :], source[rows, :].astype(BF16)
            )
    return share


def pair_back(n, place, rows_block, count, step, key_grad, value_grad, weight, first, sums_out, index, write):
    blocks = count // rows_block
    spot = lax.rem(place + n - step, n)

    @pl.loop(0, blocks)
    def _(block):
        rows = dyn(spot * blocks + block, rows_block)
        key_low = key_grad[rows, :].astype(BF16)
        value_part = value_grad[rows, :]
        sums_out[index : index + 1, :] += col_sum(value_part)
        value_low = value_part.astype(BF16)
        back = nt(key_low, weight[:, first : first + WIDE]) + nt(value_low, weight[:, first + WIDE : first + 2 * WIDE])
        write(dyn(block, rows_block), back)


def first_back(
    blocks, rows_block, g2, query_low, query_weight, first_normal, first_rstd, gain, self_out_weight,
    g1, branch, self_grad, sums_out, index,
):
    @pl.loop(0, blocks)
    def _(block):
        rows = dyn(block, rows_block)
        outer = g2[rows, :] + nt(query_low[rows, :], query_weight[...])
        normal = first_normal[rows, :]
        back = normalize_back(outer, gain[...], normal, first_rstd[rows, :])
        g1[rows, :] = back
        low = back.astype(BF16)
        branch[rows, :] = low
        sums_out[index : index + 1, :] += col_sum(outer * normal)
        sums_out[index + 1 : index + 2, :] += col_sum(outer)
        sums_out[index + 2 : index + 3, :] += col_sum(low.astype(F32))
        self_grad[rows, :] = nt(low, self_out_weight[...]).astype(BF16)


def cross_backward(n, rows_block, place_ref, ranges_ref, *refs):
    pieces, refs = refs[:n], refs[n:]
    (
        query_segment, key_segment, query, grad, keys, values, lse_ref, delta_ref, g2,
        first_normal, first_rstd, first_low, gain, query_weight, pair_weight, self_out_weight,
        self_attended_t,
        own_grad, sent_grad, query_grad_w, pair_grad_w, self_out_grad, self_grad, self_delta, g1_out, sums_out,
        wide, keys_t, query_cols, query_rows, grad_cols, grad_rows, query_grad_t, key_grad, value_grad,
        held, held_low, held_grad, query_low, branch,
    ) = refs
    count = pieces[0].shape[0]
    place = place_ref[0]
    tiles = count // TILE
    blocks = count // rows_block
    half = WIDE // n
    spread_segments(key_segment, wide)
    transpose_rows(keys, keys_t)
    prepare_back(tiles, query, grad, query_cols, query_rows, grad_cols, grad_rows)
    clear(query_grad_t)
    clear(key_grad)
    clear(value_grad)

    @pl.loop(0, tiles)
    def _(tile):
        attend_back(
            tile, ranges_ref[0, tile], ranges_ref[1, tile], query_segment, 0, wide, 0, False,
            query_cols, query_rows, grad_cols, grad_rows, keys, keys_t, values, lse_ref, delta_ref,
            query_grad_t, key_grad, value_grad, held, held_low, held_grad,
        )

    sums_out[...] = jnp.zeros(sums_out.shape, F32)
    query_finish(tiles, query_grad_t, query_low, sums_out, 0, True)
    spread_parts(n, tn(first_low[...], query_low[...]), query_grad_w, 0)
    for step in range(n):

        def write(here, back):
            if step == 0:
                own_grad[here, :] = back
            else:
                sent_grad[step - 1, here, :] = back.astype(BF16)

        pair_back(n, place, rows_block, count, step, key_grad, value_grad, pair_weight, 0, sums_out, 1, write)
    spread_parts(n, row_product(n, place, pieces, key_grad), pair_grad_w, 0)
    spread_parts(n, row_product(n, place, pieces, value_grad), pair_grad_w, half)
    first_back(
        blocks, rows_block, g2, query_low, query_weight, first_normal, first_rstd, gain, self_out_weight,
        g1_out, branch, self_grad, sums_out, 2,
    )
    spread_parts(n, nn(self_attended_t[...], branch[...]), self_out_grad, 0)
    write_delta(tiles, self_grad, self_attended_t, self_delta)


def self_backward(n, rows_block, place_ref, ranges_ref, *refs):
    pieces, refs = refs[:n], refs[n:]
    (
        query_segment, key_segment, query, grad, keys, values, lse_ref, delta_ref, g1, weight,
        own_grad, sent_grad, grad_w, sums_out,
        wide, keys_t, query_cols, query_rows, grad_cols, grad_rows, query_grad_t, key_grad, value_grad,
        held, held_low, held_grad, query_low,
    ) = refs
    count = pieces[0].shape[0]
    place = place_ref[0]
    tiles = count // TILE
    half = WIDE // n
    spread_segments(key_segment, wide)
    transpose_rows(keys, keys_t)
    prepare_back(tiles, query, grad, query_cols, query_rows, grad_cols, grad_rows)
    clear(query_grad_t)
    clear(key_grad)
    clear(value_grad)

    @pl.loop(0, tiles)
    def _(tile):
        attend_back(
            tile, ranges_ref[0, tile], ranges_ref[1, tile], query_segment, 0, wide, place * count, True,
            query_cols, query_rows, grad_cols, grad_rows, keys, keys_t, values, lse_ref, delta_ref,
            query_grad_t, key_grad, value_grad, held, held_low, held_grad,
        )

    sums_out[...] = jnp.zeros(sums_out.shape, F32)
    query_finish(tiles, query_grad_t, query_low, sums_out, 0, False)
    for step in range(n):

        def write(here, back):
            if step == 0:
                own_grad[here, :] = back + g1[here, :] + nt(query_low[here, :], weight[:, :WIDE])
            else:
                sent_grad[step - 1, here, :] = back.astype(BF16)

        pair_back(n, place, rows_block, count, step, key_grad, value_grad, weight, WIDE, sums_out, 1, write)
    spread_parts(n, tn(pieces[0][...], query_low[...]), grad_w, 0)
    spread_parts(n, row_product(n, place, pieces, key_grad), grad_w, half)
    spread_parts(n, row_product(n, place, pieces, value_grad), grad_w, 2 * half)


CORE_RATE = 0.0018
LINK_RATE = 0.0225
LATENCY = {"core": 1.0, "x": 2.2, "y": 2.2, "z": 2.6}
MARGIN = 0.5


def plan_steps(n, chunks, extras, smalls, segments):
    free = {"core": 0.0, "x": 0.0, "y": 0.0, "z": 0.0}
    now = 0.0
    pending = []
    plan = []
    crossed = set()

    def send(link, rows, rate=LINK_RATE):
        free[link] = max(free[link], now) + rows * rate
        return free[link] + LATENCY[link]

    def execute(kind, index, step):
        nonlocal now
        now += 0.15
        if kind == "chunk":
            unused, rows, y_first, unused = chunks[index]
            if step == 0:
                ready = send("core", n * rows // 2, CORE_RATE)
            elif step in (1, 2) and (step == 1) == y_first:
                ready = send("y", (n if y_first else 1) * rows // 4)
            elif step in (1, 2):
                crossed.add(index)
                ready = send("x", (n - 1) * rows // (4 if y_first else 2))
            elif step in (3, 4):
                ready = send("z", rows // 4)
            elif step == 5:
                ready = send("y", rows // 4)
            elif step == 6:
                ready = send("core", rows // 2, CORE_RATE)
            else:
                return
        elif kind == "extra":
            if step == 2:
                return
            rows = extras[index][0]
            ready = send("core", rows, CORE_RATE) if step == 0 else send("x", rows // 2)
        else:
            if step == 4:
                return
            rows = smalls[index][0]
            link, rows = (("core", n * rows), ("x", rows), ("y", rows), ("z", 4 * rows))[step]
            ready = send(link, rows, CORE_RATE if link == "core" else LINK_RATE)
        pending.append((ready, len(pending), kind, index, step + 1))

    for number in range(len(segments) + 1):
        order = []
        last = number == len(segments)
        if not last:
            now += segments[number]
            released = [("chunk", i) for i, chunk in enumerate(chunks) if chunk[3] == number]
            released += [("extra", i) for i, extra in enumerate(extras) if extra[1] == number]
            released += [("small", i) for i, small in enumerate(smalls) if small[1] == number]
            for kind, index in released:
                execute(kind, index, 0)
                order.append((kind, index, 0))
        while pending:
            pending.sort()
            first = 0
            if len(crossed) < len(chunks):
                while first < len(pending) and pending[first][2:] == ("extra", pending[first][3], 1):
                    first += 1
            if first == len(pending) or (not last and pending[first][0] + MARGIN > now):
                break
            ready, unused, kind, index, step = pending.pop(first)
            now = max(now, ready)
            execute(kind, index, step)
            order.append((kind, index, step))
        plan.append(order)
    return plan, now


class Reducer:
    def __init__(self, n, groups, chunks, field, total, total_out, small, small_out, small_spans, buffers):
        (
            self.from_core, self.from_blk, self.from_y, self.from_z,
            self.small_core, self.small_blk, self.small_y, self.small_z,
            self.sends, self.receives, self.small_sends, self.small_receives, self.stores,
        ) = buffers
        self.n, self.chunks, self.field, self.total, self.total_out = n, chunks, field, total, total_out
        self.small, self.small_out, self.small_spans = small, small_out, small_spans
        self.depth = depth = groups // 4
        self.group = group = lax.axis_index("dp")
        self.part = part = lax.axis_index("blk")
        self.core = lax.rem(group, 2)
        self.side = lax.rem(lax.div(group, 2), 2)
        self.level = lax.div(group, 4)
        self.core_peer = (group + 1 - 2 * self.core, part)
        self.side_peer = (group + 2 - 4 * self.side, part)
        self.blk_peers = [(group, lax.rem(part + step, n)) for step in range(1, n)]
        self.z_peers = [(lax.rem(group + 4 * step, groups), part) for step in range(1, depth)]
        self.per_chunk = 4 + (n - 1) + 2 * (depth - 1)

    def greet(self, far_peer=None, has_far=None):
        peers = [self.core_peer, self.side_peer] + self.blk_peers + self.z_peers
        barrier = pltpu.get_barrier_semaphore()
        for peer in peers:
            pl.semaphore_signal(barrier, inc=1, device_id=peer, device_id_type=pl.DeviceIdType.MESH)
        if far_peer is not None:

            @pl.when(has_far)
            def _():
                pl.semaphore_signal(barrier, inc=1, device_id=far_peer, device_id_type=pl.DeviceIdType.MESH)

            self.greetings = jnp.where(has_far, len(peers) + 1, len(peers))
        else:
            self.greetings = len(peers)

    def enter(self):
        pl.semaphore_wait(pltpu.get_barrier_semaphore(), self.greetings)

    def copy(self, source, target, sem, peer):
        return pltpu.make_async_remote_copy(
            src_ref=source, dst_ref=target, send_sem=self.sends.at[sem], recv_sem=self.receives.at[sem],
            device_id=peer, device_id_type=pl.DeviceIdType.MESH,
        )

    def small_copy(self, source, target, sem, peer):
        return pltpu.make_async_remote_copy(
            src_ref=source, dst_ref=target, send_sem=self.small_sends.at[sem],
            recv_sem=self.small_receives.at[sem], device_id=peer, device_id_type=pl.DeviceIdType.MESH,
        )

    def span(self, start, size):
        return pl.ds(pl.multiple_of(start, 16), size)

    def copies(self, index, step):
        start, rows, y_first, unused = self.chunks[index]
        n, depth, part = self.n, self.depth, self.part
        half, quarter = rows // 2, rows // 4
        piece = quarter // depth
        own_half = start + self.core * half
        own_quarter = own_half + self.side * quarter
        sem = index * self.per_chunk
        if step == 0:
            theirs = self.span(start + (1 - self.core) * half, half)
            return [
                self.copy(
                    self.field.at[:, theirs], self.from_core.at[:, pl.ds(start // 2, half)], sem, self.core_peer
                )
            ]
        if step in (1, 2) and (step == 1) == y_first:
            theirs = self.span(own_half + (1 - self.side) * quarter, quarter)
            into = pl.ds(start // 4, quarter)
            if y_first:
                return [self.copy(self.field.at[:, theirs], self.from_y.at[:, into], sem + 1, self.side_peer)]
            return [self.copy(self.field.at[part, theirs], self.from_y.at[0, into], sem + 1, self.side_peer)]
        if step in (1, 2):
            if y_first:
                mine, into = self.span(own_quarter, quarter), pl.ds(start // 2, quarter)
            else:
                mine, into = self.span(own_half, half), pl.ds(start // 2, half)
            return [
                self.copy(
                    self.field.at[lax.rem(part + hop, n), mine], self.from_blk.at[hop - 1, into],
                    sem + 3 + hop, self.blk_peers[hop - 1],
                )
                for hop in range(1, n)
            ]
        if step == 3:
            copies = []
            for hop in range(1, depth):
                theirs = self.span(own_quarter + lax.rem(self.level + hop, depth) * piece, piece)
                copies.append(
                    self.copy(
                        self.field.at[part, theirs], self.from_z.at[hop - 1, pl.ds(start // 4 // depth, piece)],
                        sem + 2 + n + hop, self.z_peers[hop - 1],
                    )
                )
            return copies
        if step == 4:
            mine = self.span(own_quarter + self.level * piece, piece)
            return [
                self.copy(
                    self.total.at[mine], self.total.at[mine], sem + 1 + n + depth + hop, self.z_peers[hop - 1]
                )
                for hop in range(1, depth)
            ]
        if step == 5:
            mine = self.span(own_quarter, quarter)
            return [self.copy(self.total.at[mine], self.total.at[mine], sem + 2, self.side_peer)]
        mine = self.span(own_half, half)
        return [self.copy(self.total.at[mine], self.total.at[mine], sem + 3, self.core_peer)]

    def add(self, part, start, size, terms, result=None):
        step = min(size, 64)

        @pl.loop(0, size // step)
        def _(block):
            here = self.span(start + block * step, step)
            value = self.field[part, here, :].astype(F32)
            for ref, index, begin in terms:
                value = value + ref[index, self.span(begin + block * step, step), :].astype(F32)
            if result is None:
                self.field[part, here, :] = value.astype(BF16)
            else:
                result[here, :] = value.astype(BF16)

    def store(self, index):
        rows = pl.ds(self.chunks[index][0], self.chunks[index][1])
        return pltpu.make_async_copy(self.total.at[rows], self.total_out.at[rows], self.stores.at[index])

    def chunk_step(self, index, step):
        start, rows, y_first, unused = self.chunks[index]
        n, depth, part = self.n, self.depth, self.part
        half, quarter = rows // 2, rows // 4
        piece = quarter // depth
        own_half = start + self.core * half
        own_quarter = own_half + self.side * quarter
        if step > 0:
            for copy in self.copies(index, step - 1):
                copy.wait()
        if step == 1:
            for b in range(n):
                self.add(b, own_half, half, [(self.from_core, b, start // 2)])
        elif step in (2, 3) and (step == 2) == y_first:
            for b in range(n) if y_first else [part]:
                self.add(b, own_quarter, quarter, [(self.from_y, b if y_first else 0, start // 4)])
        elif step in (2, 3):
            begin, size = (own_quarter, quarter) if y_first else (own_half, half)
            self.add(part, begin, size, [(self.from_blk, hop, start // 2) for hop in range(n - 1)])
        elif step == 4:
            self.add(
                part, own_quarter + self.level * piece, piece,
                [(self.from_z, hop, start // 4 // depth) for hop in range(depth - 1)], self.total,
            )
        if step < 7:
            for copy in self.copies(index, step):
                copy.start()
        else:
            self.store(index).start()

    def small_copies(self, index, step):
        part, n = self.part, self.n
        rows = pl.ds(*self.small_spans[index])
        first = index * (n + self.depth)
        if step == 0:
            return [self.small_copy(self.small.at[0, :, rows], self.small_core.at[:, rows], first, self.core_peer)]
        if step == 1:
            return [
                self.small_copy(
                    self.small.at[1, lax.rem(part + hop, n), rows], self.small_blk.at[hop - 1, rows], first + hop,
                    self.blk_peers[hop - 1],
                )
                for hop in range(1, n)
            ]
        if step == 2:
            return [
                self.small_copy(self.small.at[1, part, rows], self.small_y.at[rows], first + n, self.side_peer)
            ]
        return [
            self.small_copy(
                self.small_y.at[rows], self.small_z.at[hop - 1, rows], first + n + hop, self.z_peers[hop - 1]
            )
            for hop in range(1, self.depth)
        ]

    def small_step(self, index, step):
        part = self.part
        rows = pl.ds(*self.small_spans[index])
        if step > 0:
            for copy in self.small_copies(index, step - 1):
                copy.wait()
        if step == 1:
            self.small[1, :, rows] = self.small[0, :, rows] + self.small_core[:, rows]
        elif step == 2:
            held = self.small[1, part, rows]
            for hop in range(self.n - 1):
                held = held + self.small_blk[hop, rows]
            self.small[1, part, rows] = held
        elif step == 3:
            self.small_y[rows] = self.small_y[rows] + self.small[1, part, rows]
        elif step == 4:
            held = self.small_y[rows]
            for hop in range(self.depth - 1):
                held = held + self.small_z[hop, rows]
            self.small_out[rows] = held
        if step < 4:
            for copy in self.small_copies(index, step):
                copy.start()

    def finish(self):
        for index in range(len(self.chunks)):
            self.store(index).wait()


def reducer_scratch(n, groups, chunks, rows, small_shape):
    depth = groups // 4
    per_chunk = 4 + (n - 1) + 2 * (depth - 1)
    return [
        pltpu.VMEM((n, rows // 2, WIDE), BF16),
        pltpu.VMEM((n - 1, rows // 2, WIDE), BF16),
        pltpu.VMEM((n, rows // 4, WIDE), BF16),
        pltpu.VMEM((depth - 1, rows // 4 // depth, WIDE), BF16),
        pltpu.VMEM((n, *small_shape), F32),
        pltpu.VMEM((n - 1, *small_shape), F32),
        pltpu.VMEM(small_shape, F32),
        pltpu.VMEM((depth - 1, *small_shape), F32),
        pltpu.SemaphoreType.DMA((len(chunks) * per_chunk,)),
        pltpu.SemaphoreType.DMA((len(chunks) * per_chunk,)),
        pltpu.SemaphoreType.DMA((2 * (n + depth),)),
        pltpu.SemaphoreType.DMA((2 * (n + depth),)),
        pltpu.SemaphoreType.DMA((len(chunks),)),
    ]


def reduce_kernel(n, groups, chunks, plan, part_rows, *refs):
    sources, refs = refs[: len(part_rows)], refs[len(part_rows) :]
    small_in, total_out, small_out, field, total, small, load_sem = refs[:7]
    loads = []
    start = 0
    for index, source in enumerate(sources):
        loads.append(
            pltpu.make_async_copy(source, field.at[:, pl.ds(start, part_rows[index])], load_sem.at[index])
        )
        loads[-1].start()
        start += part_rows[index]
    spans = [(0, small_in.shape[1])]
    reducer = Reducer(n, groups, chunks, field, total, total_out, small, small_out, spans, refs[7:])
    small[0] = small_in[...]
    reducer.greet()
    reducer.enter()
    for load in loads:
        load.wait()
    for order in plan:
        for kind, index, step in order:
            if kind == "chunk":
                reducer.chunk_step(index, step)
            else:
                reducer.small_step(index, step)
    reducer.finish()


def reduce_all(n, groups, parts, small):
    part_rows = [part.shape[1] for part in parts]
    rows = sum(part_rows)
    chunk_rows = max(16 * groups, rows // 8)
    chunks = [(start, chunk_rows, False, 0) for start in range(0, rows, chunk_rows)]
    plan, unused = plan_steps(n, chunks, [], [(small.shape[1], 0)], [0.0])
    small_shape = small.shape[1:]
    vm = pl.BlockSpec(memory_space=pltpu.VMEM)
    hbm = pl.BlockSpec(memory_space=pl.ANY)
    return pl.pallas_call(
        functools.partial(reduce_kernel, n, groups, chunks, plan, part_rows),
        in_specs=[hbm] * len(parts) + [vm],
        out_specs=[hbm, vm],
        out_shape=[out_like((rows, WIDE), BF16), out_like(small_shape, F32)],
        scratch_shapes=[
            pltpu.VMEM((n, rows, WIDE), BF16),
            pltpu.VMEM((rows, WIDE), BF16),
            pltpu.VMEM((2, n, *small_shape), F32),
            pltpu.SemaphoreType.DMA((len(parts),)),
            *reducer_scratch(n, groups, chunks, rows, small_shape),
        ],
        compiler_params=pltpu.CompilerParams(
            vmem_limit_bytes=VMEM_LIMIT, collective_id=0, has_side_effects=True
        ),
    )(*parts, small)


Y_FIRST = [letter == "y" for letter in "xyyyyxxyyyyyyxyx"]
BACK_SEGMENTS = [
    1.6, 1.6, 2.9, 2.9, 2.9, 2.9, 1.4, 2.8, 3.2, 2.3, 2.4, 2.4, 2.9, 2.9, 1.4, 1.1, 1.1,
]


def back_chunks(half, hidden_rows):
    released = [(half, 0)] * (2 * hidden_rows // half + 1)
    released += [(half, segment) for segment in (6, 7, 7, 8, 14, 15, 16)]
    chunks = []
    start = 0
    for index, (rows, segment) in enumerate(released):
        chunks.append((start, rows, Y_FIRST[index % len(Y_FIRST)], segment))
        start += rows
    return chunks


def back_kernel(n, groups, rows_block, chunks, plan, load_plan, *refs):
    feed_refs, refs = refs[:3], refs[3:]
    streamed, refs = refs[: len(load_plan)], refs[len(load_plan) :]
    (
        target_row, memory_row, cross_query, cross_grad, cross_keys,
        cross_lse, cross_delta, feed_sums, in_bias_grad, gain, first_rstd, self_lse,
        total_out, small_out, memory_out, input_out,
        field, total, small, sums, memory_grad, input_grad, memory_sent, memory_got, input_sent, input_got, pair_low,
        wide, keys_t, query_cols, query_rows, grad_cols, grad_rows, query_grad_t, key_grad, value_grad,
        held, held_low, held_grad, query_low, branch, self_grad, self_delta, g1,
        feed_sem, load_sem, extra_send, extra_recv, extra_store,
    ) = refs[:49]
    refs = refs[49:]
    held_loads, buffers = refs[: len(load_plan)], refs[len(load_plan) :]
    count = cross_query.shape[0]
    length = cross_keys.shape[0]
    tiles = count // TILE
    blocks = count // rows_block
    half = WIDE // n
    group, part = lax.axis_index("dp"), lax.axis_index("blk")
    place = lax.rem(group, 2)
    away = place != part
    owner = (group - place + part, place)

    feed_loads = []
    start = 0
    for index, source in enumerate(feed_refs):
        rows = source.shape[1]
        feed_loads.append(
            pltpu.make_async_copy(source, field.at[:, pl.ds(start, rows)], feed_sem.at[index])
        )
        feed_loads[-1].start()
        start += rows
    loads = [
        pltpu.make_async_copy(source, target, load_sem.at[index])
        for index, (source, target) in enumerate(zip(streamed, held_loads))
    ]
    for load in loads:
        load.start()
    cross_values = held_loads[0]
    memory_pieces = [held_loads[1].at[step] for step in range(n)]
    held_loads = held_loads[2:]
    (
        pair_weight, first_low, query_weight, g2, first_normal, self_out_weight, self_attended_t,
        self_keys, self_values, self_query,
    ) = held_loads[:10]
    input_pieces = [held_loads[10].at[step] for step in range(n)]
    self_in_weight = held_loads[11]

    spans = [(0, 8), (8, small_out.shape[0] - 8)]
    reducer = Reducer(n, groups, chunks, field, total, total_out, small, small_out, spans, buffers)
    reducer.greet(owner, away)

    extras = (
        (memory_sent, memory_got, memory_grad, memory_out), (input_sent, input_got, input_grad, input_out)
    )

    def extra_copy(index, hop):
        sent, got, *unused = extras[index]
        return pltpu.make_async_remote_copy(
            src_ref=sent.at[hop], dst_ref=got.at[hop],
            send_sem=extra_send.at[2 * index + hop], recv_sem=extra_recv.at[2 * index + hop],
            device_id=reducer.core_peer if hop == 0 else owner, device_id_type=pl.DeviceIdType.MESH,
        )

    def extra_store_copy(index, from_owner):
        sent, got, unused, out = extras[index]
        return pltpu.make_async_copy((got if from_owner else sent).at[1], out, extra_store.at[index])

    def extra_step(index, step):
        sent, got, result, unused = extras[index]
        if step == 0:
            extra_copy(index, 0).start()
        elif step == 1:
            extra_copy(index, 0).wait()

            @pl.loop(0, blocks)
            def _(block):
                rows = dyn(block, rows_block)
                value = result[rows, :] + got[0, rows, :].astype(F32)
                sent[1, rows, :] = value.astype(BF16)

            @pl.when(away)
            def _():
                extra_copy(index, 1).start()

            @pl.when(jnp.logical_not(away))
            def _():
                extra_store_copy(index, False).start()
        else:

            @pl.when(away)
            def _():
                extra_copy(index, 1).wait()
                extra_store_copy(index, True).start()

    def run_steps(number):
        for kind, index, step in plan[number]:
            if kind == "chunk":
                reducer.chunk_step(index, step)
            elif kind == "small":
                reducer.small_step(index, step)
            else:
                extra_step(index, step)

    def wait_loads(first, last):
        for load in loads[first:last]:
            load.wait()

    spread_row(memory_row, wide)
    transpose_rows(cross_keys, keys_t)
    for load in feed_loads:
        load.wait()
    reducer.enter()
    run_steps(0)
    prepare_back(tiles, cross_query, cross_grad, query_cols, query_rows, grad_cols, grad_rows)
    clear(query_grad_t)
    clear(key_grad)
    clear(value_grad)
    sums[...] = jnp.zeros(sums.shape, F32)
    run_steps(1)
    wait_loads(0, 1)
    for tile in range(tiles):
        attend_back(
            tile, 0, length // TILE, target_row, place * count, wide, place * count, False,
            query_cols, query_rows, grad_cols, grad_rows, cross_keys, keys_t, cross_values,
            cross_lse, cross_delta, query_grad_t, key_grad, value_grad, held, held_low, held_grad,
        )
        run_steps(2 + tile)
    base = 2 * in_bias_grad.shape[1] // n + half
    wait_loads(1, 9)
    query_finish(tiles, query_grad_t, query_low, sums, 2, True)
    spread_parts(n, tn(first_low[...], query_low[...]), field, base)
    run_steps(6)
    for side, source in ((0, key_grad), (1, value_grad)):

        @pl.loop(0, length // rows_block)
        def _(block):
            rows = dyn(block, rows_block)
            value = source[rows, :]
            pair_low[side, rows, :] = value.astype(BF16)
            if side == 1:
                sums[3:4, :] += col_sum(value)

        spread_parts(
            n, row_product(n, place, memory_pieces, pair_low.at[side]), field, base + half + side * half
        )
    run_steps(7)
    first_back(
        blocks, rows_block, g2, query_low, query_weight, first_normal, first_rstd, gain, self_out_weight,
        g1, branch, self_grad, sums, 4,
    )
    spread_parts(n, nn(self_attended_t[...], branch[...]), field, base + 3 * half)
    write_delta(tiles, self_grad, self_attended_t, self_delta)
    small[...] = jnp.zeros(small.shape, F32)
    wide_half = in_bias_grad.shape[1] // n
    for b in range(n):
        here = slice(b * half, (b + 1) * half)
        small[0, b, 8:13, :] = sums[2:7, here]
        small[0, b, 13:19, :] = feed_sums[0:6, here]
        for row in range(wide_half // half):
            begin = b * wide_half + row * half
            small[0, b, 19 + row : 20 + row, :] = in_bias_grad[:, begin : begin + half]
    run_steps(8)

    wait_loads(9, len(loads))
    spread_row(target_row, wide)
    transpose_rows(self_keys, keys_t)
    prepare_back(tiles, self_query, self_grad, query_cols, query_rows, grad_cols, grad_rows)
    clear(query_grad_t)
    clear(key_grad)
    clear(value_grad)
    run_steps(9)
    for tile in range(tiles):
        attend_back(
            tile, 0, place * tiles + tile + 1, target_row, place * count, wide, place * count, True,
            query_cols, query_rows, grad_cols, grad_rows, self_keys, keys_t, self_values,
            self_lse, self_delta, query_grad_t, key_grad, value_grad, held, held_low, held_grad,
        )
        run_steps(10 + tile)
    query_finish(tiles, query_grad_t, query_low, sums, 0, False)
    spread_parts(n, tn(input_pieces[0][...], query_low[...]), field, base + 4 * half)
    run_steps(14)
    spread_parts(n, row_product(n, place, input_pieces, key_grad), field, base + 5 * half)
    run_steps(15)
    spread_parts(n, row_product(n, place, input_pieces, value_grad), field, base + 6 * half)
    run_steps(16)
    number = 17
    for step in range(n):
        spot = lax.rem(place + n - step, n)
        for block in range(blocks):
            rows = dyn(spot * blocks + block, rows_block)
            here = slice(block * rows_block, (block + 1) * rows_block)
            key_low, value_part = key_grad[rows, :].astype(BF16), value_grad[rows, :]
            sums[1:2, :] += col_sum(value_part)
            back = nt(key_low, self_in_weight[:, WIDE : 2 * WIDE])
            back += nt(value_part.astype(BF16), self_in_weight[:, 2 * WIDE :])
            if step == 0:
                input_grad[here, :] = back + g1[here, :] + nt(query_low[here, :], self_in_weight[:, :WIDE])
            else:
                input_sent[0, here, :] = back.astype(BF16)
            if step == n - 1 and block == blocks - 1:
                for b in range(n):
                    small[0, b, 0:2, :] = sums[0:2, b * half : (b + 1) * half]
            run_steps(number)
            number += 1
    for step in range(n):
        spot = lax.rem(place + n - step, n)
        for block in range(blocks):
            rows = dyn(spot * blocks + block, rows_block)
            here = slice(block * rows_block, (block + 1) * rows_block)
            back = nt(pair_low[0, rows, :], pair_weight[:, :WIDE]) + nt(pair_low[1, rows, :], pair_weight[:, WIDE:])
            if step == 0:
                memory_grad[here, :] = back
            else:
                memory_sent[0, here, :] = back.astype(BF16)
            run_steps(number)
            number += 1
    run_steps(number)
    for index in range(2):

        @pl.when(away)
        def _():
            extra_store_copy(index, True).wait()

        @pl.when(jnp.logical_not(away))
        def _():
            extra_store_copy(index, False).wait()

    reducer.finish()


def back_and_reduce(n, groups, rows_block, feed_grads, streamed, resident):
    count, features = resident[2].shape
    length = n * count
    hidden_rows = feed_grads[0].shape[1]
    half = features // n
    rows = sum(part.shape[1] for part in feed_grads) + 7 * half
    chunks = back_chunks(half, hidden_rows)
    steps = n * (count // rows_block)
    segments = BACK_SEGMENTS + [2.2 / steps] * steps + [2.0 / steps] * steps
    last = len(segments) - 1
    extras = [(count, last), (count, last - steps)]
    smalls = [(8, last - steps), (16, 8)]
    plan, unused = plan_steps(n, chunks, extras, smalls, segments)
    small_shape = (-(-(19 + hidden_rows // half) // 8) * 8, half)
    vm = pl.BlockSpec(memory_space=pltpu.VMEM)
    hbm = pl.BlockSpec(memory_space=pl.ANY)
    low_rows = pltpu.VMEM((count, features), BF16)
    wide_rows = pltpu.VMEM((count, features), F32)
    columns = pltpu.VMEM((features, 2 * count), BF16)
    doubled = pltpu.VMEM((2 * count, features), BF16)
    all_wide = pltpu.VMEM((length, features), F32)
    sent = pltpu.VMEM((2, count, features), BF16)
    held = (features // PAIR, BACK_KEYS, 2 * TILE)
    return pl.pallas_call(
        functools.partial(back_kernel, n, groups, rows_block, chunks, plan, [part.shape for part in streamed]),
        in_specs=[hbm] * (len(feed_grads) + len(streamed)) + [vm] * len(resident),
        out_specs=[hbm, vm, hbm, hbm],
        out_shape=[
            out_like((rows, WIDE), BF16), out_like(small_shape, F32),
            out_like((count, features), BF16), out_like((count, features), BF16),
        ],
        scratch_shapes=[
            pltpu.VMEM((n, rows, WIDE), BF16), pltpu.VMEM((rows, WIDE), BF16),
            pltpu.VMEM((2, n, *small_shape), F32), pltpu.VMEM((8, features), F32),
            wide_rows, wide_rows, sent, sent, sent, sent, pltpu.VMEM((2, length, features), BF16),
            pltpu.VMEM((length, TILE), jnp.int32), pltpu.VMEM((features, length), BF16),
            columns, doubled, columns, doubled,
            pltpu.VMEM((features, count), F32), all_wide, all_wide,
            pltpu.VMEM(held, F32), pltpu.VMEM(held, BF16), pltpu.VMEM(held, BF16),
            low_rows, low_rows, low_rows, pltpu.VMEM((features // PAIR, 2 * count), F32), wide_rows,
            pltpu.SemaphoreType.DMA((len(feed_grads),)), pltpu.SemaphoreType.DMA((len(streamed),)),
            pltpu.SemaphoreType.DMA((4,)), pltpu.SemaphoreType.DMA((4,)), pltpu.SemaphoreType.DMA((2,)),
            *[pltpu.VMEM(part.shape, part.dtype) for part in streamed],
            *reducer_scratch(n, groups, chunks, rows, small_shape),
        ],
        compiler_params=pltpu.CompilerParams(
            vmem_limit_bytes=VMEM_LIMIT, collective_id=0, has_side_effects=True
        ),
    )(*feed_grads, *streamed, *resident)


def spread_row(row_ref, wide_ref):
    @pl.loop(0, row_ref.shape[1] // TILE)
    def _(block):
        wide_ref[dyn(block, TILE), :] = jnp.broadcast_to(row_ref[:, dyn(block, TILE)], (TILE, TILE)).T


def attend_whole(
    tiles, query_row_ref, first_query, key_wide_ref, causal, query_cols, keys, values_t, attended_t, lse_ref,
    held, held_low,
):
    pairs = WIDE // PAIR
    length = keys.shape[0]

    @pl.loop(0, tiles)
    def _(tile):
        begin = pl.multiple_of(first_query + tile * TILE, TILE)
        allowed = key_wide_ref[...] == query_row_ref[:, pl.ds(begin, TILE)]
        if causal:
            key_position = lax.broadcasted_iota(jnp.int32, (length, TILE), 0)
            query_position = begin + lax.broadcasted_iota(jnp.int32, (length, TILE), 1)
            allowed = allowed & (key_position <= query_position)
        bias = jnp.where(allowed, 0.0, MASKED)
        bias = jnp.concatenate([bias, bias], axis=1)
        both = dyn(tile, 2 * TILE)
        peaks, shares = [], []
        for pair in range(pairs):
            lanes = slice(pair * PAIR, (pair + 1) * PAIR)
            scores = nn(keys[:, lanes], query_cols[lanes, both]) + bias
            held[pair] = scores
            peaks.append(jnp.max(scores, axis=0, keepdims=True))
        for pair in range(pairs):
            weights = jnp.exp(held[pair] - peaks[pair])
            total = col_sum(weights)
            held_low[pair] = weights.astype(BF16)
            lse_ref[pair : pair + 1, both] = peaks[pair] + jnp.log(total)
            shares.append(1.0 / total)
        for pair in range(pairs):
            share = shares[pair]
            mixed = nn(values_t[pair * PAIR : (pair + 1) * PAIR, :], held_low[pair])
            first = slice(pair * PAIR, pair * PAIR + HEAD)
            second = slice(pair * PAIR + HEAD, (pair + 1) * PAIR)
            attended_t[first, dyn(tile, TILE)] = (mixed[:HEAD, :TILE] * share[:, :TILE]).astype(BF16)
            attended_t[second, dyn(tile, TILE)] = (mixed[HEAD:, TILE:] * share[:, TILE:]).astype(BF16)


FORWARD_LOADS = 7
FORWARD_STORES = 16


def forward_kernel(n, groups, rows_block, *refs):
    (
        inputs, memory, cotangent, *weights_in
    ) = refs[: 3 + FORWARD_LOADS]
    refs = refs[3 + FORWARD_LOADS :]
    (
        target_here, memory_here, in_bias, self_out_bias, first_gain, first_shift, cross_bias, cross_out_bias,
        second_gain, second_shift, feed_bias, down_bias, last_gain, last_shift,
    ) = refs[:14]
    refs = refs[14:]
    stores_out, refs = refs[:FORWARD_STORES], refs[FORWARD_STORES:]
    (
        layer_output, lse_one, lse_two, delta_ref, first_rstd, sums_out, in_bias_grad, target_row, memory_row,
    ) = refs[:9]
    refs = refs[9:]
    held_weights, refs = refs[:FORWARD_LOADS], refs[FORWARD_LOADS:]
    held_stores, refs = refs[:FORWARD_STORES], refs[FORWARD_STORES:]
    (
        self_in_weight, self_out_weight, cross_weight, pair_weight, cross_out_weight, in_weight, down_weight
    ) = held_weights
    (
        input_pieces, memory_pieces, query_low, keys, values, attended_one, first_normal, first_low, cross_query,
        cross_keys, cross_values, grad_out, g2_out, in_grad, down_grad, cross_out_grad,
    ) = held_stores
    (
        cot, output_low, output_got, target_there, memory_there, wide, values_t, query_cols, held, held_low,
        attended_two, second_normal, second_rstd, second_low, second_low_t, active, slope, third, branch,
        load_sem, store_sem, own_sem, far_send, far_recv, core_send, core_recv,
    ) = refs
    count = inputs.shape[0]
    tiles = count // TILE
    blocks = count // rows_block
    half = WIDE // n
    group, part = lax.axis_index("dp"), lax.axis_index("blk")
    place = lax.rem(group, 2)
    away = place != part
    owner = (group - place + part, place)
    core_peer = (group + 1 - 2 * place, part)
    mesh_type = pl.DeviceIdType.MESH

    loads = [
        pltpu.make_async_copy(source, target, load_sem.at[index])
        for index, (source, target) in enumerate(zip(weights_in, held_weights))
    ]
    for load in loads:
        load.start()
    barrier = pltpu.get_barrier_semaphore()
    pl.semaphore_signal(barrier, inc=1, device_id=core_peer, device_id_type=mesh_type)

    @pl.when(away)
    def _():
        pl.semaphore_signal(barrier, inc=1, device_id=owner, device_id_type=mesh_type)

    pl.semaphore_wait(barrier, jnp.where(away, 2, 1))

    pieces_of = (count // 2, count // 2)
    arrivals = []
    for index, (source, target) in enumerate(((inputs, input_pieces), (memory, memory_pieces))):
        for block in range(2):
            rows = pl.ds(block * (count // 2), count // 2)
            arrivals.append((source.at[rows], target.at[0, rows], 2 * index + block))
    arrivals.append((cotangent, cot, 4))

    def far_copy(entry):
        source, target, sem = entry
        return pltpu.make_async_remote_copy(
            src_ref=source, dst_ref=target, send_sem=far_send.at[sem], recv_sem=far_recv.at[sem],
            device_id=owner, device_id_type=mesh_type,
        )

    def own_copy(entry):
        source, target, sem = entry
        return pltpu.make_async_copy(source, target, own_sem.at[sem])

    def core_copy(source, target, sem):
        return pltpu.make_async_remote_copy(
            src_ref=source, dst_ref=target, send_sem=core_send.at[sem], recv_sem=core_recv.at[sem],
            device_id=core_peer, device_id_type=mesh_type,
        )

    @pl.when(away)
    def _():
        for entry in arrivals:
            far_copy(entry).start()

    @pl.when(jnp.logical_not(away))
    def _():
        for entry in arrivals:
            own_copy(entry).start()

    def arrive(entry):
        @pl.when(away)
        def _():
            far_copy(entry).wait()

        @pl.when(jnp.logical_not(away))
        def _():
            own_copy(entry).wait()

    def forward_copy(index):
        held_piece = (input_pieces, memory_pieces)[index // 2]
        rows = pl.ds((index % 2) * (count // 2), count // 2)
        return core_copy(held_piece.at[0, rows], held_piece.at[1, rows], index)

    segment_copies = [
        core_copy(target_here, target_there, 4), core_copy(memory_here, memory_there, 5)
    ]
    for copy in segment_copies:
        copy.start()

    stores = {}

    def store(index):
        stores[index] = pltpu.make_async_copy(held_stores[index], stores_out[index], store_sem.at[index])
        stores[index].start()

    for copy in segment_copies:
        copy.wait()
    target_row[...] = jnp.where(away, target_there[...], target_here[...])
    memory_row[...] = jnp.where(away, memory_there[...], memory_here[...])
    spread_row(target_row, wide)
    loads[0].wait()

    def project(piece, block, spot):
        rows = slice(block * (count // 2), (block + 1) * (count // 2))
        first = 0 if piece == 0 else WIDE
        field = nn(input_pieces[piece, rows, :], self_in_weight[:, first:])
        here = dyn(spot * 2 + block, count // 2)
        keys[here, :] = field[:, WIDE - first : 2 * WIDE - first].astype(BF16)
        value = (field[:, 2 * WIDE - first :] + in_bias[1:2, :]).astype(BF16)
        values[here, :] = value
        values_t[:, here] = value.T
        if piece == 0:
            query = (field[:, :WIDE] + in_bias[0:1, :]).astype(BF16)
            query = (query.astype(F32) * SCALE).astype(BF16)
            query_low[rows, :] = query
            for tile in range(count // 2 // TILE):
                split_columns(
                    query[tile * TILE : (tile + 1) * TILE, :].T, query_cols, block * (count // 2 // TILE) + tile
                )

    for block in range(2):
        arrive(arrivals[block])
        forward_copy(block).start()
        project(0, block, place)
    for block in range(2):
        forward_copy(block).wait()
        project(1, block, 1 - place)
    store(0)
    store(2)
    store(3)
    store(4)
    attend_whole(
        tiles, target_row, place * count, wide, True, query_cols, keys, values_t, attended_one, lse_one,
        held, held_low,
    )
    store(5)
    for load in loads[1:4]:
        load.wait()
    for block in range(2):
        arrive(arrivals[2 + block])
        forward_copy(2 + block).start()

    @pl.loop(0, blocks)
    def _(block):
        rows = dyn(block, rows_block)
        attended = attended_one[:, rows].T
        field = input_pieces[0, rows, :].astype(F32) + nn(attended, self_out_weight[...]) + self_out_bias[...]
        normal, rstd = normalize(field)
        first_normal[rows, :] = normal
        first_rstd[rows, :] = rstd
        low = (normal * first_gain[...] + first_shift[...]).astype(BF16)
        first_low[rows, :] = low
        query = (nn(low, cross_weight[...]) + cross_bias[0:1, :]).astype(BF16)
        query = (query.astype(F32) * SCALE).astype(BF16)
        cross_query[rows, :] = query
        for tile in range(rows_block // TILE):
            split_columns(
                query[tile * TILE : (tile + 1) * TILE, :].T, query_cols, block * (rows_block // TILE) + tile
            )

    store(6)
    store(7)
    store(8)

    def project_memory(piece, spot):
        field = nn(memory_pieces[piece], pair_weight[...])
        here = dyn(spot, count)
        cross_keys[here, :] = field[:, :WIDE].astype(BF16)
        value = (field[:, WIDE:] + cross_bias[1:2, :]).astype(BF16)
        cross_values[here, :] = value
        values_t[:, here] = value.T

    project_memory(0, place)
    for block in range(2):
        forward_copy(2 + block).wait()
    project_memory(1, 1 - place)
    store(1)
    store(9)
    store(10)
    spread_row(memory_row, wide)
    attend_whole(
        tiles, target_row, place * count, wide, False, query_cols, cross_keys, values_t, attended_two, lse_two,
        held, held_low,
    )
    for load in loads[4:]:
        load.wait()

    @pl.loop(0, blocks)
    def _(block):
        rows = dyn(block, rows_block)
        attended = attended_two[:, rows].T
        first = first_normal[rows, :] * first_gain[...] + first_shift[...]
        field = first + nn(attended, cross_out_weight[...]) + cross_out_bias[...]
        normal, rstd = normalize(field)
        second_normal[rows, :] = normal
        second_rstd[rows, :] = rstd
        second = normal * second_gain[...] + second_shift[...]
        third[rows, :] = second + down_bias[...]
        low = second.astype(BF16)
        second_low[rows, :] = low
        second_low_t[:, rows] = low.T

    chunks, chunk_size = in_weight.shape[1] // WIDE, WIDE
    arrive(arrivals[4])

    @pl.loop(0, chunks // 2)
    def _(chunk):
        lanes = dyn(chunk, 2 * chunk_size)
        hidden = nn(second_low[...], in_weight[:, lanes]) + feed_bias[:, lanes]
        value, derivative = gate(hidden)
        value = value.astype(BF16)
        active[:, lanes] = value
        slope[:, lanes] = derivative
        third[...] += nn(value, down_weight[lanes, :])

    sums_out[...] = jnp.zeros(sums_out.shape, F32)

    @pl.loop(0, blocks)
    def _(block):
        rows = dyn(block, rows_block)
        normal, rstd = normalize(third[rows, :])
        output_low[rows, :] = (normal * last_gain[...] + last_shift[...]).astype(BF16)
        outer = cot[rows, :].astype(F32)
        grad = normalize_back(outer, last_gain[...], normal, rstd)
        third[rows, :] = grad
        low = grad.astype(BF16)
        branch[rows, :] = low
        sums_out[0:1, :] += col_sum(outer * normal)
        sums_out[1:2, :] += col_sum(outer)
        sums_out[2:3, :] += col_sum(low.astype(F32))

    output_copy = (output_low, output_got, 5)

    @pl.when(away)
    def _():
        far_copy(output_copy).start()

    per_half = chunks // n

    @pl.loop(0, chunks)
    def _(chunk):
        lanes = dyn(chunk, chunk_size)
        share = tn(active[:, lanes], branch[...]).astype(BF16)
        down_grad[lax.div(chunk, per_half), dyn(lax.rem(chunk, per_half), chunk_size), :] = share
        inner = nt(branch[...], down_weight[lanes, :])
        hidden_grad = (inner * slope[:, lanes]).astype(BF16)
        in_bias_grad[:, lanes] = col_sum(hidden_grad.astype(F32))
        third[...] += nt(hidden_grad, in_weight[:, lanes])
        share = nn(second_low_t[...], hidden_grad).astype(BF16)
        for b in range(n):
            in_grad[b, dyn(chunk, half), :] = share[b * half : (b + 1) * half, :]

    store(13)
    store(14)

    @pl.loop(0, blocks)
    def _(block):
        rows = dyn(block, rows_block)
        outer = third[rows, :]
        normal = second_normal[rows, :]
        grad = normalize_back(outer, second_gain[...], normal, second_rstd[rows, :])
        g2_out[rows, :] = grad
        low = grad.astype(BF16)
        branch[rows, :] = low
        sums_out[3:4, :] += col_sum(outer * normal)
        sums_out[4:5, :] += col_sum(outer)
        sums_out[5:6, :] += col_sum(low.astype(F32))
        grad_out[rows, :] = nt(low, cross_out_weight[...]).astype(BF16)

    store(11)
    store(12)
    spread_parts(n, nn(attended_two[...], branch[...]), cross_out_grad, 0)
    store(15)
    write_delta(tiles, grad_out, attended_two, delta_ref)

    @pl.when(away)
    def _():
        far_copy(output_copy).wait()
        layer_output[...] = output_got[...]

    @pl.when(jnp.logical_not(away))
    def _():
        layer_output[...] = output_low[...]

    for index in range(FORWARD_STORES):
        stores[index].wait()


def forward_all(n, groups, rows_block, activations, weights, resident):
    count, features = activations[0].shape
    length = n * count
    hidden = weights[5].shape[1]
    half = features // n
    vm = pl.BlockSpec(memory_space=pltpu.VMEM)
    hbm = pl.BlockSpec(memory_space=pl.ANY)
    low, wide, every = (count, features), (count, features), (length, features)
    stored = [
        ((2, *low), BF16), ((2, *low), BF16), (low, BF16), (every, BF16), (every, BF16), ((features, count), BF16),
        (wide, F32), (low, BF16), (low, BF16), (every, BF16), (every, BF16), (low, BF16), (wide, F32),
        ((n, hidden // n, features), BF16), ((n, hidden // n, features), BF16), ((n, half, features), BF16),
    ]
    stats = out_like((features // PAIR, 2 * count), F32)
    row_like = out_like((1, length), jnp.int32)
    row_scratch = pltpu.VMEM((1, length), jnp.int32)
    held = (features // PAIR, length, 2 * TILE)
    low_rows, wide_rows = pltpu.VMEM(low, BF16), pltpu.VMEM(wide, F32)
    return pl.pallas_call(
        functools.partial(forward_kernel, n, groups, count),
        in_specs=[hbm] * (len(activations) + len(weights)) + [vm] * len(resident),
        out_specs=[hbm] * len(stored) + [vm] * 9,
        out_shape=[out_like(*entry) for entry in stored] + [
            out_like(low, BF16), stats, stats, stats, out_like((count, 1), F32), out_like((8, features), F32),
            out_like((1, hidden), F32), row_like, row_like,
        ],
        scratch_shapes=[
            *[pltpu.VMEM(weight.shape, weight.dtype) for weight in weights],
            *[pltpu.VMEM(*entry) for entry in stored],
            low_rows, low_rows, low_rows, row_scratch, row_scratch,
            pltpu.VMEM((length, TILE), jnp.int32), pltpu.VMEM((features, length), BF16),
            pltpu.VMEM((features, 2 * count), BF16), pltpu.VMEM(held, F32), pltpu.VMEM(held, BF16),
            pltpu.VMEM((features, count), BF16), wide_rows, pltpu.VMEM((count, 1), F32), low_rows,
            pltpu.VMEM((features, count), BF16), pltpu.VMEM((count, hidden), BF16),
            pltpu.VMEM((count, hidden), F32), wide_rows, low_rows,
            pltpu.SemaphoreType.DMA((len(weights),)), pltpu.SemaphoreType.DMA((len(stored),)),
            pltpu.SemaphoreType.DMA((5,)), pltpu.SemaphoreType.DMA((6,)), pltpu.SemaphoreType.DMA((6,)),
            pltpu.SemaphoreType.DMA((6,)), pltpu.SemaphoreType.DMA((6,)),
        ],
        compiler_params=pltpu.CompilerParams(
            vmem_limit_bytes=VMEM_LIMIT, collective_id=1, has_side_effects=True
        ),
    )(*activations, *weights, *resident)


def widen_kernel(plan, source, *outs):
    for out, (start, columns) in zip(outs, plan):
        height = out.shape[0]
        for column in range(columns):
            out[:, column * WIDE : (column + 1) * WIDE] = source[
                start + column * height : start + (column + 1) * height, :
            ].astype(F32)


def finish_kernel(plan, packed, *refs):
    count = len(plan)
    input_low, memory_low, output_low, small, *refs = refs
    (
        *weights, input_grad, memory_grad, layer_output, self_bias, cross_bias, feed_bias,
    ) = refs[: count + 6]
    refs = refs[count + 6 :]
    vectors, refs = refs[:9], refs[9:]
    held, refs = refs[:count], refs[count:]
    wide, refs = refs[:count], refs[count:]
    input_held, memory_held, output_held, input_wide, memory_wide, load_sem, store_sem = refs

    def load(index):
        start, columns = plan[index]
        return pltpu.make_async_copy(
            packed.at[pl.ds(start, held[index].shape[0])], held[index], load_sem.at[index]
        )

    extra = [
        pltpu.make_async_copy(input_low, input_held, load_sem.at[count]),
        pltpu.make_async_copy(memory_low, memory_held, load_sem.at[count + 1]),
    ]
    output = pltpu.make_async_copy(output_low, output_held, load_sem.at[count + 2])
    loads = [load(index) for index in range(count)]
    order = sorted(range(count), key=lambda index: held[index].shape[0])
    for index in order:
        loads[index].start()
    for copy in extra + [output]:
        copy.start()
    stores = []
    for index in order:
        start, columns = plan[index]
        loads[index].wait()
        height = wide[index].shape[0]

        @pl.loop(0, height // 64)
        def _(block):
            for column in range(columns):
                here = pl.ds(pl.multiple_of(column * height + block * 64, 64), 64)
                wide[index][dyn(block, 64), column * WIDE : (column + 1) * WIDE] = held[index][here, :].astype(F32)

        stores.append(pltpu.make_async_copy(wide[index], weights[index], store_sem.at[index]))
        stores[-1].start()
    for index, (source, target, result) in enumerate(
        ((input_held, input_wide, input_grad), (memory_held, memory_wide, memory_grad))
    ):
        extra[index].wait()

        @pl.loop(0, target.shape[0] // 128)
        def _(block):
            target[dyn(block, 128), :] = source[dyn(block, 128), :].astype(F32)

        stores.append(pltpu.make_async_copy(target, result, store_sem.at[count + index]))
        stores[-1].start()
    output.wait()
    stores.append(pltpu.make_async_copy(output_held, layer_output, store_sem.at[count + 2]))
    stores[-1].start()
    self_bias[...] = small[0:2, :]
    cross_bias[...] = small[8:10, :]
    for index, vector in enumerate(vectors):
        vector[...] = small[10 + index, :]
    half = small.shape[1]
    for row in range(feed_bias.shape[0] // half):
        feed_bias[row * half : (row + 1) * half] = small[19 + row, :]
    for copy in stores:
        copy.wait()


def finish_all(n, packed, small, input_low, memory_low, layer_output, hidden):
    count, features = input_low.shape
    half = features // n
    plan, shapes, parts = [], [], []
    start = 0
    for height, columns in (
        (half, hidden // features), (hidden // n, 1), (half, 1), (half, 1), (half, 2), (half, 1), (half, 3)
    ):
        plan.append((start, columns))
        parts.append((height * columns, features))
        shapes.append((height, columns * features))
        start += height * columns
    vm = pl.BlockSpec(memory_space=pltpu.VMEM)
    hbm = pl.BlockSpec(memory_space=pl.ANY)
    wide = (count, features)
    return pl.pallas_call(
        functools.partial(finish_kernel, plan),
        in_specs=[hbm] * 4 + [vm],
        out_specs=[hbm] * (len(plan) + 3) + [vm] * 12,
        out_shape=[out_like(shape, F32) for shape in shapes] + [
            out_like(wide, F32), out_like(wide, F32), out_like(wide, BF16),
            out_like((2, half), F32), out_like((2, half), F32), out_like((hidden // n,), F32),
        ] + [out_like((half,), F32)] * 9,
        scratch_shapes=[pltpu.VMEM(shape, BF16) for shape in parts]
        + [pltpu.VMEM(shape, F32) for shape in shapes]
        + [
            pltpu.VMEM(wide, BF16), pltpu.VMEM(wide, BF16), pltpu.VMEM(wide, BF16), pltpu.VMEM(wide, F32),
            pltpu.VMEM(wide, F32),
            pltpu.SemaphoreType.DMA((len(plan) + 3,)), pltpu.SemaphoreType.DMA((len(plan) + 3,)),
        ],
        compiler_params=pltpu.CompilerParams(vmem_limit_bytes=VMEM_LIMIT),
    )(packed, input_low, memory_low, layer_output, small)


def key_ranges(query_segment, key_segment, tiles, limit):
    edges = query_segment.reshape(tiles, TILE)
    low = jnp.sum((key_segment[None, :] < edges[:, :1]).astype(jnp.int32), axis=1)
    high = jnp.sum((key_segment[None, :] <= edges[:, TILE - 1 :]).astype(jnp.int32), axis=1)
    if limit is not None:
        high = jnp.minimum(high, limit)
    return jnp.stack([low // TILE, (high + TILE - 1) // TILE]).astype(jnp.int32)


def apart(
    n, groups, rows_block, input_rows, memory_rows, cotangent_rows, target_segments, memory_segments,
    self_in_weight, self_in_bias, self_out_weight, self_out_bias, first_gain, first_shift,
    cross_query_weight, cross_pair_weight, cross_bias, cross_out_weight, cross_out_bias,
    second_gain, second_shift, feed_in_weight, feed_in_bias, feed_out_weight, feed_out_bias,
    third_gain, third_shift,
):
    count, features = input_rows.shape
    length = n * count
    hidden = feed_in_weight.shape[1]
    tiles = count // TILE
    half = features // n
    place = lax.axis_index("blk").astype(jnp.int32)

    def row(vector):
        return vector[None, :]

    def shifted(field, step):
        return lax.ppermute(field, "blk", [(s, (s + step) % n) for s in range(n)])

    def shifted_back(field, step):
        return lax.ppermute(field, "blk", [(s, (s - step) % n) for s in range(n)])

    input_pieces = [input_rows] + [shifted(input_rows, step) for step in range(1, n)]
    memory_pieces = [memory_rows] + [shifted(memory_rows, step) for step in range(1, n)]
    target_row, source_row = target_segments[0], memory_segments[0]
    target_here = lax.dynamic_slice_in_dim(target_row, place * count, count, 0)
    self_ranges = key_ranges(
        target_here, target_row, tiles, place * count + TILE * (1 + jnp.arange(tiles, dtype=jnp.int32))
    )
    cross_ranges = key_ranges(target_here, source_row, tiles, None)
    place_one = place[None]
    query_segment = target_here[None, :]
    target_column = target_row[:, None]
    source_column = source_row[:, None]

    stats = out_like((WIDE // PAIR, 2 * count), F32)
    low_rows = out_like((count, features), BF16)
    wide_rows = out_like((count, features), F32)
    low_row_all = out_like((length, features), BF16)
    statistic = out_like((count, 1), F32)
    wide_scratch = pltpu.VMEM((length, TILE), jnp.int32)
    values_t = pltpu.VMEM((features, length), BF16)
    query_cols = pltpu.VMEM((features, 2 * count), BF16)
    query_rows = pltpu.VMEM((2 * count, features), BF16)
    peak = pltpu.VMEM((8, 2 * TILE), F32)
    sums = pltpu.VMEM((features, TILE), F32)
    held = pltpu.VMEM((features // PAIR, KEYS, 2 * TILE), F32)
    held_low = pltpu.VMEM((features // PAIR, KEYS, 2 * TILE), BF16)
    square = 2 * count * features * features

    (
        query, keys, values, attended_t, lse, normal, rstd, first_low, cross_query
    ) = run(
        functools.partial(self_forward, n, rows_block),
        [place_one, self_ranges, *input_pieces, query_segment, target_column,
         self_in_weight, self_in_bias, self_out_weight, row(self_out_bias), row(first_gain),
         row(first_shift), cross_query_weight, cross_bias],
        2,
        [low_rows, low_row_all, low_row_all, out_like((features, count), BF16), stats, wide_rows,
         statistic, low_rows, low_rows],
        [wide_scratch, values_t, query_cols, peak, peak, sums, held, held_low],
        20 * square, 10 << 20,
    )

    (
        layer_output, cross_keys, cross_values, cross_lse, cross_delta, unused, cross_grad, g2,
        in_grad, down_grad, cross_out_grad, feed_sums, in_bias_grad,
    ) = run(
        functools.partial(cross_and_feed, n, rows_block),
        [place_one, cross_ranges, *memory_pieces, query_segment, source_column, cotangent_rows,
         cross_query, normal, row(first_gain), row(first_shift), cross_pair_weight, cross_bias,
         cross_out_weight, row(cross_out_bias), row(second_gain), row(second_shift),
         feed_in_weight, row(feed_in_bias), feed_out_weight, row(feed_out_bias),
         row(third_gain), row(third_shift)],
        2,
        [low_rows, low_row_all, low_row_all, stats, stats, out_like((8, 128), F32), low_rows, wide_rows,
         out_like((n, hidden // n, features), BF16), out_like((n, hidden // n, features), BF16),
         out_like((n, half, features), BF16), out_like((8, features), F32), out_like((1, hidden), F32)],
        [wide_scratch, values_t, query_cols, peak, peak, sums, held, held_low,
         pltpu.VMEM((features, count), BF16), pltpu.VMEM((count, features), F32),
         pltpu.VMEM((count, 1), F32), pltpu.VMEM((count, features), BF16),
         pltpu.VMEM((features, count), BF16), pltpu.VMEM((count, hidden), BF16),
         pltpu.VMEM((count, hidden), F32), pltpu.VMEM((count, features), F32),
         pltpu.VMEM((count, features), BF16), pltpu.VMEM((features, count), BF16)],
        50 * square, 20 << 20,
    )

    back_scratch = [
        wide_scratch, values_t, query_cols, query_rows, query_cols, query_rows,
        pltpu.VMEM((features, count), F32), pltpu.VMEM((length, features), F32),
        pltpu.VMEM((length, features), F32), held, held_low, held_low, pltpu.VMEM((count, features), BF16),
    ]
    sent_like = out_like((max(n - 1, 1), count, features), BF16)
    (
        memory_own, memory_sent, cross_query_grad, cross_pair_grad, self_out_grad, self_grad,
        self_delta, g1, cross_sums,
    ) = run(
        functools.partial(cross_backward, n, rows_block),
        [place_one, cross_ranges, *memory_pieces, query_segment, source_column, cross_query,
         cross_grad, cross_keys, cross_values, cross_lse, cross_delta, g2, normal, rstd, first_low,
         row(first_gain), cross_query_weight, cross_pair_weight, self_out_weight, attended_t],
        2,
        [wide_rows, sent_like, out_like((n, half, features), BF16),
         out_like((n, 2 * half, features), BF16), out_like((n, half, features), BF16), low_rows,
         stats, wide_rows, out_like((8, features), F32)],
        back_scratch + [pltpu.VMEM((count, features), BF16)],
        30 * square, 15 << 20,
    )
    (input_own, input_sent, self_in_grad, self_sums) = run(
        functools.partial(self_backward, n, rows_block),
        [place_one, self_ranges, *input_pieces, query_segment, target_column, query, self_grad,
         keys, values, lse, self_delta, g1, self_in_weight],
        2,
        [wide_rows, sent_like, out_like((n, 3 * half, features), BF16), out_like((8, features), F32)],
        back_scratch,
        30 * square, 15 << 20,
    )

    memory_grad, input_grad = memory_own, input_own
    for step in range(1, n):
        memory_grad = memory_grad + shifted_back(memory_sent[step - 1], step).astype(F32)
        input_grad = input_grad + shifted_back(input_sent[step - 1], step).astype(F32)

    vectors = jnp.concatenate([self_sums[:2], cross_sums[:5], feed_sums[:6]], axis=0)
    count_small = vectors.shape[0]
    small = jnp.concatenate(
        [
            jnp.transpose(vectors.reshape(count_small, n, half), (1, 0, 2)).reshape(n, -1),
            in_bias_grad.reshape(n, -1),
        ],
        axis=1,
    )
    amount = small.shape[1]
    small_rows = -(-amount // (8 * WIDE)) * 8
    small = jnp.pad(small, ((0, 0), (0, small_rows * WIDE - amount))).reshape(n, small_rows, WIDE)
    packed, small = reduce_all(
        n, groups,
        [in_grad, down_grad, cross_out_grad, cross_query_grad, cross_pair_grad, self_out_grad, self_in_grad],
        small,
    )
    small = small.reshape(-1)[:amount]
    return packed, small, memory_grad, input_grad, layer_output, count_small


def on_device(
    n, groups,
    inputs, memory, cotangent, target_segments, memory_segments,
    self_in_weight, self_in_bias, self_out_weight, self_out_bias, first_gain, first_shift,
    cross_query_weight, cross_pair_weight, cross_bias, cross_out_weight, cross_out_bias,
    second_gain, second_shift, feed_in_weight, feed_in_bias, feed_out_weight, feed_out_bias,
    third_gain, third_shift,
):
    input_rows, memory_rows, cotangent_rows = inputs[0], memory[0], cotangent[0]
    count, features = input_rows.shape
    length = n * count
    hidden = feed_in_weight.shape[1]
    rows_block = min(count, 256)
    tiles = count // TILE
    half = features // n
    near = n == 2 and groups % 4 == 0 and length <= 1024 and half % TILE == 0

    def row(vector):
        return vector[None, :]

    if near:
        (
            input_pieces, memory_pieces, query, keys, values, attended_t, normal, first_low, cross_query,
            cross_keys, cross_values, cross_grad, g2, in_grad, down_grad, cross_out_grad,
            layer_output, lse, cross_lse, cross_delta, rstd, feed_sums, in_bias_grad, target_row, memory_row,
        ) = forward_all(
            n, groups, rows_block,
            [input_rows, memory_rows, cotangent_rows],
            [self_in_weight, self_out_weight, cross_query_weight, cross_pair_weight, cross_out_weight,
             feed_in_weight, feed_out_weight],
            [target_segments, memory_segments, self_in_bias, row(self_out_bias), row(first_gain),
             row(first_shift), cross_bias, row(cross_out_bias), row(second_gain), row(second_shift),
             row(feed_in_bias), row(feed_out_bias), row(third_gain), row(third_shift)],
        )
        packed, small, memory_grad, input_grad = back_and_reduce(
            n, groups, rows_block,
            [in_grad, down_grad, cross_out_grad],
            [cross_values, memory_pieces, cross_pair_weight, first_low, cross_query_weight, g2, normal, self_out_weight,
             attended_t, keys, values, query, input_pieces, self_in_weight],
            [target_row, memory_row, cross_query, cross_grad, cross_keys,
             cross_lse, cross_delta, feed_sums, in_bias_grad, row(first_gain), rstd, lse],
        )
        (
            feed_in_grad, feed_out_grad, cross_out_total, cross_query_total, cross_pair_total,
            self_out_total, self_in_total, input_grad, memory_grad, layer_output, self_bias_grad,
            cross_bias_grad, in_bias_total, first_gain_grad, first_shift_grad, self_out_bias_grad,
            third_gain_grad, third_shift_grad, feed_out_bias_grad, second_gain_grad, second_shift_grad,
            cross_out_bias_grad,
        ) = finish_all(n, packed, small, input_grad, memory_grad, layer_output, hidden)
    else:
        packed, small, memory_grad, input_grad, layer_output, count_small = apart(
            n, groups, rows_block, input_rows, memory_rows, cotangent_rows, target_segments, memory_segments,
            self_in_weight, self_in_bias, self_out_weight, self_out_bias, first_gain, first_shift,
            cross_query_weight, cross_pair_weight, cross_bias, cross_out_weight, cross_out_bias,
            second_gain, second_shift, feed_in_weight, feed_in_bias, feed_out_weight, feed_out_bias,
            third_gain, third_shift,
        )
        plan = []
        start = 0
        shapes = []
        for height, columns in (
            (half, hidden // features), (hidden // n, 1), (half, 1), (half, 1), (half, 2), (half, 1), (half, 3)
        ):
            plan.append((start, columns))
            shapes.append(out_like((height, columns * features), F32))
            start += height * columns
        (
            feed_in_grad, feed_out_grad, cross_out_total, cross_query_total, cross_pair_total,
            self_out_total, self_in_total,
        ) = run(functools.partial(widen_kernel, plan), [packed], 0, shapes, [], 0, 12 << 20)
        rows_small = small[: count_small * half].reshape(count_small, half)
        (
            self_query_bias, self_value_bias, cross_query_bias, cross_value_bias, first_gain_grad,
            first_shift_grad, self_out_bias_grad, third_gain_grad, third_shift_grad, feed_out_bias_grad,
            second_gain_grad, second_shift_grad, cross_out_bias_grad,
        ) = [rows_small[index] for index in range(count_small)]
        self_bias_grad = jnp.stack([self_query_bias, self_value_bias])
        cross_bias_grad = jnp.stack([cross_query_bias, cross_value_bias])
        in_bias_total = small[count_small * half :]
    return (
        layer_output[None],
        input_grad[None],
        memory_grad[None],
        self_in_total,
        self_bias_grad,
        self_out_total,
        self_out_bias_grad,
        first_gain_grad,
        first_shift_grad,
        cross_query_total,
        cross_pair_total,
        cross_bias_grad,
        cross_out_total,
        cross_out_bias_grad,
        second_gain_grad,
        second_shift_grad,
        feed_in_grad,
        in_bias_total,
        feed_out_grad,
        feed_out_bias_grad,
        third_gain_grad,
        third_shift_grad,
    )


def solution(mesh):
    rows = P("dp", "blk", None)
    everywhere = P()
    split = P("blk", None)
    vector = P("blk")
    pair = P(None, "blk")
    return jax.shard_map(
        functools.partial(on_device, mesh.shape["blk"], mesh.shape["dp"]),
        mesh=mesh,
        in_specs=(rows, rows, rows, P("dp", None), P("dp", None)) + (everywhere,) * 19,
        out_specs=(
            rows, rows, rows, split, pair, split, vector, vector, vector, split, split, pair, split,
            vector, vector, vector, split, vector, split, vector, vector, vector,
        ),
        check_vma=False,
    )
```

```python
import functools

import jax
import jax.numpy as jnp
from jax import lax
from jax.experimental import pallas as pl
from jax.experimental.pallas import tpu as pltpu
from jax.sharding import PartitionSpec as P

HEAD = 64
TILE = 128
KEYS = 256
BACK_KEYS = 256
PAIR = 2 * HEAD
WIDE = 512
SCALE = HEAD ** (-0.5)
MASKED = -1e30
F32 = jnp.float32
BF16 = jnp.bfloat16
VMEM_LIMIT = 62 << 20


def nn(left, right):
    return lax.dot_general(left, right, (((1,), (0,)), ((), ())), preferred_element_type=F32)


def nt(left, right):
    return lax.dot_general(left, right, (((1,), (1,)), ((), ())), preferred_element_type=F32)


def tn(left, right):
    return lax.dot_general(left, right, (((0,), (0,)), ((), ())), preferred_element_type=F32)


def col_sum(field):
    return jnp.sum(field, axis=0, keepdims=True)


def normalize(field):
    centre = field - jnp.mean(field, axis=-1, keepdims=True)
    spread = jnp.mean(centre * centre, axis=-1, keepdims=True)
    rstd = lax.rsqrt(spread + 1e-05)
    return centre * rstd, rstd


def normalize_back(grad, gain, normal, rstd):
    scaled = grad * gain
    mean = jnp.mean(scaled, axis=-1, keepdims=True)
    along = jnp.mean(scaled * normal, axis=-1, keepdims=True)
    return (scaled - mean - normal * along) * rstd


def gate(hidden):
    bell = jnp.exp2(hidden * hidden * (-0.5 * 1.4426950408889634))
    ratio = 1.0 / (1.0 + (0.3275911 * 0.7071067811865476) * jnp.abs(hidden))
    series = (0.5 * 1.061405429) * ratio - 0.5 * 1.453152027
    series = series * ratio + 0.5 * 1.421413741
    series = series * ratio - 0.5 * 0.284496736
    series = series * ratio + 0.5 * 0.254829592
    tail = series * ratio * bell
    phi = jnp.where(hidden > 0.0, 1.0 - tail, tail)
    return hidden * phi, phi + hidden * (bell * 0.3989422804014327)


def dyn(index, size):
    return pl.ds(pl.multiple_of(index * size, size), size)


def even_lanes(rows, width):
    return (lax.broadcasted_iota(jnp.int32, (rows, width), 1) // HEAD) % 2 == 0


def even_rows(rows, width):
    return (lax.broadcasted_iota(jnp.int32, (rows, width), 0) // HEAD) % 2 == 0


def split_columns(tile_t, out_ref, tile):
    chosen = even_rows(*tile_t.shape)
    blank = jnp.zeros_like(tile_t)
    out_ref[:, pl.ds(pl.multiple_of(tile * 2 * TILE, 2 * TILE), TILE)] = jnp.where(chosen, tile_t, blank)
    out_ref[:, pl.ds(pl.multiple_of(tile * 2 * TILE + TILE, TILE), TILE)] = jnp.where(
        chosen, blank, tile_t
    )


def split_rows(tile_n, out_ref, tile):
    chosen = even_lanes(*tile_n.shape)
    blank = jnp.zeros_like(tile_n)
    out_ref[pl.ds(pl.multiple_of(tile * 2 * TILE, 2 * TILE), TILE), :] = jnp.where(chosen, tile_n, blank)
    out_ref[pl.ds(pl.multiple_of(tile * 2 * TILE + TILE, TILE), TILE), :] = jnp.where(
        chosen, blank, tile_n
    )


def spread_segments(column_ref, wide_ref):
    total = column_ref.shape[0]
    step = min(total, 512)

    @pl.loop(0, total // step)
    def _(block):
        rows = dyn(block, step)
        wide_ref[rows, :] = jnp.broadcast_to(column_ref[rows, :], (step, TILE))


def key_rows(low, chunk, length, size):
    wanted = low * TILE + chunk * size
    start = pl.multiple_of(jnp.minimum(wanted, length - size), TILE)
    return pl.ds(start, size), start, wanted


def chunk_bias(query_row, key_wide_ref, tile, rows, start, wanted, offset, causal):
    size = rows.size
    key_position = start + lax.broadcasted_iota(jnp.int32, (size, TILE), 0)
    allowed = (key_wide_ref[rows, :] == query_row) & (key_position >= wanted)
    if causal:
        query_position = offset + tile * TILE + lax.broadcasted_iota(jnp.int32, (size, TILE), 1)
        allowed = allowed & (key_position <= query_position)
    return jnp.where(allowed, 0.0, MASKED)


def attend(
    tiles, ranges_ref, query_row_ref, key_wide_ref, offset, causal,
    query_cols, keys, values_t, attended_t, lse_ref, peak, total, sums, held, held_low,
):
    pairs = WIDE // PAIR

    @pl.loop(0, tiles)
    def _(tile):
        peak[...] = jnp.full(peak.shape, MASKED, F32)
        total[...] = jnp.zeros(total.shape, F32)
        sums[...] = jnp.zeros(sums.shape, F32)
        query_row = query_row_ref[:, dyn(tile, TILE)]

        low, high = ranges_ref[0, tile], ranges_ref[1, tile]

        size = held.shape[1]

        @pl.loop(0, lax.div((high - low) * TILE + size - 1, size))
        def _(chunk):
            rows, start, wanted = key_rows(low, chunk, keys.shape[0], size)
            bias = chunk_bias(query_row, key_wide_ref, tile, rows, start, wanted, offset, causal)
            bias = jnp.concatenate([bias, bias], axis=1)
            factors = []
            for pair in range(pairs):
                lanes = slice(pair * PAIR, (pair + 1) * PAIR)
                scores = nn(keys[rows, lanes], query_cols[lanes, dyn(tile, 2 * TILE)]) + bias
                held[pair] = scores
                before = peak[pair : pair + 1, :]
                after = jnp.maximum(before, jnp.max(scores, axis=0, keepdims=True))
                factors.append(jnp.exp(before - after))
                peak[pair : pair + 1, :] = after
            for pair in range(pairs):
                weights = jnp.exp(held[pair] - peak[pair : pair + 1, :])
                total[pair : pair + 1, :] = total[pair : pair + 1, :] * factors[pair] + col_sum(weights)
                held_low[pair] = weights.astype(BF16)
            for pair in range(pairs):
                factor = factors[pair]
                mixed = nn(values_t[pair * PAIR : (pair + 1) * PAIR, rows], held_low[pair])
                first = slice(pair * PAIR, pair * PAIR + HEAD)
                second = slice(pair * PAIR + HEAD, (pair + 1) * PAIR)
                sums[first, :] = sums[first, :] * factor[:, :TILE] + mixed[:HEAD, :TILE]
                sums[second, :] = sums[second, :] * factor[:, TILE:] + mixed[HEAD:, TILE:]

        for pair in range(pairs):
            amount = total[pair : pair + 1, :]
            lse_ref[pair : pair + 1, dyn(tile, 2 * TILE)] = peak[pair : pair + 1, :] + jnp.log(amount)
            share = 1.0 / amount
            first = slice(pair * PAIR, pair * PAIR + HEAD)
            second = slice(pair * PAIR + HEAD, (pair + 1) * PAIR)
            attended_t[first, dyn(tile, TILE)] = (sums[first, :] * share[:, :TILE]).astype(BF16)
            attended_t[second, dyn(tile, TILE)] = (sums[second, :] * share[:, TILE:]).astype(BF16)


def attend_back(
    tile, low, high, query_row_ref, first_query, key_wide_ref, offset, causal,
    query_cols, query_rows, grad_cols, grad_rows, keys, keys_t, values, lse_ref, delta_ref,
    query_grad_t, key_grad, value_grad, held, held_low, held_grad, fresh=False,
):
    pairs = WIDE // PAIR
    query_row = query_row_ref[:, pl.ds(pl.multiple_of(first_query + tile * TILE, TILE), TILE)]
    both = dyn(tile, 2 * TILE)

    size = held.shape[1]

    @pl.loop(0, lax.div((high - low) * TILE + size - 1, size))
    def _(chunk):
        rows, start, wanted = key_rows(low, chunk, keys.shape[0], size)
        bias = chunk_bias(query_row, key_wide_ref, tile, rows, start, wanted, offset, causal)
        bias = jnp.concatenate([bias, bias], axis=1)
        for pair in range(pairs):
            lanes = slice(pair * PAIR, (pair + 1) * PAIR)
            scores = nn(keys[rows, lanes], query_cols[lanes, both]) + bias
            probs = jnp.exp(scores - lse_ref[pair : pair + 1, both])
            held[pair] = probs
            held_low[pair] = probs.astype(BF16)
        for pair in range(pairs):
            lanes = slice(pair * PAIR, (pair + 1) * PAIR)
            prob_grad = nn(values[rows, lanes], grad_cols[lanes, both])
            held_grad[pair] = (held[pair] * (prob_grad - delta_ref[pair : pair + 1, both])).astype(BF16)
        for pair in range(pairs):
            lanes = slice(pair * PAIR, (pair + 1) * PAIR)
            value_part = nn(held_low[pair], grad_rows[both, lanes])
            key_part = nn(held_grad[pair], query_rows[both, lanes])
            value_grad[rows, lanes] = value_part if fresh else value_grad[rows, lanes] + value_part
            key_grad[rows, lanes] = key_part if fresh else key_grad[rows, lanes] + key_part
            mixed = nn(keys_t[lanes, rows], held_grad[pair])
            first = slice(pair * PAIR, pair * PAIR + HEAD)
            second = slice(pair * PAIR + HEAD, (pair + 1) * PAIR)
            query_grad_t[first, dyn(tile, TILE)] += mixed[:HEAD, :TILE]
            query_grad_t[second, dyn(tile, TILE)] += mixed[HEAD:, TILE:]


def clear(ref):
    rows = ref.shape[0]
    step = min(rows, 256)

    @pl.loop(0, rows // step)
    def _(block):
        ref[dyn(block, step), :] = jnp.zeros((step, ref.shape[1]), ref.dtype)


def transpose_rows(source, target):
    @pl.loop(0, source.shape[0] // TILE)
    def _(block):
        target[:, dyn(block, TILE)] = source[dyn(block, TILE), :].T


def out_like(shape, dtype):
    return jax.ShapeDtypeStruct(shape, dtype)


def run(body, ins, smem_count, outs, scratch, flops, bytes_accessed):
    vm = pl.BlockSpec(memory_space=pltpu.VMEM)
    sm = pl.BlockSpec(memory_space=pltpu.SMEM)
    return pl.pallas_call(
        body,
        in_specs=[sm] * smem_count + [vm] * (len(ins) - smem_count),
        out_specs=[vm] * len(outs),
        out_shape=outs,
        scratch_shapes=scratch,
        cost_estimate=pl.CostEstimate(
            flops=flops, bytes_accessed=bytes_accessed, transcendentals=0
        ),
        compiler_params=pltpu.CompilerParams(vmem_limit_bytes=VMEM_LIMIT),
    )(*ins)


def self_forward(n, rows_block, place_ref, ranges_ref, *refs):
    pieces, refs = refs[:n], refs[n:]
    (
        query_segment, key_segment, weight, bias, out_weight, out_bias, gain, shift,
        cross_weight, cross_bias,
        query_out, keys, values, attended_t, lse_ref, normal_out, rstd_out, first_low, cross_query,
        wide, values_t, query_cols, peak, total, sums, held, held_low,
    ) = refs
    count = pieces[0].shape[0]
    place = place_ref[0]
    spread_segments(key_segment, wide)

    for step in range(n):
        spot = lax.rem(place + n - step, n)

        @pl.when(spot <= place)
        def _():
            @pl.loop(0, count // rows_block)
            def _(block):
                source = pieces[step][dyn(block, rows_block), :]
                rows = dyn(spot * (count // rows_block) + block, rows_block)
                keys[rows, :] = nn(source, weight[:, WIDE : 2 * WIDE]).astype(BF16)
                values[rows, :] = (nn(source, weight[:, 2 * WIDE :]) + bias[1:2, :]).astype(BF16)
                if step == 0:
                    query = (nn(source, weight[:, :WIDE]) + bias[0:1, :]).astype(BF16)
                    query_out[dyn(block, rows_block), :] = (query.astype(F32) * SCALE).astype(BF16)

        @pl.when(spot > place)
        def _():
            @pl.loop(0, count // rows_block)
            def _(block):
                rows = dyn(spot * (count // rows_block) + block, rows_block)
                keys[rows, :] = jnp.zeros((rows_block, WIDE), BF16)
                values[rows, :] = jnp.zeros((rows_block, WIDE), BF16)

    transpose_rows(values, values_t)
    tiles = count // TILE

    @pl.loop(0, tiles)
    def _(tile):
        split_columns(query_out[dyn(tile, TILE), :].T, query_cols, tile)

    attend(
        tiles, ranges_ref, query_segment, wide, place * count, True,
        query_cols, keys, values_t, attended_t, lse_ref, peak, total, sums, held, held_low,
    )

    @pl.loop(0, count // rows_block)
    def _(block):
        rows = dyn(block, rows_block)
        attended = attended_t[:, rows].T
        field = pieces[0][rows, :].astype(F32) + nn(attended, out_weight[...]) + out_bias[...]
        normal, rstd = normalize(field)
        normal_out[rows, :] = normal
        rstd_out[rows, :] = rstd
        low = (normal * gain[...] + shift[...]).astype(BF16)
        first_low[rows, :] = low
        query = (nn(low, cross_weight[...]) + cross_bias[0:1, :]).astype(BF16)
        cross_query[rows, :] = (query.astype(F32) * SCALE).astype(BF16)


def cross_and_feed(n, rows_block, place_ref, ranges_ref, *refs):
    pieces, refs = refs[:n], refs[n:]
    (
        query_segment, key_segment, cotangent, cross_query, first_normal, first_gain, first_shift,
        pair_weight, cross_bias, out_weight, out_bias, gain, shift,
        in_weight, in_bias, down_weight, down_bias, last_gain, last_shift,
        layer_output, keys, values, lse_ref, delta_ref, out_grad, grad_out, g2_out,
        in_grad, down_grad, cross_out_grad, sums_out, in_bias_grad,
        wide, values_t, query_cols, peak, total, sums, held, held_low, attended_t, second_normal, second_rstd,
        second_low, second_low_t, active, slope, third, branch, branch_t,
    ) = refs
    count = pieces[0].shape[0]
    place = place_ref[0]
    spread_segments(key_segment, wide)
    blocks = count // rows_block

    for step in range(n):
        spot = lax.rem(place + n - step, n)

        @pl.loop(0, blocks)
        def _(block):
            source = pieces[step][dyn(block, rows_block), :]
            rows = dyn(spot * blocks + block, rows_block)
            keys[rows, :] = nn(source, pair_weight[:, :WIDE]).astype(BF16)
            values[rows, :] = (nn(source, pair_weight[:, WIDE:]) + cross_bias[1:2, :]).astype(BF16)

    transpose_rows(values, values_t)
    tiles = count // TILE

    @pl.loop(0, tiles)
    def _(tile):
        split_columns(cross_query[dyn(tile, TILE), :].T, query_cols, tile)

    attend(
        tiles, ranges_ref, query_segment, wide, 0, False,
        query_cols, keys, values_t, attended_t, lse_ref, peak, total, sums, held, held_low,
    )

    @pl.loop(0, blocks)
    def _(block):
        rows = dyn(block, rows_block)
        attended = attended_t[:, rows].T
        first = first_normal[rows, :] * first_gain[...] + first_shift[...]
        field = first + nn(attended, out_weight[...]) + out_bias[...]
        normal, rstd = normalize(field)
        second_normal[rows, :] = normal
        second_rstd[rows, :] = rstd
        second = normal * gain[...] + shift[...]
        third[rows, :] = second + down_bias[...]
        low = second.astype(BF16)
        second_low[rows, :] = low
        second_low_t[:, rows] = low.T

    hidden_size = in_weight.shape[1]
    chunk_size = min(WIDE, hidden_size // n)
    chunks = hidden_size // chunk_size

    @pl.loop(0, chunks)
    def _(chunk):
        lanes = dyn(chunk, chunk_size)

        @pl.loop(0, blocks)
        def _(block):
            rows = dyn(block, rows_block)
            hidden = nn(second_low[rows, :], in_weight[:, lanes]) + in_bias[:, lanes]
            value, derivative = gate(hidden)
            value = value.astype(BF16)
            active[rows, lanes] = value
            slope[rows, lanes] = derivative.astype(slope.dtype)
            third[rows, :] += nn(value, down_weight[dyn(chunk, chunk_size), :])

    sums_out[...] = jnp.zeros(sums_out.shape, F32)
    in_bias_grad[...] = jnp.zeros(in_bias_grad.shape, F32)

    @pl.loop(0, blocks)
    def _(block):
        rows = dyn(block, rows_block)
        normal, rstd = normalize(third[rows, :])
        layer_output[rows, :] = (normal * last_gain[...] + last_shift[...]).astype(BF16)
        outer = cotangent[rows, :].astype(F32)
        grad = normalize_back(outer, last_gain[...], normal, rstd)
        third[rows, :] = grad
        low = grad.astype(BF16)
        branch[rows, :] = low
        sums_out[0:1, :] += col_sum(outer * normal)
        sums_out[1:2, :] += col_sum(outer)
        sums_out[2:3, :] += col_sum(low.astype(F32))

    half = WIDE // n
    down_half = down_weight.shape[0] // n

    @pl.loop(0, chunks)
    def _(chunk):
        lanes = dyn(chunk, chunk_size)
        share = tn(active[:, lanes], branch[...]).astype(BF16)
        per_half = down_half // chunk_size
        down_grad[lax.div(chunk, per_half), dyn(lax.rem(chunk, per_half), chunk_size), :] = share

        @pl.loop(0, blocks)
        def _(block):
            rows = dyn(block, rows_block)
            inner = nt(branch[rows, :], down_weight[dyn(chunk, chunk_size), :])
            hidden_grad = (inner * slope[rows, lanes].astype(F32)).astype(BF16)
            active[rows, lanes] = hidden_grad
            in_bias_grad[:, lanes] += col_sum(hidden_grad.astype(F32))
            third[rows, :] += nt(hidden_grad, in_weight[:, lanes])

        share = nn(second_low_t[...], active[:, lanes]).astype(BF16)
        per_block = WIDE // chunk_size
        block_rows = dyn(lax.div(chunk, per_block), half)
        block_lanes = dyn(lax.rem(chunk, per_block), chunk_size)
        for part in range(n):
            in_grad[part, block_rows, block_lanes] = share[part * half : (part + 1) * half, :]

    @pl.loop(0, blocks)
    def _(block):
        rows = dyn(block, rows_block)
        outer = third[rows, :]
        normal = second_normal[rows, :]
        grad = normalize_back(outer, gain[...], normal, second_rstd[rows, :])
        g2_out[rows, :] = grad
        low = grad.astype(BF16)
        branch[rows, :] = low
        sums_out[3:4, :] += col_sum(outer * normal)
        sums_out[4:5, :] += col_sum(outer)
        sums_out[5:6, :] += col_sum(low.astype(F32))
        grad_out[rows, :] = nt(low, out_weight[...]).astype(BF16)

    share = nn(attended_t[...], branch[...]).astype(BF16)
    for part in range(n):
        cross_out_grad[part] = share[part * half : (part + 1) * half, :]

    write_delta(tiles, grad_out, attended_t, delta_ref)


def write_delta(tiles, grad, attended_t, delta_ref):
    @pl.loop(0, tiles)
    def _(tile):
        product = grad[dyn(tile, TILE), :].astype(F32).T * attended_t[:, dyn(tile, TILE)].astype(F32)
        for pair in range(WIDE // PAIR):
            start = pair * PAIR
            delta_ref[pair : pair + 1, pl.ds(pl.multiple_of(tile * 2 * TILE, 2 * TILE), TILE)] = col_sum(
                product[start : start + HEAD, :]
            )
            delta_ref[
                pair : pair + 1, pl.ds(pl.multiple_of(tile * 2 * TILE + TILE, TILE), TILE)
            ] = col_sum(product[start + HEAD : start + PAIR, :])


def prepare_back(tiles, query, grad, query_cols, query_rows, grad_cols, grad_rows):
    @pl.loop(0, tiles)
    def _(tile):
        here = query[dyn(tile, TILE), :]
        split_columns(here.T, query_cols, tile)
        split_rows(here, query_rows, tile)
        here = grad[dyn(tile, TILE), :]
        split_columns(here.T, grad_cols, tile)
        split_rows(here, grad_rows, tile)


def query_finish(tiles, query_grad_t, query_low, sums_out, index, rounded):
    @pl.loop(0, tiles)
    def _(tile):
        rows = dyn(tile, TILE)
        wide_grad = query_grad_t[:, rows].T * SCALE
        low = wide_grad.astype(BF16)
        query_low[rows, :] = low
        sums_out[index : index + 1, :] += col_sum(low.astype(F32) if rounded else wide_grad)


def spread_parts(n, share, target, start):
    half = WIDE // n
    for part in range(n):
        target[part, start : start + half, :] = share[part * half : (part + 1) * half, :].astype(BF16)


def row_product(n, place, pieces, source):
    count = pieces[0].shape[0]
    step_rows = min(count, 512)
    share = jnp.zeros((WIDE, WIDE), F32)
    for step in range(n):
        spot = lax.rem(place + n - step, n)
        for block in range(count // step_rows):
            rows = dyn(spot * (count // step_rows) + block, step_rows)
            share += tn(
                pieces[step][block * step_rows : (block + 1) * step_rows, :], source[rows, :].astype(BF16)
            )
    return share


def pair_back(n, place, rows_block, count, step, key_grad, value_grad, weight, first, sums_out, index, write):
    blocks = count // rows_block
    spot = lax.rem(place + n - step, n)

    @pl.loop(0, blocks)
    def _(block):
        rows = dyn(spot * blocks + block, rows_block)
        key_low = key_grad[rows, :].astype(BF16)
        value_part = value_grad[rows, :]
        sums_out[index : index + 1, :] += col_sum(value_part)
        value_low = value_part.astype(BF16)
        back = nt(key_low, weight[:, first : first + WIDE]) + nt(value_low, weight[:, first + WIDE : first + 2 * WIDE])
        write(dyn(block, rows_block), back)


def first_back(
    blocks, rows_block, g2, query_low, query_weight, first_normal, first_rstd, gain, self_out_weight,
    g1, branch, self_grad, sums_out, index,
):
    @pl.loop(0, blocks)
    def _(block):
        rows = dyn(block, rows_block)
        outer = g2[rows, :] + nt(query_low[rows, :], query_weight[...])
        normal = first_normal[rows, :]
        back = normalize_back(outer, gain[...], normal, first_rstd[rows, :])
        g1[rows, :] = back
        low = back.astype(BF16)
        branch[rows, :] = low
        sums_out[index : index + 1, :] += col_sum(outer * normal)
        sums_out[index + 1 : index + 2, :] += col_sum(outer)
        sums_out[index + 2 : index + 3, :] += col_sum(low.astype(F32))
        self_grad[rows, :] = nt(low, self_out_weight[...]).astype(BF16)


def cross_backward(n, rows_block, place_ref, ranges_ref, *refs):
    pieces, refs = refs[:n], refs[n:]
    (
        query_segment, key_segment, query, grad, keys, values, lse_ref, delta_ref, g2,
        first_normal, first_rstd, first_low, gain, query_weight, pair_weight, self_out_weight,
        self_attended_t,
        own_grad, sent_grad, query_grad_w, pair_grad_w, self_out_grad, self_grad, self_delta, g1_out, sums_out,
        wide, keys_t, query_cols, query_rows, grad_cols, grad_rows, query_grad_t, key_grad, value_grad,
        held, held_low, held_grad, query_low, branch,
    ) = refs
    count = pieces[0].shape[0]
    place = place_ref[0]
    tiles = count // TILE
    blocks = count // rows_block
    half = WIDE // n
    spread_segments(key_segment, wide)
    transpose_rows(keys, keys_t)
    prepare_back(tiles, query, grad, query_cols, query_rows, grad_cols, grad_rows)
    clear(query_grad_t)
    clear(key_grad)
    clear(value_grad)

    @pl.loop(0, tiles)
    def _(tile):
        attend_back(
            tile, ranges_ref[0, tile], ranges_ref[1, tile], query_segment, 0, wide, 0, False,
            query_cols, query_rows, grad_cols, grad_rows, keys, keys_t, values, lse_ref, delta_ref,
            query_grad_t, key_grad, value_grad, held, held_low, held_grad,
        )

    sums_out[...] = jnp.zeros(sums_out.shape, F32)
    query_finish(tiles, query_grad_t, query_low, sums_out, 0, True)
    spread_parts(n, tn(first_low[...], query_low[...]), query_grad_w, 0)
    for step in range(n):

        def write(here, back):
            if step == 0:
                own_grad[here, :] = back
            else:
                sent_grad[step - 1, here, :] = back.astype(BF16)

        pair_back(n, place, rows_block, count, step, key_grad, value_grad, pair_weight, 0, sums_out, 1, write)
    spread_parts(n, row_product(n, place, pieces, key_grad), pair_grad_w, 0)
    spread_parts(n, row_product(n, place, pieces, value_grad), pair_grad_w, half)
    first_back(
        blocks, rows_block, g2, query_low, query_weight, first_normal, first_rstd, gain, self_out_weight,
        g1_out, branch, self_grad, sums_out, 2,
    )
    spread_parts(n, nn(self_attended_t[...], branch[...]), self_out_grad, 0)
    write_delta(tiles, self_grad, self_attended_t, self_delta)


def self_backward(n, rows_block, place_ref, ranges_ref, *refs):
    pieces, refs = refs[:n], refs[n:]
    (
        query_segment, key_segment, query, grad, keys, values, lse_ref, delta_ref, g1, weight,
        own_grad, sent_grad, grad_w, sums_out,
        wide, keys_t, query_cols, query_rows, grad_cols, grad_rows, query_grad_t, key_grad, value_grad,
        held, held_low, held_grad, query_low,
    ) = refs
    count = pieces[0].shape[0]
    place = place_ref[0]
    tiles = count // TILE
    half = WIDE // n
    spread_segments(key_segment, wide)
    transpose_rows(keys, keys_t)
    prepare_back(tiles, query, grad, query_cols, query_rows, grad_cols, grad_rows)
    clear(query_grad_t)
    clear(key_grad)
    clear(value_grad)

    @pl.loop(0, tiles)
    def _(tile):
        attend_back(
            tile, ranges_ref[0, tile], ranges_ref[1, tile], query_segment, 0, wide, place * count, True,
            query_cols, query_rows, grad_cols, grad_rows, keys, keys_t, values, lse_ref, delta_ref,
            query_grad_t, key_grad, value_grad, held, held_low, held_grad,
        )

    sums_out[...] = jnp.zeros(sums_out.shape, F32)
    query_finish(tiles, query_grad_t, query_low, sums_out, 0, False)
    for step in range(n):

        def write(here, back):
            if step == 0:
                own_grad[here, :] = back + g1[here, :] + nt(query_low[here, :], weight[:, :WIDE])
            else:
                sent_grad[step - 1, here, :] = back.astype(BF16)

        pair_back(n, place, rows_block, count, step, key_grad, value_grad, weight, WIDE, sums_out, 1, write)
    spread_parts(n, tn(pieces[0][...], query_low[...]), grad_w, 0)
    spread_parts(n, row_product(n, place, pieces, key_grad), grad_w, half)
    spread_parts(n, row_product(n, place, pieces, value_grad), grad_w, 2 * half)


CORE_RATE = 0.0018
LINK_RATE = 0.0225
LATENCY = {"core": 1.0, "x": 2.2, "y": 2.2, "z": 2.6}
MARGIN = 0.5


def plan_steps(n, chunks, extras, smalls, segments):
    free = {"core": 0.0, "x": 0.0, "y": 0.0, "z": 0.0}
    now = 0.0
    pending = []
    plan = []
    crossed = set()

    def send(link, rows, rate=LINK_RATE):
        free[link] = max(free[link], now) + rows * rate
        return free[link] + LATENCY[link]

    def execute(kind, index, step):
        nonlocal now
        now += 0.15
        if kind == "chunk":
            unused, rows, y_first, unused = chunks[index]
            if step == 0:
                ready = send("core", n * rows // 2, CORE_RATE)
            elif step in (1, 2) and (step == 1) == y_first:
                ready = send("y", (n if y_first else 1) * rows // 4)
            elif step in (1, 2):
                crossed.add(index)
                ready = send("x", (n - 1) * rows // (4 if y_first else 2))
            elif step in (3, 4):
                ready = send("z", rows // 4)
            elif step == 5:
                ready = send("y", rows // 4)
            elif step == 6:
                ready = send("core", rows // 2, CORE_RATE)
            else:
                return
        elif kind == "extra":
            if step == 2:
                return
            rows = extras[index][0]
            ready = send("core", rows, CORE_RATE) if step == 0 else send("x", rows // 2)
        else:
            if step == 4:
                return
            rows = smalls[index][0]
            link, rows = (("core", n * rows), ("x", rows), ("y", rows), ("z", 4 * rows))[step]
            ready = send(link, rows, CORE_RATE if link == "core" else LINK_RATE)
        pending.append((ready, len(pending), kind, index, step + 1))

    for number in range(len(segments) + 1):
        order = []
        last = number == len(segments)
        if not last:
            now += segments[number]
            released = [("chunk", i) for i, chunk in enumerate(chunks) if chunk[3] == number]
            released += [("extra", i) for i, extra in enumerate(extras) if extra[1] == number]
            released += [("small", i) for i, small in enumerate(smalls) if small[1] == number]
            for kind, index in released:
                execute(kind, index, 0)
                order.append((kind, index, 0))
        while pending:
            pending.sort()
            first = 0
            if len(crossed) < len(chunks):
                while first < len(pending) and pending[first][2:] == ("extra", pending[first][3], 1):
                    first += 1
            if first == len(pending) or (not last and pending[first][0] + MARGIN > now):
                break
            ready, unused, kind, index, step = pending.pop(first)
            now = max(now, ready)
            execute(kind, index, step)
            order.append((kind, index, step))
        plan.append(order)
    return plan, now


class Reducer:
    def __init__(self, n, groups, chunks, field, total, total_out, small, small_out, small_spans, buffers):
        (
            self.from_core, self.from_blk, self.from_y, self.from_z,
            self.small_core, self.small_blk, self.small_y, self.small_z,
            self.sends, self.receives, self.small_sends, self.small_receives, self.stores,
        ) = buffers
        self.n, self.chunks, self.field, self.total, self.total_out = n, chunks, field, total, total_out
        self.small, self.small_out, self.small_spans = small, small_out, small_spans
        self.depth = depth = groups // 4
        self.group = group = lax.axis_index("dp")
        self.part = part = lax.axis_index("blk")
        self.core = lax.rem(group, 2)
        self.side = lax.rem(lax.div(group, 2), 2)
        self.level = lax.div(group, 4)
        self.core_peer = (group + 1 - 2 * self.core, part)
        self.side_peer = (group + 2 - 4 * self.side, part)
        self.blk_peers = [(group, lax.rem(part + step, n)) for step in range(1, n)]
        self.z_peers = [(lax.rem(group + 4 * step, groups), part) for step in range(1, depth)]
        self.per_chunk = 4 + (n - 1) + 2 * (depth - 1)

    def greet(self, far_peer=None, has_far=None):
        peers = [self.core_peer, self.side_peer] + self.blk_peers + self.z_peers
        barrier = pltpu.get_barrier_semaphore()
        for peer in peers:
            pl.semaphore_signal(barrier, inc=1, device_id=peer, device_id_type=pl.DeviceIdType.MESH)
        if far_peer is not None:

            @pl.when(has_far)
            def _():
                pl.semaphore_signal(barrier, inc=1, device_id=far_peer, device_id_type=pl.DeviceIdType.MESH)

            self.greetings = jnp.where(has_far, len(peers) + 1, len(peers))
        else:
            self.greetings = len(peers)

    def enter(self):
        pl.semaphore_wait(pltpu.get_barrier_semaphore(), self.greetings)

    def copy(self, source, target, sem, peer):
        return pltpu.make_async_remote_copy(
            src_ref=source, dst_ref=target, send_sem=self.sends.at[sem], recv_sem=self.receives.at[sem],
            device_id=peer, device_id_type=pl.DeviceIdType.MESH,
        )

    def small_copy(self, source, target, sem, peer):
        return pltpu.make_async_remote_copy(
            src_ref=source, dst_ref=target, send_sem=self.small_sends.at[sem],
            recv_sem=self.small_receives.at[sem], device_id=peer, device_id_type=pl.DeviceIdType.MESH,
        )

    def span(self, start, size):
        return pl.ds(pl.multiple_of(start, 16), size)

    def copies(self, index, step):
        start, rows, y_first, unused = self.chunks[index]
        n, depth, part = self.n, self.depth, self.part
        half, quarter = rows // 2, rows // 4
        piece = quarter // depth
        own_half = start + self.core * half
        own_quarter = own_half + self.side * quarter
        sem = index * self.per_chunk
        if step == 0:
            theirs = self.span(start + (1 - self.core) * half, half)
            return [
                self.copy(
                    self.field.at[:, theirs], self.from_core.at[:, pl.ds(start // 2, half)], sem, self.core_peer
                )
            ]
        if step in (1, 2) and (step == 1) == y_first:
            theirs = self.span(own_half + (1 - self.side) * quarter, quarter)
            into = pl.ds(start // 4, quarter)
            if y_first:
                return [self.copy(self.field.at[:, theirs], self.from_y.at[:, into], sem + 1, self.side_peer)]
            return [self.copy(self.field.at[part, theirs], self.from_y.at[0, into], sem + 1, self.side_peer)]
        if step in (1, 2):
            if y_first:
                mine, into = self.span(own_quarter, quarter), pl.ds(start // 2, quarter)
            else:
                mine, into = self.span(own_half, half), pl.ds(start // 2, half)
            return [
                self.copy(
                    self.field.at[lax.rem(part + hop, n), mine], self.from_blk.at[hop - 1, into],
                    sem + 3 + hop, self.blk_peers[hop - 1],
                )
                for hop in range(1, n)
            ]
        if step == 3:
            copies = []
            for hop in range(1, depth):
                theirs = self.span(own_quarter + lax.rem(self.level + hop, depth) * piece, piece)
                copies.append(
                    self.copy(
                        self.field.at[part, theirs], self.from_z.at[hop - 1, pl.ds(start // 4 // depth, piece)],
                        sem + 2 + n + hop, self.z_peers[hop - 1],
                    )
                )
            return copies
        if step == 4:
            mine = self.span(own_quarter + self.level * piece, piece)
            return [
                self.copy(
                    self.total.at[mine], self.total.at[mine], sem + 1 + n + depth + hop, self.z_peers[hop - 1]
                )
                for hop in range(1, depth)
            ]
        if step == 5:
            mine = self.span(own_quarter, quarter)
            return [self.copy(self.total.at[mine], self.total.at[mine], sem + 2, self.side_peer)]
        mine = self.span(own_half, half)
        return [self.copy(self.total.at[mine], self.total.at[mine], sem + 3, self.core_peer)]

    def add(self, part, start, size, terms, result=None):
        step = min(size, 64)

        @pl.loop(0, size // step)
        def _(block):
            here = self.span(start + block * step, step)
            value = self.field[part, here, :].astype(F32)
            for ref, index, begin in terms:
                value = value + ref[index, self.span(begin + block * step, step), :].astype(F32)
            if result is None:
                self.field[part, here, :] = value.astype(BF16)
            else:
                result[here, :] = value.astype(BF16)

    def store(self, index):
        rows = pl.ds(self.chunks[index][0], self.chunks[index][1])
        return pltpu.make_async_copy(self.total.at[rows], self.total_out.at[rows], self.stores.at[index])

    def chunk_step(self, index, step):
        start, rows, y_first, unused = self.chunks[index]
        n, depth, part = self.n, self.depth, self.part
        half, quarter = rows // 2, rows // 4
        piece = quarter // depth
        own_half = start + self.core * half
        own_quarter = own_half + self.side * quarter
        if step > 0:
            for copy in self.copies(index, step - 1):
                copy.wait()
        if step == 1:
            for b in range(n):
                self.add(b, own_half, half, [(self.from_core, b, start // 2)])
        elif step in (2, 3) and (step == 2) == y_first:
            for b in range(n) if y_first else [part]:
                self.add(b, own_quarter, quarter, [(self.from_y, b if y_first else 0, start // 4)])
        elif step in (2, 3):
            begin, size = (own_quarter, quarter) if y_first else (own_half, half)
            self.add(part, begin, size, [(self.from_blk, hop, start // 2) for hop in range(n - 1)])
        elif step == 4:
            self.add(
                part, own_quarter + self.level * piece, piece,
                [(self.from_z, hop, start // 4 // depth) for hop in range(depth - 1)], self.total,
            )
        if step < 7:
            for copy in self.copies(index, step):
                copy.start()
        else:
            self.store(index).start()

    def small_copies(self, index, step):
        part, n = self.part, self.n
        rows = pl.ds(*self.small_spans[index])
        first = index * (n + self.depth)
        if step == 0:
            return [self.small_copy(self.small.at[0, :, rows], self.small_core.at[:, rows], first, self.core_peer)]
        if step == 1:
            return [
                self.small_copy(
                    self.small.at[1, lax.rem(part + hop, n), rows], self.small_blk.at[hop - 1, rows], first + hop,
                    self.blk_peers[hop - 1],
                )
                for hop in range(1, n)
            ]
        if step == 2:
            return [
                self.small_copy(self.small.at[1, part, rows], self.small_y.at[rows], first + n, self.side_peer)
            ]
        return [
            self.small_copy(
                self.small_y.at[rows], self.small_z.at[hop - 1, rows], first + n + hop, self.z_peers[hop - 1]
            )
            for hop in range(1, self.depth)
        ]

    def small_step(self, index, step):
        part = self.part
        rows = pl.ds(*self.small_spans[index])
        if step > 0:
            for copy in self.small_copies(index, step - 1):
                copy.wait()
        if step == 1:
            self.small[1, :, rows] = self.small[0, :, rows] + self.small_core[:, rows]
        elif step == 2:
            held = self.small[1, part, rows]
            for hop in range(self.n - 1):
                held = held + self.small_blk[hop, rows]
            self.small[1, part, rows] = held
        elif step == 3:
            self.small_y[rows] = self.small_y[rows] + self.small[1, part, rows]
        elif step == 4:
            held = self.small_y[rows]
            for hop in range(self.depth - 1):
                held = held + self.small_z[hop, rows]
            self.small_out[rows] = held
        if step < 4:
            for copy in self.small_copies(index, step):
                copy.start()

    def finish(self):
        for index in range(len(self.chunks)):
            self.store(index).wait()


def reducer_scratch(n, groups, chunks, rows, small_shape):
    depth = groups // 4
    per_chunk = 4 + (n - 1) + 2 * (depth - 1)
    return [
        pltpu.VMEM((n, rows // 2, WIDE), BF16),
        pltpu.VMEM((n - 1, rows // 2, WIDE), BF16),
        pltpu.VMEM((n, rows // 4, WIDE), BF16),
        pltpu.VMEM((depth - 1, rows // 4 // depth, WIDE), BF16),
        pltpu.VMEM((n, *small_shape), F32),
        pltpu.VMEM((n - 1, *small_shape), F32),
        pltpu.VMEM(small_shape, F32),
        pltpu.VMEM((depth - 1, *small_shape), F32),
        pltpu.SemaphoreType.DMA((len(chunks) * per_chunk,)),
        pltpu.SemaphoreType.DMA((len(chunks) * per_chunk,)),
        pltpu.SemaphoreType.DMA((2 * (n + depth),)),
        pltpu.SemaphoreType.DMA((2 * (n + depth),)),
        pltpu.SemaphoreType.DMA((len(chunks),)),
    ]


def reduce_kernel(n, groups, chunks, plan, part_rows, *refs):
    sources, refs = refs[: len(part_rows)], refs[len(part_rows) :]
    small_in, total_out, small_out, field, total, small, load_sem = refs[:7]
    loads = []
    start = 0
    for index, source in enumerate(sources):
        loads.append(
            pltpu.make_async_copy(source, field.at[:, pl.ds(start, part_rows[index])], load_sem.at[index])
        )
        loads[-1].start()
        start += part_rows[index]
    spans = [(0, small_in.shape[1])]
    reducer = Reducer(n, groups, chunks, field, total, total_out, small, small_out, spans, refs[7:])
    small[0] = small_in[...]
    reducer.greet()
    reducer.enter()
    for load in loads:
        load.wait()
    for order in plan:
        for kind, index, step in order:
            if kind == "chunk":
                reducer.chunk_step(index, step)
            else:
                reducer.small_step(index, step)
    reducer.finish()


def reduce_all(n, groups, parts, small):
    part_rows = [part.shape[1] for part in parts]
    rows = sum(part_rows)
    chunk_rows = max(16 * groups, rows // 8)
    chunks = [(start, chunk_rows, False, 0) for start in range(0, rows, chunk_rows)]
    plan, unused = plan_steps(n, chunks, [], [(small.shape[1], 0)], [0.0])
    small_shape = small.shape[1:]
    vm = pl.BlockSpec(memory_space=pltpu.VMEM)
    hbm = pl.BlockSpec(memory_space=pl.ANY)
    return pl.pallas_call(
        functools.partial(reduce_kernel, n, groups, chunks, plan, part_rows),
        in_specs=[hbm] * len(parts) + [vm],
        out_specs=[hbm, vm],
        out_shape=[out_like((rows, WIDE), BF16), out_like(small_shape, F32)],
        scratch_shapes=[
            pltpu.VMEM((n, rows, WIDE), BF16),
            pltpu.VMEM((rows, WIDE), BF16),
            pltpu.VMEM((2, n, *small_shape), F32),
            pltpu.SemaphoreType.DMA((len(parts),)),
            *reducer_scratch(n, groups, chunks, rows, small_shape),
        ],
        compiler_params=pltpu.CompilerParams(
            vmem_limit_bytes=VMEM_LIMIT, collective_id=0, has_side_effects=True
        ),
    )(*parts, small)


Y_FIRST = [letter == "y" for letter in "xyyyyxxyyyyyyxyx"]
BACK_SEGMENTS = [
    1.5, 1.3, 2.9, 2.9, 2.9, 2.9, 1.4, 2.8, 3.2, 1.9, 2.4, 2.4, 2.9, 2.9, 1.4, 1.1, 1.1,
]


def back_chunks(half, hidden_rows):
    released = [(half, 0)] * (2 * hidden_rows // half + 1)
    released += [(half, segment) for segment in (6, 7, 7, 8, 14, 15, 16)]
    chunks = []
    start = 0
    for index, (rows, segment) in enumerate(released):
        chunks.append((start, rows, Y_FIRST[index % len(Y_FIRST)], segment))
        start += rows
    return chunks


def back_kernel(n, groups, rows_block, chunks, plan, load_plan, *refs):
    feed_refs, refs = refs[:3], refs[3:]
    streamed, refs = refs[: len(load_plan)], refs[len(load_plan) :]
    (
        target_row, memory_row, cross_query, cross_grad, cross_keys,
        cross_lse, cross_delta, feed_sums, in_bias_grad, gain, first_rstd, self_lse,
        total_out, small_out, memory_out, input_out,
        field, total, small, sums, memory_grad, input_grad, memory_sent, memory_got, input_sent, input_got, pair_low,
        wide, keys_t, query_cols, query_rows, grad_cols, grad_rows, query_grad_t, key_grad, value_grad,
        held, held_low, held_grad, query_low, branch, self_grad, self_delta, g1,
        feed_sem, load_sem, extra_send, extra_recv, extra_store,
    ) = refs[:49]
    refs = refs[49:]
    held_loads, buffers = refs[: len(load_plan)], refs[len(load_plan) :]
    count = cross_query.shape[0]
    length = cross_keys.shape[0]
    tiles = count // TILE
    blocks = count // rows_block
    half = WIDE // n
    group, part = lax.axis_index("dp"), lax.axis_index("blk")
    place = lax.rem(group, 2)
    away = place != part
    owner = (group - place + part, place)

    feed_loads = []
    start = 0
    for index, source in enumerate(feed_refs):
        rows = source.shape[1]
        feed_loads.append(
            pltpu.make_async_copy(source, field.at[:, pl.ds(start, rows)], feed_sem.at[index])
        )
        feed_loads[-1].start()
        start += rows
    loads = [
        pltpu.make_async_copy(source, target, load_sem.at[index])
        for index, (source, target) in enumerate(zip(streamed, held_loads))
    ]
    for load in loads:
        load.start()
    cross_values = held_loads[0]
    memory_pieces = [held_loads[1].at[step] for step in range(n)]
    held_loads = held_loads[2:]
    (
        pair_weight, first_low, query_weight, g2, first_normal, self_out_weight, self_attended_t,
        self_keys, self_values, self_query,
    ) = held_loads[:10]
    input_pieces = [held_loads[10].at[step] for step in range(n)]
    self_in_weight = held_loads[11]

    spans = [(0, 8), (8, small_out.shape[0] - 8)]
    reducer = Reducer(n, groups, chunks, field, total, total_out, small, small_out, spans, buffers)
    reducer.greet(owner, away)

    extras = (
        (memory_sent, memory_got, memory_grad, memory_out), (input_sent, input_got, input_grad, input_out)
    )

    def extra_copy(index, hop):
        sent, got, *unused = extras[index]
        return pltpu.make_async_remote_copy(
            src_ref=sent.at[hop], dst_ref=got.at[hop],
            send_sem=extra_send.at[2 * index + hop], recv_sem=extra_recv.at[2 * index + hop],
            device_id=reducer.core_peer if hop == 0 else owner, device_id_type=pl.DeviceIdType.MESH,
        )

    def extra_store_copy(index, from_owner):
        sent, got, unused, out = extras[index]
        return pltpu.make_async_copy((got if from_owner else sent).at[1], out, extra_store.at[index])

    def extra_step(index, step):
        sent, got, result, unused = extras[index]
        if step == 0:
            extra_copy(index, 0).start()
        elif step == 1:
            extra_copy(index, 0).wait()

            @pl.loop(0, blocks)
            def _(block):
                rows = dyn(block, rows_block)
                value = result[rows, :] + got[0, rows, :].astype(F32)
                sent[1, rows, :] = value.astype(BF16)

            @pl.when(away)
            def _():
                extra_copy(index, 1).start()

            @pl.when(jnp.logical_not(away))
            def _():
                extra_store_copy(index, False).start()
        else:

            @pl.when(away)
            def _():
                extra_copy(index, 1).wait()
                extra_store_copy(index, True).start()

    def run_steps(number):
        for kind, index, step in plan[number]:
            if kind == "chunk":
                reducer.chunk_step(index, step)
            elif kind == "small":
                reducer.small_step(index, step)
            else:
                extra_step(index, step)

    def wait_loads(first, last):
        for load in loads[first:last]:
            load.wait()

    spread_row(memory_row, wide)
    transpose_rows(cross_keys, keys_t)
    for load in feed_loads:
        load.wait()
    reducer.enter()
    run_steps(0)
    prepare_back(tiles, cross_query, cross_grad, query_cols, query_rows, grad_cols, grad_rows)
    clear(query_grad_t)
    sums[...] = jnp.zeros(sums.shape, F32)
    run_steps(1)
    wait_loads(0, 1)
    for tile in range(tiles):
        attend_back(
            tile, 0, length // TILE, target_row, place * count, wide, place * count, False,
            query_cols, query_rows, grad_cols, grad_rows, cross_keys, keys_t, cross_values,
            cross_lse, cross_delta, query_grad_t, key_grad, value_grad, held, held_low, held_grad, tile == 0,
        )
        run_steps(2 + tile)
    base = 2 * in_bias_grad.shape[1] // n + half
    wait_loads(1, 9)
    query_finish(tiles, query_grad_t, query_low, sums, 2, True)
    spread_parts(n, tn(first_low[...], query_low[...]), field, base)
    run_steps(6)
    for side, source in ((0, key_grad), (1, value_grad)):

        @pl.loop(0, length // rows_block)
        def _(block):
            rows = dyn(block, rows_block)
            value = source[rows, :]
            source[rows, :] = jnp.zeros(value.shape, F32)
            pair_low[side, rows, :] = value.astype(BF16)
            if side == 1:
                sums[3:4, :] += col_sum(value)

        spread_parts(
            n, row_product(n, place, memory_pieces, pair_low.at[side]), field, base + half + side * half
        )
    run_steps(7)
    first_back(
        blocks, rows_block, g2, query_low, query_weight, first_normal, first_rstd, gain, self_out_weight,
        g1, branch, self_grad, sums, 4,
    )
    spread_parts(n, nn(self_attended_t[...], branch[...]), field, base + 3 * half)
    write_delta(tiles, self_grad, self_attended_t, self_delta)
    small[...] = jnp.zeros(small.shape, F32)
    wide_half = in_bias_grad.shape[1] // n
    for b in range(n):
        here = slice(b * half, (b + 1) * half)
        small[0, b, 8:13, :] = sums[2:7, here]
        small[0, b, 13:19, :] = feed_sums[0:6, here]
        for row in range(wide_half // half):
            begin = b * wide_half + row * half
            small[0, b, 19 + row : 20 + row, :] = in_bias_grad[:, begin : begin + half]
    run_steps(8)

    wait_loads(9, len(loads))
    spread_row(target_row, wide)
    transpose_rows(self_keys, keys_t)
    prepare_back(tiles, self_query, self_grad, query_cols, query_rows, grad_cols, grad_rows)
    clear(query_grad_t)
    run_steps(9)
    for tile in range(tiles):
        attend_back(
            tile, 0, place * tiles + tile + 1, target_row, place * count, wide, place * count, True,
            query_cols, query_rows, grad_cols, grad_rows, self_keys, keys_t, self_values,
            self_lse, self_delta, query_grad_t, key_grad, value_grad, held, held_low, held_grad,
        )
        run_steps(10 + tile)
    query_finish(tiles, query_grad_t, query_low, sums, 0, False)
    spread_parts(n, tn(input_pieces[0][...], query_low[...]), field, base + 4 * half)
    run_steps(14)
    spread_parts(n, row_product(n, place, input_pieces, key_grad), field, base + 5 * half)
    run_steps(15)
    spread_parts(n, row_product(n, place, input_pieces, value_grad), field, base + 6 * half)
    run_steps(16)
    number = 17
    for step in range(n):
        spot = lax.rem(place + n - step, n)
        for block in range(blocks):
            rows = dyn(spot * blocks + block, rows_block)
            here = slice(block * rows_block, (block + 1) * rows_block)
            key_low, value_part = key_grad[rows, :].astype(BF16), value_grad[rows, :]
            sums[1:2, :] += col_sum(value_part)
            back = nt(key_low, self_in_weight[:, WIDE : 2 * WIDE])
            back += nt(value_part.astype(BF16), self_in_weight[:, 2 * WIDE :])
            if step == 0:
                input_grad[here, :] = back + g1[here, :] + nt(query_low[here, :], self_in_weight[:, :WIDE])
            else:
                input_sent[0, here, :] = back.astype(BF16)
            if step == n - 1 and block == blocks - 1:
                for b in range(n):
                    small[0, b, 0:2, :] = sums[0:2, b * half : (b + 1) * half]
            run_steps(number)
            number += 1
    for step in range(n):
        spot = lax.rem(place + n - step, n)
        for block in range(blocks):
            rows = dyn(spot * blocks + block, rows_block)
            here = slice(block * rows_block, (block + 1) * rows_block)
            back = nt(pair_low[0, rows, :], pair_weight[:, :WIDE]) + nt(pair_low[1, rows, :], pair_weight[:, WIDE:])
            if step == 0:
                memory_grad[here, :] = back
            else:
                memory_sent[0, here, :] = back.astype(BF16)
            run_steps(number)
            number += 1
    run_steps(number)
    for index in range(2):

        @pl.when(away)
        def _():
            extra_store_copy(index, True).wait()

        @pl.when(jnp.logical_not(away))
        def _():
            extra_store_copy(index, False).wait()

    reducer.finish()


def back_and_reduce(n, groups, rows_block, feed_grads, streamed, resident):
    count, features = resident[2].shape
    length = n * count
    hidden_rows = feed_grads[0].shape[1]
    half = features // n
    rows = sum(part.shape[1] for part in feed_grads) + 7 * half
    chunks = back_chunks(half, hidden_rows)
    steps = n * (count // rows_block)
    segments = BACK_SEGMENTS + [2.2 / steps] * steps + [2.0 / steps] * steps
    last = len(segments) - 1
    extras = [(count, last), (count, last - steps)]
    smalls = [(8, last - steps), (16, 8)]
    plan, unused = plan_steps(n, chunks, extras, smalls, segments)
    small_shape = (-(-(19 + hidden_rows // half) // 8) * 8, half)
    vm = pl.BlockSpec(memory_space=pltpu.VMEM)
    hbm = pl.BlockSpec(memory_space=pl.ANY)
    low_rows = pltpu.VMEM((count, features), BF16)
    wide_rows = pltpu.VMEM((count, features), F32)
    columns = pltpu.VMEM((features, 2 * count), BF16)
    doubled = pltpu.VMEM((2 * count, features), BF16)
    all_wide = pltpu.VMEM((length, features), F32)
    sent = pltpu.VMEM((2, count, features), BF16)
    held = (features // PAIR, BACK_KEYS, 2 * TILE)
    return pl.pallas_call(
        functools.partial(back_kernel, n, groups, rows_block, chunks, plan, [part.shape for part in streamed]),
        in_specs=[hbm] * (len(feed_grads) + len(streamed)) + [vm] * len(resident),
        out_specs=[hbm, vm, hbm, hbm],
        out_shape=[
            out_like((rows, WIDE), BF16), out_like(small_shape, F32),
            out_like((count, features), BF16), out_like((count, features), BF16),
        ],
        scratch_shapes=[
            pltpu.VMEM((n, rows, WIDE), BF16), pltpu.VMEM((rows, WIDE), BF16),
            pltpu.VMEM((2, n, *small_shape), F32), pltpu.VMEM((8, features), F32),
            wide_rows, wide_rows, sent, sent, sent, sent, pltpu.VMEM((2, length, features), BF16),
            pltpu.VMEM((length, TILE), jnp.int32), pltpu.VMEM((features, length), BF16),
            columns, doubled, columns, doubled,
            pltpu.VMEM((features, count), F32), all_wide, all_wide,
            pltpu.VMEM(held, F32), pltpu.VMEM(held, BF16), pltpu.VMEM(held, BF16),
            low_rows, low_rows, low_rows, pltpu.VMEM((features // PAIR, 2 * count), F32), wide_rows,
            pltpu.SemaphoreType.DMA((len(feed_grads),)), pltpu.SemaphoreType.DMA((len(streamed),)),
            pltpu.SemaphoreType.DMA((4,)), pltpu.SemaphoreType.DMA((4,)), pltpu.SemaphoreType.DMA((2,)),
            *[pltpu.VMEM(part.shape, part.dtype) for part in streamed],
            *reducer_scratch(n, groups, chunks, rows, small_shape),
        ],
        compiler_params=pltpu.CompilerParams(
            vmem_limit_bytes=VMEM_LIMIT, collective_id=0, has_side_effects=True
        ),
    )(*feed_grads, *streamed, *resident)


def spread_row(row_ref, wide_ref):
    @pl.loop(0, row_ref.shape[1] // TILE)
    def _(block):
        wide_ref[dyn(block, TILE), :] = jnp.broadcast_to(row_ref[:, dyn(block, TILE)], (TILE, TILE)).T


def attend_whole(
    tiles, query_row_ref, first_query, key_wide_ref, causal, query_cols, keys, values_t, attended_t, lse_ref,
    held, held_low,
):
    pairs = WIDE // PAIR
    length = keys.shape[0]

    @pl.loop(0, tiles)
    def _(tile):
        begin = pl.multiple_of(first_query + tile * TILE, TILE)
        allowed = key_wide_ref[...] == query_row_ref[:, pl.ds(begin, TILE)]
        if causal:
            key_position = lax.broadcasted_iota(jnp.int32, (length, TILE), 0)
            query_position = begin + lax.broadcasted_iota(jnp.int32, (length, TILE), 1)
            allowed = allowed & (key_position <= query_position)
        bias = jnp.where(allowed, 0.0, MASKED)
        bias = jnp.concatenate([bias, bias], axis=1)
        both = dyn(tile, 2 * TILE)
        peaks, shares = [], []
        for pair in range(pairs):
            lanes = slice(pair * PAIR, (pair + 1) * PAIR)
            scores = nn(keys[:, lanes], query_cols[lanes, both]) + bias
            held[pair] = scores
            peaks.append(jnp.max(scores, axis=0, keepdims=True))
        for pair in range(pairs):
            weights = jnp.exp(held[pair] - peaks[pair])
            total = col_sum(weights)
            held_low[pair] = weights.astype(BF16)
            lse_ref[pair : pair + 1, both] = peaks[pair] + jnp.log(total)
            shares.append(1.0 / total)
        for pair in range(pairs):
            share = shares[pair]
            mixed = nn(values_t[pair * PAIR : (pair + 1) * PAIR, :], held_low[pair])
            first = slice(pair * PAIR, pair * PAIR + HEAD)
            second = slice(pair * PAIR + HEAD, (pair + 1) * PAIR)
            attended_t[first, dyn(tile, TILE)] = (mixed[:HEAD, :TILE] * share[:, :TILE]).astype(BF16)
            attended_t[second, dyn(tile, TILE)] = (mixed[HEAD:, TILE:] * share[:, TILE:]).astype(BF16)


FORWARD_LOADS = 7
FORWARD_STORES = 16


def forward_kernel(n, groups, rows_block, *refs):
    (
        inputs, memory, cotangent, *weights_in
    ) = refs[: 3 + FORWARD_LOADS]
    refs = refs[3 + FORWARD_LOADS :]
    (
        target_here, memory_here, in_bias, self_out_bias, first_gain, first_shift, cross_bias, cross_out_bias,
        second_gain, second_shift, feed_bias, down_bias, last_gain, last_shift,
    ) = refs[:14]
    refs = refs[14:]
    stores_out, refs = refs[:FORWARD_STORES], refs[FORWARD_STORES:]
    (
        layer_output, lse_one, lse_two, delta_ref, first_rstd, sums_out, in_bias_grad, target_row, memory_row,
    ) = refs[:9]
    refs = refs[9:]
    held_weights, refs = refs[:FORWARD_LOADS], refs[FORWARD_LOADS:]
    held_stores, refs = refs[:FORWARD_STORES], refs[FORWARD_STORES:]
    (
        self_in_weight, self_out_weight, cross_weight, pair_weight, cross_out_weight, in_weight, down_weight
    ) = held_weights
    (
        input_pieces, memory_pieces, query_low, keys, values, attended_one, first_normal, first_low, cross_query,
        cross_keys, cross_values, grad_out, g2_out, in_grad, down_grad, cross_out_grad,
    ) = held_stores
    (
        cot, output_low, output_got, target_there, memory_there, wide, values_t, cross_values_t, query_cols, held,
        held_low, attended_two, second_normal, second_rstd, second_low, second_low_t, active, slope, third, branch,
        load_sem, store_sem, own_sem, far_send, far_recv, core_send, core_recv,
    ) = refs
    count = inputs.shape[0]
    tiles = count // TILE
    blocks = count // rows_block
    half = WIDE // n
    group, part = lax.axis_index("dp"), lax.axis_index("blk")
    place = lax.rem(group, 2)
    away = place != part
    owner = (group - place + part, place)
    core_peer = (group + 1 - 2 * place, part)
    mesh_type = pl.DeviceIdType.MESH

    loads = [
        pltpu.make_async_copy(source, target, load_sem.at[index])
        for index, (source, target) in enumerate(zip(weights_in, held_weights))
    ]
    for load in loads:
        load.start()
    barrier = pltpu.get_barrier_semaphore()
    pl.semaphore_signal(barrier, inc=1, device_id=core_peer, device_id_type=mesh_type)

    @pl.when(away)
    def _():
        pl.semaphore_signal(barrier, inc=1, device_id=owner, device_id_type=mesh_type)

    pl.semaphore_wait(barrier, jnp.where(away, 2, 1))

    pieces_of = (count // 2, count // 2)
    arrivals = []
    for index, (source, target) in enumerate(((inputs, input_pieces), (memory, memory_pieces))):
        for block in range(2):
            rows = pl.ds(block * (count // 2), count // 2)
            arrivals.append((source.at[rows], target.at[0, rows], 2 * index + block))
    arrivals.append((cotangent, cot, 4))

    def far_copy(entry):
        source, target, sem = entry
        return pltpu.make_async_remote_copy(
            src_ref=source, dst_ref=target, send_sem=far_send.at[sem], recv_sem=far_recv.at[sem],
            device_id=owner, device_id_type=mesh_type,
        )

    def own_copy(entry):
        source, target, sem = entry
        return pltpu.make_async_copy(source, target, own_sem.at[sem])

    def core_copy(source, target, sem):
        return pltpu.make_async_remote_copy(
            src_ref=source, dst_ref=target, send_sem=core_send.at[sem], recv_sem=core_recv.at[sem],
            device_id=core_peer, device_id_type=mesh_type,
        )

    @pl.when(away)
    def _():
        for entry in arrivals:
            far_copy(entry).start()

    @pl.when(jnp.logical_not(away))
    def _():
        for entry in arrivals:
            own_copy(entry).start()

    def arrive(entry):
        @pl.when(away)
        def _():
            far_copy(entry).wait()

        @pl.when(jnp.logical_not(away))
        def _():
            own_copy(entry).wait()

    def forward_copy(index):
        held_piece = (input_pieces, memory_pieces)[index // 2]
        rows = pl.ds((index % 2) * (count // 2), count // 2)
        return core_copy(held_piece.at[0, rows], held_piece.at[1, rows], index)

    segment_copies = [
        core_copy(target_here, target_there, 4), core_copy(memory_here, memory_there, 5)
    ]
    for copy in segment_copies:
        copy.start()

    stores = {}

    def store(index):
        stores[index] = pltpu.make_async_copy(held_stores[index], stores_out[index], store_sem.at[index])
        stores[index].start()

    for copy in segment_copies:
        copy.wait()
    target_row[...] = jnp.where(away, target_there[...], target_here[...])
    memory_row[...] = jnp.where(away, memory_there[...], memory_here[...])
    spread_row(target_row, wide)
    loads[0].wait()

    def project(piece, block, spot):
        rows = slice(block * (count // 2), (block + 1) * (count // 2))
        source = input_pieces[piece, rows, :]
        field = nn(source, self_in_weight[:, WIDE:])
        here = dyn(spot * 2 + block, count // 2)
        keys[here, :] = field[:, :WIDE].astype(BF16)
        value = (field[:, WIDE:] + in_bias[1:2, :]).astype(BF16)
        values[here, :] = value
        values_t[:, here] = value.T

        @pl.when(piece == 0)
        def _():
            query = (nn(source, self_in_weight[:, :WIDE]) + in_bias[0:1, :]).astype(BF16)
            query = (query.astype(F32) * SCALE).astype(BF16)
            query_low[rows, :] = query
            for tile in range(count // 2 // TILE):
                split_columns(
                    query[tile * TILE : (tile + 1) * TILE, :].T, query_cols, block * (count // 2 // TILE) + tile
                )

    def project_memory(piece, spot):
        field = nn(memory_pieces[piece], pair_weight[...])
        here = dyn(spot, count)
        cross_keys[here, :] = field[:, :WIDE].astype(BF16)
        value = (field[:, WIDE:] + cross_bias[1:2, :]).astype(BF16)
        cross_values[here, :] = value
        cross_values_t[:, here] = value.T

    early = jnp.where(away, 1, 0)

    @pl.when(jnp.logical_not(away))
    def _():
        for index in range(4):
            own_copy(arrivals[index]).wait()
            forward_copy(index).start()

    @pl.when(away)
    def _():
        for index in range(2):
            forward_copy(index).wait_recv()

    for block in range(2):
        project(early, block, part)
    loads[3].wait()

    @pl.when(away)
    def _():
        for index in range(2, 4):
            forward_copy(index).wait_recv()

    project_memory(early, part)
    for block in range(2):

        @pl.when(away)
        def _():
            far_copy(arrivals[block]).wait()
            forward_copy(block).start()

        @pl.when(jnp.logical_not(away))
        def _():
            forward_copy(block).wait_recv()

        project(1 - early, block, 1 - part)
    for index in range(2):
        forward_copy(index).wait_send()
    store(0)
    store(2)
    store(3)
    store(4)
    attend_whole(
        tiles, target_row, place * count, wide, True, query_cols, keys, values_t, attended_one, lse_one,
        held, held_low,
    )
    store(5)
    for load in loads[1:3]:
        load.wait()

    @pl.when(away)
    def _():
        for index in range(2, 4):
            far_copy(arrivals[index]).wait()
            forward_copy(index).start()

    @pl.loop(0, blocks)
    def _(block):
        rows = dyn(block, rows_block)
        attended = attended_one[:, rows].T
        field = input_pieces[0, rows, :].astype(F32) + nn(attended, self_out_weight[...]) + self_out_bias[...]
        normal, rstd = normalize(field)
        first_normal[rows, :] = normal
        first_rstd[rows, :] = rstd
        low = (normal * first_gain[...] + first_shift[...]).astype(BF16)
        first_low[rows, :] = low
        query = (nn(low, cross_weight[...]) + cross_bias[0:1, :]).astype(BF16)
        query = (query.astype(F32) * SCALE).astype(BF16)
        cross_query[rows, :] = query
        for tile in range(rows_block // TILE):
            split_columns(
                query[tile * TILE : (tile + 1) * TILE, :].T, query_cols, block * (rows_block // TILE) + tile
            )

    store(6)
    store(7)
    store(8)

    @pl.when(jnp.logical_not(away))
    def _():
        for index in range(2, 4):
            forward_copy(index).wait_recv()

    project_memory(1 - early, 1 - part)
    for index in range(2, 4):
        forward_copy(index).wait_send()
    store(1)
    store(9)
    store(10)
    spread_row(memory_row, wide)
    attend_whole(
        tiles, target_row, place * count, wide, False, query_cols, cross_keys, cross_values_t, attended_two, lse_two,
        held, held_low,
    )
    for load in loads[4:]:
        load.wait()

    @pl.loop(0, blocks)
    def _(block):
        rows = dyn(block, rows_block)
        attended = attended_two[:, rows].T
        first = first_normal[rows, :] * first_gain[...] + first_shift[...]
        field = first + nn(attended, cross_out_weight[...]) + cross_out_bias[...]
        normal, rstd = normalize(field)
        second_normal[rows, :] = normal
        second_rstd[rows, :] = rstd
        second = normal * second_gain[...] + second_shift[...]
        third[rows, :] = second + down_bias[...]
        low = second.astype(BF16)
        second_low[rows, :] = low
        second_low_t[:, rows] = low.T

    chunks, chunk_size = in_weight.shape[1] // WIDE, WIDE
    arrive(arrivals[4])

    @pl.loop(0, chunks // 2)
    def _(chunk):
        lanes = dyn(chunk, 2 * chunk_size)
        hidden = nn(second_low[...], in_weight[:, lanes]) + feed_bias[:, lanes]
        value, derivative = gate(hidden)
        value = value.astype(BF16)
        active[:, lanes] = value
        slope[:, lanes] = derivative
        third[...] += nn(value, down_weight[lanes, :])

    sums_out[...] = jnp.zeros(sums_out.shape, F32)

    @pl.loop(0, blocks)
    def _(block):
        rows = dyn(block, rows_block)
        normal, rstd = normalize(third[rows, :])
        output_low[rows, :] = (normal * last_gain[...] + last_shift[...]).astype(BF16)
        outer = cot[rows, :].astype(F32)
        grad = normalize_back(outer, last_gain[...], normal, rstd)
        third[rows, :] = grad
        low = grad.astype(BF16)
        branch[rows, :] = low
        sums_out[0:1, :] += col_sum(outer * normal)
        sums_out[1:2, :] += col_sum(outer)
        sums_out[2:3, :] += col_sum(low.astype(F32))

    output_copy = (output_low, output_got, 5)

    @pl.when(away)
    def _():
        far_copy(output_copy).start()

    per_half = chunks // n

    @pl.loop(0, chunks)
    def _(chunk):
        lanes = dyn(chunk, chunk_size)
        share = tn(active[:, lanes], branch[...]).astype(BF16)
        down_grad[lax.div(chunk, per_half), dyn(lax.rem(chunk, per_half), chunk_size), :] = share
        inner = nt(branch[...], down_weight[lanes, :])
        hidden_grad = (inner * slope[:, lanes]).astype(BF16)
        in_bias_grad[:, lanes] = col_sum(hidden_grad.astype(F32))
        third[...] += nt(hidden_grad, in_weight[:, lanes])
        share = nn(second_low_t[...], hidden_grad).astype(BF16)
        for b in range(n):
            in_grad[b, dyn(chunk, half), :] = share[b * half : (b + 1) * half, :]

    store(13)
    store(14)

    @pl.loop(0, blocks)
    def _(block):
        rows = dyn(block, rows_block)
        outer = third[rows, :]
        normal = second_normal[rows, :]
        grad = normalize_back(outer, second_gain[...], normal, second_rstd[rows, :])
        g2_out[rows, :] = grad
        low = grad.astype(BF16)
        branch[rows, :] = low
        sums_out[3:4, :] += col_sum(outer * normal)
        sums_out[4:5, :] += col_sum(outer)
        sums_out[5:6, :] += col_sum(low.astype(F32))
        grad_out[rows, :] = nt(low, cross_out_weight[...]).astype(BF16)

    store(11)
    store(12)
    spread_parts(n, nn(attended_two[...], branch[...]), cross_out_grad, 0)
    store(15)
    write_delta(tiles, grad_out, attended_two, delta_ref)

    @pl.when(away)
    def _():
        far_copy(output_copy).wait()
        layer_output[...] = output_got[...]

    @pl.when(jnp.logical_not(away))
    def _():
        layer_output[...] = output_low[...]

    for index in range(FORWARD_STORES):
        stores[index].wait()


def forward_all(n, groups, rows_block, activations, weights, resident):
    count, features = activations[0].shape
    length = n * count
    hidden = weights[5].shape[1]
    half = features // n
    vm = pl.BlockSpec(memory_space=pltpu.VMEM)
    hbm = pl.BlockSpec(memory_space=pl.ANY)
    low, wide, every = (count, features), (count, features), (length, features)
    stored = [
        ((2, *low), BF16), ((2, *low), BF16), (low, BF16), (every, BF16), (every, BF16), ((features, count), BF16),
        (wide, F32), (low, BF16), (low, BF16), (every, BF16), (every, BF16), (low, BF16), (wide, F32),
        ((n, hidden // n, features), BF16), ((n, hidden // n, features), BF16), ((n, half, features), BF16),
    ]
    stats = out_like((features // PAIR, 2 * count), F32)
    row_like = out_like((1, length), jnp.int32)
    row_scratch = pltpu.VMEM((1, length), jnp.int32)
    held = (features // PAIR, length, 2 * TILE)
    low_rows, wide_rows = pltpu.VMEM(low, BF16), pltpu.VMEM(wide, F32)
    return pl.pallas_call(
        functools.partial(forward_kernel, n, groups, count),
        in_specs=[hbm] * (len(activations) + len(weights)) + [vm] * len(resident),
        out_specs=[hbm] * len(stored) + [vm] * 9,
        out_shape=[out_like(*entry) for entry in stored] + [
            out_like(low, BF16), stats, stats, stats, out_like((count, 1), F32), out_like((8, features), F32),
            out_like((1, hidden), F32), row_like, row_like,
        ],
        scratch_shapes=[
            *[pltpu.VMEM(weight.shape, weight.dtype) for weight in weights],
            *[pltpu.VMEM(*entry) for entry in stored],
            low_rows, low_rows, low_rows, row_scratch, row_scratch,
            pltpu.VMEM((length, TILE), jnp.int32), pltpu.VMEM((features, length), BF16),
            pltpu.VMEM((features, length), BF16), pltpu.VMEM((features, 2 * count), BF16), pltpu.VMEM(held, F32), pltpu.VMEM(held, BF16),
            pltpu.VMEM((features, count), BF16), wide_rows, pltpu.VMEM((count, 1), F32), low_rows,
            pltpu.VMEM((features, count), BF16), pltpu.VMEM((count, hidden), BF16),
            pltpu.VMEM((count, hidden), F32), wide_rows, low_rows,
            pltpu.SemaphoreType.DMA((len(weights),)), pltpu.SemaphoreType.DMA((len(stored),)),
            pltpu.SemaphoreType.DMA((5,)), pltpu.SemaphoreType.DMA((6,)), pltpu.SemaphoreType.DMA((6,)),
            pltpu.SemaphoreType.DMA((6,)), pltpu.SemaphoreType.DMA((6,)),
        ],
        compiler_params=pltpu.CompilerParams(
            vmem_limit_bytes=VMEM_LIMIT, collective_id=1, has_side_effects=True
        ),
    )(*activations, *weights, *resident)


def widen_kernel(plan, source, *outs):
    for out, (start, columns) in zip(outs, plan):
        height = out.shape[0]
        for column in range(columns):
            out[:, column * WIDE : (column + 1) * WIDE] = source[
                start + column * height : start + (column + 1) * height, :
            ].astype(F32)


def finish_kernel(plan, packed, *refs):
    count = len(plan)
    input_low, memory_low, output_low, small, *refs = refs
    (
        *weights, input_grad, memory_grad, layer_output, self_bias, cross_bias, feed_bias,
    ) = refs[: count + 6]
    refs = refs[count + 6 :]
    vectors, refs = refs[:9], refs[9:]
    held, refs = refs[:count], refs[count:]
    wide, refs = refs[:count], refs[count:]
    input_held, memory_held, output_held, input_wide, memory_wide, load_sem, store_sem = refs

    def load(index):
        start, columns = plan[index]
        return pltpu.make_async_copy(
            packed.at[pl.ds(start, held[index].shape[0])], held[index], load_sem.at[index]
        )

    extra = [
        pltpu.make_async_copy(input_low, input_held, load_sem.at[count]),
        pltpu.make_async_copy(memory_low, memory_held, load_sem.at[count + 1]),
    ]
    output = pltpu.make_async_copy(output_low, output_held, load_sem.at[count + 2])
    loads = [load(index) for index in range(count)]
    order = sorted(range(count), key=lambda index: held[index].shape[0])
    for index in order:
        loads[index].start()
    for copy in extra + [output]:
        copy.start()
    stores = []
    for index in order:
        start, columns = plan[index]
        loads[index].wait()
        height = wide[index].shape[0]

        @pl.loop(0, height // 64)
        def _(block):
            for column in range(columns):
                here = pl.ds(pl.multiple_of(column * height + block * 64, 64), 64)
                wide[index][dyn(block, 64), column * WIDE : (column + 1) * WIDE] = held[index][here, :].astype(F32)

        stores.append(pltpu.make_async_copy(wide[index], weights[index], store_sem.at[index]))
        stores[-1].start()
    for index, (source, target, result) in enumerate(
        ((input_held, input_wide, input_grad), (memory_held, memory_wide, memory_grad))
    ):
        extra[index].wait()

        @pl.loop(0, target.shape[0] // 128)
        def _(block):
            target[dyn(block, 128), :] = source[dyn(block, 128), :].astype(F32)

        stores.append(pltpu.make_async_copy(target, result, store_sem.at[count + index]))
        stores[-1].start()
    output.wait()
    stores.append(pltpu.make_async_copy(output_held, layer_output, store_sem.at[count + 2]))
    stores[-1].start()
    self_bias[...] = small[0:2, :]
    cross_bias[...] = small[8:10, :]
    for index, vector in enumerate(vectors):
        vector[...] = small[10 + index, :]
    half = small.shape[1]
    for row in range(feed_bias.shape[0] // half):
        feed_bias[row * half : (row + 1) * half] = small[19 + row, :]
    for copy in stores:
        copy.wait()


def finish_all(n, packed, small, input_low, memory_low, layer_output, hidden):
    count, features = input_low.shape
    half = features // n
    plan, shapes, parts = [], [], []
    start = 0
    for height, columns in (
        (half, hidden // features), (hidden // n, 1), (half, 1), (half, 1), (half, 2), (half, 1), (half, 3)
    ):
        plan.append((start, columns))
        parts.append((height * columns, features))
        shapes.append((height, columns * features))
        start += height * columns
    vm = pl.BlockSpec(memory_space=pltpu.VMEM)
    hbm = pl.BlockSpec(memory_space=pl.ANY)
    wide = (count, features)
    return pl.pallas_call(
        functools.partial(finish_kernel, plan),
        in_specs=[hbm] * 4 + [vm],
        out_specs=[hbm] * (len(plan) + 3) + [vm] * 12,
        out_shape=[out_like(shape, F32) for shape in shapes] + [
            out_like(wide, F32), out_like(wide, F32), out_like(wide, BF16),
            out_like((2, half), F32), out_like((2, half), F32), out_like((hidden // n,), F32),
        ] + [out_like((half,), F32)] * 9,
        scratch_shapes=[pltpu.VMEM(shape, BF16) for shape in parts]
        + [pltpu.VMEM(shape, F32) for shape in shapes]
        + [
            pltpu.VMEM(wide, BF16), pltpu.VMEM(wide, BF16), pltpu.VMEM(wide, BF16), pltpu.VMEM(wide, F32),
            pltpu.VMEM(wide, F32),
            pltpu.SemaphoreType.DMA((len(plan) + 3,)), pltpu.SemaphoreType.DMA((len(plan) + 3,)),
        ],
        compiler_params=pltpu.CompilerParams(vmem_limit_bytes=VMEM_LIMIT),
    )(packed, input_low, memory_low, layer_output, small)


def key_ranges(query_segment, key_segment, tiles, limit):
    edges = query_segment.reshape(tiles, TILE)
    low = jnp.sum((key_segment[None, :] < edges[:, :1]).astype(jnp.int32), axis=1)
    high = jnp.sum((key_segment[None, :] <= edges[:, TILE - 1 :]).astype(jnp.int32), axis=1)
    if limit is not None:
        high = jnp.minimum(high, limit)
    return jnp.stack([low // TILE, (high + TILE - 1) // TILE]).astype(jnp.int32)


def apart(
    n, groups, rows_block, input_rows, memory_rows, cotangent_rows, target_segments, memory_segments,
    self_in_weight, self_in_bias, self_out_weight, self_out_bias, first_gain, first_shift,
    cross_query_weight, cross_pair_weight, cross_bias, cross_out_weight, cross_out_bias,
    second_gain, second_shift, feed_in_weight, feed_in_bias, feed_out_weight, feed_out_bias,
    third_gain, third_shift,
):
    count, features = input_rows.shape
    length = n * count
    hidden = feed_in_weight.shape[1]
    tiles = count // TILE
    half = features // n
    place = lax.axis_index("blk").astype(jnp.int32)

    def row(vector):
        return vector[None, :]

    def shifted(field, step):
        return lax.ppermute(field, "blk", [(s, (s + step) % n) for s in range(n)])

    def shifted_back(field, step):
        return lax.ppermute(field, "blk", [(s, (s - step) % n) for s in range(n)])

    input_pieces = [input_rows] + [shifted(input_rows, step) for step in range(1, n)]
    memory_pieces = [memory_rows] + [shifted(memory_rows, step) for step in range(1, n)]
    target_row, source_row = target_segments[0], memory_segments[0]
    target_here = lax.dynamic_slice_in_dim(target_row, place * count, count, 0)
    self_ranges = key_ranges(
        target_here, target_row, tiles, place * count + TILE * (1 + jnp.arange(tiles, dtype=jnp.int32))
    )
    cross_ranges = key_ranges(target_here, source_row, tiles, None)
    place_one = place[None]
    query_segment = target_here[None, :]
    target_column = target_row[:, None]
    source_column = source_row[:, None]

    stats = out_like((WIDE // PAIR, 2 * count), F32)
    low_rows = out_like((count, features), BF16)
    wide_rows = out_like((count, features), F32)
    low_row_all = out_like((length, features), BF16)
    statistic = out_like((count, 1), F32)
    wide_scratch = pltpu.VMEM((length, TILE), jnp.int32)
    values_t = pltpu.VMEM((features, length), BF16)
    query_cols = pltpu.VMEM((features, 2 * count), BF16)
    query_rows = pltpu.VMEM((2 * count, features), BF16)
    peak = pltpu.VMEM((8, 2 * TILE), F32)
    sums = pltpu.VMEM((features, TILE), F32)
    held = pltpu.VMEM((features // PAIR, KEYS, 2 * TILE), F32)
    held_low = pltpu.VMEM((features // PAIR, KEYS, 2 * TILE), BF16)
    square = 2 * count * features * features

    (
        query, keys, values, attended_t, lse, normal, rstd, first_low, cross_query
    ) = run(
        functools.partial(self_forward, n, rows_block),
        [place_one, self_ranges, *input_pieces, query_segment, target_column,
         self_in_weight, self_in_bias, self_out_weight, row(self_out_bias), row(first_gain),
         row(first_shift), cross_query_weight, cross_bias],
        2,
        [low_rows, low_row_all, low_row_all, out_like((features, count), BF16), stats, wide_rows,
         statistic, low_rows, low_rows],
        [wide_scratch, values_t, query_cols, peak, peak, sums, held, held_low],
        20 * square, 10 << 20,
    )

    (
        layer_output, cross_keys, cross_values, cross_lse, cross_delta, unused, cross_grad, g2,
        in_grad, down_grad, cross_out_grad, feed_sums, in_bias_grad,
    ) = run(
        functools.partial(cross_and_feed, n, rows_block),
        [place_one, cross_ranges, *memory_pieces, query_segment, source_column, cotangent_rows,
         cross_query, normal, row(first_gain), row(first_shift), cross_pair_weight, cross_bias,
         cross_out_weight, row(cross_out_bias), row(second_gain), row(second_shift),
         feed_in_weight, row(feed_in_bias), feed_out_weight, row(feed_out_bias),
         row(third_gain), row(third_shift)],
        2,
        [low_rows, low_row_all, low_row_all, stats, stats, out_like((8, 128), F32), low_rows, wide_rows,
         out_like((n, hidden // n, features), BF16), out_like((n, hidden // n, features), BF16),
         out_like((n, half, features), BF16), out_like((8, features), F32), out_like((1, hidden), F32)],
        [wide_scratch, values_t, query_cols, peak, peak, sums, held, held_low,
         pltpu.VMEM((features, count), BF16), pltpu.VMEM((count, features), F32),
         pltpu.VMEM((count, 1), F32), pltpu.VMEM((count, features), BF16),
         pltpu.VMEM((features, count), BF16), pltpu.VMEM((count, hidden), BF16),
         pltpu.VMEM((count, hidden), F32), pltpu.VMEM((count, features), F32),
         pltpu.VMEM((count, features), BF16), pltpu.VMEM((features, count), BF16)],
        50 * square, 20 << 20,
    )

    back_scratch = [
        wide_scratch, values_t, query_cols, query_rows, query_cols, query_rows,
        pltpu.VMEM((features, count), F32), pltpu.VMEM((length, features), F32),
        pltpu.VMEM((length, features), F32), held, held_low, held_low, pltpu.VMEM((count, features), BF16),
    ]
    sent_like = out_like((max(n - 1, 1), count, features), BF16)
    (
        memory_own, memory_sent, cross_query_grad, cross_pair_grad, self_out_grad, self_grad,
        self_delta, g1, cross_sums,
    ) = run(
        functools.partial(cross_backward, n, rows_block),
        [place_one, cross_ranges, *memory_pieces, query_segment, source_column, cross_query,
         cross_grad, cross_keys, cross_values, cross_lse, cross_delta, g2, normal, rstd, first_low,
         row(first_gain), cross_query_weight, cross_pair_weight, self_out_weight, attended_t],
        2,
        [wide_rows, sent_like, out_like((n, half, features), BF16),
         out_like((n, 2 * half, features), BF16), out_like((n, half, features), BF16), low_rows,
         stats, wide_rows, out_like((8, features), F32)],
        back_scratch + [pltpu.VMEM((count, features), BF16)],
        30 * square, 15 << 20,
    )
    (input_own, input_sent, self_in_grad, self_sums) = run(
        functools.partial(self_backward, n, rows_block),
        [place_one, self_ranges, *input_pieces, query_segment, target_column, query, self_grad,
         keys, values, lse, self_delta, g1, self_in_weight],
        2,
        [wide_rows, sent_like, out_like((n, 3 * half, features), BF16), out_like((8, features), F32)],
        back_scratch,
        30 * square, 15 << 20,
    )

    memory_grad, input_grad = memory_own, input_own
    for step in range(1, n):
        memory_grad = memory_grad + shifted_back(memory_sent[step - 1], step).astype(F32)
        input_grad = input_grad + shifted_back(input_sent[step - 1], step).astype(F32)

    vectors = jnp.concatenate([self_sums[:2], cross_sums[:5], feed_sums[:6]], axis=0)
    count_small = vectors.shape[0]
    small = jnp.concatenate(
        [
            jnp.transpose(vectors.reshape(count_small, n, half), (1, 0, 2)).reshape(n, -1),
            in_bias_grad.reshape(n, -1),
        ],
        axis=1,
    )
    amount = small.shape[1]
    small_rows = -(-amount // (8 * WIDE)) * 8
    small = jnp.pad(small, ((0, 0), (0, small_rows * WIDE - amount))).reshape(n, small_rows, WIDE)
    packed, small = reduce_all(
        n, groups,
        [in_grad, down_grad, cross_out_grad, cross_query_grad, cross_pair_grad, self_out_grad, self_in_grad],
        small,
    )
    small = small.reshape(-1)[:amount]
    return packed, small, memory_grad, input_grad, layer_output, count_small


def on_device(
    n, groups,
    inputs, memory, cotangent, target_segments, memory_segments,
    self_in_weight, self_in_bias, self_out_weight, self_out_bias, first_gain, first_shift,
    cross_query_weight, cross_pair_weight, cross_bias, cross_out_weight, cross_out_bias,
    second_gain, second_shift, feed_in_weight, feed_in_bias, feed_out_weight, feed_out_bias,
    third_gain, third_shift,
):
    input_rows, memory_rows, cotangent_rows = inputs[0], memory[0], cotangent[0]
    count, features = input_rows.shape
    length = n * count
    hidden = feed_in_weight.shape[1]
    rows_block = min(count, 256)
    tiles = count // TILE
    half = features // n
    near = n == 2 and groups % 4 == 0 and length <= 1024 and half % TILE == 0

    def row(vector):
        return vector[None, :]

    if near:
        (
            input_pieces, memory_pieces, query, keys, values, attended_t, normal, first_low, cross_query,
            cross_keys, cross_values, cross_grad, g2, in_grad, down_grad, cross_out_grad,
            layer_output, lse, cross_lse, cross_delta, rstd, feed_sums, in_bias_grad, target_row, memory_row,
        ) = forward_all(
            n, groups, rows_block,
            [input_rows, memory_rows, cotangent_rows],
            [self_in_weight, self_out_weight, cross_query_weight, cross_pair_weight, cross_out_weight,
             feed_in_weight, feed_out_weight],
            [target_segments, memory_segments, self_in_bias, row(self_out_bias), row(first_gain),
             row(first_shift), cross_bias, row(cross_out_bias), row(second_gain), row(second_shift),
             row(feed_in_bias), row(feed_out_bias), row(third_gain), row(third_shift)],
        )
        packed, small, memory_grad, input_grad = back_and_reduce(
            n, groups, rows_block,
            [in_grad, down_grad, cross_out_grad],
            [cross_values, memory_pieces, cross_pair_weight, first_low, cross_query_weight, g2, normal, self_out_weight,
             attended_t, keys, values, query, input_pieces, self_in_weight],
            [target_row, memory_row, cross_query, cross_grad, cross_keys,
             cross_lse, cross_delta, feed_sums, in_bias_grad, row(first_gain), rstd, lse],
        )
        (
            feed_in_grad, feed_out_grad, cross_out_total, cross_query_total, cross_pair_total,
            self_out_total, self_in_total, input_grad, memory_grad, layer_output, self_bias_grad,
            cross_bias_grad, in_bias_total, first_gain_grad, first_shift_grad, self_out_bias_grad,
            third_gain_grad, third_shift_grad, feed_out_bias_grad, second_gain_grad, second_shift_grad,
            cross_out_bias_grad,
        ) = finish_all(n, packed, small, input_grad, memory_grad, layer_output, hidden)
    else:
        packed, small, memory_grad, input_grad, layer_output, count_small = apart(
            n, groups, rows_block, input_rows, memory_rows, cotangent_rows, target_segments, memory_segments,
            self_in_weight, self_in_bias, self_out_weight, self_out_bias, first_gain, first_shift,
            cross_query_weight, cross_pair_weight, cross_bias, cross_out_weight, cross_out_bias,
            second_gain, second_shift, feed_in_weight, feed_in_bias, feed_out_weight, feed_out_bias,
            third_gain, third_shift,
        )
        plan = []
        start = 0
        shapes = []
        for height, columns in (
            (half, hidden // features), (hidden // n, 1), (half, 1), (half, 1), (half, 2), (half, 1), (half, 3)
        ):
            plan.append((start, columns))
            shapes.append(out_like((height, columns * features), F32))
            start += height * columns
        (
            feed_in_grad, feed_out_grad, cross_out_total, cross_query_total, cross_pair_total,
            self_out_total, self_in_total,
        ) = run(functools.partial(widen_kernel, plan), [packed], 0, shapes, [], 0, 12 << 20)
        rows_small = small[: count_small * half].reshape(count_small, half)
        (
            self_query_bias, self_value_bias, cross_query_bias, cross_value_bias, first_gain_grad,
            first_shift_grad, self_out_bias_grad, third_gain_grad, third_shift_grad, feed_out_bias_grad,
            second_gain_grad, second_shift_grad, cross_out_bias_grad,
        ) = [rows_small[index] for index in range(count_small)]
        self_bias_grad = jnp.stack([self_query_bias, self_value_bias])
        cross_bias_grad = jnp.stack([cross_query_bias, cross_value_bias])
        in_bias_total = small[count_small * half :]
    return (
        layer_output[None],
        input_grad[None],
        memory_grad[None],
        self_in_total,
        self_bias_grad,
        self_out_total,
        self_out_bias_grad,
        first_gain_grad,
        first_shift_grad,
        cross_query_total,
        cross_pair_total,
        cross_bias_grad,
        cross_out_total,
        cross_out_bias_grad,
        second_gain_grad,
        second_shift_grad,
        feed_in_grad,
        in_bias_total,
        feed_out_grad,
        feed_out_bias_grad,
        third_gain_grad,
        third_shift_grad,
    )


def solution(mesh):
    rows = P("dp", "blk", None)
    everywhere = P()
    split = P("blk", None)
    vector = P("blk")
    pair = P(None, "blk")
    return jax.shard_map(
        functools.partial(on_device, mesh.shape["blk"], mesh.shape["dp"]),
        mesh=mesh,
        in_specs=(rows, rows, rows, P("dp", None), P("dp", None)) + (everywhere,) * 19,
        out_specs=(
            rows, rows, rows, split, pair, split, vector, vector, vector, split, split, pair, split,
            vector, vector, vector, split, vector, split, vector, vector, vector,
        ),
        check_vma=False,
    )
```

```python
import functools

import jax
import jax.numpy as jnp
from jax import lax
from jax.experimental import pallas as pl
from jax.experimental.pallas import tpu as pltpu
from jax.sharding import PartitionSpec as P

HEAD = 64
TILE = 128
KEYS = 256
BACK_KEYS = 512
PAIR = 2 * HEAD
WIDE = 512
SCALE = HEAD ** (-0.5)
MASKED = -1e30
F32 = jnp.float32
BF16 = jnp.bfloat16
VMEM_LIMIT = 62 << 20


def nn(left, right):
    return lax.dot_general(left, right, (((1,), (0,)), ((), ())), preferred_element_type=F32)


def nt(left, right):
    return lax.dot_general(left, right, (((1,), (1,)), ((), ())), preferred_element_type=F32)


def tn(left, right):
    return lax.dot_general(left, right, (((0,), (0,)), ((), ())), preferred_element_type=F32)


def col_sum(field):
    return jnp.sum(field, axis=0, keepdims=True)


def normalize(field):
    centre = field - jnp.mean(field, axis=-1, keepdims=True)
    spread = jnp.mean(centre * centre, axis=-1, keepdims=True)
    rstd = lax.rsqrt(spread + 1e-05)
    return centre * rstd, rstd


def normalize_back(grad, gain, normal, rstd):
    scaled = grad * gain
    mean = jnp.mean(scaled, axis=-1, keepdims=True)
    along = jnp.mean(scaled * normal, axis=-1, keepdims=True)
    return (scaled - mean - normal * along) * rstd


def gate(hidden):
    bell = jnp.exp2(hidden * hidden * (-0.5 * 1.4426950408889634))
    ratio = 1.0 / (1.0 + (0.3275911 * 0.7071067811865476) * jnp.abs(hidden))
    series = (0.5 * 1.061405429) * ratio - 0.5 * 1.453152027
    series = series * ratio + 0.5 * 1.421413741
    series = series * ratio - 0.5 * 0.284496736
    series = series * ratio + 0.5 * 0.254829592
    tail = series * ratio * bell
    phi = jnp.where(hidden > 0.0, 1.0 - tail, tail)
    return hidden * phi, phi + hidden * (bell * 0.3989422804014327)


def dyn(index, size):
    return pl.ds(pl.multiple_of(index * size, size), size)


def even_lanes(rows, width):
    return (lax.broadcasted_iota(jnp.int32, (rows, width), 1) // HEAD) % 2 == 0


def even_rows(rows, width):
    return (lax.broadcasted_iota(jnp.int32, (rows, width), 0) // HEAD) % 2 == 0


def split_columns(tile_t, out_ref, tile):
    chosen = even_rows(*tile_t.shape)
    blank = jnp.zeros_like(tile_t)
    out_ref[:, pl.ds(pl.multiple_of(tile * 2 * TILE, 2 * TILE), TILE)] = jnp.where(chosen, tile_t, blank)
    out_ref[:, pl.ds(pl.multiple_of(tile * 2 * TILE + TILE, TILE), TILE)] = jnp.where(
        chosen, blank, tile_t
    )


def split_rows(tile_n, out_ref, tile):
    chosen = even_lanes(*tile_n.shape)
    blank = jnp.zeros_like(tile_n)
    out_ref[pl.ds(pl.multiple_of(tile * 2 * TILE, 2 * TILE), TILE), :] = jnp.where(chosen, tile_n, blank)
    out_ref[pl.ds(pl.multiple_of(tile * 2 * TILE + TILE, TILE), TILE), :] = jnp.where(
        chosen, blank, tile_n
    )


def spread_segments(column_ref, wide_ref):
    total = column_ref.shape[0]
    step = min(total, 512)

    @pl.loop(0, total // step)
    def _(block):
        rows = dyn(block, step)
        wide_ref[rows, :] = jnp.broadcast_to(column_ref[rows, :], (step, TILE))


def key_rows(low, chunk, length, size):
    wanted = low * TILE + chunk * size
    start = pl.multiple_of(jnp.minimum(wanted, length - size), TILE)
    return pl.ds(start, size), start, wanted


def chunk_bias(query_row, key_wide_ref, tile, rows, start, wanted, offset, causal):
    size = rows.size
    key_position = start + lax.broadcasted_iota(jnp.int32, (size, TILE), 0)
    allowed = (key_wide_ref[rows, :] == query_row) & (key_position >= wanted)
    if causal:
        query_position = offset + tile * TILE + lax.broadcasted_iota(jnp.int32, (size, TILE), 1)
        allowed = allowed & (key_position <= query_position)
    return jnp.where(allowed, 0.0, MASKED)


def attend(
    tiles, ranges_ref, query_row_ref, key_wide_ref, offset, causal,
    query_cols, keys, values_t, attended_t, lse_ref, peak, total, sums, held, held_low,
):
    pairs = WIDE // PAIR

    @pl.loop(0, tiles)
    def _(tile):
        peak[...] = jnp.full(peak.shape, MASKED, F32)
        total[...] = jnp.zeros(total.shape, F32)
        sums[...] = jnp.zeros(sums.shape, F32)
        query_row = query_row_ref[:, dyn(tile, TILE)]

        low, high = ranges_ref[0, tile], ranges_ref[1, tile]

        size = held.shape[1]

        @pl.loop(0, lax.div((high - low) * TILE + size - 1, size))
        def _(chunk):
            rows, start, wanted = key_rows(low, chunk, keys.shape[0], size)
            bias = chunk_bias(query_row, key_wide_ref, tile, rows, start, wanted, offset, causal)
            bias = jnp.concatenate([bias, bias], axis=1)
            factors = []
            for pair in range(pairs):
                lanes = slice(pair * PAIR, (pair + 1) * PAIR)
                scores = nn(keys[rows, lanes], query_cols[lanes, dyn(tile, 2 * TILE)]) + bias
                held[pair] = scores
                before = peak[pair : pair + 1, :]
                after = jnp.maximum(before, jnp.max(scores, axis=0, keepdims=True))
                factors.append(jnp.exp(before - after))
                peak[pair : pair + 1, :] = after
            for pair in range(pairs):
                weights = jnp.exp(held[pair] - peak[pair : pair + 1, :])
                total[pair : pair + 1, :] = total[pair : pair + 1, :] * factors[pair] + col_sum(weights)
                held_low[pair] = weights.astype(BF16)
            for pair in range(pairs):
                factor = factors[pair]
                mixed = nn(values_t[pair * PAIR : (pair + 1) * PAIR, rows], held_low[pair])
                first = slice(pair * PAIR, pair * PAIR + HEAD)
                second = slice(pair * PAIR + HEAD, (pair + 1) * PAIR)
                sums[first, :] = sums[first, :] * factor[:, :TILE] + mixed[:HEAD, :TILE]
                sums[second, :] = sums[second, :] * factor[:, TILE:] + mixed[HEAD:, TILE:]

        for pair in range(pairs):
            amount = total[pair : pair + 1, :]
            lse_ref[pair : pair + 1, dyn(tile, 2 * TILE)] = peak[pair : pair + 1, :] + jnp.log(amount)
            share = 1.0 / amount
            first = slice(pair * PAIR, pair * PAIR + HEAD)
            second = slice(pair * PAIR + HEAD, (pair + 1) * PAIR)
            attended_t[first, dyn(tile, TILE)] = (sums[first, :] * share[:, :TILE]).astype(BF16)
            attended_t[second, dyn(tile, TILE)] = (sums[second, :] * share[:, TILE:]).astype(BF16)


def attend_back(
    tile, low, high, query_row_ref, first_query, key_wide_ref, offset, causal,
    query_cols, query_rows, grad_cols, grad_rows, keys, keys_t, values, lse_ref, delta_ref,
    query_grad_t, key_grad, value_grad, held, held_low, held_grad, fresh=False,
):
    pairs = WIDE // PAIR
    query_row = query_row_ref[:, pl.ds(pl.multiple_of(first_query + tile * TILE, TILE), TILE)]
    both = dyn(tile, 2 * TILE)

    size = held.shape[1]

    @pl.loop(0, lax.div((high - low) * TILE + size - 1, size))
    def _(chunk):
        rows, start, wanted = key_rows(low, chunk, keys.shape[0], size)
        bias = chunk_bias(query_row, key_wide_ref, tile, rows, start, wanted, offset, causal)
        bias = jnp.concatenate([bias, bias], axis=1)
        for pair in range(pairs):
            lanes = slice(pair * PAIR, (pair + 1) * PAIR)
            scores = nn(keys[rows, lanes], query_cols[lanes, both]) + bias
            probs = jnp.exp(scores - lse_ref[pair : pair + 1, both])
            held[pair] = probs
            held_low[pair] = probs.astype(BF16)
        for pair in range(pairs):
            lanes = slice(pair * PAIR, (pair + 1) * PAIR)
            prob_grad = nn(values[rows, lanes], grad_cols[lanes, both])
            held_grad[pair] = (held[pair] * (prob_grad - delta_ref[pair : pair + 1, both])).astype(BF16)
        for pair in range(pairs):
            lanes = slice(pair * PAIR, (pair + 1) * PAIR)
            value_part = nn(held_low[pair], grad_rows[both, lanes])
            key_part = nn(held_grad[pair], query_rows[both, lanes])
            value_grad[rows, lanes] = value_part if fresh else value_grad[rows, lanes] + value_part
            key_grad[rows, lanes] = key_part if fresh else key_grad[rows, lanes] + key_part
            mixed = nn(keys_t[lanes, rows], held_grad[pair])
            first = slice(pair * PAIR, pair * PAIR + HEAD)
            second = slice(pair * PAIR + HEAD, (pair + 1) * PAIR)
            query_grad_t[first, dyn(tile, TILE)] += mixed[:HEAD, :TILE]
            query_grad_t[second, dyn(tile, TILE)] += mixed[HEAD:, TILE:]


def clear(ref):
    rows = ref.shape[0]
    step = min(rows, 256)

    @pl.loop(0, rows // step)
    def _(block):
        ref[dyn(block, step), :] = jnp.zeros((step, ref.shape[1]), ref.dtype)


def transpose_rows(source, target):
    @pl.loop(0, source.shape[0] // TILE)
    def _(block):
        target[:, dyn(block, TILE)] = source[dyn(block, TILE), :].T


def out_like(shape, dtype):
    return jax.ShapeDtypeStruct(shape, dtype)


def run(body, ins, smem_count, outs, scratch, flops, bytes_accessed):
    vm = pl.BlockSpec(memory_space=pltpu.VMEM)
    sm = pl.BlockSpec(memory_space=pltpu.SMEM)
    return pl.pallas_call(
        body,
        in_specs=[sm] * smem_count + [vm] * (len(ins) - smem_count),
        out_specs=[vm] * len(outs),
        out_shape=outs,
        scratch_shapes=scratch,
        cost_estimate=pl.CostEstimate(
            flops=flops, bytes_accessed=bytes_accessed, transcendentals=0
        ),
        compiler_params=pltpu.CompilerParams(vmem_limit_bytes=VMEM_LIMIT),
    )(*ins)


def self_forward(n, rows_block, place_ref, ranges_ref, *refs):
    pieces, refs = refs[:n], refs[n:]
    (
        query_segment, key_segment, weight, bias, out_weight, out_bias, gain, shift,
        cross_weight, cross_bias,
        query_out, keys, values, attended_t, lse_ref, normal_out, rstd_out, first_low, cross_query,
        wide, values_t, query_cols, peak, total, sums, held, held_low,
    ) = refs
    count = pieces[0].shape[0]
    place = place_ref[0]
    spread_segments(key_segment, wide)

    for step in range(n):
        spot = lax.rem(place + n - step, n)

        @pl.when(spot <= place)
        def _():
            @pl.loop(0, count // rows_block)
            def _(block):
                source = pieces[step][dyn(block, rows_block), :]
                rows = dyn(spot * (count // rows_block) + block, rows_block)
                keys[rows, :] = nn(source, weight[:, WIDE : 2 * WIDE]).astype(BF16)
                values[rows, :] = (nn(source, weight[:, 2 * WIDE :]) + bias[1:2, :]).astype(BF16)
                if step == 0:
                    query = (nn(source, weight[:, :WIDE]) + bias[0:1, :]).astype(BF16)
                    query_out[dyn(block, rows_block), :] = (query.astype(F32) * SCALE).astype(BF16)

        @pl.when(spot > place)
        def _():
            @pl.loop(0, count // rows_block)
            def _(block):
                rows = dyn(spot * (count // rows_block) + block, rows_block)
                keys[rows, :] = jnp.zeros((rows_block, WIDE), BF16)
                values[rows, :] = jnp.zeros((rows_block, WIDE), BF16)

    transpose_rows(values, values_t)
    tiles = count // TILE

    @pl.loop(0, tiles)
    def _(tile):
        split_columns(query_out[dyn(tile, TILE), :].T, query_cols, tile)

    attend(
        tiles, ranges_ref, query_segment, wide, place * count, True,
        query_cols, keys, values_t, attended_t, lse_ref, peak, total, sums, held, held_low,
    )

    @pl.loop(0, count // rows_block)
    def _(block):
        rows = dyn(block, rows_block)
        attended = attended_t[:, rows].T
        field = pieces[0][rows, :].astype(F32) + nn(attended, out_weight[...]) + out_bias[...]
        normal, rstd = normalize(field)
        normal_out[rows, :] = normal
        rstd_out[rows, :] = rstd
        low = (normal * gain[...] + shift[...]).astype(BF16)
        first_low[rows, :] = low
        query = (nn(low, cross_weight[...]) + cross_bias[0:1, :]).astype(BF16)
        cross_query[rows, :] = (query.astype(F32) * SCALE).astype(BF16)


def cross_and_feed(n, rows_block, place_ref, ranges_ref, *refs):
    pieces, refs = refs[:n], refs[n:]
    (
        query_segment, key_segment, cotangent, cross_query, first_normal, first_gain, first_shift,
        pair_weight, cross_bias, out_weight, out_bias, gain, shift,
        in_weight, in_bias, down_weight, down_bias, last_gain, last_shift,
        layer_output, keys, values, lse_ref, delta_ref, out_grad, grad_out, g2_out,
        in_grad, down_grad, cross_out_grad, sums_out, in_bias_grad,
        wide, values_t, query_cols, peak, total, sums, held, held_low, attended_t, second_normal, second_rstd,
        second_low, second_low_t, active, slope, third, branch, branch_t,
    ) = refs
    count = pieces[0].shape[0]
    place = place_ref[0]
    spread_segments(key_segment, wide)
    blocks = count // rows_block

    for step in range(n):
        spot = lax.rem(place + n - step, n)

        @pl.loop(0, blocks)
        def _(block):
            source = pieces[step][dyn(block, rows_block), :]
            rows = dyn(spot * blocks + block, rows_block)
            keys[rows, :] = nn(source, pair_weight[:, :WIDE]).astype(BF16)
            values[rows, :] = (nn(source, pair_weight[:, WIDE:]) + cross_bias[1:2, :]).astype(BF16)

    transpose_rows(values, values_t)
    tiles = count // TILE

    @pl.loop(0, tiles)
    def _(tile):
        split_columns(cross_query[dyn(tile, TILE), :].T, query_cols, tile)

    attend(
        tiles, ranges_ref, query_segment, wide, 0, False,
        query_cols, keys, values_t, attended_t, lse_ref, peak, total, sums, held, held_low,
    )

    @pl.loop(0, blocks)
    def _(block):
        rows = dyn(block, rows_block)
        attended = attended_t[:, rows].T
        first = first_normal[rows, :] * first_gain[...] + first_shift[...]
        field = first + nn(attended, out_weight[...]) + out_bias[...]
        normal, rstd = normalize(field)
        second_normal[rows, :] = normal
        second_rstd[rows, :] = rstd
        second = normal * gain[...] + shift[...]
        third[rows, :] = second + down_bias[...]
        low = second.astype(BF16)
        second_low[rows, :] = low
        second_low_t[:, rows] = low.T

    hidden_size = in_weight.shape[1]
    chunk_size = min(WIDE, hidden_size // n)
    chunks = hidden_size // chunk_size

    @pl.loop(0, chunks)
    def _(chunk):
        lanes = dyn(chunk, chunk_size)

        @pl.loop(0, blocks)
        def _(block):
            rows = dyn(block, rows_block)
            hidden = nn(second_low[rows, :], in_weight[:, lanes]) + in_bias[:, lanes]
            value, derivative = gate(hidden)
            value = value.astype(BF16)
            active[rows, lanes] = value
            slope[rows, lanes] = derivative.astype(slope.dtype)
            third[rows, :] += nn(value, down_weight[dyn(chunk, chunk_size), :])

    sums_out[...] = jnp.zeros(sums_out.shape, F32)
    in_bias_grad[...] = jnp.zeros(in_bias_grad.shape, F32)

    @pl.loop(0, blocks)
    def _(block):
        rows = dyn(block, rows_block)
        normal, rstd = normalize(third[rows, :])
        layer_output[rows, :] = (normal * last_gain[...] + last_shift[...]).astype(BF16)
        outer = cotangent[rows, :].astype(F32)
        grad = normalize_back(outer, last_gain[...], normal, rstd)
        third[rows, :] = grad
        low = grad.astype(BF16)
        branch[rows, :] = low
        sums_out[0:1, :] += col_sum(outer * normal)
        sums_out[1:2, :] += col_sum(outer)
        sums_out[2:3, :] += col_sum(low.astype(F32))

    half = WIDE // n
    down_half = down_weight.shape[0] // n

    @pl.loop(0, chunks)
    def _(chunk):
        lanes = dyn(chunk, chunk_size)
        share = tn(active[:, lanes], branch[...]).astype(BF16)
        per_half = down_half // chunk_size
        down_grad[lax.div(chunk, per_half), dyn(lax.rem(chunk, per_half), chunk_size), :] = share

        @pl.loop(0, blocks)
        def _(block):
            rows = dyn(block, rows_block)
            inner = nt(branch[rows, :], down_weight[dyn(chunk, chunk_size), :])
            hidden_grad = (inner * slope[rows, lanes].astype(F32)).astype(BF16)
            active[rows, lanes] = hidden_grad
            in_bias_grad[:, lanes] += col_sum(hidden_grad.astype(F32))
            third[rows, :] += nt(hidden_grad, in_weight[:, lanes])

        share = nn(second_low_t[...], active[:, lanes]).astype(BF16)
        per_block = WIDE // chunk_size
        block_rows = dyn(lax.div(chunk, per_block), half)
        block_lanes = dyn(lax.rem(chunk, per_block), chunk_size)
        for part in range(n):
            in_grad[part, block_rows, block_lanes] = share[part * half : (part + 1) * half, :]

    @pl.loop(0, blocks)
    def _(block):
        rows = dyn(block, rows_block)
        outer = third[rows, :]
        normal = second_normal[rows, :]
        grad = normalize_back(outer, gain[...], normal, second_rstd[rows, :])
        g2_out[rows, :] = grad
        low = grad.astype(BF16)
        branch[rows, :] = low
        sums_out[3:4, :] += col_sum(outer * normal)
        sums_out[4:5, :] += col_sum(outer)
        sums_out[5:6, :] += col_sum(low.astype(F32))
        grad_out[rows, :] = nt(low, out_weight[...]).astype(BF16)

    share = nn(attended_t[...], branch[...]).astype(BF16)
    for part in range(n):
        cross_out_grad[part] = share[part * half : (part + 1) * half, :]

    write_delta(tiles, grad_out, attended_t, delta_ref)


def write_delta(tiles, grad, attended_t, delta_ref):
    @pl.loop(0, tiles)
    def _(tile):
        product = grad[dyn(tile, TILE), :].astype(F32).T * attended_t[:, dyn(tile, TILE)].astype(F32)
        for pair in range(WIDE // PAIR):
            start = pair * PAIR
            delta_ref[pair : pair + 1, pl.ds(pl.multiple_of(tile * 2 * TILE, 2 * TILE), TILE)] = col_sum(
                product[start : start + HEAD, :]
            )
            delta_ref[
                pair : pair + 1, pl.ds(pl.multiple_of(tile * 2 * TILE + TILE, TILE), TILE)
            ] = col_sum(product[start + HEAD : start + PAIR, :])


def prepare_back(tiles, query, grad, query_cols, query_rows, grad_cols, grad_rows):
    @pl.loop(0, tiles)
    def _(tile):
        here = query[dyn(tile, TILE), :]
        split_columns(here.T, query_cols, tile)
        split_rows(here, query_rows, tile)
        here = grad[dyn(tile, TILE), :]
        split_columns(here.T, grad_cols, tile)
        split_rows(here, grad_rows, tile)


def query_finish(tiles, query_grad_t, query_low, sums_out, index, rounded):
    @pl.loop(0, tiles)
    def _(tile):
        rows = dyn(tile, TILE)
        wide_grad = query_grad_t[:, rows].T * SCALE
        low = wide_grad.astype(BF16)
        query_low[rows, :] = low
        sums_out[index : index + 1, :] += col_sum(low.astype(F32) if rounded else wide_grad)


def spread_parts(n, share, target, start):
    half = WIDE // n
    for part in range(n):
        target[part, start : start + half, :] = share[part * half : (part + 1) * half, :].astype(BF16)


def row_product(n, place, pieces, source):
    count = pieces[0].shape[0]
    step_rows = min(count, 512)
    share = jnp.zeros((WIDE, WIDE), F32)
    for step in range(n):
        spot = lax.rem(place + n - step, n)
        for block in range(count // step_rows):
            rows = dyn(spot * (count // step_rows) + block, step_rows)
            share += tn(
                pieces[step][block * step_rows : (block + 1) * step_rows, :], source[rows, :].astype(BF16)
            )
    return share


def pair_back(n, place, rows_block, count, step, key_grad, value_grad, weight, first, sums_out, index, write):
    blocks = count // rows_block
    spot = lax.rem(place + n - step, n)

    @pl.loop(0, blocks)
    def _(block):
        rows = dyn(spot * blocks + block, rows_block)
        key_low = key_grad[rows, :].astype(BF16)
        value_part = value_grad[rows, :]
        sums_out[index : index + 1, :] += col_sum(value_part)
        value_low = value_part.astype(BF16)
        back = nt(key_low, weight[:, first : first + WIDE]) + nt(value_low, weight[:, first + WIDE : first + 2 * WIDE])
        write(dyn(block, rows_block), back)


def first_back(
    blocks, rows_block, g2, query_low, query_weight, first_normal, first_rstd, gain, self_out_weight,
    g1, branch, self_grad, sums_out, index,
):
    @pl.loop(0, blocks)
    def _(block):
        rows = dyn(block, rows_block)
        outer = g2[rows, :] + nt(query_low[rows, :], query_weight[...])
        normal = first_normal[rows, :]
        back = normalize_back(outer, gain[...], normal, first_rstd[rows, :])
        g1[rows, :] = back
        low = back.astype(BF16)
        branch[rows, :] = low
        sums_out[index : index + 1, :] += col_sum(outer * normal)
        sums_out[index + 1 : index + 2, :] += col_sum(outer)
        sums_out[index + 2 : index + 3, :] += col_sum(low.astype(F32))
        self_grad[rows, :] = nt(low, self_out_weight[...]).astype(BF16)


def cross_backward(n, rows_block, place_ref, ranges_ref, *refs):
    pieces, refs = refs[:n], refs[n:]
    (
        query_segment, key_segment, query, grad, keys, values, lse_ref, delta_ref, g2,
        first_normal, first_rstd, first_low, gain, query_weight, pair_weight, self_out_weight,
        self_attended_t,
        own_grad, sent_grad, query_grad_w, pair_grad_w, self_out_grad, self_grad, self_delta, g1_out, sums_out,
        wide, keys_t, query_cols, query_rows, grad_cols, grad_rows, query_grad_t, key_grad, value_grad,
        held, held_low, held_grad, query_low, branch,
    ) = refs
    count = pieces[0].shape[0]
    place = place_ref[0]
    tiles = count // TILE
    blocks = count // rows_block
    half = WIDE // n
    spread_segments(key_segment, wide)
    transpose_rows(keys, keys_t)
    prepare_back(tiles, query, grad, query_cols, query_rows, grad_cols, grad_rows)
    clear(query_grad_t)
    clear(key_grad)
    clear(value_grad)

    @pl.loop(0, tiles)
    def _(tile):
        attend_back(
            tile, ranges_ref[0, tile], ranges_ref[1, tile], query_segment, 0, wide, 0, False,
            query_cols, query_rows, grad_cols, grad_rows, keys, keys_t, values, lse_ref, delta_ref,
            query_grad_t, key_grad, value_grad, held, held_low, held_grad,
        )

    sums_out[...] = jnp.zeros(sums_out.shape, F32)
    query_finish(tiles, query_grad_t, query_low, sums_out, 0, True)
    spread_parts(n, tn(first_low[...], query_low[...]), query_grad_w, 0)
    for step in range(n):

        def write(here, back):
            if step == 0:
                own_grad[here, :] = back
            else:
                sent_grad[step - 1, here, :] = back.astype(BF16)

        pair_back(n, place, rows_block, count, step, key_grad, value_grad, pair_weight, 0, sums_out, 1, write)
    spread_parts(n, row_product(n, place, pieces, key_grad), pair_grad_w, 0)
    spread_parts(n, row_product(n, place, pieces, value_grad), pair_grad_w, half)
    first_back(
        blocks, rows_block, g2, query_low, query_weight, first_normal, first_rstd, gain, self_out_weight,
        g1_out, branch, self_grad, sums_out, 2,
    )
    spread_parts(n, nn(self_attended_t[...], branch[...]), self_out_grad, 0)
    write_delta(tiles, self_grad, self_attended_t, self_delta)


def self_backward(n, rows_block, place_ref, ranges_ref, *refs):
    pieces, refs = refs[:n], refs[n:]
    (
        query_segment, key_segment, query, grad, keys, values, lse_ref, delta_ref, g1, weight,
        own_grad, sent_grad, grad_w, sums_out,
        wide, keys_t, query_cols, query_rows, grad_cols, grad_rows, query_grad_t, key_grad, value_grad,
        held, held_low, held_grad, query_low,
    ) = refs
    count = pieces[0].shape[0]
    place = place_ref[0]
    tiles = count // TILE
    half = WIDE // n
    spread_segments(key_segment, wide)
    transpose_rows(keys, keys_t)
    prepare_back(tiles, query, grad, query_cols, query_rows, grad_cols, grad_rows)
    clear(query_grad_t)
    clear(key_grad)
    clear(value_grad)

    @pl.loop(0, tiles)
    def _(tile):
        attend_back(
            tile, ranges_ref[0, tile], ranges_ref[1, tile], query_segment, 0, wide, place * count, True,
            query_cols, query_rows, grad_cols, grad_rows, keys, keys_t, values, lse_ref, delta_ref,
            query_grad_t, key_grad, value_grad, held, held_low, held_grad,
        )

    sums_out[...] = jnp.zeros(sums_out.shape, F32)
    query_finish(tiles, query_grad_t, query_low, sums_out, 0, False)
    for step in range(n):

        def write(here, back):
            if step == 0:
                own_grad[here, :] = back + g1[here, :] + nt(query_low[here, :], weight[:, :WIDE])
            else:
                sent_grad[step - 1, here, :] = back.astype(BF16)

        pair_back(n, place, rows_block, count, step, key_grad, value_grad, weight, WIDE, sums_out, 1, write)
    spread_parts(n, tn(pieces[0][...], query_low[...]), grad_w, 0)
    spread_parts(n, row_product(n, place, pieces, key_grad), grad_w, half)
    spread_parts(n, row_product(n, place, pieces, value_grad), grad_w, 2 * half)


CORE_RATE = 0.0018
LINK_RATE = 0.0225
LATENCY = {"core": 1.0, "x": 2.2, "y": 2.2, "z": 2.6}
MARGIN = 0.5


def plan_steps(n, chunks, extras, smalls, segments):
    free = {"core": 0.0, "x": 0.0, "y": 0.0, "z": 0.0}
    now = 0.0
    pending = []
    plan = []
    crossed = set()

    def send(link, rows, rate=LINK_RATE):
        free[link] = max(free[link], now) + rows * rate
        return free[link] + LATENCY[link]

    def execute(kind, index, step):
        nonlocal now
        now += 0.15
        if kind == "chunk":
            unused, rows, y_first, unused = chunks[index]
            if step == 0:
                ready = send("core", n * rows // 2, CORE_RATE)
            elif step in (1, 2) and (step == 1) == y_first:
                ready = send("y", (n if y_first else 1) * rows // 4)
            elif step in (1, 2):
                crossed.add(index)
                ready = send("x", (n - 1) * rows // (4 if y_first else 2))
            elif step in (3, 4):
                ready = send("z", rows // 4)
            elif step == 5:
                ready = send("y", rows // 4)
            elif step == 6:
                ready = send("core", rows // 2, CORE_RATE)
            else:
                return
        elif kind == "extra":
            if step == 2:
                return
            rows = extras[index][0]
            ready = send("core", rows, CORE_RATE) if step == 0 else send("x", rows // 2)
        else:
            if step == 4:
                return
            rows = smalls[index][0]
            link, rows = (("core", n * rows), ("x", rows), ("y", rows), ("z", 4 * rows))[step]
            ready = send(link, rows, CORE_RATE if link == "core" else LINK_RATE)
        pending.append((ready, len(pending), kind, index, step + 1))

    for number in range(len(segments) + 1):
        order = []
        last = number == len(segments)
        if not last:
            now += segments[number]
            released = [("chunk", i) for i, chunk in enumerate(chunks) if chunk[3] == number]
            released += [("extra", i) for i, extra in enumerate(extras) if extra[1] == number]
            released += [("small", i) for i, small in enumerate(smalls) if small[1] == number]
            for kind, index in released:
                execute(kind, index, 0)
                order.append((kind, index, 0))
        while pending:
            pending.sort()
            first = 0
            if len(crossed) < len(chunks):
                while first < len(pending) and pending[first][2:] == ("extra", pending[first][3], 1):
                    first += 1
            if first == len(pending) or (not last and pending[first][0] + MARGIN > now):
                break
            ready, unused, kind, index, step = pending.pop(first)
            now = max(now, ready)
            execute(kind, index, step)
            order.append((kind, index, step))
        plan.append(order)
    return plan, now


class Reducer:
    def __init__(self, n, groups, chunks, field, total, total_out, small, small_out, small_spans, buffers):
        (
            self.from_core, self.from_blk, self.from_y, self.from_z,
            self.small_core, self.small_blk, self.small_y, self.small_z,
            self.sends, self.receives, self.small_sends, self.small_receives, self.stores,
        ) = buffers
        self.n, self.chunks, self.field, self.total, self.total_out = n, chunks, field, total, total_out
        self.small, self.small_out, self.small_spans = small, small_out, small_spans
        self.depth = depth = groups // 4
        self.group = group = lax.axis_index("dp")
        self.part = part = lax.axis_index("blk")
        self.core = lax.rem(group, 2)
        self.side = lax.rem(lax.div(group, 2), 2)
        self.level = lax.div(group, 4)
        self.core_peer = (group + 1 - 2 * self.core, part)
        self.side_peer = (group + 2 - 4 * self.side, part)
        self.blk_peers = [(group, lax.rem(part + step, n)) for step in range(1, n)]
        self.z_peers = [(lax.rem(group + 4 * step, groups), part) for step in range(1, depth)]
        self.per_chunk = 4 + (n - 1) + 2 * (depth - 1)

    def greet(self, far_peer=None, has_far=None):
        peers = [self.core_peer, self.side_peer] + self.blk_peers + self.z_peers
        barrier = pltpu.get_barrier_semaphore()
        for peer in peers:
            pl.semaphore_signal(barrier, inc=1, device_id=peer, device_id_type=pl.DeviceIdType.MESH)
        if far_peer is not None:

            @pl.when(has_far)
            def _():
                pl.semaphore_signal(barrier, inc=1, device_id=far_peer, device_id_type=pl.DeviceIdType.MESH)

            self.greetings = jnp.where(has_far, len(peers) + 1, len(peers))
        else:
            self.greetings = len(peers)

    def enter(self):
        pl.semaphore_wait(pltpu.get_barrier_semaphore(), self.greetings)

    def copy(self, source, target, sem, peer):
        return pltpu.make_async_remote_copy(
            src_ref=source, dst_ref=target, send_sem=self.sends.at[sem], recv_sem=self.receives.at[sem],
            device_id=peer, device_id_type=pl.DeviceIdType.MESH,
        )

    def small_copy(self, source, target, sem, peer):
        return pltpu.make_async_remote_copy(
            src_ref=source, dst_ref=target, send_sem=self.small_sends.at[sem],
            recv_sem=self.small_receives.at[sem], device_id=peer, device_id_type=pl.DeviceIdType.MESH,
        )

    def span(self, start, size):
        return pl.ds(pl.multiple_of(start, 16), size)

    def copies(self, index, step):
        start, rows, y_first, unused = self.chunks[index]
        n, depth, part = self.n, self.depth, self.part
        half, quarter = rows // 2, rows // 4
        piece = quarter // depth
        own_half = start + self.core * half
        own_quarter = own_half + self.side * quarter
        sem = index * self.per_chunk
        if step == 0:
            theirs = self.span(start + (1 - self.core) * half, half)
            return [
                self.copy(
                    self.field.at[:, theirs], self.from_core.at[:, pl.ds(start // 2, half)], sem, self.core_peer
                )
            ]
        if step in (1, 2) and (step == 1) == y_first:
            theirs = self.span(own_half + (1 - self.side) * quarter, quarter)
            into = pl.ds(start // 4, quarter)
            if y_first:
                return [self.copy(self.field.at[:, theirs], self.from_y.at[:, into], sem + 1, self.side_peer)]
            return [self.copy(self.field.at[part, theirs], self.from_y.at[0, into], sem + 1, self.side_peer)]
        if step in (1, 2):
            if y_first:
                mine, into = self.span(own_quarter, quarter), pl.ds(start // 2, quarter)
            else:
                mine, into = self.span(own_half, half), pl.ds(start // 2, half)
            return [
                self.copy(
                    self.field.at[lax.rem(part + hop, n), mine], self.from_blk.at[hop - 1, into],
                    sem + 3 + hop, self.blk_peers[hop - 1],
                )
                for hop in range(1, n)
            ]
        if step == 3:
            copies = []
            for hop in range(1, depth):
                theirs = self.span(own_quarter + lax.rem(self.level + hop, depth) * piece, piece)
                copies.append(
                    self.copy(
                        self.field.at[part, theirs], self.from_z.at[hop - 1, pl.ds(start // 4 // depth, piece)],
                        sem + 2 + n + hop, self.z_peers[hop - 1],
                    )
                )
            return copies
        if step == 4:
            mine = self.span(own_quarter + self.level * piece, piece)
            return [
                self.copy(
                    self.total.at[mine], self.total.at[mine], sem + 1 + n + depth + hop, self.z_peers[hop - 1]
                )
                for hop in range(1, depth)
            ]
        if step == 5:
            mine = self.span(own_quarter, quarter)
            return [self.copy(self.total.at[mine], self.total.at[mine], sem + 2, self.side_peer)]
        mine = self.span(own_half, half)
        return [self.copy(self.total.at[mine], self.total.at[mine], sem + 3, self.core_peer)]

    def add(self, part, start, size, terms, result=None):
        step = min(size, 64)

        @pl.loop(0, size // step)
        def _(block):
            here = self.span(start + block * step, step)
            value = self.field[part, here, :].astype(F32)
            for ref, index, begin in terms:
                value = value + ref[index, self.span(begin + block * step, step), :].astype(F32)
            if result is None:
                self.field[part, here, :] = value.astype(BF16)
            else:
                result[here, :] = value.astype(BF16)

    def store(self, index):
        rows = pl.ds(self.chunks[index][0], self.chunks[index][1])
        return pltpu.make_async_copy(self.total.at[rows], self.total_out.at[rows], self.stores.at[index])

    def chunk_step(self, index, step):
        start, rows, y_first, unused = self.chunks[index]
        n, depth, part = self.n, self.depth, self.part
        half, quarter = rows // 2, rows // 4
        piece = quarter // depth
        own_half = start + self.core * half
        own_quarter = own_half + self.side * quarter
        if step > 0:
            for copy in self.copies(index, step - 1):
                copy.wait()
        if step == 1:
            for b in range(n):
                self.add(b, own_half, half, [(self.from_core, b, start // 2)])
        elif step in (2, 3) and (step == 2) == y_first:
            for b in range(n) if y_first else [part]:
                self.add(b, own_quarter, quarter, [(self.from_y, b if y_first else 0, start // 4)])
        elif step in (2, 3):
            begin, size = (own_quarter, quarter) if y_first else (own_half, half)
            self.add(part, begin, size, [(self.from_blk, hop, start // 2) for hop in range(n - 1)])
        elif step == 4:
            self.add(
                part, own_quarter + self.level * piece, piece,
                [(self.from_z, hop, start // 4 // depth) for hop in range(depth - 1)], self.total,
            )
        if step < 7:
            for copy in self.copies(index, step):
                copy.start()
        else:
            self.store(index).start()

    def small_copies(self, index, step):
        part, n = self.part, self.n
        rows = pl.ds(*self.small_spans[index])
        first = index * (n + self.depth)
        if step == 0:
            return [self.small_copy(self.small.at[0, :, rows], self.small_core.at[:, rows], first, self.core_peer)]
        if step == 1:
            return [
                self.small_copy(
                    self.small.at[1, lax.rem(part + hop, n), rows], self.small_blk.at[hop - 1, rows], first + hop,
                    self.blk_peers[hop - 1],
                )
                for hop in range(1, n)
            ]
        if step == 2:
            return [
                self.small_copy(self.small.at[1, part, rows], self.small_y.at[rows], first + n, self.side_peer)
            ]
        return [
            self.small_copy(
                self.small_y.at[rows], self.small_z.at[hop - 1, rows], first + n + hop, self.z_peers[hop - 1]
            )
            for hop in range(1, self.depth)
        ]

    def small_step(self, index, step):
        part = self.part
        rows = pl.ds(*self.small_spans[index])
        if step > 0:
            for copy in self.small_copies(index, step - 1):
                copy.wait()
        if step == 1:
            self.small[1, :, rows] = self.small[0, :, rows] + self.small_core[:, rows]
        elif step == 2:
            held = self.small[1, part, rows]
            for hop in range(self.n - 1):
                held = held + self.small_blk[hop, rows]
            self.small[1, part, rows] = held
        elif step == 3:
            self.small_y[rows] = self.small_y[rows] + self.small[1, part, rows]
        elif step == 4:
            held = self.small_y[rows]
            for hop in range(self.depth - 1):
                held = held + self.small_z[hop, rows]
            self.small_out[rows] = held
        if step < 4:
            for copy in self.small_copies(index, step):
                copy.start()

    def finish(self):
        for index in range(len(self.chunks)):
            self.store(index).wait()


def reducer_scratch(n, groups, chunks, rows, small_shape):
    depth = groups // 4
    per_chunk = 4 + (n - 1) + 2 * (depth - 1)
    return [
        pltpu.VMEM((n, rows // 2, WIDE), BF16),
        pltpu.VMEM((n - 1, rows // 2, WIDE), BF16),
        pltpu.VMEM((n, rows // 4, WIDE), BF16),
        pltpu.VMEM((depth - 1, rows // 4 // depth, WIDE), BF16),
        pltpu.VMEM((n, *small_shape), F32),
        pltpu.VMEM((n - 1, *small_shape), F32),
        pltpu.VMEM(small_shape, F32),
        pltpu.VMEM((depth - 1, *small_shape), F32),
        pltpu.SemaphoreType.DMA((len(chunks) * per_chunk,)),
        pltpu.SemaphoreType.DMA((len(chunks) * per_chunk,)),
        pltpu.SemaphoreType.DMA((2 * (n + depth),)),
        pltpu.SemaphoreType.DMA((2 * (n + depth),)),
        pltpu.SemaphoreType.DMA((len(chunks),)),
    ]


def reduce_kernel(n, groups, chunks, plan, part_rows, *refs):
    sources, refs = refs[: len(part_rows)], refs[len(part_rows) :]
    small_in, total_out, small_out, field, total, small, load_sem = refs[:7]
    loads = []
    start = 0
    for index, source in enumerate(sources):
        loads.append(
            pltpu.make_async_copy(source, field.at[:, pl.ds(start, part_rows[index])], load_sem.at[index])
        )
        loads[-1].start()
        start += part_rows[index]
    spans = [(0, small_in.shape[1])]
    reducer = Reducer(n, groups, chunks, field, total, total_out, small, small_out, spans, refs[7:])
    small[0] = small_in[...]
    reducer.greet()
    reducer.enter()
    for load in loads:
        load.wait()
    for order in plan:
        for kind, index, step in order:
            if kind == "chunk":
                reducer.chunk_step(index, step)
            else:
                reducer.small_step(index, step)
    reducer.finish()


def reduce_all(n, groups, parts, small):
    part_rows = [part.shape[1] for part in parts]
    rows = sum(part_rows)
    chunk_rows = max(16 * groups, rows // 8)
    chunks = [(start, chunk_rows, False, 0) for start in range(0, rows, chunk_rows)]
    plan, unused = plan_steps(n, chunks, [], [(small.shape[1], 0)], [0.0])
    small_shape = small.shape[1:]
    vm = pl.BlockSpec(memory_space=pltpu.VMEM)
    hbm = pl.BlockSpec(memory_space=pl.ANY)
    return pl.pallas_call(
        functools.partial(reduce_kernel, n, groups, chunks, plan, part_rows),
        in_specs=[hbm] * len(parts) + [vm],
        out_specs=[hbm, vm],
        out_shape=[out_like((rows, WIDE), BF16), out_like(small_shape, F32)],
        scratch_shapes=[
            pltpu.VMEM((n, rows, WIDE), BF16),
            pltpu.VMEM((rows, WIDE), BF16),
            pltpu.VMEM((2, n, *small_shape), F32),
            pltpu.SemaphoreType.DMA((len(parts),)),
            *reducer_scratch(n, groups, chunks, rows, small_shape),
        ],
        compiler_params=pltpu.CompilerParams(
            vmem_limit_bytes=VMEM_LIMIT, collective_id=0, has_side_effects=True
        ),
    )(*parts, small)


Y_FIRST = [letter == "y" for letter in "xyyyyxxyyyyyyxyx"]
BACK_SEGMENTS = [
    1.5, 1.3, 2.9, 2.9, 2.9, 2.9, 1.4, 2.8, 3.2, 1.9, 2.4, 2.4, 2.9, 2.9, 1.4, 1.1, 1.1,
]


def back_chunks(half, hidden_rows):
    released = [(half, 0)] * (2 * hidden_rows // half + 1)
    released += [(half, segment) for segment in (6, 7, 7, 8, 14, 15, 16)]
    chunks = []
    start = 0
    for index, (rows, segment) in enumerate(released):
        chunks.append((start, rows, Y_FIRST[index % len(Y_FIRST)], segment))
        start += rows
    return chunks


def back_kernel(n, groups, rows_block, chunks, plan, load_plan, *refs):
    feed_refs, refs = refs[:3], refs[3:]
    streamed, refs = refs[: len(load_plan)], refs[len(load_plan) :]
    (
        target_row, memory_row, cross_query, cross_grad, cross_keys,
        cross_lse, cross_delta, feed_sums, in_bias_grad, gain, first_rstd, self_lse,
        total_out, small_out, memory_out, input_out,
        field, total, small, sums, memory_grad, input_grad, memory_sent, memory_got, input_sent, input_got, pair_low,
        wide, keys_t, query_cols, query_rows, grad_cols, grad_rows, query_grad_t, key_grad, value_grad,
        held, held_low, held_grad, query_low, branch, self_grad, self_delta, g1,
        feed_sem, load_sem, extra_send, extra_recv, extra_store,
    ) = refs[:49]
    refs = refs[49:]
    held_loads, buffers = refs[: len(load_plan)], refs[len(load_plan) :]
    count = cross_query.shape[0]
    length = cross_keys.shape[0]
    tiles = count // TILE
    blocks = count // rows_block
    half = WIDE // n
    group, part = lax.axis_index("dp"), lax.axis_index("blk")
    place = lax.rem(group, 2)
    away = place != part
    owner = (group - place + part, place)

    feed_loads = []
    start = 0
    for index, source in enumerate(feed_refs):
        rows = source.shape[1]
        feed_loads.append(
            pltpu.make_async_copy(source, field.at[:, pl.ds(start, rows)], feed_sem.at[index])
        )
        feed_loads[-1].start()
        start += rows
    loads = [
        pltpu.make_async_copy(source, target, load_sem.at[index])
        for index, (source, target) in enumerate(zip(streamed, held_loads))
    ]
    for load in loads:
        load.start()
    cross_values = held_loads[0]
    memory_pieces = [held_loads[1].at[step] for step in range(n)]
    held_loads = held_loads[2:]
    (
        pair_weight, first_low, query_weight, g2, first_normal, self_out_weight, self_attended_t,
        self_keys, self_values, self_query,
    ) = held_loads[:10]
    input_pieces = [held_loads[10].at[step] for step in range(n)]
    self_in_weight = held_loads[11]

    spans = [(0, 8), (8, small_out.shape[0] - 8)]
    reducer = Reducer(n, groups, chunks, field, total, total_out, small, small_out, spans, buffers)
    reducer.greet(owner, away)

    extras = (
        (memory_sent, memory_got, memory_grad, memory_out), (input_sent, input_got, input_grad, input_out)
    )

    def extra_copy(index, hop):
        sent, got, *unused = extras[index]
        return pltpu.make_async_remote_copy(
            src_ref=sent.at[hop], dst_ref=got.at[hop],
            send_sem=extra_send.at[2 * index + hop], recv_sem=extra_recv.at[2 * index + hop],
            device_id=reducer.core_peer if hop == 0 else owner, device_id_type=pl.DeviceIdType.MESH,
        )

    def extra_store_copy(index, from_owner):
        sent, got, unused, out = extras[index]
        return pltpu.make_async_copy((got if from_owner else sent).at[1], out, extra_store.at[index])

    def extra_step(index, step):
        sent, got, result, unused = extras[index]
        if step == 0:
            extra_copy(index, 0).start()
        elif step == 1:
            extra_copy(index, 0).wait()

            @pl.loop(0, blocks)
            def _(block):
                rows = dyn(block, rows_block)
                value = result[rows, :] + got[0, rows, :].astype(F32)
                sent[1, rows, :] = value.astype(BF16)

            @pl.when(away)
            def _():
                extra_copy(index, 1).start()

            @pl.when(jnp.logical_not(away))
            def _():
                extra_store_copy(index, False).start()
        else:

            @pl.when(away)
            def _():
                extra_copy(index, 1).wait()
                extra_store_copy(index, True).start()

    def run_steps(number):
        for kind, index, step in plan[number]:
            if kind == "chunk":
                reducer.chunk_step(index, step)
            elif kind == "small":
                reducer.small_step(index, step)
            else:
                extra_step(index, step)

    def wait_loads(first, last):
        for load in loads[first:last]:
            load.wait()

    spread_row(memory_row, wide)
    transpose_rows(cross_keys, keys_t)
    for load in feed_loads:
        load.wait()
    reducer.enter()
    run_steps(0)
    prepare_back(tiles, cross_query, cross_grad, query_cols, query_rows, grad_cols, grad_rows)
    clear(query_grad_t)
    sums[...] = jnp.zeros(sums.shape, F32)
    run_steps(1)
    wait_loads(0, 1)
    for tile in range(tiles):
        attend_back(
            tile, 0, length // TILE, target_row, place * count, wide, place * count, False,
            query_cols, query_rows, grad_cols, grad_rows, cross_keys, keys_t, cross_values,
            cross_lse, cross_delta, query_grad_t, key_grad, value_grad, held, held_low, held_grad, tile == 0,
        )
        run_steps(2 + tile)
    base = 2 * in_bias_grad.shape[1] // n + half
    wait_loads(1, 9)
    query_finish(tiles, query_grad_t, query_low, sums, 2, True)
    spread_parts(n, tn(first_low[...], query_low[...]), field, base)
    run_steps(6)
    for side, source in ((0, key_grad), (1, value_grad)):

        @pl.loop(0, length // rows_block)
        def _(block):
            rows = dyn(block, rows_block)
            value = source[rows, :]
            source[rows, :] = jnp.zeros(value.shape, F32)
            pair_low[side, rows, :] = value.astype(BF16)
            if side == 1:
                sums[3:4, :] += col_sum(value)

        spread_parts(
            n, row_product(n, place, memory_pieces, pair_low.at[side]), field, base + half + side * half
        )
    run_steps(7)
    first_back(
        blocks, rows_block, g2, query_low, query_weight, first_normal, first_rstd, gain, self_out_weight,
        g1, branch, self_grad, sums, 4,
    )
    spread_parts(n, nn(self_attended_t[...], branch[...]), field, base + 3 * half)
    write_delta(tiles, self_grad, self_attended_t, self_delta)
    small[...] = jnp.zeros(small.shape, F32)
    wide_half = in_bias_grad.shape[1] // n
    for b in range(n):
        here = slice(b * half, (b + 1) * half)
        small[0, b, 8:13, :] = sums[2:7, here]
        small[0, b, 13:19, :] = feed_sums[0:6, here]
        for row in range(wide_half // half):
            begin = b * wide_half + row * half
            small[0, b, 19 + row : 20 + row, :] = in_bias_grad[:, begin : begin + half]
    run_steps(8)

    narrow = [ref.at[:, pl.ds(0, KEYS)] for ref in (held, held_low, held_grad)]
    wait_loads(9, len(loads))
    spread_row(target_row, wide)
    transpose_rows(self_keys, keys_t)
    prepare_back(tiles, self_query, self_grad, query_cols, query_rows, grad_cols, grad_rows)
    clear(query_grad_t)
    run_steps(9)
    for tile in range(tiles):
        attend_back(
            tile, 0, place * tiles + tile + 1, target_row, place * count, wide, place * count, True,
            query_cols, query_rows, grad_cols, grad_rows, self_keys, keys_t, self_values,
            self_lse, self_delta, query_grad_t, key_grad, value_grad, *narrow,
        )
        run_steps(10 + tile)
    query_finish(tiles, query_grad_t, query_low, sums, 0, False)
    spread_parts(n, tn(input_pieces[0][...], query_low[...]), field, base + 4 * half)
    run_steps(14)
    spread_parts(n, row_product(n, place, input_pieces, key_grad), field, base + 5 * half)
    run_steps(15)
    spread_parts(n, row_product(n, place, input_pieces, value_grad), field, base + 6 * half)
    run_steps(16)
    number = 17
    for step in range(n):
        spot = lax.rem(place + n - step, n)
        for block in range(blocks):
            rows = dyn(spot * blocks + block, rows_block)
            here = slice(block * rows_block, (block + 1) * rows_block)
            key_low, value_part = key_grad[rows, :].astype(BF16), value_grad[rows, :]
            sums[1:2, :] += col_sum(value_part)
            back = nt(key_low, self_in_weight[:, WIDE : 2 * WIDE])
            back += nt(value_part.astype(BF16), self_in_weight[:, 2 * WIDE :])
            if step == 0:
                input_grad[here, :] = back + g1[here, :] + nt(query_low[here, :], self_in_weight[:, :WIDE])
            else:
                input_sent[0, here, :] = back.astype(BF16)
            if step == n - 1 and block == blocks - 1:
                for b in range(n):
                    small[0, b, 0:2, :] = sums[0:2, b * half : (b + 1) * half]
            run_steps(number)
            number += 1
    for step in range(n):
        spot = lax.rem(place + n - step, n)
        for block in range(blocks):
            rows = dyn(spot * blocks + block, rows_block)
            here = slice(block * rows_block, (block + 1) * rows_block)
            back = nt(pair_low[0, rows, :], pair_weight[:, :WIDE]) + nt(pair_low[1, rows, :], pair_weight[:, WIDE:])
            if step == 0:
                memory_grad[here, :] = back
            else:
                memory_sent[0, here, :] = back.astype(BF16)
            run_steps(number)
            number += 1
    run_steps(number)
    for index in range(2):

        @pl.when(away)
        def _():
            extra_store_copy(index, True).wait()

        @pl.when(jnp.logical_not(away))
        def _():
            extra_store_copy(index, False).wait()

    reducer.finish()


def back_and_reduce(n, groups, rows_block, feed_grads, streamed, resident):
    count, features = resident[2].shape
    length = n * count
    hidden_rows = feed_grads[0].shape[1]
    half = features // n
    rows = sum(part.shape[1] for part in feed_grads) + 7 * half
    chunks = back_chunks(half, hidden_rows)
    steps = n * (count // rows_block)
    segments = BACK_SEGMENTS + [2.2 / steps] * steps + [2.0 / steps] * steps
    last = len(segments) - 1
    extras = [(count, last), (count, last - steps)]
    smalls = [(8, last - steps), (16, 8)]
    plan, unused = plan_steps(n, chunks, extras, smalls, segments)
    small_shape = (-(-(19 + hidden_rows // half) // 8) * 8, half)
    vm = pl.BlockSpec(memory_space=pltpu.VMEM)
    hbm = pl.BlockSpec(memory_space=pl.ANY)
    low_rows = pltpu.VMEM((count, features), BF16)
    wide_rows = pltpu.VMEM((count, features), F32)
    columns = pltpu.VMEM((features, 2 * count), BF16)
    doubled = pltpu.VMEM((2 * count, features), BF16)
    all_wide = pltpu.VMEM((length, features), F32)
    sent = pltpu.VMEM((2, count, features), BF16)
    held = (features // PAIR, BACK_KEYS, 2 * TILE)
    return pl.pallas_call(
        functools.partial(back_kernel, n, groups, rows_block, chunks, plan, [part.shape for part in streamed]),
        in_specs=[hbm] * (len(feed_grads) + len(streamed)) + [vm] * len(resident),
        out_specs=[hbm, vm, hbm, hbm],
        out_shape=[
            out_like((rows, WIDE), BF16), out_like(small_shape, F32),
            out_like((count, features), BF16), out_like((count, features), BF16),
        ],
        scratch_shapes=[
            pltpu.VMEM((n, rows, WIDE), BF16), pltpu.VMEM((rows, WIDE), BF16),
            pltpu.VMEM((2, n, *small_shape), F32), pltpu.VMEM((8, features), F32),
            wide_rows, wide_rows, sent, sent, sent, sent, pltpu.VMEM((2, length, features), BF16),
            pltpu.VMEM((length, TILE), jnp.int32), pltpu.VMEM((features, length), BF16),
            columns, doubled, columns, doubled,
            pltpu.VMEM((features, count), F32), all_wide, all_wide,
            pltpu.VMEM(held, F32), pltpu.VMEM(held, BF16), pltpu.VMEM(held, BF16),
            low_rows, low_rows, low_rows, pltpu.VMEM((features // PAIR, 2 * count), F32), wide_rows,
            pltpu.SemaphoreType.DMA((len(feed_grads),)), pltpu.SemaphoreType.DMA((len(streamed),)),
            pltpu.SemaphoreType.DMA((4,)), pltpu.SemaphoreType.DMA((4,)), pltpu.SemaphoreType.DMA((2,)),
            *[pltpu.VMEM(part.shape, part.dtype) for part in streamed],
            *reducer_scratch(n, groups, chunks, rows, small_shape),
        ],
        compiler_params=pltpu.CompilerParams(
            vmem_limit_bytes=VMEM_LIMIT, collective_id=0, has_side_effects=True
        ),
    )(*feed_grads, *streamed, *resident)


def spread_row(row_ref, wide_ref):
    @pl.loop(0, row_ref.shape[1] // TILE)
    def _(block):
        wide_ref[dyn(block, TILE), :] = jnp.broadcast_to(row_ref[:, dyn(block, TILE)], (TILE, TILE)).T


def attend_whole(
    tiles, query_row_ref, first_query, key_wide_ref, causal, query_cols, keys, values_t, attended_t, lse_ref,
    held, held_low,
):
    pairs = WIDE // PAIR
    length = keys.shape[0]

    @pl.loop(0, tiles)
    def _(tile):
        begin = pl.multiple_of(first_query + tile * TILE, TILE)
        allowed = key_wide_ref[...] == query_row_ref[:, pl.ds(begin, TILE)]
        if causal:
            key_position = lax.broadcasted_iota(jnp.int32, (length, TILE), 0)
            query_position = begin + lax.broadcasted_iota(jnp.int32, (length, TILE), 1)
            allowed = allowed & (key_position <= query_position)
        bias = jnp.where(allowed, 0.0, MASKED)
        bias = jnp.concatenate([bias, bias], axis=1)
        both = dyn(tile, 2 * TILE)
        peaks, shares = [], []
        for pair in range(pairs):
            lanes = slice(pair * PAIR, (pair + 1) * PAIR)
            scores = nn(keys[:, lanes], query_cols[lanes, both]) + bias
            held[pair] = scores
            peaks.append(jnp.max(scores, axis=0, keepdims=True))
        for pair in range(pairs):
            weights = jnp.exp(held[pair] - peaks[pair])
            total = col_sum(weights)
            held_low[pair] = weights.astype(BF16)
            lse_ref[pair : pair + 1, both] = peaks[pair] + jnp.log(total)
            shares.append(1.0 / total)
        for pair in range(pairs):
            share = shares[pair]
            mixed = nn(values_t[pair * PAIR : (pair + 1) * PAIR, :], held_low[pair])
            first = slice(pair * PAIR, pair * PAIR + HEAD)
            second = slice(pair * PAIR + HEAD, (pair + 1) * PAIR)
            attended_t[first, dyn(tile, TILE)] = (mixed[:HEAD, :TILE] * share[:, :TILE]).astype(BF16)
            attended_t[second, dyn(tile, TILE)] = (mixed[HEAD:, TILE:] * share[:, TILE:]).astype(BF16)


FORWARD_LOADS = 7
FORWARD_STORES = 16


def forward_kernel(n, groups, rows_block, *refs):
    (
        inputs, memory, cotangent, *weights_in
    ) = refs[: 3 + FORWARD_LOADS]
    refs = refs[3 + FORWARD_LOADS :]
    (
        target_here, memory_here, in_bias, self_out_bias, first_gain, first_shift, cross_bias, cross_out_bias,
        second_gain, second_shift, feed_bias, down_bias, last_gain, last_shift,
    ) = refs[:14]
    refs = refs[14:]
    stores_out, refs = refs[:FORWARD_STORES], refs[FORWARD_STORES:]
    (
        layer_output, lse_one, lse_two, delta_ref, first_rstd, sums_out, in_bias_grad, target_row, memory_row,
    ) = refs[:9]
    refs = refs[9:]
    held_weights, refs = refs[:FORWARD_LOADS], refs[FORWARD_LOADS:]
    held_stores, refs = refs[:FORWARD_STORES], refs[FORWARD_STORES:]
    (
        self_in_weight, self_out_weight, cross_weight, pair_weight, cross_out_weight, in_weight, down_weight
    ) = held_weights
    (
        input_pieces, memory_pieces, query_low, keys, values, attended_one, first_normal, first_low, cross_query,
        cross_keys, cross_values, grad_out, g2_out, in_grad, down_grad, cross_out_grad,
    ) = held_stores
    (
        cot, output_low, output_got, target_there, memory_there, wide, values_t, cross_values_t, query_cols, held,
        held_low, attended_two, second_normal, second_rstd, second_low, second_low_t, active, slope, third, branch,
        load_sem, store_sem, own_sem, far_send, far_recv, core_send, core_recv,
    ) = refs
    count = inputs.shape[0]
    tiles = count // TILE
    blocks = count // rows_block
    half = WIDE // n
    group, part = lax.axis_index("dp"), lax.axis_index("blk")
    place = lax.rem(group, 2)
    away = place != part
    owner = (group - place + part, place)
    core_peer = (group + 1 - 2 * place, part)
    mesh_type = pl.DeviceIdType.MESH

    loads = [
        pltpu.make_async_copy(source, target, load_sem.at[index])
        for index, (source, target) in enumerate(zip(weights_in, held_weights))
    ]
    for load in loads:
        load.start()
    barrier = pltpu.get_barrier_semaphore()
    pl.semaphore_signal(barrier, inc=1, device_id=core_peer, device_id_type=mesh_type)

    @pl.when(away)
    def _():
        pl.semaphore_signal(barrier, inc=1, device_id=owner, device_id_type=mesh_type)

    pl.semaphore_wait(barrier, jnp.where(away, 2, 1))

    pieces_of = (count // 2, count // 2)
    arrivals = []
    for index, (source, target) in enumerate(((inputs, input_pieces), (memory, memory_pieces))):
        for block in range(2):
            rows = pl.ds(block * (count // 2), count // 2)
            arrivals.append((source.at[rows], target.at[0, rows], 2 * index + block))
    arrivals.append((cotangent, cot, 4))

    def far_copy(entry):
        source, target, sem = entry
        return pltpu.make_async_remote_copy(
            src_ref=source, dst_ref=target, send_sem=far_send.at[sem], recv_sem=far_recv.at[sem],
            device_id=owner, device_id_type=mesh_type,
        )

    def own_copy(entry):
        source, target, sem = entry
        return pltpu.make_async_copy(source, target, own_sem.at[sem])

    def core_copy(source, target, sem):
        return pltpu.make_async_remote_copy(
            src_ref=source, dst_ref=target, send_sem=core_send.at[sem], recv_sem=core_recv.at[sem],
            device_id=core_peer, device_id_type=mesh_type,
        )

    @pl.when(away)
    def _():
        for entry in arrivals:
            far_copy(entry).start()

    @pl.when(jnp.logical_not(away))
    def _():
        for entry in arrivals:
            own_copy(entry).start()

    def arrive(entry):
        @pl.when(away)
        def _():
            far_copy(entry).wait()

        @pl.when(jnp.logical_not(away))
        def _():
            own_copy(entry).wait()

    def forward_copy(index):
        held_piece = (input_pieces, memory_pieces)[index // 2]
        rows = pl.ds((index % 2) * (count // 2), count // 2)
        return core_copy(held_piece.at[0, rows], held_piece.at[1, rows], index)

    segment_copies = [
        core_copy(target_here, target_there, 4), core_copy(memory_here, memory_there, 5)
    ]
    for copy in segment_copies:
        copy.start()

    stores = {}

    def store(index):
        stores[index] = pltpu.make_async_copy(held_stores[index], stores_out[index], store_sem.at[index])
        stores[index].start()

    for copy in segment_copies:
        copy.wait()
    target_row[...] = jnp.where(away, target_there[...], target_here[...])
    memory_row[...] = jnp.where(away, memory_there[...], memory_here[...])
    spread_row(target_row, wide)
    loads[0].wait()

    def project(piece, block, spot):
        rows = slice(block * (count // 2), (block + 1) * (count // 2))
        source = input_pieces[piece, rows, :]
        field = nn(source, self_in_weight[:, WIDE:])
        here = dyn(spot * 2 + block, count // 2)
        keys[here, :] = field[:, :WIDE].astype(BF16)
        value = (field[:, WIDE:] + in_bias[1:2, :]).astype(BF16)
        values[here, :] = value
        values_t[:, here] = value.T

        @pl.when(piece == 0)
        def _():
            query = (nn(source, self_in_weight[:, :WIDE]) + in_bias[0:1, :]).astype(BF16)
            query = (query.astype(F32) * SCALE).astype(BF16)
            query_low[rows, :] = query
            for tile in range(count // 2 // TILE):
                split_columns(
                    query[tile * TILE : (tile + 1) * TILE, :].T, query_cols, block * (count // 2 // TILE) + tile
                )

    def project_memory(piece, spot):
        field = nn(memory_pieces[piece], pair_weight[...])
        here = dyn(spot, count)
        cross_keys[here, :] = field[:, :WIDE].astype(BF16)
        value = (field[:, WIDE:] + cross_bias[1:2, :]).astype(BF16)
        cross_values[here, :] = value
        cross_values_t[:, here] = value.T

    early = jnp.where(away, 1, 0)

    @pl.when(jnp.logical_not(away))
    def _():
        for index in range(4):
            own_copy(arrivals[index]).wait()
            forward_copy(index).start()

    @pl.when(away)
    def _():
        for index in range(2):
            forward_copy(index).wait_recv()

    for block in range(2):
        project(early, block, part)
    loads[3].wait()

    @pl.when(away)
    def _():
        for index in range(2, 4):
            forward_copy(index).wait_recv()

    project_memory(early, part)
    for block in range(2):

        @pl.when(away)
        def _():
            far_copy(arrivals[block]).wait()
            forward_copy(block).start()

        @pl.when(jnp.logical_not(away))
        def _():
            forward_copy(block).wait_recv()

        project(1 - early, block, 1 - part)
    for index in range(2):
        forward_copy(index).wait_send()
    store(0)
    store(2)
    store(3)
    store(4)
    attend_whole(
        tiles, target_row, place * count, wide, True, query_cols, keys, values_t, attended_one, lse_one,
        held, held_low,
    )
    store(5)
    for load in loads[1:3]:
        load.wait()

    @pl.when(away)
    def _():
        for index in range(2, 4):
            far_copy(arrivals[index]).wait()
            forward_copy(index).start()

    @pl.loop(0, blocks)
    def _(block):
        rows = dyn(block, rows_block)
        attended = attended_one[:, rows].T
        field = input_pieces[0, rows, :].astype(F32) + nn(attended, self_out_weight[...]) + self_out_bias[...]
        normal, rstd = normalize(field)
        first_normal[rows, :] = normal
        first_rstd[rows, :] = rstd
        low = (normal * first_gain[...] + first_shift[...]).astype(BF16)
        first_low[rows, :] = low
        query = (nn(low, cross_weight[...]) + cross_bias[0:1, :]).astype(BF16)
        query = (query.astype(F32) * SCALE).astype(BF16)
        cross_query[rows, :] = query
        for tile in range(rows_block // TILE):
            split_columns(
                query[tile * TILE : (tile + 1) * TILE, :].T, query_cols, block * (rows_block // TILE) + tile
            )

    store(6)
    store(7)
    store(8)

    @pl.when(jnp.logical_not(away))
    def _():
        for index in range(2, 4):
            forward_copy(index).wait_recv()

    project_memory(1 - early, 1 - part)
    for index in range(2, 4):
        forward_copy(index).wait_send()
    store(1)
    store(9)
    store(10)
    spread_row(memory_row, wide)
    attend_whole(
        tiles, target_row, place * count, wide, False, query_cols, cross_keys, cross_values_t, attended_two, lse_two,
        held, held_low,
    )
    for load in loads[4:]:
        load.wait()

    @pl.loop(0, blocks)
    def _(block):
        rows = dyn(block, rows_block)
        attended = attended_two[:, rows].T
        first = first_normal[rows, :] * first_gain[...] + first_shift[...]
        field = first + nn(attended, cross_out_weight[...]) + cross_out_bias[...]
        normal, rstd = normalize(field)
        second_normal[rows, :] = normal
        second_rstd[rows, :] = rstd
        second = normal * second_gain[...] + second_shift[...]
        third[rows, :] = second + down_bias[...]
        low = second.astype(BF16)
        second_low[rows, :] = low
        second_low_t[:, rows] = low.T

    chunks, chunk_size = in_weight.shape[1] // WIDE, WIDE
    arrive(arrivals[4])

    @pl.loop(0, chunks // 2)
    def _(chunk):
        lanes = dyn(chunk, 2 * chunk_size)
        hidden = nn(second_low[...], in_weight[:, lanes]) + feed_bias[:, lanes]
        value, derivative = gate(hidden)
        value = value.astype(BF16)
        active[:, lanes] = value
        slope[:, lanes] = derivative
        third[...] += nn(value, down_weight[lanes, :])

    sums_out[...] = jnp.zeros(sums_out.shape, F32)

    @pl.loop(0, blocks)
    def _(block):
        rows = dyn(block, rows_block)
        normal, rstd = normalize(third[rows, :])
        output_low[rows, :] = (normal * last_gain[...] + last_shift[...]).astype(BF16)
        outer = cot[rows, :].astype(F32)
        grad = normalize_back(outer, last_gain[...], normal, rstd)
        third[rows, :] = grad
        low = grad.astype(BF16)
        branch[rows, :] = low
        sums_out[0:1, :] += col_sum(outer * normal)
        sums_out[1:2, :] += col_sum(outer)
        sums_out[2:3, :] += col_sum(low.astype(F32))

    output_copy = (output_low, output_got, 5)

    @pl.when(away)
    def _():
        far_copy(output_copy).start()

    per_half = chunks // n

    @pl.loop(0, chunks)
    def _(chunk):
        lanes = dyn(chunk, chunk_size)
        share = tn(active[:, lanes], branch[...]).astype(BF16)
        down_grad[lax.div(chunk, per_half), dyn(lax.rem(chunk, per_half), chunk_size), :] = share
        inner = nt(branch[...], down_weight[lanes, :])
        hidden_grad = (inner * slope[:, lanes]).astype(BF16)
        in_bias_grad[:, lanes] = col_sum(hidden_grad.astype(F32))
        third[...] += nt(hidden_grad, in_weight[:, lanes])
        share = nn(second_low_t[...], hidden_grad).astype(BF16)
        for b in range(n):
            in_grad[b, dyn(chunk, half), :] = share[b * half : (b + 1) * half, :]

    store(13)
    store(14)

    @pl.loop(0, blocks)
    def _(block):
        rows = dyn(block, rows_block)
        outer = third[rows, :]
        normal = second_normal[rows, :]
        grad = normalize_back(outer, second_gain[...], normal, second_rstd[rows, :])
        g2_out[rows, :] = grad
        low = grad.astype(BF16)
        branch[rows, :] = low
        sums_out[3:4, :] += col_sum(outer * normal)
        sums_out[4:5, :] += col_sum(outer)
        sums_out[5:6, :] += col_sum(low.astype(F32))
        grad_out[rows, :] = nt(low, cross_out_weight[...]).astype(BF16)

    store(11)
    store(12)
    spread_parts(n, nn(attended_two[...], branch[...]), cross_out_grad, 0)
    store(15)
    write_delta(tiles, grad_out, attended_two, delta_ref)

    @pl.when(away)
    def _():
        far_copy(output_copy).wait()
        layer_output[...] = output_got[...]

    @pl.when(jnp.logical_not(away))
    def _():
        layer_output[...] = output_low[...]

    for index in range(FORWARD_STORES):
        stores[index].wait()


def forward_all(n, groups, rows_block, activations, weights, resident):
    count, features = activations[0].shape
    length = n * count
    hidden = weights[5].shape[1]
    half = features // n
    vm = pl.BlockSpec(memory_space=pltpu.VMEM)
    hbm = pl.BlockSpec(memory_space=pl.ANY)
    low, wide, every = (count, features), (count, features), (length, features)
    stored = [
        ((2, *low), BF16), ((2, *low), BF16), (low, BF16), (every, BF16), (every, BF16), ((features, count), BF16),
        (wide, F32), (low, BF16), (low, BF16), (every, BF16), (every, BF16), (low, BF16), (wide, F32),
        ((n, hidden // n, features), BF16), ((n, hidden // n, features), BF16), ((n, half, features), BF16),
    ]
    stats = out_like((features // PAIR, 2 * count), F32)
    row_like = out_like((1, length), jnp.int32)
    row_scratch = pltpu.VMEM((1, length), jnp.int32)
    held = (features // PAIR, length, 2 * TILE)
    low_rows, wide_rows = pltpu.VMEM(low, BF16), pltpu.VMEM(wide, F32)
    return pl.pallas_call(
        functools.partial(forward_kernel, n, groups, count),
        in_specs=[hbm] * (len(activations) + len(weights)) + [vm] * len(resident),
        out_specs=[hbm] * len(stored) + [vm] * 9,
        out_shape=[out_like(*entry) for entry in stored] + [
            out_like(low, BF16), stats, stats, stats, out_like((count, 1), F32), out_like((8, features), F32),
            out_like((1, hidden), F32), row_like, row_like,
        ],
        scratch_shapes=[
            *[pltpu.VMEM(weight.shape, weight.dtype) for weight in weights],
            *[pltpu.VMEM(*entry) for entry in stored],
            low_rows, low_rows, low_rows, row_scratch, row_scratch,
            pltpu.VMEM((length, TILE), jnp.int32), pltpu.VMEM((features, length), BF16),
            pltpu.VMEM((features, length), BF16), pltpu.VMEM((features, 2 * count), BF16), pltpu.VMEM(held, F32), pltpu.VMEM(held, BF16),
            pltpu.VMEM((features, count), BF16), wide_rows, pltpu.VMEM((count, 1), F32), low_rows,
            pltpu.VMEM((features, count), BF16), pltpu.VMEM((count, hidden), BF16),
            pltpu.VMEM((count, hidden), F32), wide_rows, low_rows,
            pltpu.SemaphoreType.DMA((len(weights),)), pltpu.SemaphoreType.DMA((len(stored),)),
            pltpu.SemaphoreType.DMA((5,)), pltpu.SemaphoreType.DMA((6,)), pltpu.SemaphoreType.DMA((6,)),
            pltpu.SemaphoreType.DMA((6,)), pltpu.SemaphoreType.DMA((6,)),
        ],
        compiler_params=pltpu.CompilerParams(
            vmem_limit_bytes=VMEM_LIMIT, collective_id=1, has_side_effects=True
        ),
    )(*activations, *weights, *resident)


def widen_kernel(plan, source, *outs):
    for out, (start, columns) in zip(outs, plan):
        height = out.shape[0]
        for column in range(columns):
            out[:, column * WIDE : (column + 1) * WIDE] = source[
                start + column * height : start + (column + 1) * height, :
            ].astype(F32)


def finish_kernel(plan, packed, *refs):
    count = len(plan)
    input_low, memory_low, output_low, small, *refs = refs
    (
        *weights, input_grad, memory_grad, layer_output, self_bias, cross_bias, feed_bias,
    ) = refs[: count + 6]
    refs = refs[count + 6 :]
    vectors, refs = refs[:9], refs[9:]
    held, refs = refs[:count], refs[count:]
    wide, refs = refs[:count], refs[count:]
    input_held, memory_held, output_held, input_wide, memory_wide, load_sem, store_sem = refs

    def load(index):
        start, columns = plan[index]
        return pltpu.make_async_copy(
            packed.at[pl.ds(start, held[index].shape[0])], held[index], load_sem.at[index]
        )

    extra = [
        pltpu.make_async_copy(input_low, input_held, load_sem.at[count]),
        pltpu.make_async_copy(memory_low, memory_held, load_sem.at[count + 1]),
    ]
    output = pltpu.make_async_copy(output_low, output_held, load_sem.at[count + 2])
    loads = [load(index) for index in range(count)]
    order = sorted(range(count), key=lambda index: held[index].shape[0])
    for index in order:
        loads[index].start()
    for copy in extra + [output]:
        copy.start()
    stores = []
    for index in order:
        start, columns = plan[index]
        loads[index].wait()
        height = wide[index].shape[0]

        @pl.loop(0, height // 64)
        def _(block):
            for column in range(columns):
                here = pl.ds(pl.multiple_of(column * height + block * 64, 64), 64)
                wide[index][dyn(block, 64), column * WIDE : (column + 1) * WIDE] = held[index][here, :].astype(F32)

        stores.append(pltpu.make_async_copy(wide[index], weights[index], store_sem.at[index]))
        stores[-1].start()
    for index, (source, target, result) in enumerate(
        ((input_held, input_wide, input_grad), (memory_held, memory_wide, memory_grad))
    ):
        extra[index].wait()

        @pl.loop(0, target.shape[0] // 128)
        def _(block):
            target[dyn(block, 128), :] = source[dyn(block, 128), :].astype(F32)

        stores.append(pltpu.make_async_copy(target, result, store_sem.at[count + index]))
        stores[-1].start()
    output.wait()
    stores.append(pltpu.make_async_copy(output_held, layer_output, store_sem.at[count + 2]))
    stores[-1].start()
    self_bias[...] = small[0:2, :]
    cross_bias[...] = small[8:10, :]
    for index, vector in enumerate(vectors):
        vector[...] = small[10 + index, :]
    half = small.shape[1]
    for row in range(feed_bias.shape[0] // half):
        feed_bias[row * half : (row + 1) * half] = small[19 + row, :]
    for copy in stores:
        copy.wait()


def finish_all(n, packed, small, input_low, memory_low, layer_output, hidden):
    count, features = input_low.shape
    half = features // n
    plan, shapes, parts = [], [], []
    start = 0
    for height, columns in (
        (half, hidden // features), (hidden // n, 1), (half, 1), (half, 1), (half, 2), (half, 1), (half, 3)
    ):
        plan.append((start, columns))
        parts.append((height * columns, features))
        shapes.append((height, columns * features))
        start += height * columns
    vm = pl.BlockSpec(memory_space=pltpu.VMEM)
    hbm = pl.BlockSpec(memory_space=pl.ANY)
    wide = (count, features)
    return pl.pallas_call(
        functools.partial(finish_kernel, plan),
        in_specs=[hbm] * 4 + [vm],
        out_specs=[hbm] * (len(plan) + 3) + [vm] * 12,
        out_shape=[out_like(shape, F32) for shape in shapes] + [
            out_like(wide, F32), out_like(wide, F32), out_like(wide, BF16),
            out_like((2, half), F32), out_like((2, half), F32), out_like((hidden // n,), F32),
        ] + [out_like((half,), F32)] * 9,
        scratch_shapes=[pltpu.VMEM(shape, BF16) for shape in parts]
        + [pltpu.VMEM(shape, F32) for shape in shapes]
        + [
            pltpu.VMEM(wide, BF16), pltpu.VMEM(wide, BF16), pltpu.VMEM(wide, BF16), pltpu.VMEM(wide, F32),
            pltpu.VMEM(wide, F32),
            pltpu.SemaphoreType.DMA((len(plan) + 3,)), pltpu.SemaphoreType.DMA((len(plan) + 3,)),
        ],
        compiler_params=pltpu.CompilerParams(vmem_limit_bytes=VMEM_LIMIT),
    )(packed, input_low, memory_low, layer_output, small)


def key_ranges(query_segment, key_segment, tiles, limit):
    edges = query_segment.reshape(tiles, TILE)
    low = jnp.sum((key_segment[None, :] < edges[:, :1]).astype(jnp.int32), axis=1)
    high = jnp.sum((key_segment[None, :] <= edges[:, TILE - 1 :]).astype(jnp.int32), axis=1)
    if limit is not None:
        high = jnp.minimum(high, limit)
    return jnp.stack([low // TILE, (high + TILE - 1) // TILE]).astype(jnp.int32)


def apart(
    n, groups, rows_block, input_rows, memory_rows, cotangent_rows, target_segments, memory_segments,
    self_in_weight, self_in_bias, self_out_weight, self_out_bias, first_gain, first_shift,
    cross_query_weight, cross_pair_weight, cross_bias, cross_out_weight, cross_out_bias,
    second_gain, second_shift, feed_in_weight, feed_in_bias, feed_out_weight, feed_out_bias,
    third_gain, third_shift,
):
    count, features = input_rows.shape
    length = n * count
    hidden = feed_in_weight.shape[1]
    tiles = count // TILE
    half = features // n
    place = lax.axis_index("blk").astype(jnp.int32)

    def row(vector):
        return vector[None, :]

    def shifted(field, step):
        return lax.ppermute(field, "blk", [(s, (s + step) % n) for s in range(n)])

    def shifted_back(field, step):
        return lax.ppermute(field, "blk", [(s, (s - step) % n) for s in range(n)])

    input_pieces = [input_rows] + [shifted(input_rows, step) for step in range(1, n)]
    memory_pieces = [memory_rows] + [shifted(memory_rows, step) for step in range(1, n)]
    target_row, source_row = target_segments[0], memory_segments[0]
    target_here = lax.dynamic_slice_in_dim(target_row, place * count, count, 0)
    self_ranges = key_ranges(
        target_here, target_row, tiles, place * count + TILE * (1 + jnp.arange(tiles, dtype=jnp.int32))
    )
    cross_ranges = key_ranges(target_here, source_row, tiles, None)
    place_one = place[None]
    query_segment = target_here[None, :]
    target_column = target_row[:, None]
    source_column = source_row[:, None]

    stats = out_like((WIDE // PAIR, 2 * count), F32)
    low_rows = out_like((count, features), BF16)
    wide_rows = out_like((count, features), F32)
    low_row_all = out_like((length, features), BF16)
    statistic = out_like((count, 1), F32)
    wide_scratch = pltpu.VMEM((length, TILE), jnp.int32)
    values_t = pltpu.VMEM((features, length), BF16)
    query_cols = pltpu.VMEM((features, 2 * count), BF16)
    query_rows = pltpu.VMEM((2 * count, features), BF16)
    peak = pltpu.VMEM((8, 2 * TILE), F32)
    sums = pltpu.VMEM((features, TILE), F32)
    held = pltpu.VMEM((features // PAIR, KEYS, 2 * TILE), F32)
    held_low = pltpu.VMEM((features // PAIR, KEYS, 2 * TILE), BF16)
    square = 2 * count * features * features

    (
        query, keys, values, attended_t, lse, normal, rstd, first_low, cross_query
    ) = run(
        functools.partial(self_forward, n, rows_block),
        [place_one, self_ranges, *input_pieces, query_segment, target_column,
         self_in_weight, self_in_bias, self_out_weight, row(self_out_bias), row(first_gain),
         row(first_shift), cross_query_weight, cross_bias],
        2,
        [low_rows, low_row_all, low_row_all, out_like((features, count), BF16), stats, wide_rows,
         statistic, low_rows, low_rows],
        [wide_scratch, values_t, query_cols, peak, peak, sums, held, held_low],
        20 * square, 10 << 20,
    )

    (
        layer_output, cross_keys, cross_values, cross_lse, cross_delta, unused, cross_grad, g2,
        in_grad, down_grad, cross_out_grad, feed_sums, in_bias_grad,
    ) = run(
        functools.partial(cross_and_feed, n, rows_block),
        [place_one, cross_ranges, *memory_pieces, query_segment, source_column, cotangent_rows,
         cross_query, normal, row(first_gain), row(first_shift), cross_pair_weight, cross_bias,
         cross_out_weight, row(cross_out_bias), row(second_gain), row(second_shift),
         feed_in_weight, row(feed_in_bias), feed_out_weight, row(feed_out_bias),
         row(third_gain), row(third_shift)],
        2,
        [low_rows, low_row_all, low_row_all, stats, stats, out_like((8, 128), F32), low_rows, wide_rows,
         out_like((n, hidden // n, features), BF16), out_like((n, hidden // n, features), BF16),
         out_like((n, half, features), BF16), out_like((8, features), F32), out_like((1, hidden), F32)],
        [wide_scratch, values_t, query_cols, peak, peak, sums, held, held_low,
         pltpu.VMEM((features, count), BF16), pltpu.VMEM((count, features), F32),
         pltpu.VMEM((count, 1), F32), pltpu.VMEM((count, features), BF16),
         pltpu.VMEM((features, count), BF16), pltpu.VMEM((count, hidden), BF16),
         pltpu.VMEM((count, hidden), F32), pltpu.VMEM((count, features), F32),
         pltpu.VMEM((count, features), BF16), pltpu.VMEM((features, count), BF16)],
        50 * square, 20 << 20,
    )

    back_scratch = [
        wide_scratch, values_t, query_cols, query_rows, query_cols, query_rows,
        pltpu.VMEM((features, count), F32), pltpu.VMEM((length, features), F32),
        pltpu.VMEM((length, features), F32), held, held_low, held_low, pltpu.VMEM((count, features), BF16),
    ]
    sent_like = out_like((max(n - 1, 1), count, features), BF16)
    (
        memory_own, memory_sent, cross_query_grad, cross_pair_grad, self_out_grad, self_grad,
        self_delta, g1, cross_sums,
    ) = run(
        functools.partial(cross_backward, n, rows_block),
        [place_one, cross_ranges, *memory_pieces, query_segment, source_column, cross_query,
         cross_grad, cross_keys, cross_values, cross_lse, cross_delta, g2, normal, rstd, first_low,
         row(first_gain), cross_query_weight, cross_pair_weight, self_out_weight, attended_t],
        2,
        [wide_rows, sent_like, out_like((n, half, features), BF16),
         out_like((n, 2 * half, features), BF16), out_like((n, half, features), BF16), low_rows,
         stats, wide_rows, out_like((8, features), F32)],
        back_scratch + [pltpu.VMEM((count, features), BF16)],
        30 * square, 15 << 20,
    )
    (input_own, input_sent, self_in_grad, self_sums) = run(
        functools.partial(self_backward, n, rows_block),
        [place_one, self_ranges, *input_pieces, query_segment, target_column, query, self_grad,
         keys, values, lse, self_delta, g1, self_in_weight],
        2,
        [wide_rows, sent_like, out_like((n, 3 * half, features), BF16), out_like((8, features), F32)],
        back_scratch,
        30 * square, 15 << 20,
    )

    memory_grad, input_grad = memory_own, input_own
    for step in range(1, n):
        memory_grad = memory_grad + shifted_back(memory_sent[step - 1], step).astype(F32)
        input_grad = input_grad + shifted_back(input_sent[step - 1], step).astype(F32)

    vectors = jnp.concatenate([self_sums[:2], cross_sums[:5], feed_sums[:6]], axis=0)
    count_small = vectors.shape[0]
    small = jnp.concatenate(
        [
            jnp.transpose(vectors.reshape(count_small, n, half), (1, 0, 2)).reshape(n, -1),
            in_bias_grad.reshape(n, -1),
        ],
        axis=1,
    )
    amount = small.shape[1]
    small_rows = -(-amount // (8 * WIDE)) * 8
    small = jnp.pad(small, ((0, 0), (0, small_rows * WIDE - amount))).reshape(n, small_rows, WIDE)
    packed, small = reduce_all(
        n, groups,
        [in_grad, down_grad, cross_out_grad, cross_query_grad, cross_pair_grad, self_out_grad, self_in_grad],
        small,
    )
    small = small.reshape(-1)[:amount]
    return packed, small, memory_grad, input_grad, layer_output, count_small


def on_device(
    n, groups,
    inputs, memory, cotangent, target_segments, memory_segments,
    self_in_weight, self_in_bias, self_out_weight, self_out_bias, first_gain, first_shift,
    cross_query_weight, cross_pair_weight, cross_bias, cross_out_weight, cross_out_bias,
    second_gain, second_shift, feed_in_weight, feed_in_bias, feed_out_weight, feed_out_bias,
    third_gain, third_shift,
):
    input_rows, memory_rows, cotangent_rows = inputs[0], memory[0], cotangent[0]
    count, features = input_rows.shape
    length = n * count
    hidden = feed_in_weight.shape[1]
    rows_block = min(count, 256)
    tiles = count // TILE
    half = features // n
    near = n == 2 and groups % 4 == 0 and length <= 1024 and half % TILE == 0

    def row(vector):
        return vector[None, :]

    if near:
        (
            input_pieces, memory_pieces, query, keys, values, attended_t, normal, first_low, cross_query,
            cross_keys, cross_values, cross_grad, g2, in_grad, down_grad, cross_out_grad,
            layer_output, lse, cross_lse, cross_delta, rstd, feed_sums, in_bias_grad, target_row, memory_row,
        ) = forward_all(
            n, groups, rows_block,
            [input_rows, memory_rows, cotangent_rows],
            [self_in_weight, self_out_weight, cross_query_weight, cross_pair_weight, cross_out_weight,
             feed_in_weight, feed_out_weight],
            [target_segments, memory_segments, self_in_bias, row(self_out_bias), row(first_gain),
             row(first_shift), cross_bias, row(cross_out_bias), row(second_gain), row(second_shift),
             row(feed_in_bias), row(feed_out_bias), row(third_gain), row(third_shift)],
        )
        packed, small, memory_grad, input_grad = back_and_reduce(
            n, groups, rows_block,
            [in_grad, down_grad, cross_out_grad],
            [cross_values, memory_pieces, cross_pair_weight, first_low, cross_query_weight, g2, normal, self_out_weight,
             attended_t, keys, values, query, input_pieces, self_in_weight],
            [target_row, memory_row, cross_query, cross_grad, cross_keys,
             cross_lse, cross_delta, feed_sums, in_bias_grad, row(first_gain), rstd, lse],
        )
        (
            feed_in_grad, feed_out_grad, cross_out_total, cross_query_total, cross_pair_total,
            self_out_total, self_in_total, input_grad, memory_grad, layer_output, self_bias_grad,
            cross_bias_grad, in_bias_total, first_gain_grad, first_shift_grad, self_out_bias_grad,
            third_gain_grad, third_shift_grad, feed_out_bias_grad, second_gain_grad, second_shift_grad,
            cross_out_bias_grad,
        ) = finish_all(n, packed, small, input_grad, memory_grad, layer_output, hidden)
    else:
        packed, small, memory_grad, input_grad, layer_output, count_small = apart(
            n, groups, rows_block, input_rows, memory_rows, cotangent_rows, target_segments, memory_segments,
            self_in_weight, self_in_bias, self_out_weight, self_out_bias, first_gain, first_shift,
            cross_query_weight, cross_pair_weight, cross_bias, cross_out_weight, cross_out_bias,
            second_gain, second_shift, feed_in_weight, feed_in_bias, feed_out_weight, feed_out_bias,
            third_gain, third_shift,
        )
        plan = []
        start = 0
        shapes = []
        for height, columns in (
            (half, hidden // features), (hidden // n, 1), (half, 1), (half, 1), (half, 2), (half, 1), (half, 3)
        ):
            plan.append((start, columns))
            shapes.append(out_like((height, columns * features), F32))
            start += height * columns
        (
            feed_in_grad, feed_out_grad, cross_out_total, cross_query_total, cross_pair_total,
            self_out_total, self_in_total,
        ) = run(functools.partial(widen_kernel, plan), [packed], 0, shapes, [], 0, 12 << 20)
        rows_small = small[: count_small * half].reshape(count_small, half)
        (
            self_query_bias, self_value_bias, cross_query_bias, cross_value_bias, first_gain_grad,
            first_shift_grad, self_out_bias_grad, third_gain_grad, third_shift_grad, feed_out_bias_grad,
            second_gain_grad, second_shift_grad, cross_out_bias_grad,
        ) = [rows_small[index] for index in range(count_small)]
        self_bias_grad = jnp.stack([self_query_bias, self_value_bias])
        cross_bias_grad = jnp.stack([cross_query_bias, cross_value_bias])
        in_bias_total = small[count_small * half :]
    return (
        layer_output[None],
        input_grad[None],
        memory_grad[None],
        self_in_total,
        self_bias_grad,
        self_out_total,
        self_out_bias_grad,
        first_gain_grad,
        first_shift_grad,
        cross_query_total,
        cross_pair_total,
        cross_bias_grad,
        cross_out_total,
        cross_out_bias_grad,
        second_gain_grad,
        second_shift_grad,
        feed_in_grad,
        in_bias_total,
        feed_out_grad,
        feed_out_bias_grad,
        third_gain_grad,
        third_shift_grad,
    )


def solution(mesh):
    rows = P("dp", "blk", None)
    everywhere = P()
    split = P("blk", None)
    vector = P("blk")
    pair = P(None, "blk")
    return jax.shard_map(
        functools.partial(on_device, mesh.shape["blk"], mesh.shape["dp"]),
        mesh=mesh,
        in_specs=(rows, rows, rows, P("dp", None), P("dp", None)) + (everywhere,) * 19,
        out_specs=(
            rows, rows, rows, split, pair, split, vector, vector, vector, split, split, pair, split,
            vector, vector, vector, split, vector, split, vector, vector, vector,
        ),
        check_vma=False,
    )
```
